32 devices in a mesh: dp: 4 (over x, core), expert: 8 (over z, y).
Axes of the slice: x: 2, y: 2, z: 4, core: 2. Of those that a mesh axis runs over, the one named last changes fastest.
Arguments:
- designs: bfloat16 [4096, 1024], P(('dp', 'expert')), may hold values from -6 to 6
- archetype: int32 [4096, 1], P(('dp', 'expert')), may hold values from 0 to 3; in each aligned block of 128 rows (0 to 127, 128 to 255, ...) at most 36 rows name the same one
- w_gate: bfloat16 [1024, 16384], P(None, 'expert'), may hold values from -0.1875 to 0.1875
- w_up: bfloat16 [1024, 16384], P(None, 'expert'), may hold values from -0.1875 to 0.1875
- w_down: bfloat16 [16384, 1024], P('expert'), may hold values from -0.09375 to 0.09375
- cotangent: bfloat16 [4096, 1024], P(('dp', 'expert')), may hold values from -0.75 to 0.75
Outputs:
- outputs: bfloat16 [4096, 1024], P(('dp', 'expert'))
- grad_gate: bfloat16 [1024, 16384], P('dp', 'expert')
- grad_up: bfloat16 [1024, 16384], P('dp', 'expert')
The draws below stay inside these ranges and needn't reach their ends.
Inputs may be any that keep to these rules, and one draw needn't show every extreme that they name: In each aligned block of 128 rows (the rows of one device) no archetype is named by more than 36 rows.
All inputs are finite; a program needn't handle non-finite values.
Results may differ from the reference program's by a relative error of at most 0.009.
Values may be sent and summed in bfloat16 or wider, within the bound.
No kernel may reach another device: no remote copies, remote signals or barrier semaphores. Data moves between devices by JAX's collectives and lax.ppermute only.
A program may use at most 128 MiB of HBM per device.

```python
import math
import jax
import jax.numpy as jnp
import numpy as np
from jax import lax

D = 1024
FF = 4096
EXPERTS = 4
TOK_DEV = 128
CAP = 36
GROUP = 2
FF_DEV = 2048
ROWS = 4096
N_DP = 4
N_EXPERT = 8


def strengthened(entries, key, source, target, blocks, factor):
    owner, partner = [(jnp.arange(entries.shape[dim]) // (entries.shape[dim] // blocks)).reshape([-1 if axis == dim else 1 for axis in range(entries.ndim)]) for dim in (source, target)]
    chosen = jax.random.permutation(key, blocks)[partner]
    strong = (owner == chosen) | (owner == (partner + blocks // 2) % blocks)
    return jnp.where(strong, factor * entries, entries)


def shard_levels(rng, dims, cuts, least, largest):
    level = 1.0
    for dim, shards_of in cuts:
        heights = jax.random.uniform(jax.random.fold_in(jax.random.fold_in(rng, 6), dim), (shards_of,), jnp.float32, least / len(cuts), largest / len(cuts))
        level = level * jnp.repeat(jnp.exp(heights), dims[dim] // shards_of).reshape((-1,) + (1,) * (len(dims) - 1 - dim))
    return level


def assign_block(rng, own, number, rows, number_of, top, most, skew):
    order = jax.random.permutation(rng, number_of)
    packed, ordinary = shares(number_of, rows * top, most, skew, True), shares(number_of, rows * top, most, skew, False)
    places = jnp.arange(number_of)

    def named(sizes, turn):
        used = int((sizes > 0).sum())
        fixed = max(1, used // 4)
        shifted = fixed + (places - fixed + turn * (used - fixed)) % max(1, number_of - fixed)
        return jnp.zeros((number_of,), jnp.int32).at[order[jnp.where(places < fixed, places, shifted)]].set(jnp.asarray(sizes, jnp.int32))

    sizes = jnp.where(number % 4 == 0, named(packed, number // 4), named(ordinary, number - number // 4 - 1))
    mixed = jax.random.permutation(jax.random.fold_in(own, 3), number_of)
    donor, sink = mixed[0:number_of // 2 * 2:2], mixed[1:number_of // 2 * 2:2]
    room = jnp.minimum(sizes[donor] - 1, most - sizes[sink]) // 2
    room = jnp.where((donor == order[0]) | (sink == order[0]) | (sizes[sink] == 0), 0, jnp.maximum(room, 0))
    shifted = jax.random.randint(jax.random.fold_in(own, 4), (number_of // 2,), 0, 1 << 20) % (room + 1)
    sizes = sizes.at[donor].add(-shifted).at[sink].add(shifted)
    items = jnp.searchsorted(jnp.cumsum(sizes), jnp.arange(rows * top), side="right").astype(jnp.int32)
    table = items.reshape(top, rows).T
    table = table[jax.random.permutation(jax.random.fold_in(own, 1), rows)]
    turn = jax.random.randint(jax.random.fold_in(own, 2), (rows, 1), 0, top)
    return jnp.take_along_axis(table, (jnp.arange(top)[None, :] + turn) % top, axis=1)


def shares(amount, total, limit, skew, full):
    loads = [(1 << 20) // math.isqrt(rank ** skew) + 1 for rank in range(1, amount + 1)]
    largest = limit if full else min(limit, max(-(-total // amount), total * loads[0] // sum(loads)))
    least = 1 if total - largest >= amount - 1 else 0
    holding, rest = [largest] + [least] * (amount - 1), total - largest - least * (amount - 1)
    while rest > 0:
        movable = [i for i in range(1, amount) if holding[i] < largest] or [i for i in range(1, amount) if holding[i] < limit]
        whole, budget = sum([loads[i] for i in movable]), rest
        for i in movable:
            addition = min(limit - holding[i], max(1, budget * loads[i] // whole), rest)
            holding[i] = holding[i] + addition
            rest = rest - addition
    return np.array(holding)


def bell_draw(own_key, dims, scale, limit, pieces=(), held_as=jnp.bfloat16):
    gain = shard_levels(own_key, dims, pieces, -0.22, 0.18) if pieces else 1.0
    values = jax.random.normal(own_key, dims, jnp.float32) * scale * gain
    return jnp.minimum(jnp.maximum(values, -limit), limit).astype(held_as)


def gaussian_with(rng, dims, deviation, bound, shards, heavy, kind=jnp.bfloat16):
    drawn = deviation * jax.random.normal(rng, dims, jnp.float32)
    if shards:
        drawn = drawn * shard_levels(rng, dims, shards, -0.22, 0.18)
    return jnp.clip(strengthened(drawn, jax.random.fold_in(rng, 3), *heavy), -bound, bound).astype(kind)


def setup_inputs(seed: int = 0) -> dict:
    arg_keys = jax.random.split(jax.random.key(seed), 7)
    designs = gaussian_with(arg_keys[0], (ROWS, D), 1.0, 6.0, ((0, 32),), (0, 1, 32, 2.75))
    archetype_keys = jax.random.split(jax.random.fold_in(arg_keys[1], 1), ROWS // TOK_DEV)
    archetype_turns = jax.random.permutation(jax.random.fold_in(arg_keys[1], 3), ROWS // TOK_DEV)
    archetype = jax.vmap(lambda own, number: assign_block(jax.random.fold_in(arg_keys[1], 2), own, number, TOK_DEV, EXPERTS, 1, CAP, 2))(archetype_keys, archetype_turns).reshape((ROWS, 1))
    w_gate = bell_draw(arg_keys[2], (D, EXPERTS * FF), D ** -0.5, 0.1875, ((1, 8),))
    w_up = bell_draw(arg_keys[3], (D, EXPERTS * FF), D ** -0.5, 0.1875, ((1, 8),))
    w_down = bell_draw(arg_keys[4], (EXPERTS * FF, D), FF ** -0.5, 0.09375, ((0, 8),))
    cotangent = bell_draw(arg_keys[5], (ROWS, D), (4.0 * (EXPERTS / ROWS) ** 0.5), 0.75, ((0, 32),))
    return {"designs": designs, "archetype": archetype, "w_gate": w_gate, "w_up": w_up, "w_down": w_down, "cotangent": cotangent}


def silu_parts(gate):
    sigma = jax.nn.sigmoid(gate)
    return gate * sigma, sigma * (1.0 + gate * (1.0 - sigma))


def contract_rows(left, right):
    return lax.dot_general(left, right, (((0,), (0,)), ((), ())), preferred_element_type=jnp.float32)


def rounded(value):
    return lax.optimization_barrier(value.astype(jnp.bfloat16)).astype(jnp.float32)


def reference(designs, archetype, w_gate, w_up, w_down, cotangent):
    width = designs.shape[1]
    group_rows = N_EXPERT * TOK_DEV
    keep = N_EXPERT * CAP
    blocks_x = designs.reshape(N_DP, group_rows, width)
    blocks_g = cotangent.reshape(N_DP, group_rows, width)
    blocks_id = archetype.reshape(N_DP, group_rows)

    def one_group(carry, items):
        rows_x, rows_g, labels = items
        results = jnp.zeros((group_rows, width), jnp.float32)
        gate_terms = []
        up_terms = []
        for expert in range(EXPERTS):
            order = jnp.argsort((labels != expert).astype(jnp.int32), stable=True)[:keep].astype(jnp.int32)
            live = labels[order] == expert
            sel_x = jnp.where(live[:, None], rows_x[order], jnp.zeros((), jnp.bfloat16))
            sel_g = jnp.where(live[:, None], rows_g[order], jnp.zeros((), jnp.bfloat16))
            first = expert * FF
            gate = jnp.dot(sel_x, w_gate[:, first:first + FF], preferred_element_type=jnp.float32)
            up = jnp.dot(sel_x, w_up[:, first:first + FF], preferred_element_type=jnp.float32)
            act, slope = silu_parts(gate)
            hidden = (act * up).astype(jnp.bfloat16)
            down_rows = w_down[first:first + FF, :]
            result = jnp.zeros((keep, width), jnp.float32)
            for block in range(GROUP):
                lower = block * FF_DEV
                piece = jnp.dot(hidden[:, lower:lower + FF_DEV], down_rows[lower:lower + FF_DEV, :], preferred_element_type=jnp.float32)
                result = result + rounded(piece)
            results = results.at[order].add(jnp.where(live[:, None], result, jnp.zeros((), jnp.float32)))
            d_hidden = lax.dot_general(sel_g, down_rows, (((1,), (1,)), ((), ())), preferred_element_type=jnp.float32)
            d_gate = (d_hidden * up * slope).astype(jnp.bfloat16)
            d_up = (d_hidden * act).astype(jnp.bfloat16)
            gate_terms.append(contract_rows(sel_x, d_gate))
            up_terms.append(contract_rows(sel_x, d_up))
        sum_gate = carry[0] + rounded(jnp.concatenate(gate_terms, axis=1))
        sum_up = carry[1] + rounded(jnp.concatenate(up_terms, axis=1))
        return (sum_gate, sum_up), results.astype(jnp.bfloat16)

    start = (jnp.zeros((width, EXPERTS * FF), jnp.float32), jnp.zeros((width, EXPERTS * FF), jnp.float32))
    totals, outputs = lax.scan(one_group, start, (blocks_x, blocks_g, blocks_id))
    return (outputs.reshape(ROWS, width), totals[0].astype(jnp.bfloat16), totals[1].astype(jnp.bfloat16))
```

```python
import functools

import jax
import jax.numpy as jnp
from jax import lax
from jax.experimental import pallas as pl
from jax.experimental.pallas import tpu as pltpu
from jax.sharding import Mesh
from jax.sharding import PartitionSpec as P

EXPERTS = 4
CAP = 36
SLOT = 40
BLOCK = 256
VMEM_LIMIT = 48 * 1024 * 1024
F32 = jnp.float32
BF16 = jnp.bfloat16


def silu_parts(gate):
    sigma = jax.nn.sigmoid(gate)
    return (gate * sigma, sigma * (1.0 + gate * (1.0 - sigma)))


def contract_rows(left, right):
    return lax.dot_general(left, right, (((0,), (0,)), ((), ())), preferred_element_type=F32)


def contract_cols(left, right):
    return lax.dot_general(left, right, (((1,), (1,)), ((), ())), preferred_element_type=F32)


def pack_kernel(plane_ref, kind_ref, x_ref, g_ref, *outs):
    rows = kind_ref.shape[0]
    key = kind_ref[...] ^ plane_ref[0]
    lane = lax.broadcasted_iota(jnp.int32, (rows, 128), 1)
    onehot = (key == lane).astype(F32)
    below = lax.broadcasted_iota(jnp.int32, (rows, rows), 0) > lax.broadcasted_iota(
        jnp.int32, (rows, rows), 1
    )
    ranks = jnp.dot(below.astype(BF16), onehot.astype(BF16), preferred_element_type=F32)
    rank = jnp.sum(ranks * onehot, axis=1, keepdims=True).astype(jnp.int32)
    place = key * SLOT + rank
    slots = EXPERTS * SLOT
    chosen = (place == lax.broadcasted_iota(jnp.int32, (rows, slots), 1)).astype(F32)
    outs[2 * EXPERTS][...] = chosen.astype(BF16)
    placer = chosen.T.astype(BF16)
    for source, first in ((x_ref, 0), (g_ref, EXPERTS)):
        packed = jnp.dot(placer, source[...], preferred_element_type=F32)
        for k in range(EXPERTS):
            outs[first + k][...] = packed[k * SLOT : (k + 1) * SLOT].astype(BF16)


def pack(plane, kind, x, g):
    rows, width = x.shape
    block = jax.ShapeDtypeStruct((SLOT, width), BF16)
    return pl.pallas_call(
        pack_kernel,
        out_shape=[block] * (2 * EXPERTS) + [jax.ShapeDtypeStruct((rows, EXPERTS * SLOT), BF16)],
        in_specs=[pl.BlockSpec(memory_space=pltpu.SMEM)] + [pl.BlockSpec(memory_space=pltpu.VMEM)] * 3,
        name="pack",
    )(plane, kind, x, g)


def forward_kernel(with_down, xa_ref, xb_ref, wg_ref, wu_ref, wd_ref, *refs):
    if with_down:
        act_ref, coef_ref, sa_ref, sb_ref, x_ref, acc_ref = refs
    else:
        act_ref, coef_ref, x_ref = refs
    step = pl.program_id(0)
    half = xa_ref.shape[0]

    @pl.when(step == 0)
    def _():
        x_ref[:half, :] = xa_ref[...]
        x_ref[half:, :] = xb_ref[...]

    x = x_ref[...]
    gate = jnp.dot(x, wg_ref[...], preferred_element_type=F32)
    up = jnp.dot(x, wu_ref[...], preferred_element_type=F32)
    act, slope = silu_parts(gate)
    act_ref[...] = act.astype(BF16)
    coef_ref[...] = (up * slope).astype(BF16)
    if with_down:
        hidden = (act * up).astype(BF16)
        part = jnp.dot(hidden, wd_ref[...], preferred_element_type=F32)

        @pl.when(step == 0)
        def _():
            acc_ref[...] = part

        @pl.when(step > 0)
        def _():
            acc_ref[...] += part

        @pl.when(step == pl.num_programs(0) - 1)
        def _():
            sa_ref[...] = acc_ref[:half, :].astype(BF16)
            sb_ref[...] = acc_ref[half:, :].astype(BF16)


def forward(xa, xb, wg, wu, wd, with_down):
    half, width = xa.shape
    cols = wg.shape[1]
    rows = 2 * half
    whole = pl.BlockSpec((half, width), lambda j: (0, 0))
    wide = pl.BlockSpec((rows, BLOCK), lambda j: (0, j))
    out_shape = [jax.ShapeDtypeStruct((rows, cols), BF16)] * 2
    out_specs = [wide, wide]
    scratch = [pltpu.VMEM((rows, width), BF16)]
    if with_down:
        out_shape += [jax.ShapeDtypeStruct((half, width), BF16)] * 2
        out_specs += [whole, whole]
        scratch += [pltpu.VMEM((rows, width), F32)]
    count = 3 if with_down else 2
    down_spec = pl.BlockSpec((BLOCK, width), (lambda j: (j, 0)) if with_down else (lambda j: (0, 0)))
    return pl.pallas_call(
        functools.partial(forward_kernel, with_down),
        grid=(cols // BLOCK,),
        in_specs=[
            whole,
            whole,
            pl.BlockSpec((width, BLOCK), lambda j: (0, j)),
            pl.BlockSpec((width, BLOCK), lambda j: (0, j)),
            down_spec,
        ],
        out_specs=out_specs,
        out_shape=out_shape,
        scratch_shapes=scratch,
        compiler_params=pltpu.CompilerParams(vmem_limit_bytes=VMEM_LIMIT),
        cost_estimate=pl.CostEstimate(
            flops=2 * count * rows * width * cols,
            bytes_accessed=2 * count * width * cols + 4 * rows * cols,
            transcendentals=rows * cols,
        ),
        name="forward_down" if with_down else "forward",
    )(xa, xb, wg, wu, wd)


def backward_kernel(where_ref, *refs):
    xs, gs = refs[0:4], refs[4:8]
    act0, coef0, act1, coef1, wd_ref = refs[8:13]
    own_gate, own_up, sib_gate, sib_up = refs[13:17]
    g_ref, xt_ref = refs[17:19]
    part = xs[0].shape[0]
    share = own_gate.shape[0]

    @pl.when(pl.program_id(0) == 0)
    def _():
        for i in range(4):
            g_ref[i * part : (i + 1) * part, :] = gs[i][...]
        whole = jnp.concatenate([x[...].astype(F32) for x in xs], axis=0)
        xt_ref[...] = whole.T.astype(BF16)

    d_hidden = contract_cols(g_ref[...], wd_ref[...])
    act = jnp.concatenate([act0[...], act1[...]], axis=0).astype(F32)
    coef = jnp.concatenate([coef0[...], coef1[...]], axis=0).astype(F32)
    d_gate = (d_hidden * coef).astype(BF16)
    d_up = (d_hidden * act).astype(BF16)
    mine = pl.multiple_of(where_ref[1] * share, share)
    other = pl.multiple_of((1 - where_ref[1]) * share, share)
    x_mine = xt_ref[pl.ds(mine, share), :]
    x_other = xt_ref[pl.ds(other, share), :]
    sib_gate[...] = jnp.dot(x_other, d_gate, preferred_element_type=F32).astype(BF16)
    sib_up[...] = jnp.dot(x_other, d_up, preferred_element_type=F32).astype(BF16)
    own_gate[...] = jnp.dot(x_mine, d_gate, preferred_element_type=F32).astype(BF16)
    own_up[...] = jnp.dot(x_mine, d_up, preferred_element_type=F32).astype(BF16)


def backward(where, xs, gs, act0, coef0, act1, coef1, wd, share):
    part, width = xs[0].shape
    cols = wd.shape[0]
    rows = 4 * part
    half = 2 * share
    wide = pl.BlockSpec((2 * part, BLOCK), lambda j, w: (0, j))
    grad = pl.BlockSpec((share, BLOCK), lambda j, w: (0, j))
    return pl.pallas_call(
        backward_kernel,
        grid_spec=pltpu.PrefetchScalarGridSpec(
            num_scalar_prefetch=1,
            grid=(cols // BLOCK,),
            in_specs=[pl.BlockSpec((part, half), lambda j, w: (0, w[0]))] * 4
            + [pl.BlockSpec((part, width), lambda j, w: (0, 0))] * 4
            + [wide] * 4
            + [pl.BlockSpec((BLOCK, width), lambda j, w: (j, 0))],
            out_specs=[grad] * 4,
            scratch_shapes=[pltpu.VMEM((rows, width), BF16), pltpu.VMEM((half, rows), BF16)],
        ),
        out_shape=[jax.ShapeDtypeStruct((share, cols), BF16)] * 4,
        compiler_params=pltpu.CompilerParams(vmem_limit_bytes=VMEM_LIMIT),
        cost_estimate=pl.CostEstimate(
            flops=2 * rows * cols * (width + 2 * half),
            bytes_accessed=2 * width * cols + 8 * rows * cols + 8 * share * cols,
            transcendentals=0,
        ),
        name="backward",
    )(where, *xs, *gs, act0, coef0, act1, coef1, wd)


def combine_kernel(mine_ref, theirs_ref, *outs):
    total = mine_ref[...].astype(F32) + theirs_ref[...].astype(F32)
    for k in range(EXPERTS):
        outs[k][...] = total[k * SLOT : (k + 1) * SLOT].astype(BF16)


def combine(mine, theirs):
    width = mine.shape[1]
    return pl.pallas_call(
        combine_kernel,
        out_shape=[jax.ShapeDtypeStruct((SLOT, width), BF16)] * EXPERTS,
        name="combine",
    )(mine, theirs)


def unpack_kernel(chosen_ref, *refs):
    parts = [r[...].astype(F32) for r in refs[:EXPERTS]]
    packed = jnp.concatenate(parts, axis=0).astype(BF16)
    refs[EXPERTS][...] = jnp.dot(chosen_ref[...], packed, preferred_element_type=F32).astype(BF16)


def unpack(chosen, parts):
    width = parts[0].shape[1]
    return pl.pallas_call(
        unpack_kernel,
        out_shape=jax.ShapeDtypeStruct((chosen.shape[0], width), BF16),
        name="unpack",
    )(chosen, *parts)


def swap(value, axes, sizes):
    count = 1
    for size in sizes:
        count *= size
    return lax.ppermute(value, axes, [(i, i ^ (count - 1)) for i in range(count)])


def to_planes(blocks):
    moved = [blocks[0]]
    for k in range(1, EXPERTS):
        moved.append(lax.ppermute(blocks[k], "arch", [(i, i ^ k) for i in range(EXPERTS)]))
    return moved


def gathering(designs, archetype, w_gate, w_up, w_down, cotangent):
    plane = lax.axis_index("arch").astype(jnp.int32)
    far = lax.axis_index("far").astype(jnp.int32)
    core = lax.axis_index("core").astype(jnp.int32)
    width = designs.shape[1]
    share = width // 4
    packed = pack(plane[None], archetype, designs, cotangent)
    chosen = packed[2 * EXPERTS]
    groups = []
    for blocks in (packed[:EXPERTS], packed[EXPERTS : 2 * EXPERTS]):
        own = jnp.concatenate(to_planes(blocks), axis=0)
        near = swap(own, "half", (2,))
        across = swap(own, "far", (2,))
        corner = swap(own, ("far", "half"), (2, 2))
        groups.append([own, near, across, corner])
    xs, gs = groups
    act0, coef0, share_own, share_near = forward(xs[0], xs[1], w_gate, w_up, w_down, True)
    returned = swap(share_near, "half", (2,))
    act1, coef1 = forward(xs[2], xs[3], w_gate, w_up, w_down, False)
    outputs = unpack(chosen, to_planes(combine(share_own, returned)))
    own_gate, own_up, sib_gate, sib_up = backward(
        jnp.stack([far, core]), xs, gs, act0, coef0, act1, coef1, w_down, share
    )
    got_gate = swap(sib_gate, "core", (2,))
    got_up = swap(sib_up, "core", (2,))
    grad_gate = (own_gate.astype(F32) + got_gate.astype(F32)).astype(BF16)
    grad_up = (own_up.astype(F32) + got_up.astype(F32)).astype(BF16)
    return outputs, grad_gate, grad_up


def reducing(designs, archetype, w_gate, w_up, w_down, cotangent):
    width = designs.shape[1]
    owners = lax.axis_size("expert")
    sharers = owners // EXPERTS
    hidden_cols = w_gate.shape[1]
    labels = archetype[:, 0]
    onehot = (labels[:, None] == jnp.arange(EXPERTS, dtype=jnp.int32)[None, :]).astype(jnp.int32)
    ranks = jnp.cumsum(onehot, axis=0) - onehot
    target = labels * CAP + jnp.sum(ranks * onehot, axis=1)
    placer = (jnp.arange(EXPERTS * CAP, dtype=jnp.int32)[:, None] == target[None, :]).astype(BF16)
    received = []
    for rows in (designs, cotangent):
        packed = jnp.dot(placer, rows, preferred_element_type=F32).astype(BF16)
        send = jnp.repeat(packed.reshape(EXPERTS, CAP, width), sharers, axis=0)
        received.append(
            lax.all_to_all(send, "expert", split_axis=0, concat_axis=0, tiled=True).reshape(
                owners * CAP, width
            )
        )
    flat_x, flat_g = received
    gate = jnp.dot(flat_x, w_gate, preferred_element_type=F32)
    up = jnp.dot(flat_x, w_up, preferred_element_type=F32)
    act, slope = silu_parts(gate)
    hidden = (act * up).astype(BF16)
    partial_value = (
        jnp.dot(hidden, w_down, preferred_element_type=F32).astype(BF16).reshape(owners, CAP, width)
    )
    returned = lax.all_to_all(partial_value, "expert", split_axis=0, concat_axis=0, tiled=True)
    summed = jnp.sum(returned.astype(F32).reshape(EXPERTS, sharers, CAP, width), axis=1).reshape(
        EXPERTS * CAP, width
    )
    outputs = jnp.take(summed, target, axis=0).astype(BF16)
    d_hidden = contract_cols(flat_g, w_down)
    d_gate = (d_hidden * up * slope).astype(BF16)
    d_up = (d_hidden * act).astype(BF16)
    grads = jnp.concatenate([contract_rows(flat_x, d_gate), contract_rows(flat_x, d_up)], axis=1)
    mine = lax.psum_scatter(grads.astype(BF16), "dp", scatter_dimension=0, tiled=True)
    return outputs, mine[:, :hidden_cols], mine[:, hidden_cols:]


def solution(mesh):
    dp, owners = mesh.devices.shape
    if (dp, owners) == (4, 2 * EXPERTS):
        rows, cols = ("far", "core"), ("arch", "half")
        mesh = Mesh(mesh.devices.reshape(2, 2, EXPERTS, 2), rows + cols)
        body = gathering
    else:
        rows, cols = ("dp",), ("expert",)
        body = reducing
    tokens = P(rows + cols, None)
    return jax.shard_map(
        body,
        mesh=mesh,
        in_specs=(tokens, tokens, P(None, cols), P(None, cols), P(cols, None), tokens),
        out_specs=(tokens, P(rows, cols), P(rows, cols)),
        check_vma=False,
    )
```

```python
import functools

import jax
import jax.numpy as jnp
from jax import lax
from jax.experimental import pallas as pl
from jax.experimental.pallas import tpu as pltpu
from jax.sharding import Mesh
from jax.sharding import PartitionSpec as P

EXPERTS = 4
CAP = 36
BLOCK = 512
STRIP = 256
VMEM_LIMIT = 24 * 1024 * 1024
F32 = jnp.float32
BF16 = jnp.bfloat16


def silu_parts(gate):
    sigma = 0.5 * jnp.tanh(0.5 * gate) + 0.5
    return (gate * sigma, sigma * (1.0 + gate * (1.0 - sigma)))


def contract_rows(left, right):
    return lax.dot_general(left, right, (((0,), (0,)), ((), ())), preferred_element_type=F32)


def contract_cols(left, right):
    return lax.dot_general(left, right, (((1,), (1,)), ((), ())), preferred_element_type=F32)


def stacked(values):
    return jnp.concatenate([v.astype(F32) for v in values], axis=0).astype(BF16)


def pack_kernel(plane_ref, kind_ref, x_ref, g_ref, placer_ref, *outs):
    tokens = kind_ref.shape[1]
    key = kind_ref[...] ^ plane_ref[0]
    onehot = (key == lax.broadcasted_iota(jnp.int32, (8, tokens), 0)).astype(F32)
    before = lax.broadcasted_iota(jnp.int32, (tokens, tokens), 0) < lax.broadcasted_iota(
        jnp.int32, (tokens, tokens), 1
    )
    ranks = jnp.dot(onehot.astype(BF16), before.astype(BF16), preferred_element_type=F32)
    rank = jnp.sum(ranks * onehot, axis=0, keepdims=True).astype(jnp.int32)
    place = key * CAP + rank
    slots = EXPERTS * CAP
    placer = (place == lax.broadcasted_iota(jnp.int32, (slots, tokens), 0)).astype(F32)
    placer_ref[...] = placer.astype(BF16)
    placer = placer.astype(BF16)
    packed_x = jnp.dot(placer, x_ref[...], preferred_element_type=F32)
    packed_g = jnp.dot(placer, g_ref[...], preferred_element_type=F32)
    for k in range(EXPERTS):
        rows = slice(k * CAP, (k + 1) * CAP)
        outs[k][...] = jnp.concatenate([packed_x[rows], packed_g[rows]], axis=0).astype(BF16)


def pack(plane, kind, x, g):
    tokens, width = x.shape
    return pl.pallas_call(
        pack_kernel,
        out_shape=[jax.ShapeDtypeStruct((EXPERTS * CAP, tokens), BF16)]
        + [jax.ShapeDtypeStruct((2 * CAP, width), BF16)] * EXPERTS,
        in_specs=[pl.BlockSpec(memory_space=pltpu.SMEM)] + [pl.BlockSpec(memory_space=pltpu.VMEM)] * 3,
        name="pack",
    )(plane, kind, x, g)


def split_kernel(*refs):
    blocks = [r[...].astype(F32) for r in refs[:EXPERTS]]
    refs[EXPERTS][...] = jnp.concatenate([b[:CAP] for b in blocks], axis=0).astype(BF16)
    refs[EXPERTS + 1][...] = jnp.concatenate([b[CAP:] for b in blocks], axis=0).astype(BF16)


def split(blocks):
    width = blocks[0].shape[1]
    return pl.pallas_call(
        split_kernel,
        out_shape=[jax.ShapeDtypeStruct((EXPERTS * CAP, width), BF16)] * 2,
        name="split",
    )(*blocks)


def slopes(x, g, wg, wu, wd):
    gate = jnp.dot(x, wg, preferred_element_type=F32)
    up = jnp.dot(x, wu, preferred_element_type=F32)
    d_hidden = contract_cols(g, wd)
    act, slope = silu_parts(gate)
    d_gate = (d_hidden * (up * slope)).astype(BF16)
    d_up = (d_hidden * act).astype(BF16)
    return (act * up).astype(BF16), d_gate, d_up


def chunk_kernel(n, *refs):
    xs, gs = refs[:n], refs[n : 2 * n]
    wg_ref, wu_ref, wd_ref, dg_ref, du_ref = refs[2 * n : 2 * n + 5]
    shares = refs[2 * n + 5 : 2 * n + 5 + EXPERTS]
    x_ref, g_ref, acc_ref = refs[2 * n + 5 + EXPERTS :]
    part = xs[0].shape[0]
    step = pl.program_id(0)

    @pl.when(step == 0)
    def _():
        for i in range(n):
            x_ref[i * part : (i + 1) * part, :] = xs[i][...]
            g_ref[i * part : (i + 1) * part, :] = gs[i][...]
        acc_ref[...] = jnp.zeros_like(acc_ref)

    x, g = x_ref[...], g_ref[...]
    total = acc_ref[...]
    for first in range(0, BLOCK, STRIP):
        cols = slice(first, first + STRIP)
        hidden, d_gate, d_up = slopes(x, g, wg_ref[:, cols], wu_ref[:, cols], wd_ref[cols, :])
        dg_ref[:, cols] = d_gate
        du_ref[:, cols] = d_up
        total += jnp.dot(hidden[:part], wd_ref[cols, :], preferred_element_type=F32)
    acc_ref[...] = total

    @pl.when(step == pl.num_programs(0) - 1)
    def _():
        for k in range(EXPERTS):
            shares[k][...] = total[k * CAP : (k + 1) * CAP].astype(BF16)


def chunk(xs, gs, wg, wu, wd):
    n = len(xs)
    part, width = xs[0].shape
    cols = wg.shape[1]
    rows = n * part
    whole = pl.BlockSpec((part, width), lambda j: (0, 0))
    wide = pl.BlockSpec((rows, BLOCK), lambda j: (0, j))
    deep = pl.BlockSpec((width, BLOCK), lambda j: (0, j))
    return pl.pallas_call(
        functools.partial(chunk_kernel, n),
        grid=(cols // BLOCK,),
        in_specs=[whole] * (2 * n) + [deep, deep, pl.BlockSpec((BLOCK, width), lambda j: (j, 0))],
        out_specs=[wide, wide] + [pl.BlockSpec((CAP, width), lambda j: (0, 0))] * EXPERTS,
        out_shape=[jax.ShapeDtypeStruct((rows, cols), BF16)] * 2
        + [jax.ShapeDtypeStruct((CAP, width), BF16)] * EXPERTS,
        scratch_shapes=[pltpu.VMEM((rows, width), BF16)] * 2 + [pltpu.VMEM((part, width), F32)],
        compiler_params=pltpu.CompilerParams(vmem_limit_bytes=VMEM_LIMIT),
        cost_estimate=pl.CostEstimate(
            flops=2 * (3 * rows + part) * width * cols,
            bytes_accessed=6 * width * cols + 4 * rows * cols,
            transcendentals=rows * cols,
        ),
        name="chunk",
    )(*xs, *gs, wg, wu, wd)


def grads_kernel(where_ref, *refs):
    own_x, sib_x = refs[0:4], refs[4:8]
    x_ref, g_ref, dg0, du0, dg1, du1, wg_ref, wu_ref, wd_ref, own_ref, sib_ref = refs[8:19]
    xt_ref, dg_ref, du_ref = refs[19:]
    part = x_ref.shape[0]
    share = own_ref.shape[0] // 2

    @pl.when(pl.program_id(0) == 0)
    def _():
        for first, blocks in ((0, own_x), (share, sib_x)):
            whole = jnp.concatenate([b[...].astype(F32) for b in blocks], axis=0)
            xt_ref[first : first + share, :] = whole.T.astype(BF16)

    _, d_gate, d_up = slopes(x_ref[...], g_ref[...], wg_ref[...], wu_ref[...], wd_ref[...])
    for whole, parts in ((dg_ref, (dg0[...], dg1[...], d_gate)), (du_ref, (du0[...], du1[...], d_up))):
        first = 0
        for value in parts:
            whole[first : first + value.shape[0], :] = value
            first += value.shape[0]
    for row, whole in ((0, dg_ref), (share, du_ref)):
        total = jnp.dot(xt_ref[...], whole[...], preferred_element_type=F32).astype(BF16)
        own_ref[row : row + share, :] = total[:share]
        sib_ref[row : row + share, :] = total[share:]


def grads(where, xs, g, dg0, du0, dg1, du1, wg, wu, wd, share, first, cols):
    part, width = xs[0].shape
    rows = 4 * part
    base = first // STRIP
    whole = pl.BlockSpec((part, width), lambda j, w: (0, 0))
    one = pl.BlockSpec((part, STRIP), lambda j, w: (0, base + j))
    two = pl.BlockSpec((2 * part, STRIP), lambda j, w: (0, base + j))
    deep = pl.BlockSpec((width, STRIP), lambda j, w: (0, base + j))
    out = pl.BlockSpec((2 * share, STRIP), lambda j, w: (0, j))
    return pl.pallas_call(
        grads_kernel,
        grid_spec=pltpu.PrefetchScalarGridSpec(
            num_scalar_prefetch=1,
            grid=(cols // STRIP,),
            in_specs=[pl.BlockSpec((part, share), lambda j, w: (0, w[0]))] * 4
            + [pl.BlockSpec((part, share), lambda j, w: (0, w[1]))] * 4
            + [whole, whole, one, one, two, two, deep, deep]
            + [pl.BlockSpec((STRIP, width), lambda j, w: (base + j, 0))],
            out_specs=[out, out],
            scratch_shapes=[pltpu.VMEM((2 * share, rows), BF16)] + [pltpu.VMEM((rows, STRIP), BF16)] * 2,
        ),
        out_shape=[jax.ShapeDtypeStruct((2 * share, cols), BF16)] * 2,
        compiler_params=pltpu.CompilerParams(vmem_limit_bytes=VMEM_LIMIT),
        cost_estimate=pl.CostEstimate(
            flops=2 * cols * (3 * part * width + 4 * rows * share),
            bytes_accessed=6 * width * cols + 4 * rows * cols + 8 * share * cols,
            transcendentals=part * cols,
        ),
        name="grads",
    )(where, *xs, *xs, xs[3], g, dg0, du0, dg1, du1, wg, wu, wd)


def finish_kernel(*refs):
    gate_ref, up_ref = refs[8:]
    half = refs[0].shape[1]
    for i in range(2):
        cols = slice(i * half, (i + 1) * half)
        own_gate, own_up, got_gate, got_up = [r[...].astype(F32) for r in refs[4 * i : 4 * i + 4]]
        gate_ref[:, cols] = (own_gate + got_gate).astype(BF16)
        up_ref[:, cols] = (own_up + got_up).astype(BF16)


def finish(own0, got0, own1, got1):
    share, half = own0.shape[0] // 2, own0.shape[1]
    steps = 4
    lines = share // steps
    upper = pl.BlockSpec((lines, half), lambda i: (i, 0))
    lower = pl.BlockSpec((lines, half), lambda i: (i + steps, 0))
    return pl.pallas_call(
        finish_kernel,
        grid=(steps,),
        in_specs=[upper, lower] * 4,
        out_specs=[pl.BlockSpec((lines, 2 * half), lambda i: (i, 0))] * 2,
        out_shape=[jax.ShapeDtypeStruct((share, 2 * half), BF16)] * 2,
        name="finish",
    )(own0, own0, got0, got0, own1, own1, got1, got1)


def unpack_kernel(placer_ref, *refs):
    mine = stacked([r[...] for r in refs[:EXPERTS]])
    theirs = stacked([r[...] for r in refs[EXPERTS : 2 * EXPERTS]])
    chosen = placer_ref[...].astype(F32).T.astype(BF16)
    total = jnp.dot(chosen, mine, preferred_element_type=F32)
    total += jnp.dot(chosen, theirs, preferred_element_type=F32)
    refs[2 * EXPERTS][...] = total.astype(BF16)


def unpack(placer, mine, theirs):
    width = mine[0].shape[1]
    return pl.pallas_call(
        unpack_kernel,
        out_shape=jax.ShapeDtypeStruct((placer.shape[1], width), BF16),
        name="unpack",
    )(placer, *mine, *theirs)


def swap(value, axis):
    return lax.ppermute(value, axis, [(0, 1), (1, 0)])


def across_planes(value, k):
    return lax.ppermute(value, "arch", [(i, i ^ k) for i in range(EXPERTS)])


def across_planes_and_halves(value, k):
    return lax.ppermute(value, ("arch", "half"), [(i, i ^ (2 * k + 1)) for i in range(2 * EXPERTS)])


def gathering(designs, archetype, w_gate, w_up, w_down, cotangent):
    plane = lax.axis_index("arch").astype(jnp.int32)
    far = lax.axis_index("far").astype(jnp.int32)
    core = lax.axis_index("core").astype(jnp.int32)
    tokens, width = designs.shape
    cols = w_gate.shape[1]
    share = width // 4
    weights = (w_gate, w_up, w_down)
    placer, *blocks = pack(plane[None], archetype.reshape(1, tokens), designs, cotangent)
    moved = {k: across_planes(blocks[k], k) for k in (3, 2, 1)}
    x_own, g_own = split([blocks[0], moved[1], moved[2], moved[3]])
    x_near = swap(x_own, "half")
    g_far = swap(g_own, "far")
    x_far = swap(x_own, "far")
    g_near = swap(g_own, "half")
    x_corner = swap(x_near, "far")
    g_corner = swap(g_far, "half")
    dg0, du0, *shares = chunk([x_own], [g_own], *weights)
    mine = [shares[0]] + [across_planes(shares[k], k) for k in range(1, EXPERTS)]
    dg1, du1, *shares = chunk([x_near, x_far], [g_near, g_far], *weights)
    theirs = [across_planes_and_halves(shares[k], k) for k in range(EXPERTS)]
    where = jnp.stack([2 * far + core, 2 * far + 1 - core])
    xs = [x_own, x_near, x_far, x_corner]
    half = cols // 2
    where, *mine = lax.optimization_barrier((where, *mine))
    own0, sib0 = grads(where, xs, g_corner, dg0, du0, dg1, du1, *weights, share, 0, half)
    got0 = swap(sib0, "core")
    own1, sib1 = grads(where, xs, g_corner, dg0, du0, dg1, du1, *weights, share, half, half)
    got1 = swap(sib1, "core")
    grad_gate, grad_up = finish(own0, got0, own1, got1)
    return unpack(placer, mine, theirs), grad_gate, grad_up


def reducing(designs, archetype, w_gate, w_up, w_down, cotangent):
    width = designs.shape[1]
    owners = lax.axis_size("expert")
    sharers = owners // EXPERTS
    hidden_cols = w_gate.shape[1]
    labels = archetype[:, 0]
    onehot = (labels[:, None] == jnp.arange(EXPERTS, dtype=jnp.int32)[None, :]).astype(jnp.int32)
    ranks = jnp.cumsum(onehot, axis=0) - onehot
    target = labels * CAP + jnp.sum(ranks * onehot, axis=1)
    placer = (jnp.arange(EXPERTS * CAP, dtype=jnp.int32)[:, None] == target[None, :]).astype(BF16)
    received = []
    for rows in (designs, cotangent):
        packed = jnp.dot(placer, rows, preferred_element_type=F32).astype(BF16)
        send = jnp.repeat(packed.reshape(EXPERTS, CAP, width), sharers, axis=0)
        received.append(
            lax.all_to_all(send, "expert", split_axis=0, concat_axis=0, tiled=True).reshape(
                owners * CAP, width
            )
        )
    flat_x, flat_g = received
    gate = jnp.dot(flat_x, w_gate, preferred_element_type=F32)
    up = jnp.dot(flat_x, w_up, preferred_element_type=F32)
    act, slope = silu_parts(gate)
    hidden = (act * up).astype(BF16)
    partial_value = (
        jnp.dot(hidden, w_down, preferred_element_type=F32).astype(BF16).reshape(owners, CAP, width)
    )
    returned = lax.all_to_all(partial_value, "expert", split_axis=0, concat_axis=0, tiled=True)
    summed = jnp.sum(returned.astype(F32).reshape(EXPERTS, sharers, CAP, width), axis=1).reshape(
        EXPERTS * CAP, width
    )
    outputs = jnp.take(summed, target, axis=0).astype(BF16)
    d_hidden = contract_cols(flat_g, w_down)
    d_gate = (d_hidden * up * slope).astype(BF16)
    d_up = (d_hidden * act).astype(BF16)
    grads = jnp.concatenate([contract_rows(flat_x, d_gate), contract_rows(flat_x, d_up)], axis=1)
    mine = lax.psum_scatter(grads.astype(BF16), "dp", scatter_dimension=0, tiled=True)
    return outputs, mine[:, :hidden_cols], mine[:, hidden_cols:]


def solution(mesh):
    dp, owners = mesh.devices.shape
    if (dp, owners) == (4, 2 * EXPERTS):
        rows, cols = ("far", "core"), ("arch", "half")
        mesh = Mesh(mesh.devices.reshape(2, 2, EXPERTS, 2), rows + cols)
        body = gathering
    else:
        rows, cols = ("dp",), ("expert",)
        body = reducing
    tokens = P(rows + cols, None)
    return jax.shard_map(
        body,
        mesh=mesh,
        in_specs=(tokens, tokens, P(None, cols), P(None, cols), P(cols, None), tokens),
        out_specs=(tokens, P(rows, cols), P(rows, cols)),
        check_vma=False,
    )
```

```python
import functools

import jax
import jax.numpy as jnp
from jax import lax
from jax.experimental import pallas as pl
from jax.experimental.pallas import tpu as pltpu
from jax.sharding import Mesh
from jax.sharding import PartitionSpec as P

EXPERTS = 4
CAP = 36
BLOCK = 512
STRIP = 256
MIB = 1024 * 1024
LARGE = pltpu.CompilerParams(vmem_limit_bytes=54 * MIB)
CHEAP = pl.CostEstimate(flops=0, bytes_accessed=0, transcendentals=0)
SMALL = pltpu.CompilerParams(vmem_limit_bytes=12 * MIB)
F32 = jnp.float32
BF16 = jnp.bfloat16


def silu_parts(gate):
    sigma = 0.5 * jnp.tanh(0.5 * gate) + 0.5
    return (gate * sigma, sigma * (1.0 + gate * (1.0 - sigma)))


def contract_rows(left, right):
    return lax.dot_general(left, right, (((0,), (0,)), ((), ())), preferred_element_type=F32)


def contract_cols(left, right):
    return lax.dot_general(left, right, (((1,), (1,)), ((), ())), preferred_element_type=F32)


def stacked(refs):
    return jnp.concatenate([r[...].astype(F32) for r in refs], axis=0)


def pack_kernel(plane_ref, kind_ref, x_ref, g_ref, placer_ref, *outs):
    tokens = kind_ref.shape[1]
    key = kind_ref[...] ^ plane_ref[0]
    onehot = (key == lax.broadcasted_iota(jnp.int32, (8, tokens), 0)).astype(F32)
    before = lax.broadcasted_iota(jnp.int32, (tokens, tokens), 0) < lax.broadcasted_iota(
        jnp.int32, (tokens, tokens), 1
    )
    ranks = jnp.dot(onehot.astype(BF16), before.astype(BF16), preferred_element_type=F32)
    rank = jnp.sum(ranks * onehot, axis=0, keepdims=True).astype(jnp.int32)
    place = key * CAP + rank
    slots = EXPERTS * CAP
    placer = (place == lax.broadcasted_iota(jnp.int32, (slots, tokens), 0)).astype(F32).astype(BF16)
    placer_ref[...] = placer
    for source, first in ((x_ref, 0), (g_ref, EXPERTS)):
        packed = jnp.dot(placer, source[...], preferred_element_type=F32)
        for k in range(EXPERTS):
            outs[first + k][...] = packed[k * CAP : (k + 1) * CAP].astype(BF16)


def pack(plane, kind, x, g):
    tokens, width = x.shape
    return pl.pallas_call(
        pack_kernel,
        out_shape=[jax.ShapeDtypeStruct((EXPERTS * CAP, tokens), BF16)]
        + [jax.ShapeDtypeStruct((CAP, width), BF16)] * (2 * EXPERTS),
        in_specs=[pl.BlockSpec(memory_space=pltpu.SMEM)] + [pl.BlockSpec(memory_space=pltpu.VMEM)] * 3,
        compiler_params=SMALL,
        cost_estimate=CHEAP,
        name="pack",
    )(plane, kind, x, g)


def join_kernel(*refs):
    refs[EXPERTS][...] = stacked(refs[:EXPERTS]).astype(BF16)


def join(blocks):
    width = blocks[0].shape[1]
    return pl.pallas_call(
        join_kernel,
        out_shape=jax.ShapeDtypeStruct((EXPERTS * CAP, width), BF16),
        compiler_params=SMALL,
        cost_estimate=CHEAP,
        name="join",
    )(*blocks)


def forward_kernel(down, xa_ref, xb_ref, wg_ref, wu_ref, *refs):
    if down:
        wd_ref, act_ref, coef_ref, sa_ref, sb_ref, x_ref, acc_ref = refs
    else:
        act_ref, coef_ref, x_ref = refs
    step = pl.program_id(0)
    half = xa_ref.shape[0]

    @pl.when(step == 0)
    def _():
        x_ref[:half, :] = xa_ref[...]
        x_ref[half:, :] = xb_ref[...]
        if down:
            acc_ref[...] = jnp.zeros_like(acc_ref)

    x = x_ref[...]
    for first in range(0, BLOCK, STRIP):
        cols = slice(first, first + STRIP)
        gate = jnp.dot(x, wg_ref[:, cols], preferred_element_type=F32)
        up = jnp.dot(x, wu_ref[:, cols], preferred_element_type=F32)
        act, slope = silu_parts(gate)
        act_ref[:, cols] = act.astype(BF16)
        coef_ref[:, cols] = (up * slope).astype(BF16)
        if down:
            hidden = (act * up).astype(BF16)
            acc_ref[...] += jnp.dot(hidden, wd_ref[cols, :], preferred_element_type=F32)

    if down:

        @pl.when(step == pl.num_programs(0) - 1)
        def _():
            sa_ref[...] = acc_ref[:half, :].astype(BF16)
            sb_ref[...] = acc_ref[half:, :].astype(BF16)


def forward(xa, xb, wg, wu, wd=None):
    half, width = xa.shape
    cols = wg.shape[1]
    rows = 2 * half
    down = wd is not None
    whole = pl.BlockSpec((half, width), lambda j: (0, 0))
    wide = pl.BlockSpec((rows, BLOCK), lambda j: (0, j))
    deep = pl.BlockSpec((width, BLOCK), lambda j: (0, j))
    tall = pl.BlockSpec((BLOCK, width), lambda j: (j, 0))
    count = 3 if down else 2
    return pl.pallas_call(
        functools.partial(forward_kernel, down),
        grid=(cols // BLOCK,),
        in_specs=[whole, whole, deep, deep] + [tall] * down,
        out_specs=[wide, wide] + [whole, whole] * down,
        out_shape=[jax.ShapeDtypeStruct((rows, cols), BF16)] * 2
        + [jax.ShapeDtypeStruct((half, width), BF16)] * (2 * down),
        scratch_shapes=[pltpu.VMEM((rows, width), BF16)] + [pltpu.VMEM((rows, width), F32)] * down,
        compiler_params=LARGE,
        cost_estimate=CHEAP,
        name="forward_down" if down else "forward",
    )(xa, xb, wg, wu, *([wd] * down))


def turn_kernel(where_ref, *refs):
    refs[8][: refs[0].shape[1], :] = stacked(refs[0:4]).T.astype(BF16)
    refs[8][refs[0].shape[1] :, :] = stacked(refs[4:8]).T.astype(BF16)


def turn(where, xs, share):
    part = xs[0].shape[0]
    rows = len(xs) * part
    return pl.pallas_call(
        turn_kernel,
        grid_spec=pltpu.PrefetchScalarGridSpec(
            num_scalar_prefetch=1,
            grid=(1,),
            in_specs=[pl.BlockSpec((part, share), lambda j, w: (0, w[0]))] * 4
            + [pl.BlockSpec((part, share), lambda j, w: (0, w[1]))] * 4,
            out_specs=pl.BlockSpec((2 * share, rows), lambda j, w: (0, 0)),
        ),
        out_shape=jax.ShapeDtypeStruct((2 * share, rows), BF16),
        compiler_params=SMALL,
        cost_estimate=CHEAP,
        name="turn",
    )(where, *xs, *xs)


def backward_kernel(xt_ref, *refs):
    gs = refs[0:4]
    act0, coef0, act1, coef1, wd_ref, own_ref, sib_ref, g_ref = refs[4:]
    part = gs[0].shape[0]
    share = own_ref.shape[0] // 2

    @pl.when(pl.program_id(0) == 0)
    def _():
        for i in range(4):
            g_ref[i * part : (i + 1) * part, :] = gs[i][...]

    for first in range(0, BLOCK, STRIP):
        cols = slice(first, first + STRIP)
        d_hidden = contract_cols(g_ref[...], wd_ref[cols, :])
        for row, low, high in ((0, coef0, coef1), (share, act0, act1)):
            factor = jnp.concatenate([low[:, cols], high[:, cols]], axis=0).astype(F32)
            d_cols = (d_hidden * factor).astype(BF16)
            total = jnp.dot(xt_ref[...], d_cols, preferred_element_type=F32).astype(BF16)
            own_ref[row : row + share, cols] = total[:share]
            sib_ref[row : row + share, cols] = total[share:]


def backward(xt, gs, act0, coef0, act1, coef1, wd, first, cols):
    part, width = gs[0].shape
    height, rows = xt.shape
    base = first // BLOCK
    wide = pl.BlockSpec((2 * part, BLOCK), lambda j: (0, base + j))
    out = pl.BlockSpec((height, BLOCK), lambda j: (0, j))
    return pl.pallas_call(
        backward_kernel,
        grid=(cols // BLOCK,),
        in_specs=[pl.BlockSpec((height, rows), lambda j: (0, 0))]
        + [pl.BlockSpec((part, width), lambda j: (0, 0))] * 4
        + [wide] * 4
        + [pl.BlockSpec((BLOCK, width), lambda j: (base + j, 0))],
        out_specs=[out, out],
        scratch_shapes=[pltpu.VMEM((rows, width), BF16)],
        out_shape=[jax.ShapeDtypeStruct((height, cols), BF16)] * 2,
        compiler_params=LARGE,
        cost_estimate=CHEAP,
        name="backward",
    )(xt, *gs, act0, coef0, act1, coef1, wd)


def finish_kernel(*refs):
    gate_ref, up_ref = refs[8:]
    half = refs[0].shape[1]
    for i in range(2):
        cols = slice(i * half, (i + 1) * half)
        own_gate, own_up, got_gate, got_up = [r[...].astype(F32) for r in refs[4 * i : 4 * i + 4]]
        gate_ref[:, cols] = (own_gate + got_gate).astype(BF16)
        up_ref[:, cols] = (own_up + got_up).astype(BF16)


def finish(own0, got0, own1, got1):
    share, half = own0.shape[0] // 2, own0.shape[1]
    steps = 2
    upper = pl.BlockSpec((share // steps, half), lambda i: (i, 0))
    lower = pl.BlockSpec((share // steps, half), lambda i: (i + steps, 0))
    return pl.pallas_call(
        finish_kernel,
        grid=(steps,),
        in_specs=[upper, lower] * 4,
        out_specs=[pl.BlockSpec((share // steps, 2 * half), lambda i: (i, 0))] * 2,
        out_shape=[jax.ShapeDtypeStruct((share, 2 * half), BF16)] * 2,
        compiler_params=SMALL,
        cost_estimate=CHEAP,
        name="finish",
    )(own0, own0, got0, got0, own1, own1, got1, got1)


def combine_kernel(mine_ref, theirs_ref, *outs):
    total = mine_ref[...].astype(F32) + theirs_ref[...].astype(F32)
    for k in range(EXPERTS):
        outs[k][...] = total[k * CAP : (k + 1) * CAP].astype(BF16)


def combine(mine, theirs):
    width = mine.shape[1]
    return pl.pallas_call(
        combine_kernel,
        out_shape=[jax.ShapeDtypeStruct((CAP, width), BF16)] * EXPERTS,
        compiler_params=SMALL,
        cost_estimate=CHEAP,
        name="combine",
    )(mine, theirs)


def unpack_kernel(placer_ref, *refs):
    packed = stacked(refs[:EXPERTS]).astype(BF16)
    chosen = placer_ref[...].astype(F32).T.astype(BF16)
    refs[EXPERTS][...] = jnp.dot(chosen, packed, preferred_element_type=F32).astype(BF16)


def unpack(placer, blocks):
    width = blocks[0].shape[1]
    return pl.pallas_call(
        unpack_kernel,
        out_shape=jax.ShapeDtypeStruct((placer.shape[1], width), BF16),
        compiler_params=SMALL,
        cost_estimate=CHEAP,
        name="unpack",
    )(placer, *blocks)


def swap(value, axis):
    return lax.ppermute(value, axis, [(0, 1), (1, 0)])


def across_planes(blocks):
    return [blocks[0]] + [
        lax.ppermute(blocks[k], "arch", [(i, i ^ k) for i in range(EXPERTS)]) for k in range(1, EXPERTS)
    ]


def after(values, earlier):
    n = len(values)
    return lax.optimization_barrier((*values, *earlier))[:n]


def gathering(designs, archetype, w_gate, w_up, w_down, cotangent):
    plane = lax.axis_index("arch").astype(jnp.int32)
    far = lax.axis_index("far").astype(jnp.int32)
    core = lax.axis_index("core").astype(jnp.int32)
    tokens, width = designs.shape
    share = width // 4
    placer, *blocks = pack(plane[None], archetype.reshape(1, tokens), designs, cotangent)

    x_own = join(across_planes(blocks[:EXPERTS]))
    x_near, x_far = after([swap(x_own, "half"), swap(x_own, "far")], [])
    x_corner = swap(x_near, "far")

    g_own = join(across_planes(after(blocks[EXPERTS:], [x_own])))
    g_near, g_far = after([swap(g_own, "half"), swap(g_own, "far")], [])
    g_corner = swap(g_near, "far")

    act0, coef0, share_own, share_near = forward(x_own, x_near, w_gate, w_up, w_down)
    act1, coef1 = forward(x_far, x_corner, w_gate, w_up)
    (share_got,) = after([swap(share_near, "half")], [act1])
    returned = across_planes(combine(share_own, share_got))
    outputs = unpack(placer, returned)

    where = jnp.stack([2 * far + core, 2 * far + 1 - core])
    xt = turn(where, [x_own, x_near, x_far, x_corner], share)
    gs = [g_own, g_near, g_far, g_corner]
    half = w_down.shape[0] // 2
    own0, sib0 = backward(xt, gs, act0, coef0, act1, coef1, w_down, 0, half)
    (xt,) = after([xt], returned[1:])
    own1, sib1 = backward(xt, gs, act0, coef0, act1, coef1, w_down, half, half)
    grad_gate, grad_up = finish(own0, swap(sib0, "core"), own1, swap(sib1, "core"))
    return outputs, grad_gate, grad_up


def reducing(designs, archetype, w_gate, w_up, w_down, cotangent):
    width = designs.shape[1]
    owners = lax.axis_size("expert")
    sharers = owners // EXPERTS
    hidden_cols = w_gate.shape[1]
    labels = archetype[:, 0]
    onehot = (labels[:, None] == jnp.arange(EXPERTS, dtype=jnp.int32)[None, :]).astype(jnp.int32)
    ranks = jnp.cumsum(onehot, axis=0) - onehot
    target = labels * CAP + jnp.sum(ranks * onehot, axis=1)
    placer = (jnp.arange(EXPERTS * CAP, dtype=jnp.int32)[:, None] == target[None, :]).astype(BF16)
    received = []
    for rows in (designs, cotangent):
        packed = jnp.dot(placer, rows, preferred_element_type=F32).astype(BF16)
        send = jnp.repeat(packed.reshape(EXPERTS, CAP, width), sharers, axis=0)
        received.append(
            lax.all_to_all(send, "expert", split_axis=0, concat_axis=0, tiled=True).reshape(
                owners * CAP, width
            )
        )
    flat_x, flat_g = received
    gate = jnp.dot(flat_x, w_gate, preferred_element_type=F32)
    up = jnp.dot(flat_x, w_up, preferred_element_type=F32)
    act, slope = silu_parts(gate)
    hidden = (act * up).astype(BF16)
    partial_value = (
        jnp.dot(hidden, w_down, preferred_element_type=F32).astype(BF16).reshape(owners, CAP, width)
    )
    returned = lax.all_to_all(partial_value, "expert", split_axis=0, concat_axis=0, tiled=True)
    summed = jnp.sum(returned.astype(F32).reshape(EXPERTS, sharers, CAP, width), axis=1).reshape(
        EXPERTS * CAP, width
    )
    outputs = jnp.take(summed, target, axis=0).astype(BF16)
    d_hidden = contract_cols(flat_g, w_down)
    d_gate = (d_hidden * up * slope).astype(BF16)
    d_up = (d_hidden * act).astype(BF16)
    grads = jnp.concatenate([contract_rows(flat_x, d_gate), contract_rows(flat_x, d_up)], axis=1)
    mine = lax.psum_scatter(grads.astype(BF16), "dp", scatter_dimension=0, tiled=True)
    return outputs, mine[:, :hidden_cols], mine[:, hidden_cols:]


def solution(mesh):
    dp, owners = mesh.devices.shape
    if (dp, owners) == (4, 2 * EXPERTS):
        rows, cols = ("far", "core"), ("arch", "half")
        mesh = Mesh(mesh.devices.reshape(2, 2, EXPERTS, 2), rows + cols)
        body = gathering
    else:
        rows, cols = ("dp",), ("expert",)
        body = reducing
    tokens = P(rows + cols, None)
    return jax.shard_map(
        body,
        mesh=mesh,
        in_specs=(tokens, tokens, P(None, cols), P(None, cols), P(cols, None), tokens),
        out_specs=(tokens, P(rows, cols), P(rows, cols)),
        check_vma=False,
    )
```

```python
import functools

import jax
import jax.numpy as jnp
from jax import lax
from jax.experimental import pallas as pl
from jax.experimental.pallas import tpu as pltpu
from jax.sharding import Mesh
from jax.sharding import PartitionSpec as P

EXPERTS = 4
CAP = 36
STRIP = 256
PAIR = 2 * STRIP
MIB = 1024 * 1024
LARGE = pltpu.CompilerParams(vmem_limit_bytes=16 * MIB)
SMALL = pltpu.CompilerParams(vmem_limit_bytes=12 * MIB)
CHEAP = pl.CostEstimate(flops=0, bytes_accessed=0, transcendentals=0)
F32 = jnp.float32
BF16 = jnp.bfloat16
HERE = pl.BlockSpec(memory_space=pltpu.VMEM)
AFAR = pl.BlockSpec(memory_space=pltpu.HBM)


def silu_parts(gate):
    sigma = 0.5 * jnp.tanh(0.5 * gate) + 0.5
    return (gate * sigma, sigma * (1.0 + gate * (1.0 - sigma)))


def contract_rows(left, right):
    return lax.dot_general(left, right, (((0,), (0,)), ((), ())), preferred_element_type=F32)


def contract_cols(left, right):
    return lax.dot_general(left, right, (((1,), (1,)), ((), ())), preferred_element_type=F32)


def stacked(refs):
    return jnp.concatenate([r[...].astype(F32) for r in refs], axis=0)


def kept(value):
    return pltpu.with_memory_space_constraint(value, pltpu.HBM)


def pack_kernel(plane_ref, kind_ref, x_ref, g_ref, placer_ref, *refs):
    outs, (kind, x, g, sems) = refs[: 2 * EXPERTS], refs[2 * EXPERTS :]
    copies = [
        pltpu.make_async_copy(source, target, sems.at[i])
        for i, (source, target) in enumerate(((kind_ref, kind), (x_ref, x), (g_ref, g)))
    ]
    for copy in copies:
        copy.start()
    tokens = kind.shape[1]
    copies[0].wait()
    key = kind[...] ^ plane_ref[0]
    onehot = (key == lax.broadcasted_iota(jnp.int32, (8, tokens), 0)).astype(F32)
    before = lax.broadcasted_iota(jnp.int32, (tokens, tokens), 0) < lax.broadcasted_iota(
        jnp.int32, (tokens, tokens), 1
    )
    ranks = jnp.dot(onehot.astype(BF16), before.astype(BF16), preferred_element_type=F32)
    rank = jnp.sum(ranks * onehot, axis=0, keepdims=True).astype(jnp.int32)
    place = key * CAP + rank
    slots = EXPERTS * CAP
    placer = (place == lax.broadcasted_iota(jnp.int32, (slots, tokens), 0)).astype(F32).astype(BF16)
    placer_ref[...] = placer
    for copy, source, first in ((copies[1], x, 0), (copies[2], g, EXPERTS)):
        copy.wait()
        packed = jnp.dot(placer, source[...], preferred_element_type=F32)
        for k in range(EXPERTS):
            outs[first + k][...] = packed[k * CAP : (k + 1) * CAP].astype(BF16)


def pack(plane, kind, x, g):
    tokens, width = x.shape
    return pl.pallas_call(
        pack_kernel,
        out_shape=[jax.ShapeDtypeStruct((EXPERTS * CAP, tokens), BF16)]
        + [jax.ShapeDtypeStruct((CAP, width), BF16)] * (2 * EXPERTS),
        in_specs=[pl.BlockSpec(memory_space=pltpu.SMEM)] + [AFAR] * 3,
        scratch_shapes=[
            pltpu.VMEM((1, tokens), jnp.int32),
            pltpu.VMEM((tokens, width), BF16),
            pltpu.VMEM((tokens, width), BF16),
            pltpu.SemaphoreType.DMA((3,)),
        ],
        compiler_params=SMALL,
        cost_estimate=CHEAP,
        name="pack",
    )(plane, kept(kind), kept(x), kept(g))


def load_kernel(pieces, *refs):
    n = len(refs) // 2
    sems = refs[2 * n]
    copies = []
    for i in range(n):
        lines = refs[i].shape[0] // pieces
        for j in range(pieces):
            rows = pl.ds(j * lines, lines)
            copies.append(
                pltpu.make_async_copy(refs[i].at[rows], refs[n + i].at[rows], sems.at[i * pieces + j])
            )
    for copy in copies:
        copy.start()
    for copy in copies:
        copy.wait()


def load(arrays, pieces=4):
    return pl.pallas_call(
        functools.partial(load_kernel, pieces),
        out_shape=[pltpu.VMEM(a.shape, a.dtype) for a in arrays],
        in_specs=[AFAR] * len(arrays),
        out_specs=[HERE] * len(arrays),
        scratch_shapes=[pltpu.SemaphoreType.DMA((len(arrays) * pieces,))],
        compiler_params=SMALL,
        cost_estimate=CHEAP,
        name="load",
    )(*[kept(a) for a in arrays])


def join_kernel(*refs):
    refs[EXPERTS][...] = stacked(refs[:EXPERTS]).astype(BF16)


def join(blocks):
    width = blocks[0].shape[1]
    return pl.pallas_call(
        join_kernel,
        out_shape=jax.ShapeDtypeStruct((EXPERTS * CAP, width), BF16),
        compiler_params=SMALL,
        cost_estimate=CHEAP,
        name="join",
    )(*blocks)


def forward_kernel(n, down, *refs):
    xs, refs = refs[:n], refs[n:]
    if down:
        wg_ref, wu_ref, wd_ref, act_ref, coef_ref, share_ref = refs[:6]
        acc_ref = refs[6]
        acc_ref[...] = jnp.zeros_like(acc_ref)
    else:
        wg_ref, wu_ref, act_ref, coef_ref = refs[:4]
    if n == 1:
        x_ref = xs[0]
    else:
        x_ref = refs[-1]
        part = xs[0].shape[0]
        for i in range(n):
            x_ref[i * part : (i + 1) * part, :] = xs[i][...]

    @pl.loop(0, wg_ref.shape[1] // PAIR)
    def _(j):
        for i in range(PAIR // STRIP):
            cols = pl.ds(pl.multiple_of(j * PAIR + i * STRIP, STRIP), STRIP)
            gate = jnp.dot(x_ref[...], wg_ref[:, cols], preferred_element_type=F32)
            up = jnp.dot(x_ref[...], wu_ref[:, cols], preferred_element_type=F32)
            act, slope = silu_parts(gate)
            act_ref[:, cols] = act.astype(BF16)
            coef_ref[:, cols] = (up * slope).astype(BF16)
            if down:
                hidden = (act * up).astype(BF16)
                acc_ref[...] += jnp.dot(hidden, wd_ref[cols, :], preferred_element_type=F32)

    if down:
        share_ref[...] = acc_ref[...].astype(BF16)


def forward(xs, wg, wu, wd=None):
    n, (part, width) = len(xs), xs[0].shape
    cols = wg.shape[1]
    rows = n * part
    down = wd is not None
    return pl.pallas_call(
        functools.partial(forward_kernel, n, down),
        out_shape=[jax.ShapeDtypeStruct((rows, cols), BF16)] * 2
        + [jax.ShapeDtypeStruct((rows, width), BF16)] * down,
        in_specs=[HERE] * (n + 2 + down),
        scratch_shapes=[pltpu.VMEM((rows, width), F32)] * down
        + [pltpu.VMEM((rows, width), BF16)] * (n > 1),
        compiler_params=LARGE,
        cost_estimate=CHEAP,
        name="forward_down" if down else "forward",
    )(*xs, wg, wu, *([wd] * down))


def turn_kernel(where_ref, *refs):
    refs[8][: refs[0].shape[1], :] = stacked(refs[0:4]).T.astype(BF16)
    refs[8][refs[0].shape[1] :, :] = stacked(refs[4:8]).T.astype(BF16)


def turn(where, xs, share):
    part = xs[0].shape[0]
    rows = len(xs) * part
    return pl.pallas_call(
        turn_kernel,
        grid_spec=pltpu.PrefetchScalarGridSpec(
            num_scalar_prefetch=1,
            grid=(1,),
            in_specs=[pl.BlockSpec((part, share), lambda j, w: (0, w[0]))] * 4
            + [pl.BlockSpec((part, share), lambda j, w: (0, w[1]))] * 4,
            out_specs=pl.BlockSpec((2 * share, rows), lambda j, w: (0, 0)),
        ),
        out_shape=jax.ShapeDtypeStruct((2 * share, rows), BF16),
        compiler_params=SMALL,
        cost_estimate=CHEAP,
        name="turn",
    )(where, *xs, *xs)


def backward_kernel(first, counts, xt_ref, *refs):
    n = len(counts)
    gs, acts, coefs = refs[:4], refs[4 : 4 + n], refs[4 + n : 4 + 2 * n]
    wd_ref, own_ref, sib_ref, g_ref = refs[4 + 2 * n :]
    part = gs[0].shape[0]
    share = own_ref.shape[0] // 2
    for i in range(4):
        g_ref[i * part : (i + 1) * part, :] = gs[i][...]

    @pl.loop(0, own_ref.shape[1] // PAIR)
    def _(j):
        for i in range(PAIR // STRIP):
            here = pl.ds(pl.multiple_of(j * PAIR + i * STRIP, STRIP), STRIP)
            cols = pl.ds(pl.multiple_of(j * PAIR + i * STRIP + first, STRIP), STRIP)
            d_hidden = contract_cols(g_ref[...], wd_ref[cols, :])
            for row, parts in ((0, coefs), (share, acts)):
                factor = jnp.concatenate([p[:, cols] for p in parts], axis=0).astype(F32)
                d_cols = (d_hidden * factor).astype(BF16)
                total = jnp.dot(xt_ref[...], d_cols, preferred_element_type=F32).astype(BF16)
                own_ref[row : row + share, here] = total[:share]
                sib_ref[row : row + share, here] = total[share:]


def backward(xt, gs, acts, coefs, wd, first, cols):
    part, width = gs[0].shape
    height, rows = xt.shape
    counts = tuple(a.shape[0] for a in acts)
    return pl.pallas_call(
        functools.partial(backward_kernel, first, counts),
        out_shape=[jax.ShapeDtypeStruct((height, cols), BF16)] * 2,
        in_specs=[HERE] * (6 + 2 * len(acts)),
        scratch_shapes=[pltpu.VMEM((rows, width), BF16)],
        compiler_params=LARGE,
        cost_estimate=CHEAP,
        name="backward",
    )(xt, *gs, *acts, *coefs, wd)


def finish_kernel(*refs):
    gate_ref, up_ref = refs[8:]
    half = refs[0].shape[1]
    for i in range(2):
        cols = slice(i * half, (i + 1) * half)
        own_gate, own_up, got_gate, got_up = [r[...].astype(F32) for r in refs[4 * i : 4 * i + 4]]
        gate_ref[:, cols] = (own_gate + got_gate).astype(BF16)
        up_ref[:, cols] = (own_up + got_up).astype(BF16)


def finish(own0, got0, own1, got1):
    share, half = own0.shape[0] // 2, own0.shape[1]
    steps = 2
    upper = pl.BlockSpec((share // steps, half), lambda i: (i, 0))
    lower = pl.BlockSpec((share // steps, half), lambda i: (i + steps, 0))
    return pl.pallas_call(
        finish_kernel,
        grid=(steps,),
        in_specs=[upper, lower] * 4,
        out_specs=[pl.BlockSpec((share // steps, 2 * half), lambda i: (i, 0))] * 2,
        out_shape=[jax.ShapeDtypeStruct((share, 2 * half), BF16)] * 2,
        compiler_params=SMALL,
        cost_estimate=CHEAP,
        name="finish",
    )(own0, own0, got0, got0, own1, own1, got1, got1)


def combine_kernel(mine_ref, theirs_ref, *outs):
    total = mine_ref[...].astype(F32) + theirs_ref[...].astype(F32)
    for k in range(EXPERTS):
        outs[k][...] = total[k * CAP : (k + 1) * CAP].astype(BF16)


def combine(mine, theirs):
    width = mine.shape[1]
    return pl.pallas_call(
        combine_kernel,
        out_shape=[jax.ShapeDtypeStruct((CAP, width), BF16)] * EXPERTS,
        compiler_params=SMALL,
        cost_estimate=CHEAP,
        name="combine",
    )(mine, theirs)


def unpack_kernel(placer_ref, *refs):
    packed = stacked(refs[:EXPERTS]).astype(BF16)
    chosen = placer_ref[...].astype(F32).T.astype(BF16)
    refs[EXPERTS][...] = jnp.dot(chosen, packed, preferred_element_type=F32).astype(BF16)


def unpack(placer, blocks):
    width = blocks[0].shape[1]
    return pl.pallas_call(
        unpack_kernel,
        out_shape=jax.ShapeDtypeStruct((placer.shape[1], width), BF16),
        compiler_params=SMALL,
        cost_estimate=CHEAP,
        name="unpack",
    )(placer, *blocks)


def swap(value, axis):
    return lax.ppermute(value, axis, [(0, 1), (1, 0)])


def across_planes(blocks):
    return [blocks[0]] + [
        lax.ppermute(blocks[k], "arch", [(i, i ^ k) for i in range(EXPERTS)]) for k in range(1, EXPERTS)
    ]


def after(values, earlier):
    n = len(values)
    return list(lax.optimization_barrier((*values, *earlier))[:n])


def gathering(designs, archetype, w_gate, w_up, w_down, cotangent):
    plane = lax.axis_index("arch").astype(jnp.int32)
    far = lax.axis_index("far").astype(jnp.int32)
    core = lax.axis_index("core").astype(jnp.int32)
    tokens, width = designs.shape
    share = width // 4
    placer, *blocks = pack(plane[None], archetype.reshape(1, tokens), designs, cotangent)
    wg, wu, wd = load(after([w_gate, w_up, w_down], [placer]))

    moved = across_planes(blocks[:EXPERTS])
    x_own = join(after(moved[:1], [wg]) + moved[1:])
    x_near, x_far = after([swap(x_own, "half"), swap(x_own, "far")], [])
    x_corner = swap(x_near, "far")

    act0, coef0, share_own = forward([x_own], wg, wu, wd)
    moved = across_planes(after(blocks[EXPERTS:], [x_own]))
    g_own = join(after(moved[:1], [act0, x_near, x_far]) + moved[1:])
    g_near, g_far = after([swap(g_own, "half"), swap(g_own, "far")], [])
    g_corner = swap(g_near, "far")

    (x_near,) = after([x_near], [act0])
    act1, coef1, share_near = forward([x_near], wg, wu, wd)
    act2, coef2 = forward([x_far, x_corner], wg, wu)
    (share_got,) = after([swap(share_near, "half")], [act2])
    returned = across_planes(combine(share_own, share_got))
    outputs = unpack(placer, returned)

    where = jnp.stack([2 * far + core, 2 * far + 1 - core])
    xt = turn(where, [x_own, x_near, x_far, x_corner], share)
    gs, acts, coefs = [g_own, g_near, g_far, g_corner], [act0, act1, act2], [coef0, coef1, coef2]
    half = w_down.shape[0] // 2
    own0, sib0 = backward(xt, gs, acts, coefs, wd, 0, half)
    (xt,) = after([xt], returned[1:])
    own1, sib1 = backward(xt, gs, acts, coefs, wd, half, half)
    grad_gate, grad_up = finish(own0, swap(sib0, "core"), own1, swap(sib1, "core"))
    return outputs, grad_gate, grad_up


def reducing(designs, archetype, w_gate, w_up, w_down, cotangent):
    width = designs.shape[1]
    owners = lax.axis_size("expert")
    sharers = owners // EXPERTS
    hidden_cols = w_gate.shape[1]
    labels = archetype[:, 0]
    onehot = (labels[:, None] == jnp.arange(EXPERTS, dtype=jnp.int32)[None, :]).astype(jnp.int32)
    ranks = jnp.cumsum(onehot, axis=0) - onehot
    target = labels * CAP + jnp.sum(ranks * onehot, axis=1)
    placer = (jnp.arange(EXPERTS * CAP, dtype=jnp.int32)[:, None] == target[None, :]).astype(BF16)
    received = []
    for rows in (designs, cotangent):
        packed = jnp.dot(placer, rows, preferred_element_type=F32).astype(BF16)
        send = jnp.repeat(packed.reshape(EXPERTS, CAP, width), sharers, axis=0)
        received.append(
            lax.all_to_all(send, "expert", split_axis=0, concat_axis=0, tiled=True).reshape(
                owners * CAP, width
            )
        )
    flat_x, flat_g = received
    gate = jnp.dot(flat_x, w_gate, preferred_element_type=F32)
    up = jnp.dot(flat_x, w_up, preferred_element_type=F32)
    act, slope = silu_parts(gate)
    hidden = (act * up).astype(BF16)
    partial_value = (
        jnp.dot(hidden, w_down, preferred_element_type=F32).astype(BF16).reshape(owners, CAP, width)
    )
    returned = lax.all_to_all(partial_value, "expert", split_axis=0, concat_axis=0, tiled=True)
    summed = jnp.sum(returned.astype(F32).reshape(EXPERTS, sharers, CAP, width), axis=1).reshape(
        EXPERTS * CAP, width
    )
    outputs = jnp.take(summed, target, axis=0).astype(BF16)
    d_hidden = contract_cols(flat_g, w_down)
    d_gate = (d_hidden * up * slope).astype(BF16)
    d_up = (d_hidden * act).astype(BF16)
    grads = jnp.concatenate([contract_rows(flat_x, d_gate), contract_rows(flat_x, d_up)], axis=1)
    mine = lax.psum_scatter(grads.astype(BF16), "dp", scatter_dimension=0, tiled=True)
    return outputs, mine[:, :hidden_cols], mine[:, hidden_cols:]


def solution(mesh):
    dp, owners = mesh.devices.shape
    if (dp, owners) == (4, 2 * EXPERTS):
        rows, cols = ("far", "core"), ("arch", "half")
        mesh = Mesh(mesh.devices.reshape(2, 2, EXPERTS, 2), rows + cols)
        body = gathering
    else:
        rows, cols = ("dp",), ("expert",)
        body = reducing
    tokens = P(rows + cols, None)
    return jax.shard_map(
        body,
        mesh=mesh,
        in_specs=(tokens, tokens, P(None, cols), P(None, cols), P(cols, None), tokens),
        out_specs=(tokens, P(rows, cols), P(rows, cols)),
        check_vma=False,
    )
```

```python
import functools

import jax
import jax.numpy as jnp
from jax import lax
from jax.experimental import pallas as pl
from jax.experimental.pallas import tpu as pltpu
from jax.sharding import Mesh
from jax.sharding import PartitionSpec as P

EXPERTS = 4
CAP = 36
STRIP = 256
PAIR = 2 * STRIP
MIB = 1024 * 1024
LARGE = pltpu.CompilerParams(vmem_limit_bytes=16 * MIB)
SMALL = pltpu.CompilerParams(vmem_limit_bytes=12 * MIB)
CHEAP = pl.CostEstimate(flops=0, bytes_accessed=0, transcendentals=0)
F32 = jnp.float32
BF16 = jnp.bfloat16
HERE = pl.BlockSpec(memory_space=pltpu.VMEM)
AFAR = pl.BlockSpec(memory_space=pltpu.HBM)


def silu_parts(gate):
    sigma = 0.5 * jnp.tanh(0.5 * gate) + 0.5
    return (gate * sigma, sigma * (1.0 + gate * (1.0 - sigma)))


def contract_rows(left, right):
    return lax.dot_general(left, right, (((0,), (0,)), ((), ())), preferred_element_type=F32)


def contract_cols(left, right):
    return lax.dot_general(left, right, (((1,), (1,)), ((), ())), preferred_element_type=F32)


def stacked(refs):
    return jnp.concatenate([r[...].astype(F32) for r in refs], axis=0)


def kept(value):
    return pltpu.with_memory_space_constraint(value, pltpu.HBM)


def pack_kernel(plane_ref, _, __, kind_ref, x_ref, g_ref, placer_ref, *refs):
    outs, (kind, x, g, sems) = refs[: 2 * EXPERTS], refs[2 * EXPERTS :]
    copies = [
        pltpu.make_async_copy(source, target, sems.at[i])
        for i, (source, target) in enumerate(((kind_ref, kind), (x_ref, x), (g_ref, g)))
    ]
    for copy in copies:
        copy.start()
    tokens = kind.shape[1]
    copies[0].wait()
    key = kind[...] ^ plane_ref[0]
    onehot = (key == lax.broadcasted_iota(jnp.int32, (8, tokens), 0)).astype(F32)
    before = lax.broadcasted_iota(jnp.int32, (tokens, tokens), 0) < lax.broadcasted_iota(
        jnp.int32, (tokens, tokens), 1
    )
    ranks = jnp.dot(onehot.astype(BF16), before.astype(BF16), preferred_element_type=F32)
    rank = jnp.sum(ranks * onehot, axis=0, keepdims=True).astype(jnp.int32)
    place = key * CAP + rank
    slots = EXPERTS * CAP
    placer = (place == lax.broadcasted_iota(jnp.int32, (slots, tokens), 0)).astype(F32).astype(BF16)
    placer_ref[...] = placer
    for copy, source, first in ((copies[1], x, 0), (copies[2], g, EXPERTS)):
        copy.wait()
        packed = jnp.dot(placer, source[...], preferred_element_type=F32)
        for k in range(EXPERTS):
            outs[first + k][...] = packed[k * CAP : (k + 1) * CAP].astype(BF16)


def pack(scalars, kind, x, g):
    tokens, width = x.shape
    return pl.pallas_call(
        pack_kernel,
        out_shape=[jax.ShapeDtypeStruct((EXPERTS * CAP, tokens), BF16)]
        + [jax.ShapeDtypeStruct((CAP, width), BF16)] * (2 * EXPERTS),
        in_specs=[pl.BlockSpec(memory_space=pltpu.SMEM)] * 3 + [AFAR] * 3,
        scratch_shapes=[
            pltpu.VMEM((1, tokens), jnp.int32),
            pltpu.VMEM((tokens, width), BF16),
            pltpu.VMEM((tokens, width), BF16),
            pltpu.SemaphoreType.DMA((3,)),
        ],
        compiler_params=SMALL,
        cost_estimate=CHEAP,
        name="pack",
    )(*scalars, kept(kind), kept(x), kept(g))


def load_kernel(pieces, *refs):
    n = len(refs) // 2
    sems = refs[2 * n]
    copies = []
    for i in range(n):
        lines = refs[i].shape[0] // pieces
        for j in range(pieces):
            rows = pl.ds(j * lines, lines)
            copies.append(
                pltpu.make_async_copy(refs[i].at[rows], refs[n + i].at[rows], sems.at[i * pieces + j])
            )
    for copy in copies:
        copy.start()
    for copy in copies:
        copy.wait()


def load(arrays, pieces=4):
    return pl.pallas_call(
        functools.partial(load_kernel, pieces),
        out_shape=[pltpu.VMEM(a.shape, a.dtype) for a in arrays],
        in_specs=[AFAR] * len(arrays),
        out_specs=[HERE] * len(arrays),
        scratch_shapes=[pltpu.SemaphoreType.DMA((len(arrays) * pieces,))],
        compiler_params=SMALL,
        cost_estimate=CHEAP,
        name="load",
    )(*[kept(a) for a in arrays])


def join_kernel(*refs):
    refs[EXPERTS][...] = stacked(refs[EXPERTS - 1 :: -1]).astype(BF16)


def join(blocks):
    width = blocks[0].shape[1]
    return pl.pallas_call(
        join_kernel,
        out_shape=jax.ShapeDtypeStruct((EXPERTS * CAP, width), BF16),
        compiler_params=SMALL,
        cost_estimate=CHEAP,
        name="join",
    )(*blocks[::-1])


def flip_kernel(source_ref, target_ref):
    @pl.loop(0, source_ref.shape[0] // STRIP)
    def _(j):
        rows = pl.ds(pl.multiple_of(j * STRIP, STRIP), STRIP)
        target_ref[:, rows] = source_ref[rows, :].T


def flip(value):
    return pl.pallas_call(
        flip_kernel,
        out_shape=pltpu.VMEM(value.shape[::-1], value.dtype),
        in_specs=[HERE],
        out_specs=HERE,
        compiler_params=SMALL,
        cost_estimate=CHEAP,
        name="flip",
    )(value)


def forward_kernel(n, down, *refs):
    xs, refs = refs[:n], refs[n:]
    if down:
        wg_ref, wu_ref, wd_ref, act_ref, coef_ref, share_ref = refs[:6]
        acc_ref = refs[6]
        acc_ref[...] = jnp.zeros_like(acc_ref)
    else:
        wg_ref, wu_ref, act_ref, coef_ref = refs[:4]
    if n == 1:
        x_ref = xs[0]
    else:
        x_ref = refs[-1]
        part = xs[0].shape[0]
        for i in range(n):
            x_ref[i * part : (i + 1) * part, :] = xs[i][...]

    @pl.loop(0, wg_ref.shape[1] // PAIR)
    def _(j):
        for i in range(PAIR // STRIP):
            cols = pl.ds(pl.multiple_of(j * PAIR + i * STRIP, STRIP), STRIP)
            gate = jnp.dot(x_ref[...], wg_ref[:, cols], preferred_element_type=F32)
            up = jnp.dot(x_ref[...], wu_ref[:, cols], preferred_element_type=F32)
            act, slope = silu_parts(gate)
            act_ref[:, cols] = act.astype(BF16)
            coef_ref[:, cols] = (up * slope).astype(BF16)
            if down:
                hidden = (act * up).astype(BF16)
                acc_ref[...] += jnp.dot(hidden, wd_ref[cols, :], preferred_element_type=F32)

    if down:
        share_ref[...] = acc_ref[...].astype(BF16)


def forward(xs, wg, wu, wd=None):
    n, (part, width) = len(xs), xs[0].shape
    cols = wg.shape[1]
    rows = n * part
    down = wd is not None
    return pl.pallas_call(
        functools.partial(forward_kernel, n, down),
        out_shape=[jax.ShapeDtypeStruct((rows, cols), BF16)] * 2
        + [jax.ShapeDtypeStruct((rows, width), BF16)] * down,
        in_specs=[HERE] * (n + 2 + down),
        scratch_shapes=[pltpu.VMEM((rows, width), F32)] * down
        + [pltpu.VMEM((rows, width), BF16)] * (n > 1),
        compiler_params=LARGE,
        cost_estimate=CHEAP,
        name="forward_down" if down else "forward",
    )(*xs, wg, wu, *([wd] * down))


def turn_kernel(_, __, *refs):
    refs[8][: refs[0].shape[1], :] = stacked(refs[0:4]).T.astype(BF16)
    refs[8][refs[0].shape[1] :, :] = stacked(refs[4:8]).T.astype(BF16)


def turn(own, sib, xs, share):
    part = xs[0].shape[0]
    rows = len(xs) * part
    return pl.pallas_call(
        turn_kernel,
        grid_spec=pltpu.PrefetchScalarGridSpec(
            num_scalar_prefetch=2,
            grid=(1,),
            in_specs=[pl.BlockSpec((part, share), lambda j, a, b: (0, a[0]))] * 4
            + [pl.BlockSpec((part, share), lambda j, a, b: (0, b[0]))] * 4,
            out_specs=pl.BlockSpec((2 * share, rows), lambda j, a, b: (0, 0)),
        ),
        out_shape=jax.ShapeDtypeStruct((2 * share, rows), BF16),
        compiler_params=SMALL,
        cost_estimate=CHEAP,
        name="turn",
    )(own, sib, *xs, *xs)


def backward_kernel(first, counts, xt_ref, *refs):
    n = len(counts)
    gs, acts, coefs = refs[:4], refs[4 : 4 + n], refs[4 + n : 4 + 2 * n]
    wdt_ref, own_ref, sib_ref, g_ref = refs[4 + 2 * n :]
    part = gs[0].shape[0]
    share = own_ref.shape[0] // 2
    for i in range(4):
        g_ref[i * part : (i + 1) * part, :] = gs[i][...]

    @pl.loop(0, own_ref.shape[1] // PAIR)
    def _(j):
        for i in range(PAIR // STRIP):
            here = pl.ds(pl.multiple_of(j * PAIR + i * STRIP, STRIP), STRIP)
            cols = pl.ds(pl.multiple_of(j * PAIR + i * STRIP + first, STRIP), STRIP)
            d_hidden = jnp.dot(g_ref[...], wdt_ref[:, cols], preferred_element_type=F32)
            for row, parts in ((0, coefs), (share, acts)):
                factor = jnp.concatenate([p[:, cols] for p in parts], axis=0).astype(F32)
                d_cols = (d_hidden * factor).astype(BF16)
                total = jnp.dot(xt_ref[...], d_cols, preferred_element_type=F32).astype(BF16)
                own_ref[row : row + share, here] = total[:share]
                sib_ref[row : row + share, here] = total[share:]


def backward(xt, gs, acts, coefs, wdt, first, cols):
    part, width = gs[0].shape
    height, rows = xt.shape
    counts = tuple(a.shape[0] for a in acts)
    return pl.pallas_call(
        functools.partial(backward_kernel, first, counts),
        out_shape=[jax.ShapeDtypeStruct((height, cols), BF16)] * 2,
        in_specs=[HERE] * (6 + 2 * len(acts)),
        scratch_shapes=[pltpu.VMEM((rows, width), BF16)],
        compiler_params=LARGE,
        cost_estimate=CHEAP,
        name="backward",
    )(xt, *gs, *acts, *coefs, wdt)


def finish_kernel(*refs):
    gate_ref, up_ref = refs[8:]
    half = refs[0].shape[1]
    for i in range(2):
        cols = slice(i * half, (i + 1) * half)
        own_gate, own_up, got_gate, got_up = [r[...].astype(F32) for r in refs[4 * i : 4 * i + 4]]
        gate_ref[:, cols] = (own_gate + got_gate).astype(BF16)
        up_ref[:, cols] = (own_up + got_up).astype(BF16)


def finish(own0, got0, own1, got1):
    share, half = own0.shape[0] // 2, own0.shape[1]
    steps = 2
    upper = pl.BlockSpec((share // steps, half), lambda i: (i, 0))
    lower = pl.BlockSpec((share // steps, half), lambda i: (i + steps, 0))
    return pl.pallas_call(
        finish_kernel,
        grid=(steps,),
        in_specs=[upper, lower] * 4,
        out_specs=[pl.BlockSpec((share // steps, 2 * half), lambda i: (i, 0))] * 2,
        out_shape=[jax.ShapeDtypeStruct((share, 2 * half), BF16)] * 2,
        compiler_params=SMALL,
        cost_estimate=CHEAP,
        name="finish",
    )(own0, own0, got0, got0, own1, own1, got1, got1)


def combine_kernel(mine_ref, theirs_ref, *outs):
    total = mine_ref[...].astype(F32) + theirs_ref[...].astype(F32)
    for k in range(EXPERTS):
        outs[k][...] = total[k * CAP : (k + 1) * CAP].astype(BF16)


def combine(mine, theirs):
    width = mine.shape[1]
    return pl.pallas_call(
        combine_kernel,
        out_shape=[jax.ShapeDtypeStruct((CAP, width), BF16)] * EXPERTS,
        compiler_params=SMALL,
        cost_estimate=CHEAP,
        name="combine",
    )(mine, theirs)


def unpack_kernel(placer_ref, *refs):
    packed = stacked(refs[:EXPERTS]).astype(BF16)
    chosen = placer_ref[...].astype(F32).T.astype(BF16)
    refs[EXPERTS][...] = jnp.dot(chosen, packed, preferred_element_type=F32).astype(BF16)


def unpack(placer, blocks):
    width = blocks[0].shape[1]
    return pl.pallas_call(
        unpack_kernel,
        out_shape=jax.ShapeDtypeStruct((placer.shape[1], width), BF16),
        compiler_params=SMALL,
        cost_estimate=CHEAP,
        name="unpack",
    )(placer, *blocks)


def swap(value, axis):
    return lax.ppermute(value, axis, [(0, 1), (1, 0)])


def across_planes(blocks):
    return [blocks[0]] + [
        lax.ppermute(blocks[k], "arch", [(i, i ^ k) for i in range(EXPERTS)]) for k in range(1, EXPERTS)
    ]


def after(values, earlier):
    n = len(values)
    return list(lax.optimization_barrier((*values, *earlier))[:n])


def gathering(designs, archetype, w_gate, w_up, w_down, cotangent):
    far, core = lax.axis_index("far"), lax.axis_index("core")
    scalars = [lax.axis_index("arch"), 2 * far + core, 2 * far + 1 - core]
    scalars = [v.astype(jnp.int32)[None] for v in scalars]
    tokens, width = designs.shape
    share = width // 4
    placer, *blocks = pack(scalars, archetype.reshape(1, tokens), designs, cotangent)
    wg, wu, wd = load(after([w_gate, w_up, w_down], [placer]))
    wdt = flip(wd)

    moved = across_planes(blocks[:EXPERTS])
    x_own = join(after(moved[:1], [wdt]) + moved[1:])
    x_near, x_far = after([swap(x_own, "half"), swap(x_own, "far")], [])

    g_own = join(across_planes(blocks[EXPERTS:]))
    g_near, g_far = after([swap(g_own, "half"), swap(g_own, "far")], [])

    act0, coef0, share_own = forward([x_own], wg, wu, wd)
    (x_near,) = after([x_near], [act0])
    act1, coef1, share_near = forward([x_near], wg, wu, wd)
    x_pass, g_pass = after([x_near, g_far], [act1, g_near])
    x_corner, g_corner = swap(x_pass, "far"), swap(g_pass, "half")
    (x_far,) = after([x_far], [act1])
    act2, coef2 = forward([x_far], wg, wu)
    (x_corner,) = after([x_corner], [act2])
    act3, coef3 = forward([x_corner], wg, wu)
    xt = turn(*scalars[1:], [x_own, x_near, x_far, x_corner], share)

    (share_near,) = after([share_near], [g_corner, act3])
    share_got = swap(share_near, "half")
    gs = [g_own, g_near, g_far, g_corner]
    acts, coefs = [act0, act1, act2, act3], [coef0, coef1, coef2, coef3]
    half = w_down.shape[0] // 2
    own0, sib0 = backward(xt, gs, acts, coefs, wdt, 0, half)
    (share_got,) = after([share_got], [own0])
    sums = combine(share_own, share_got)
    (xt,) = after([xt], [sums[0]])
    own1, sib1 = backward(xt, gs, acts, coefs, wdt, half, half)
    outputs = unpack(placer, across_planes(sums))
    (sib1,) = after([sib1], [outputs])
    grad_gate, grad_up = finish(own0, swap(sib0, "core"), own1, swap(sib1, "core"))
    return outputs, grad_gate, grad_up


def reducing(designs, archetype, w_gate, w_up, w_down, cotangent):
    width = designs.shape[1]
    owners = lax.axis_size("expert")
    sharers = owners // EXPERTS
    hidden_cols = w_gate.shape[1]
    labels = archetype[:, 0]
    onehot = (labels[:, None] == jnp.arange(EXPERTS, dtype=jnp.int32)[None, :]).astype(jnp.int32)
    ranks = jnp.cumsum(onehot, axis=0) - onehot
    target = labels * CAP + jnp.sum(ranks * onehot, axis=1)
    placer = (jnp.arange(EXPERTS * CAP, dtype=jnp.int32)[:, None] == target[None, :]).astype(BF16)
    received = []
    for rows in (designs, cotangent):
        packed = jnp.dot(placer, rows, preferred_element_type=F32).astype(BF16)
        send = jnp.repeat(packed.reshape(EXPERTS, CAP, width), sharers, axis=0)
        received.append(
            lax.all_to_all(send, "expert", split_axis=0, concat_axis=0, tiled=True).reshape(
                owners * CAP, width
            )
        )
    flat_x, flat_g = received
    gate = jnp.dot(flat_x, w_gate, preferred_element_type=F32)
    up = jnp.dot(flat_x, w_up, preferred_element_type=F32)
    act, slope = silu_parts(gate)
    hidden = (act * up).astype(BF16)
    partial_value = (
        jnp.dot(hidden, w_down, preferred_element_type=F32).astype(BF16).reshape(owners, CAP, width)
    )
    returned = lax.all_to_all(partial_value, "expert", split_axis=0, concat_axis=0, tiled=True)
    summed = jnp.sum(returned.astype(F32).reshape(EXPERTS, sharers, CAP, width), axis=1).reshape(
        EXPERTS * CAP, width
    )
    outputs = jnp.take(summed, target, axis=0).astype(BF16)
    d_hidden = contract_cols(flat_g, w_down)
    d_gate = (d_hidden * up * slope).astype(BF16)
    d_up = (d_hidden * act).astype(BF16)
    grads = jnp.concatenate([contract_rows(flat_x, d_gate), contract_rows(flat_x, d_up)], axis=1)
    mine = lax.psum_scatter(grads.astype(BF16), "dp", scatter_dimension=0, tiled=True)
    return outputs, mine[:, :hidden_cols], mine[:, hidden_cols:]


def solution(mesh):
    dp, owners = mesh.devices.shape
    if (dp, owners) == (4, 2 * EXPERTS):
        rows, cols = ("far", "core"), ("arch", "half")
        mesh = Mesh(mesh.devices.reshape(2, 2, EXPERTS, 2), rows + cols)
        body = gathering
    else:
        rows, cols = ("dp",), ("expert",)
        body = reducing
    tokens = P(rows + cols, None)
    return jax.shard_map(
        body,
        mesh=mesh,
        in_specs=(tokens, tokens, P(None, cols), P(None, cols), P(cols, None), tokens),
        out_specs=(tokens, P(rows, cols), P(rows, cols)),
        check_vma=False,
    )
```

```python
import functools

import jax
import jax.numpy as jnp
from jax import lax
from jax.experimental import pallas as pl
from jax.experimental.pallas import tpu as pltpu
from jax.sharding import Mesh
from jax.sharding import PartitionSpec as P

EXPERTS = 4
CAP = 36
STRIP = 256
PAIR = 2 * STRIP
MIB = 1024 * 1024
LARGE = pltpu.CompilerParams(vmem_limit_bytes=16 * MIB)
SMALL = pltpu.CompilerParams(vmem_limit_bytes=12 * MIB)
CHEAP = pl.CostEstimate(flops=0, bytes_accessed=0, transcendentals=0)
F32 = jnp.float32
BF16 = jnp.bfloat16
HERE = pl.BlockSpec(memory_space=pltpu.VMEM)
AFAR = pl.BlockSpec(memory_space=pltpu.HBM)


def silu_parts(gate):
    sigma = 0.5 * jnp.tanh(0.5 * gate) + 0.5
    return (gate * sigma, sigma * (1.0 + gate * (1.0 - sigma)))


def contract_rows(left, right):
    return lax.dot_general(left, right, (((0,), (0,)), ((), ())), preferred_element_type=F32)


def contract_cols(left, right):
    return lax.dot_general(left, right, (((1,), (1,)), ((), ())), preferred_element_type=F32)


def stacked(refs):
    return jnp.concatenate([r[...].astype(F32) for r in refs], axis=0)


def kept(value):
    return pltpu.with_memory_space_constraint(value, pltpu.HBM)


def pack_kernel(plane_ref, _, __, kind_ref, x_ref, g_ref, placer_ref, *refs):
    outs, (kind, x, g, sems) = refs[: 2 * EXPERTS], refs[2 * EXPERTS :]
    copies = [
        pltpu.make_async_copy(source, target, sems.at[i])
        for i, (source, target) in enumerate(((kind_ref, kind), (x_ref, x), (g_ref, g)))
    ]
    for copy in copies:
        copy.start()
    tokens = kind.shape[1]
    copies[0].wait()
    key = kind[...] ^ plane_ref[0]
    onehot = (key == lax.broadcasted_iota(jnp.int32, (8, tokens), 0)).astype(F32)
    before = lax.broadcasted_iota(jnp.int32, (tokens, tokens), 0) < lax.broadcasted_iota(
        jnp.int32, (tokens, tokens), 1
    )
    ranks = jnp.dot(onehot.astype(BF16), before.astype(BF16), preferred_element_type=F32)
    rank = jnp.sum(ranks * onehot, axis=0, keepdims=True).astype(jnp.int32)
    place = key * CAP + rank
    slots = EXPERTS * CAP
    placer = (place == lax.broadcasted_iota(jnp.int32, (slots, tokens), 0)).astype(F32).astype(BF16)
    placer_ref[...] = placer
    for copy, source, first in ((copies[1], x, 0), (copies[2], g, EXPERTS)):
        copy.wait()
        packed = jnp.dot(placer, source[...], preferred_element_type=F32)
        for k in range(EXPERTS):
            outs[first + k][...] = packed[k * CAP : (k + 1) * CAP].astype(BF16)


def pack(scalars, kind, x, g):
    tokens, width = x.shape
    return pl.pallas_call(
        pack_kernel,
        out_shape=[jax.ShapeDtypeStruct((EXPERTS * CAP, tokens), BF16)]
        + [jax.ShapeDtypeStruct((CAP, width), BF16)] * (2 * EXPERTS),
        in_specs=[pl.BlockSpec(memory_space=pltpu.SMEM)] * 3 + [AFAR] * 3,
        scratch_shapes=[
            pltpu.VMEM((1, tokens), jnp.int32),
            pltpu.VMEM((tokens, width), BF16),
            pltpu.VMEM((tokens, width), BF16),
            pltpu.SemaphoreType.DMA((3,)),
        ],
        compiler_params=SMALL,
        cost_estimate=CHEAP,
        name="pack",
    )(*scalars, kept(kind), kept(x), kept(g))


def join_kernel(*refs):
    refs[EXPERTS][...] = stacked(refs[EXPERTS - 1 :: -1]).astype(BF16)


def join(blocks):
    width = blocks[0].shape[1]
    return pl.pallas_call(
        join_kernel,
        out_shape=jax.ShapeDtypeStruct((EXPERTS * CAP, width), BF16),
        compiler_params=SMALL,
        cost_estimate=CHEAP,
        name="join",
    )(*blocks[::-1])


def flip_kernel(source_ref, target_ref):
    @pl.loop(0, source_ref.shape[0] // STRIP)
    def _(j):
        rows = pl.ds(pl.multiple_of(j * STRIP, STRIP), STRIP)
        target_ref[:, rows] = source_ref[rows, :].T


def flip(value):
    return pl.pallas_call(
        flip_kernel,
        out_shape=pltpu.VMEM(value.shape[::-1], value.dtype),
        in_specs=[HERE],
        out_specs=HERE,
        compiler_params=SMALL,
        cost_estimate=CHEAP,
        name="flip",
    )(value)


def forward_kernel(down, fetch, x_ref, *refs):
    if fetch:
        sources, refs = refs[:3], refs[3:]
        act_ref, coef_ref, share_ref, wg_ref, wu_ref, wd_ref, acc_ref, sems = refs
        targets = (wg_ref, wu_ref, wd_ref)
    elif down:
        wg_ref, wu_ref, wd_ref, act_ref, coef_ref, share_ref, acc_ref = refs
    else:
        wg_ref, wu_ref, act_ref, coef_ref = refs
    steps = wg_ref.shape[1] // PAIR

    def copies(j):
        cols = pl.ds(pl.multiple_of(j * PAIR, PAIR), PAIR)
        views = ((slice(None), cols), (slice(None), cols), (cols, slice(None)))
        return [
            pltpu.make_async_copy(source.at[view], target.at[view], sems.at[j, i])
            for i, (source, target, view) in enumerate(zip(sources, targets, views))
        ]

    if fetch:
        for j in range(steps):
            for copy in copies(j):
                copy.start()
    if down:
        acc_ref[...] = jnp.zeros_like(acc_ref)

    @pl.loop(0, steps)
    def _(j):
        if fetch:
            for copy in copies(j):
                copy.wait()
        for i in range(PAIR // STRIP):
            cols = pl.ds(pl.multiple_of(j * PAIR + i * STRIP, STRIP), STRIP)
            gate = jnp.dot(x_ref[...], wg_ref[:, cols], preferred_element_type=F32)
            up = jnp.dot(x_ref[...], wu_ref[:, cols], preferred_element_type=F32)
            act, slope = silu_parts(gate)
            act_ref[:, cols] = act.astype(BF16)
            coef_ref[:, cols] = (up * slope).astype(BF16)
            if down:
                hidden = (act * up).astype(BF16)
                acc_ref[...] += jnp.dot(hidden, wd_ref[cols, :], preferred_element_type=F32)

    if down:
        share_ref[...] = acc_ref[...].astype(BF16)


def forward(x, wg, wu, wd=None, fetch=False):
    (rows, width), cols = x.shape, wg.shape[1]
    down = wd is not None
    weights = [wg, wu, wd][: 2 + down]
    return pl.pallas_call(
        functools.partial(forward_kernel, down, fetch),
        out_shape=[jax.ShapeDtypeStruct((rows, cols), BF16)] * 2
        + [jax.ShapeDtypeStruct((rows, width), BF16)] * down
        + [pltpu.VMEM(w.shape, w.dtype) for w in weights] * fetch,
        in_specs=[HERE] + [AFAR if fetch else HERE] * len(weights),
        scratch_shapes=[pltpu.VMEM((rows, width), F32)] * down
        + [pltpu.SemaphoreType.DMA((cols // PAIR, 3))] * fetch,
        compiler_params=LARGE,
        cost_estimate=CHEAP,
        name="forward_fetch" if fetch else "forward_down" if down else "forward",
    )(x, *([kept(w) for w in weights] if fetch else weights))


def turn_kernel(_, __, *refs):
    refs[8][: refs[0].shape[1], :] = stacked(refs[0:4]).T.astype(BF16)
    refs[8][refs[0].shape[1] :, :] = stacked(refs[4:8]).T.astype(BF16)


def turn(own, sib, xs, share):
    part = xs[0].shape[0]
    rows = len(xs) * part
    return pl.pallas_call(
        turn_kernel,
        grid_spec=pltpu.PrefetchScalarGridSpec(
            num_scalar_prefetch=2,
            grid=(1,),
            in_specs=[pl.BlockSpec((part, share), lambda j, a, b: (0, a[0]))] * 4
            + [pl.BlockSpec((part, share), lambda j, a, b: (0, b[0]))] * 4,
            out_specs=pl.BlockSpec((2 * share, rows), lambda j, a, b: (0, 0)),
        ),
        out_shape=jax.ShapeDtypeStruct((2 * share, rows), BF16),
        compiler_params=SMALL,
        cost_estimate=CHEAP,
        name="turn",
    )(own, sib, *xs, *xs)


def backward_kernel(first, counts, xt_ref, *refs):
    n = len(counts)
    gs, acts, coefs = refs[:4], refs[4 : 4 + n], refs[4 + n : 4 + 2 * n]
    wdt_ref, own_ref, sib_ref, g_ref = refs[4 + 2 * n :]
    part = gs[0].shape[0]
    share = own_ref.shape[0] // 2
    for i in range(4):
        g_ref[i * part : (i + 1) * part, :] = gs[i][...]

    @pl.loop(0, own_ref.shape[1] // PAIR)
    def _(j):
        for i in range(PAIR // STRIP):
            here = pl.ds(pl.multiple_of(j * PAIR + i * STRIP, STRIP), STRIP)
            cols = pl.ds(pl.multiple_of(j * PAIR + i * STRIP + first, STRIP), STRIP)
            d_hidden = jnp.dot(g_ref[...], wdt_ref[:, cols], preferred_element_type=F32)
            for row, parts in ((0, coefs), (share, acts)):
                factor = jnp.concatenate([p[:, cols] for p in parts], axis=0).astype(F32)
                d_cols = (d_hidden * factor).astype(BF16)
                total = jnp.dot(xt_ref[...], d_cols, preferred_element_type=F32).astype(BF16)
                own_ref[row : row + share, here] = total[:share]
                sib_ref[row : row + share, here] = total[share:]


def backward(xt, gs, acts, coefs, wdt, first, cols):
    part, width = gs[0].shape
    height, rows = xt.shape
    counts = tuple(a.shape[0] for a in acts)
    return pl.pallas_call(
        functools.partial(backward_kernel, first, counts),
        out_shape=[jax.ShapeDtypeStruct((height, cols), BF16)] * 2,
        in_specs=[HERE] * (6 + 2 * len(acts)),
        scratch_shapes=[pltpu.VMEM((rows, width), BF16)],
        compiler_params=LARGE,
        cost_estimate=CHEAP,
        name="backward",
    )(xt, *gs, *acts, *coefs, wdt)


def finish_kernel(*refs):
    gate_ref, up_ref = refs[8:]
    half = refs[0].shape[1]
    for i in range(2):
        cols = slice(i * half, (i + 1) * half)
        own_gate, own_up, got_gate, got_up = [r[...].astype(F32) for r in refs[4 * i : 4 * i + 4]]
        gate_ref[:, cols] = (own_gate + got_gate).astype(BF16)
        up_ref[:, cols] = (own_up + got_up).astype(BF16)


def finish(own0, got0, own1, got1):
    share, half = own0.shape[0] // 2, own0.shape[1]
    steps = 2
    upper = pl.BlockSpec((share // steps, half), lambda i: (i, 0))
    lower = pl.BlockSpec((share // steps, half), lambda i: (i + steps, 0))
    return pl.pallas_call(
        finish_kernel,
        grid=(steps,),
        in_specs=[upper, lower] * 4,
        out_specs=[pl.BlockSpec((share // steps, 2 * half), lambda i: (i, 0))] * 2,
        out_shape=[jax.ShapeDtypeStruct((share, 2 * half), BF16)] * 2,
        compiler_params=SMALL,
        cost_estimate=CHEAP,
        name="finish",
    )(own0, own0, got0, got0, own1, own1, got1, got1)


def combine_kernel(mine_ref, theirs_ref, *outs):
    total = mine_ref[...].astype(F32) + theirs_ref[...].astype(F32)
    for k in range(EXPERTS):
        outs[k][...] = total[k * CAP : (k + 1) * CAP].astype(BF16)


def combine(mine, theirs):
    width = mine.shape[1]
    return pl.pallas_call(
        combine_kernel,
        out_shape=[jax.ShapeDtypeStruct((CAP, width), BF16)] * EXPERTS,
        compiler_params=SMALL,
        cost_estimate=CHEAP,
        name="combine",
    )(mine, theirs)


def unpack_kernel(placer_ref, *refs):
    packed = stacked(refs[:EXPERTS]).astype(BF16)
    chosen = placer_ref[...].astype(F32).T.astype(BF16)
    refs[EXPERTS][...] = jnp.dot(chosen, packed, preferred_element_type=F32).astype(BF16)


def unpack(placer, blocks):
    width = blocks[0].shape[1]
    return pl.pallas_call(
        unpack_kernel,
        out_shape=jax.ShapeDtypeStruct((placer.shape[1], width), BF16),
        compiler_params=SMALL,
        cost_estimate=CHEAP,
        name="unpack",
    )(placer, *blocks)


def swap(value, axis):
    return lax.ppermute(value, axis, [(0, 1), (1, 0)])


def across_planes(blocks):
    return [blocks[0]] + [
        lax.ppermute(blocks[k], "arch", [(i, i ^ k) for i in range(EXPERTS)]) for k in range(1, EXPERTS)
    ]


def after(values, earlier):
    n = len(values)
    return list(lax.optimization_barrier((*values, *earlier))[:n])


def gathering(designs, archetype, w_gate, w_up, w_down, cotangent):
    far, core = lax.axis_index("far"), lax.axis_index("core")
    scalars = [lax.axis_index("arch"), 2 * far + core, 2 * far + 1 - core]
    scalars = [v.astype(jnp.int32)[None] for v in scalars]
    tokens, width = designs.shape
    share = width // 4
    placer, *blocks = pack(scalars, archetype.reshape(1, tokens), designs, cotangent)
    moved = across_planes(blocks[:EXPERTS])
    x_own = join(moved)
    x_near, x_far = after([swap(x_own, "half"), swap(x_own, "far")], [])

    moved = across_planes(blocks[EXPERTS:])
    g_own = join(after(moved[:1], [x_own]) + moved[1:])
    g_near, g_far = after([swap(g_own, "half"), swap(g_own, "far")], [])

    act0, coef0, share_own, wg, wu, wd = forward(x_own, w_gate, w_up, w_down, fetch=True)
    (x_near,) = after([x_near], [act0])
    act1, coef1, share_near = forward(x_near, wg, wu, wd)
    x_pass, g_pass = after([x_near, g_far], [act0, g_near])
    x_corner, g_corner = swap(x_pass, "far"), swap(g_pass, "half")
    (x_far,) = after([x_far], [act1])
    act2, coef2 = forward(x_far, wg, wu)
    wdt = flip(after([wd], [act2])[0])
    (x_corner,) = after([x_corner], [act2, wdt])
    act3, coef3 = forward(x_corner, wg, wu)
    xt = turn(*scalars[1:], [x_own, x_near, x_far, x_corner], share)

    (share_near,) = after([share_near], [g_corner, act3])
    share_got = swap(share_near, "half")
    gs = [g_own, g_near, g_far, g_corner]
    acts, coefs = [act0, act1, act2, act3], [coef0, coef1, coef2, coef3]
    half = w_down.shape[0] // 2
    own0, sib0 = backward(xt, gs, acts, coefs, wdt, 0, half)
    (share_got,) = after([share_got], [own0])
    sums = combine(share_own, share_got)
    (xt,) = after([xt], [sums[0]])
    own1, sib1 = backward(xt, gs, acts, coefs, wdt, half, half)
    returned = across_planes(sums)
    (sib1,) = after([sib1], returned[1:])
    outputs = unpack(placer, returned)
    grad_gate, grad_up = finish(own0, swap(sib0, "core"), own1, swap(sib1, "core"))
    return outputs, grad_gate, grad_up


def reducing(designs, archetype, w_gate, w_up, w_down, cotangent):
    width = designs.shape[1]
    owners = lax.axis_size("expert")
    sharers = owners // EXPERTS
    hidden_cols = w_gate.shape[1]
    labels = archetype[:, 0]
    onehot = (labels[:, None] == jnp.arange(EXPERTS, dtype=jnp.int32)[None, :]).astype(jnp.int32)
    ranks = jnp.cumsum(onehot, axis=0) - onehot
    target = labels * CAP + jnp.sum(ranks * onehot, axis=1)
    placer = (jnp.arange(EXPERTS * CAP, dtype=jnp.int32)[:, None] == target[None, :]).astype(BF16)
    received = []
    for rows in (designs, cotangent):
        packed = jnp.dot(placer, rows, preferred_element_type=F32).astype(BF16)
        send = jnp.repeat(packed.reshape(EXPERTS, CAP, width), sharers, axis=0)
        received.append(
            lax.all_to_all(send, "expert", split_axis=0, concat_axis=0, tiled=True).reshape(
                owners * CAP, width
            )
        )
    flat_x, flat_g = received
    gate = jnp.dot(flat_x, w_gate, preferred_element_type=F32)
    up = jnp.dot(flat_x, w_up, preferred_element_type=F32)
    act, slope = silu_parts(gate)
    hidden = (act * up).astype(BF16)
    partial_value = (
        jnp.dot(hidden, w_down, preferred_element_type=F32).astype(BF16).reshape(owners, CAP, width)
    )
    returned = lax.all_to_all(partial_value, "expert", split_axis=0, concat_axis=0, tiled=True)
    summed = jnp.sum(returned.astype(F32).reshape(EXPERTS, sharers, CAP, width), axis=1).reshape(
        EXPERTS * CAP, width
    )
    outputs = jnp.take(summed, target, axis=0).astype(BF16)
    d_hidden = contract_cols(flat_g, w_down)
    d_gate = (d_hidden * up * slope).astype(BF16)
    d_up = (d_hidden * act).astype(BF16)
    grads = jnp.concatenate([contract_rows(flat_x, d_gate), contract_rows(flat_x, d_up)], axis=1)
    mine = lax.psum_scatter(grads.astype(BF16), "dp", scatter_dimension=0, tiled=True)
    return outputs, mine[:, :hidden_cols], mine[:, hidden_cols:]


def solution(mesh):
    dp, owners = mesh.devices.shape
    if (dp, owners) == (4, 2 * EXPERTS):
        rows, cols = ("far", "core"), ("arch", "half")
        mesh = Mesh(mesh.devices.reshape(2, 2, EXPERTS, 2), rows + cols)
        body = gathering
    else:
        rows, cols = ("dp",), ("expert",)
        body = reducing
    tokens = P(rows + cols, None)
    return jax.shard_map(
        body,
        mesh=mesh,
        in_specs=(tokens, tokens, P(None, cols), P(None, cols), P(cols, None), tokens),
        out_specs=(tokens, P(rows, cols), P(rows, cols)),
        check_vma=False,
    )
```

```python
import functools

import jax
import jax.numpy as jnp
from jax import lax
from jax.experimental import pallas as pl
from jax.experimental.pallas import tpu as pltpu
from jax.sharding import Mesh
from jax.sharding import PartitionSpec as P

EXPERTS = 4
CAP = 36
STRIP = 256
PAIR = 2 * STRIP
MIB = 1024 * 1024
LARGE = pltpu.CompilerParams(vmem_limit_bytes=16 * MIB)
SMALL = pltpu.CompilerParams(vmem_limit_bytes=12 * MIB)
CHEAP = pl.CostEstimate(flops=0, bytes_accessed=0, transcendentals=0)
F32 = jnp.float32
BF16 = jnp.bfloat16
HERE = pl.BlockSpec(memory_space=pltpu.VMEM)
AFAR = pl.BlockSpec(memory_space=pltpu.HBM)
ANYWHERE = pl.BlockSpec(memory_space=pl.ANY)


def silu_parts(gate):
    sigma = 0.5 * jnp.tanh(0.5 * gate) + 0.5
    return (gate * sigma, sigma * (1.0 + gate * (1.0 - sigma)))


def contract_rows(left, right):
    return lax.dot_general(left, right, (((0,), (0,)), ((), ())), preferred_element_type=F32)


def contract_cols(left, right):
    return lax.dot_general(left, right, (((1,), (1,)), ((), ())), preferred_element_type=F32)


def stacked(refs):
    return jnp.concatenate([r[...].astype(F32) for r in refs], axis=0)


def kept(value):
    return pltpu.with_memory_space_constraint(value, pltpu.HBM)


def pack_kernel(plane_ref, _, __, kind_ref, x_ref, g_ref, placer_ref, *refs):
    outs, (kind, x, g, sems) = refs[: 2 * EXPERTS], refs[2 * EXPERTS :]
    copies = [
        pltpu.make_async_copy(source, target, sems.at[i])
        for i, (source, target) in enumerate(((kind_ref, kind), (x_ref, x), (g_ref, g)))
    ]
    for copy in copies:
        copy.start()
    tokens = kind.shape[1]
    copies[0].wait()
    key = kind[...] ^ plane_ref[0]
    onehot = (key == lax.broadcasted_iota(jnp.int32, (8, tokens), 0)).astype(F32)
    before = lax.broadcasted_iota(jnp.int32, (tokens, tokens), 0) < lax.broadcasted_iota(
        jnp.int32, (tokens, tokens), 1
    )
    ranks = jnp.dot(onehot.astype(BF16), before.astype(BF16), preferred_element_type=F32)
    rank = jnp.sum(ranks * onehot, axis=0, keepdims=True).astype(jnp.int32)
    place = key * CAP + rank
    slots = EXPERTS * CAP
    placer = (place == lax.broadcasted_iota(jnp.int32, (slots, tokens), 0)).astype(F32).astype(BF16)
    placer_ref[...] = placer
    for copy, source, first in ((copies[1], x, 0), (copies[2], g, EXPERTS)):
        copy.wait()
        packed = jnp.dot(placer, source[...], preferred_element_type=F32)
        for k in range(EXPERTS):
            outs[first + k][...] = packed[k * CAP : (k + 1) * CAP].astype(BF16)


def pack(scalars, kind, x, g):
    tokens, width = x.shape
    return pl.pallas_call(
        pack_kernel,
        out_shape=[jax.ShapeDtypeStruct((EXPERTS * CAP, tokens), BF16)]
        + [jax.ShapeDtypeStruct((CAP, width), BF16)] * (2 * EXPERTS),
        in_specs=[pl.BlockSpec(memory_space=pltpu.SMEM)] * 3 + [AFAR] * 3,
        scratch_shapes=[
            pltpu.VMEM((1, tokens), jnp.int32),
            pltpu.VMEM((tokens, width), BF16),
            pltpu.VMEM((tokens, width), BF16),
            pltpu.SemaphoreType.DMA((3,)),
        ],
        compiler_params=SMALL,
        cost_estimate=CHEAP,
        name="pack",
    )(*scalars, kept(kind), kept(x), kept(g))


def join_kernel(*refs):
    refs[-1][...] = stacked(refs[EXPERTS - 1 :: -1]).astype(BF16)


def join(blocks, earlier=()):
    width = blocks[0].shape[1]
    return pl.pallas_call(
        join_kernel,
        out_shape=jax.ShapeDtypeStruct((EXPERTS * CAP, width), BF16),
        in_specs=[HERE] * EXPERTS + [ANYWHERE] * len(earlier),
        compiler_params=SMALL,
        cost_estimate=CHEAP,
        name="join",
    )(*blocks[::-1], *earlier)


def relay_kernel(n, *refs):
    for i in range(n):
        refs[len(refs) - n + i][...] = refs[i][...]


def relay(values, earlier):
    n = len(values)
    return pl.pallas_call(
        functools.partial(relay_kernel, n),
        out_shape=[jax.ShapeDtypeStruct(v.shape, v.dtype) for v in values],
        in_specs=[HERE] * n + [ANYWHERE] * len(earlier),
        compiler_params=SMALL,
        cost_estimate=CHEAP,
        name="relay",
    )(*values, *earlier)


def mark_kernel(value_ref, mark_ref):
    mark_ref[...] = value_ref[: mark_ref.shape[0], : mark_ref.shape[1]]


def mark(value):
    return pl.pallas_call(
        mark_kernel,
        out_shape=jax.ShapeDtypeStruct((16, 128), value.dtype),
        in_specs=[HERE],
        compiler_params=SMALL,
        cost_estimate=CHEAP,
        name="mark",
    )(value)


def flip_kernel(source_ref, here_ref, flipped_ref, sems):
    steps = source_ref.shape[0] // STRIP
    copies = []
    for j in range(steps):
        rows = pl.ds(j * STRIP, STRIP)
        copies.append(pltpu.make_async_copy(source_ref.at[rows], here_ref.at[rows], sems.at[j]))
        copies[j].start()
    for j in range(steps):
        copies[j].wait()
        rows = slice(j * STRIP, (j + 1) * STRIP)
        flipped_ref[:, rows] = here_ref[rows, :].T


def flip(value):
    return pl.pallas_call(
        flip_kernel,
        out_shape=[pltpu.VMEM(value.shape, value.dtype), pltpu.VMEM(value.shape[::-1], value.dtype)],
        in_specs=[AFAR],
        out_specs=[HERE, HERE],
        scratch_shapes=[pltpu.SemaphoreType.DMA((value.shape[0] // STRIP,))],
        compiler_params=SMALL,
        cost_estimate=CHEAP,
        name="flip",
    )(kept(value))


def forward_kernel(fetch, down, pair, unused, x_ref, wg_ref, wu_ref, *refs):
    refs = list(refs)
    wd_ref = refs.pop(0) if down else None
    other_ref = refs.pop(0) if pair else None
    refs = refs[unused:]
    act_ref, coef_ref = refs.pop(0), refs.pop(0)
    if down:
        shares = [refs.pop(0) for _ in range(EXPERTS if pair else 1)]
    if fetch:
        sources, sems = (wg_ref, wu_ref), refs.pop()
        wg_ref, wu_ref = refs.pop(0), refs.pop(0)
    if down:
        acc_ref = refs.pop(0)
    steps = wg_ref.shape[1] // PAIR

    def copies(j):
        cols = pl.ds(pl.multiple_of(j * PAIR, PAIR), PAIR)
        return [
            pltpu.make_async_copy(source.at[:, cols], target.at[:, cols], sems.at[j, i])
            for i, (source, target) in enumerate(zip(sources, (wg_ref, wu_ref)))
        ]

    if fetch:
        for j in range(steps):
            for copy in copies(j):
                copy.start()
    if down:
        acc_ref[...] = jnp.zeros_like(acc_ref)

    @pl.loop(0, steps)
    def _(j):
        if fetch:
            for copy in copies(j):
                copy.wait()
        for i in range(PAIR // STRIP):
            cols = pl.ds(pl.multiple_of(j * PAIR + i * STRIP, STRIP), STRIP)
            gate = jnp.dot(x_ref[...], wg_ref[:, cols], preferred_element_type=F32)
            up = jnp.dot(x_ref[...], wu_ref[:, cols], preferred_element_type=F32)
            act, slope = silu_parts(gate)
            act_ref[:, cols] = act.astype(BF16)
            coef_ref[:, cols] = (up * slope).astype(BF16)
            if down:
                hidden = (act * up).astype(BF16)
                acc_ref[...] += jnp.dot(hidden, wd_ref[cols, :], preferred_element_type=F32)

    if pair:
        other = other_ref[...].astype(F32)
        for k in range(EXPERTS):
            rows = slice(k * CAP, (k + 1) * CAP)
            shares[k][...] = jnp.concatenate([other[rows], acc_ref[rows, :]], axis=0).astype(BF16)
    elif down:
        shares[0][...] = acc_ref[...].astype(BF16)


def forward(x, wg, wu, wd=None, other=None, fetch=False, earlier=()):
    (rows, width), cols = x.shape, wg.shape[1]
    down, pair = wd is not None, other is not None
    shares = [jax.ShapeDtypeStruct((rows, width), BF16)]
    if pair:
        shares = [jax.ShapeDtypeStruct((2 * CAP, width), BF16)] * EXPERTS
    weights = [kept(wg), kept(wu)] if fetch else [wg, wu]
    return pl.pallas_call(
        functools.partial(forward_kernel, fetch, down, pair, len(earlier)),
        out_shape=[jax.ShapeDtypeStruct((rows, cols), BF16)] * 2
        + shares * down
        + [pltpu.VMEM(wg.shape, wg.dtype)] * (2 * fetch),
        in_specs=[HERE] + [AFAR if fetch else HERE] * 2 + [HERE] * (down + pair) + [ANYWHERE] * len(earlier),
        scratch_shapes=[pltpu.VMEM((rows, width), F32)] * down
        + [pltpu.SemaphoreType.DMA((cols // PAIR, 2))] * fetch,
        compiler_params=LARGE,
        cost_estimate=CHEAP,
        name="forward" + "_fetch" * fetch + "_down" * down,
    )(x, *weights, *([wd] * down), *([other] * pair), *earlier)


def turn_kernel(_, __, *refs):
    refs[8][: refs[0].shape[1], :] = stacked(refs[0:4]).T.astype(BF16)
    refs[8][refs[0].shape[1] :, :] = stacked(refs[4:8]).T.astype(BF16)


def turn(own, sib, xs, share):
    part = xs[0].shape[0]
    rows = len(xs) * part
    return pl.pallas_call(
        turn_kernel,
        grid_spec=pltpu.PrefetchScalarGridSpec(
            num_scalar_prefetch=2,
            grid=(1,),
            in_specs=[pl.BlockSpec((part, share), lambda j, a, b: (0, a[0]))] * 4
            + [pl.BlockSpec((part, share), lambda j, a, b: (0, b[0]))] * 4,
            out_specs=pl.BlockSpec((2 * share, rows), lambda j, a, b: (0, 0)),
        ),
        out_shape=jax.ShapeDtypeStruct((2 * share, rows), BF16),
        compiler_params=SMALL,
        cost_estimate=CHEAP,
        name="turn",
    )(own, sib, *xs, *xs)


def backward_kernel(first, counts, xt_ref, *refs):
    n = len(counts)
    gs, acts, coefs = refs[:4], refs[4 : 4 + n], refs[4 + n : 4 + 2 * n]
    wdt_ref, own_ref, sib_ref, g_ref = refs[4 + 2 * n :]
    part = gs[0].shape[0]
    share = own_ref.shape[0] // 2
    for i in range(4):
        g_ref[i * part : (i + 1) * part, :] = gs[i][...]

    @pl.loop(0, own_ref.shape[1] // PAIR)
    def _(j):
        for i in range(PAIR // STRIP):
            here = pl.ds(pl.multiple_of(j * PAIR + i * STRIP, STRIP), STRIP)
            cols = pl.ds(pl.multiple_of(j * PAIR + i * STRIP + first, STRIP), STRIP)
            d_hidden = jnp.dot(g_ref[...], wdt_ref[:, cols], preferred_element_type=F32)
            for row, parts in ((0, coefs), (share, acts)):
                factor = jnp.concatenate([p[:, cols] for p in parts], axis=0).astype(F32)
                d_cols = (d_hidden * factor).astype(BF16)
                total = jnp.dot(xt_ref[...], d_cols, preferred_element_type=F32).astype(BF16)
                own_ref[row : row + share, here] = total[:share]
                sib_ref[row : row + share, here] = total[share:]


def backward(xt, gs, acts, coefs, wdt, first, cols):
    part, width = gs[0].shape
    height, rows = xt.shape
    counts = tuple(a.shape[0] for a in acts)
    return pl.pallas_call(
        functools.partial(backward_kernel, first, counts),
        out_shape=[jax.ShapeDtypeStruct((height, cols), BF16)] * 2,
        in_specs=[HERE] * (6 + 2 * len(acts)),
        scratch_shapes=[pltpu.VMEM((rows, width), BF16)],
        compiler_params=LARGE,
        cost_estimate=CHEAP,
        name="backward",
    )(xt, *gs, *acts, *coefs, wdt)


def finish_kernel(*refs):
    gate_ref, up_ref = refs[8:]
    half = refs[0].shape[1]
    for i in range(2):
        cols = slice(i * half, (i + 1) * half)
        own_gate, own_up, got_gate, got_up = [r[...].astype(F32) for r in refs[4 * i : 4 * i + 4]]
        gate_ref[:, cols] = (own_gate + got_gate).astype(BF16)
        up_ref[:, cols] = (own_up + got_up).astype(BF16)


def finish(own0, got0, own1, got1):
    share, half = own0.shape[0] // 2, own0.shape[1]
    steps = 2
    upper = pl.BlockSpec((share // steps, half), lambda i: (i, 0))
    lower = pl.BlockSpec((share // steps, half), lambda i: (i + steps, 0))
    return pl.pallas_call(
        finish_kernel,
        grid=(steps,),
        in_specs=[upper, lower] * 4,
        out_specs=[pl.BlockSpec((share // steps, 2 * half), lambda i: (i, 0))] * 2,
        out_shape=[jax.ShapeDtypeStruct((share, 2 * half), BF16)] * 2,
        compiler_params=SMALL,
        cost_estimate=CHEAP,
        name="finish",
    )(own0, own0, got0, got0, own1, own1, got1, got1)


def split_kernel(*refs):
    blocks = [r[...].astype(F32) for r in refs[:EXPERTS]]
    refs[EXPERTS][...] = jnp.concatenate([b[:CAP] for b in blocks], axis=0).astype(BF16)
    refs[EXPERTS + 1][...] = jnp.concatenate([b[CAP:] for b in blocks], axis=0).astype(BF16)


def split(blocks):
    width = blocks[0].shape[1]
    return pl.pallas_call(
        split_kernel,
        out_shape=[jax.ShapeDtypeStruct((EXPERTS * CAP, width), BF16)] * 2,
        compiler_params=SMALL,
        cost_estimate=CHEAP,
        name="split",
    )(*blocks)


def unpack_kernel(placer_ref, mine_ref, got_ref, out_ref):
    chosen = placer_ref[...].astype(F32).T.astype(BF16)
    total = jnp.dot(chosen, mine_ref[...], preferred_element_type=F32)
    total += jnp.dot(chosen, got_ref[...], preferred_element_type=F32)
    out_ref[...] = total.astype(BF16)


def unpack(placer, mine, got):
    return pl.pallas_call(
        unpack_kernel,
        out_shape=jax.ShapeDtypeStruct((placer.shape[1], mine.shape[1]), BF16),
        compiler_params=SMALL,
        cost_estimate=CHEAP,
        name="unpack",
    )(placer, mine, got)


def swap(value, axis):
    return lax.ppermute(value, axis, [(0, 1), (1, 0)])


def across_planes(blocks):
    return [blocks[0]] + [
        lax.ppermute(blocks[k], "arch", [(i, i ^ k) for i in range(EXPERTS)]) for k in range(1, EXPERTS)
    ]


def after(values, earlier):
    n = len(values)
    return list(lax.optimization_barrier((*values, *earlier))[:n])


def gathering(designs, archetype, w_gate, w_up, w_down, cotangent):
    far, core = lax.axis_index("far"), lax.axis_index("core")
    scalars = [lax.axis_index("arch"), 2 * far + core, 2 * far + 1 - core]
    scalars = [v.astype(jnp.int32)[None] for v in scalars]
    tokens, width = designs.shape
    share = width // 4
    placer, *blocks = pack(scalars, archetype.reshape(1, tokens), designs, cotangent)
    wd, wdt = flip(after([w_down], [placer])[0])

    moved = across_planes(blocks[:EXPERTS])
    x_own = join(moved, [wdt])
    x_near, x_far = swap(x_own, "half"), swap(x_own, "far")
    moved = across_planes(blocks[EXPERTS:])
    g_own = join(moved, [x_own])
    g_near, g_far = swap(g_own, "half"), swap(g_own, "far")

    act0, coef0, share_own, wg, wu = forward(x_own, w_gate, w_up, wd, fetch=True)
    act1, coef1, *shares = forward(x_near, wg, wu, wd, other=share_own, earlier=[x_far])
    x_pass, g_pass = relay([x_near, g_far], [mark(act1), g_near])
    x_corner, g_corner = swap(x_pass, "far"), swap(g_pass, "half")
    returned = across_planes(shares)
    (x_far,) = after([x_far], [act1])
    act2, coef2 = forward(x_far, wg, wu)
    (x_corner,) = after([x_corner], [act2])
    act3, coef3 = forward(x_corner, wg, wu)
    xt = turn(*scalars[1:], [x_own, x_near, x_far, x_corner], share)

    gs = [g_own, g_near, g_far, g_corner]
    acts, coefs = [act0, act1, act2, act3], [coef0, coef1, coef2, coef3]
    half = w_down.shape[0] // 2
    own0, sib0 = backward(xt, gs, acts, coefs, wdt, 0, half)
    mine, theirs = split(after(returned[:1], [own0]) + returned[1:])
    (xt,) = after([xt], [mine])
    own1, sib1 = backward(xt, gs, acts, coefs, wdt, half, half)
    got = swap(theirs, "half")
    (sib1,) = after([sib1], [got])
    outputs = unpack(placer, mine, got)
    grad_gate, grad_up = finish(own0, swap(sib0, "core"), own1, swap(sib1, "core"))
    return outputs, grad_gate, grad_up


def reducing(designs, archetype, w_gate, w_up, w_down, cotangent):
    width = designs.shape[1]
    owners = lax.axis_size("expert")
    sharers = owners // EXPERTS
    hidden_cols = w_gate.shape[1]
    labels = archetype[:, 0]
    onehot = (labels[:, None] == jnp.arange(EXPERTS, dtype=jnp.int32)[None, :]).astype(jnp.int32)
    ranks = jnp.cumsum(onehot, axis=0) - onehot
    target = labels * CAP + jnp.sum(ranks * onehot, axis=1)
    placer = (jnp.arange(EXPERTS * CAP, dtype=jnp.int32)[:, None] == target[None, :]).astype(BF16)
    received = []
    for rows in (designs, cotangent):
        packed = jnp.dot(placer, rows, preferred_element_type=F32).astype(BF16)
        send = jnp.repeat(packed.reshape(EXPERTS, CAP, width), sharers, axis=0)
        received.append(
            lax.all_to_all(send, "expert", split_axis=0, concat_axis=0, tiled=True).reshape(
                owners * CAP, width
            )
        )
    flat_x, flat_g = received
    gate = jnp.dot(flat_x, w_gate, preferred_element_type=F32)
    up = jnp.dot(flat_x, w_up, preferred_element_type=F32)
    act, slope = silu_parts(gate)
    hidden = (act * up).astype(BF16)
    partial_value = (
        jnp.dot(hidden, w_down, preferred_element_type=F32).astype(BF16).reshape(owners, CAP, width)
    )
    returned = lax.all_to_all(partial_value, "expert", split_axis=0, concat_axis=0, tiled=True)
    summed = jnp.sum(returned.astype(F32).reshape(EXPERTS, sharers, CAP, width), axis=1).reshape(
        EXPERTS * CAP, width
    )
    outputs = jnp.take(summed, target, axis=0).astype(BF16)
    d_hidden = contract_cols(flat_g, w_down)
    d_gate = (d_hidden * up * slope).astype(BF16)
    d_up = (d_hidden * act).astype(BF16)
    grads = jnp.concatenate([contract_rows(flat_x, d_gate), contract_rows(flat_x, d_up)], axis=1)
    mine = lax.psum_scatter(grads.astype(BF16), "dp", scatter_dimension=0, tiled=True)
    return outputs, mine[:, :hidden_cols], mine[:, hidden_cols:]


def solution(mesh):
    dp, owners = mesh.devices.shape
    if (dp, owners) == (4, 2 * EXPERTS):
        rows, cols = ("far", "core"), ("arch", "half")
        mesh = Mesh(mesh.devices.reshape(2, 2, EXPERTS, 2), rows + cols)
        body = gathering
    else:
        rows, cols = ("dp",), ("expert",)
        body = reducing
    tokens = P(rows + cols, None)
    return jax.shard_map(
        body,
        mesh=mesh,
        in_specs=(tokens, tokens, P(None, cols), P(None, cols), P(cols, None), tokens),
        out_specs=(tokens, P(rows, cols), P(rows, cols)),
        check_vma=False,
    )
```

```python
import functools

import jax
import jax.numpy as jnp
from jax import lax
from jax.experimental import pallas as pl
from jax.experimental.pallas import tpu as pltpu
from jax.sharding import Mesh
from jax.sharding import PartitionSpec as P

EXPERTS = 4
CAP = 36
STRIP = 256
PAIR = 2 * STRIP
MIB = 1024 * 1024
LARGE = pltpu.CompilerParams(vmem_limit_bytes=16 * MIB)
SMALL = pltpu.CompilerParams(vmem_limit_bytes=12 * MIB)
CHEAP = pl.CostEstimate(flops=0, bytes_accessed=0, transcendentals=0)
DEAR = pl.CostEstimate(flops=20_000_000_000, bytes_accessed=0, transcendentals=0)
F32 = jnp.float32
BF16 = jnp.bfloat16
HERE = pl.BlockSpec(memory_space=pltpu.VMEM)
AFAR = pl.BlockSpec(memory_space=pltpu.HBM)
ANYWHERE = pl.BlockSpec(memory_space=pl.ANY)


def silu_parts(gate):
    sigma = 0.5 * jnp.tanh(0.5 * gate) + 0.5
    return (gate * sigma, sigma * (1.0 + gate * (1.0 - sigma)))


def contract_rows(left, right):
    return lax.dot_general(left, right, (((0,), (0,)), ((), ())), preferred_element_type=F32)


def contract_cols(left, right):
    return lax.dot_general(left, right, (((1,), (1,)), ((), ())), preferred_element_type=F32)


def stacked(refs):
    return jnp.concatenate([r[...].astype(F32) for r in refs], axis=0)


def kept(value):
    return pltpu.with_memory_space_constraint(value, pltpu.HBM)


def pack_kernel(plane_ref, _, __, kind_ref, x_ref, g_ref, placer_ref, *refs):
    outs, (kind, x, g, sems) = refs[: 2 * EXPERTS], refs[2 * EXPERTS :]
    copies = [
        pltpu.make_async_copy(source, target, sems.at[i])
        for i, (source, target) in enumerate(((kind_ref, kind), (x_ref, x), (g_ref, g)))
    ]
    for copy in copies:
        copy.start()
    tokens = kind.shape[1]
    copies[0].wait()
    key = kind[...] ^ plane_ref[0]
    onehot = (key == lax.broadcasted_iota(jnp.int32, (8, tokens), 0)).astype(F32)
    before = lax.broadcasted_iota(jnp.int32, (tokens, tokens), 0) < lax.broadcasted_iota(
        jnp.int32, (tokens, tokens), 1
    )
    ranks = jnp.dot(onehot.astype(BF16), before.astype(BF16), preferred_element_type=F32)
    rank = jnp.sum(ranks * onehot, axis=0, keepdims=True).astype(jnp.int32)
    place = key * CAP + rank
    slots = EXPERTS * CAP
    placer = (place == lax.broadcasted_iota(jnp.int32, (slots, tokens), 0)).astype(F32).astype(BF16)
    placer_ref[...] = placer
    for copy, source, first in ((copies[1], x, 0), (copies[2], g, EXPERTS)):
        copy.wait()
        packed = jnp.dot(placer, source[...], preferred_element_type=F32)
        for k in range(EXPERTS):
            outs[first + k][...] = packed[k * CAP : (k + 1) * CAP].astype(BF16)


def pack(scalars, kind, x, g):
    tokens, width = x.shape
    return pl.pallas_call(
        pack_kernel,
        out_shape=[jax.ShapeDtypeStruct((EXPERTS * CAP, tokens), BF16)]
        + [jax.ShapeDtypeStruct((CAP, width), BF16)] * (2 * EXPERTS),
        in_specs=[pl.BlockSpec(memory_space=pltpu.SMEM)] * 3 + [AFAR] * 3,
        scratch_shapes=[
            pltpu.VMEM((1, tokens), jnp.int32),
            pltpu.VMEM((tokens, width), BF16),
            pltpu.VMEM((tokens, width), BF16),
            pltpu.SemaphoreType.DMA((3,)),
        ],
        compiler_params=SMALL,
        cost_estimate=CHEAP,
        name="pack",
    )(*scalars, kept(kind), kept(x), kept(g))


def join_kernel(*refs):
    refs[-1][...] = stacked(refs[EXPERTS - 1 :: -1]).astype(BF16)


def join(blocks, earlier=()):
    width = blocks[0].shape[1]
    return pl.pallas_call(
        join_kernel,
        out_shape=jax.ShapeDtypeStruct((EXPERTS * CAP, width), BF16),
        in_specs=[HERE] * EXPERTS + [ANYWHERE] * len(earlier),
        compiler_params=SMALL,
        cost_estimate=CHEAP,
        name="join",
    )(*blocks[::-1], *earlier)


def relay_kernel(n, *refs):
    for i in range(n):
        refs[len(refs) - n + i][...] = refs[i][...]


def relay(values, earlier):
    n = len(values)
    return pl.pallas_call(
        functools.partial(relay_kernel, n),
        out_shape=[jax.ShapeDtypeStruct(v.shape, v.dtype) for v in values],
        in_specs=[HERE] * n + [ANYWHERE] * len(earlier),
        compiler_params=SMALL,
        cost_estimate=CHEAP,
        name="relay",
    )(*values, *earlier)


def mark_kernel(value_ref, mark_ref):
    mark_ref[...] = value_ref[: mark_ref.shape[0], : mark_ref.shape[1]]


def mark(value):
    return pl.pallas_call(
        mark_kernel,
        out_shape=jax.ShapeDtypeStruct((16, 128), value.dtype),
        in_specs=[HERE],
        compiler_params=SMALL,
        cost_estimate=CHEAP,
        name="mark",
    )(value)


def flip_kernel(source_ref, here_ref, flipped_ref, sems):
    steps = source_ref.shape[0] // STRIP
    copies = []
    for j in range(steps):
        rows = pl.ds(j * STRIP, STRIP)
        copies.append(pltpu.make_async_copy(source_ref.at[rows], here_ref.at[rows], sems.at[j]))
        copies[j].start()
    for j in range(steps):
        copies[j].wait()
        rows = slice(j * STRIP, (j + 1) * STRIP)
        flipped_ref[:, rows] = here_ref[rows, :].T


def flip(value):
    return pl.pallas_call(
        flip_kernel,
        out_shape=[pltpu.VMEM(value.shape, value.dtype), pltpu.VMEM(value.shape[::-1], value.dtype)],
        in_specs=[AFAR],
        out_specs=[HERE, HERE],
        scratch_shapes=[pltpu.SemaphoreType.DMA((value.shape[0] // STRIP,))],
        compiler_params=SMALL,
        cost_estimate=CHEAP,
        name="flip",
    )(kept(value))


def forward_kernel(n, fetch, down, pair, unused, *refs):
    refs = list(refs)
    xs = [refs.pop(0) for _ in range(n)]
    wg_ref, wu_ref = refs.pop(0), refs.pop(0)
    wd_ref = refs.pop(0) if down else None
    other_ref = refs.pop(0) if pair else None
    refs = refs[unused:]
    act_ref, coef_ref = refs.pop(0), refs.pop(0)
    shares = [refs.pop(0) for _ in range(EXPERTS if pair else down)]
    if fetch:
        sources, sems = (wg_ref, wu_ref), refs.pop()
        wg_ref, wu_ref = refs.pop(0), refs.pop(0)
    acc_ref = refs.pop(0) if down else None
    part = xs[0].shape[0]
    x_ref = xs[0]
    if n > 1:
        x_ref = refs.pop(0)
        for i in range(n):
            x_ref[i * part : (i + 1) * part, :] = xs[i][...]
    steps = wg_ref.shape[1] // PAIR

    def copies(j):
        cols = pl.ds(pl.multiple_of(j * PAIR, PAIR), PAIR)
        return [
            pltpu.make_async_copy(source.at[:, cols], target.at[:, cols], sems.at[j, i])
            for i, (source, target) in enumerate(zip(sources, (wg_ref, wu_ref)))
        ]

    if fetch:
        for j in range(steps):
            for copy in copies(j):
                copy.start()
    if down:
        acc_ref[...] = jnp.zeros_like(acc_ref)

    @pl.loop(0, steps)
    def _(j):
        if fetch:
            for copy in copies(j):
                copy.wait()
        for i in range(PAIR // STRIP):
            cols = pl.ds(pl.multiple_of(j * PAIR + i * STRIP, STRIP), STRIP)
            gate = jnp.dot(x_ref[...], wg_ref[:, cols], preferred_element_type=F32)
            up = jnp.dot(x_ref[...], wu_ref[:, cols], preferred_element_type=F32)
            act, slope = silu_parts(gate)
            act_ref[:, cols] = act.astype(BF16)
            coef_ref[:, cols] = (up * slope).astype(BF16)
            if down:
                hidden = (act[:part] * up[:part]).astype(BF16)
                acc_ref[...] += jnp.dot(hidden, wd_ref[cols, :], preferred_element_type=F32)

    if pair:
        other = other_ref[...].astype(F32)
        for k in range(EXPERTS):
            rows = slice(k * CAP, (k + 1) * CAP)
            block = jnp.concatenate([other[rows], acc_ref[rows, :]], axis=0).astype(BF16)
            shares[k][...] = block
    elif down:
        shares[0][...] = acc_ref[...].astype(BF16)


def forward(xs, wg, wu, wd=None, other=None, fetch=False, earlier=()):
    n, (part, width), cols = len(xs), xs[0].shape, wg.shape[1]
    rows = n * part
    down, pair = wd is not None, other is not None
    shares = [jax.ShapeDtypeStruct((part, width), BF16)] * down
    if pair:
        shares = [jax.ShapeDtypeStruct((2 * CAP, width), BF16)] * EXPERTS
    weights = [kept(wg), kept(wu)] if fetch else [wg, wu]
    return pl.pallas_call(
        functools.partial(forward_kernel, n, fetch, down, pair, len(earlier)),
        out_shape=[jax.ShapeDtypeStruct((rows, cols), BF16)] * 2
        + shares
        + [pltpu.VMEM(wg.shape, wg.dtype)] * (2 * fetch),
        in_specs=[HERE] * n
        + [AFAR if fetch else HERE] * 2
        + [HERE] * (down + pair)
        + [ANYWHERE] * len(earlier),
        scratch_shapes=[pltpu.VMEM((part, width), F32)] * down
        + [pltpu.VMEM((rows, width), BF16)] * (n > 1)
        + [pltpu.SemaphoreType.DMA((cols // PAIR, 2))] * fetch,
        compiler_params=LARGE,
        cost_estimate=CHEAP,
        name="forward" + "_fetch" * fetch + "_down" * down,
    )(*xs, *weights, *([wd] * down), *([other] * pair), *earlier)


def turn_kernel(_, __, *refs):
    refs[8][: refs[0].shape[1], :] = stacked(refs[0:4]).T.astype(BF16)
    refs[8][refs[0].shape[1] :, :] = stacked(refs[4:8]).T.astype(BF16)


def turn(own, sib, xs, share):
    part = xs[0].shape[0]
    rows = len(xs) * part
    return pl.pallas_call(
        turn_kernel,
        grid_spec=pltpu.PrefetchScalarGridSpec(
            num_scalar_prefetch=2,
            grid=(1,),
            in_specs=[pl.BlockSpec((part, share), lambda j, a, b: (0, a[0]))] * 4
            + [pl.BlockSpec((part, share), lambda j, a, b: (0, b[0]))] * 4,
            out_specs=pl.BlockSpec((2 * share, rows), lambda j, a, b: (0, 0)),
        ),
        out_shape=jax.ShapeDtypeStruct((2 * share, rows), BF16),
        compiler_params=SMALL,
        cost_estimate=CHEAP,
        name="turn",
    )(own, sib, *xs, *xs)


def backward_kernel(first, counts, xt_ref, *refs):
    n = len(counts)
    gs, acts, coefs = refs[:4], refs[4 : 4 + n], refs[4 + n : 4 + 2 * n]
    wdt_ref, *_, own_ref, sib_ref, g_ref = refs[4 + 2 * n :]
    part = gs[0].shape[0]
    share = own_ref.shape[0] // 2
    for i in range(4):
        g_ref[i * part : (i + 1) * part, :] = gs[i][...]

    def strip(start):
        here = pl.ds(pl.multiple_of(start, STRIP), STRIP)
        cols = pl.ds(pl.multiple_of(start + first, STRIP), STRIP)
        d_hidden = jnp.dot(g_ref[...], wdt_ref[:, cols], preferred_element_type=F32)
        for row, parts in ((0, coefs), (share, acts)):
            factor = jnp.concatenate([p[:, cols] for p in parts], axis=0).astype(F32)
            d_cols = (d_hidden * factor).astype(BF16)
            total = jnp.dot(xt_ref[...], d_cols, preferred_element_type=F32).astype(BF16)
            own_ref[row : row + share, here] = total[:share]
            sib_ref[row : row + share, here] = total[share:]

    pairs = own_ref.shape[1] // PAIR

    @pl.loop(0, pairs)
    def _(j):
        for i in range(PAIR // STRIP):
            strip(j * PAIR + i * STRIP)

    for start in range(pairs * PAIR, own_ref.shape[1], STRIP):
        strip(start)


def backward(xt, gs, acts, coefs, wdt, first, cols, earlier=()):
    part, width = gs[0].shape
    height, rows = xt.shape
    counts = tuple(a.shape[0] for a in acts)
    return pl.pallas_call(
        functools.partial(backward_kernel, first, counts),
        out_shape=[jax.ShapeDtypeStruct((height, cols), BF16)] * 2,
        in_specs=[HERE] * (6 + 2 * len(acts)) + [ANYWHERE] * len(earlier),
        scratch_shapes=[pltpu.VMEM((rows, width), BF16)],
        compiler_params=LARGE,
        cost_estimate=DEAR,
        name="backward",
    )(xt, *gs, *acts, *coefs, wdt, *earlier)


def finish_kernel(spans, more, *refs):
    n = len(spans)
    pairs = [refs[2 * i : 2 * i + 2] for i in range(n)]
    gate_ref, up_ref, gate, up, sems = refs[2 * n + 2 * more :]
    share = gate_ref.shape[0]
    low = spans[0][0]
    copies = []
    for i, ((first, cols), (own, got)) in enumerate(zip(spans, pairs)):
        for j, (target, held) in enumerate(((gate_ref, gate), (up_ref, up))):
            rows = slice(j * share, (j + 1) * share)
            here = pl.ds(first - low, cols)
            held[:, here] = (own[rows, :].astype(F32) + got[rows, :].astype(F32)).astype(BF16)
            copies.append(
                pltpu.make_async_copy(held.at[:, here], target.at[:, pl.ds(first, cols)], sems.at[i, j])
            )
            copies[-1].start()
    for copy in copies:
        copy.wait()


def finish(owns, gots, firsts, width, held=()):
    share = owns[0].shape[0] // 2
    spans = tuple((first, own.shape[1]) for first, own in zip(firsts, owns))
    total = sum(cols for _, cols in spans)
    n, more = len(owns), len(held) > 0
    return pl.pallas_call(
        functools.partial(finish_kernel, spans, more),
        out_shape=[jax.ShapeDtypeStruct((share, width), BF16)] * 2,
        in_specs=[HERE] * (2 * n) + [ANYWHERE] * (2 * more),
        out_specs=[ANYWHERE] * 2,
        scratch_shapes=[pltpu.VMEM((share, total), BF16)] * 2 + [pltpu.SemaphoreType.DMA((n, 2))],
        input_output_aliases={2 * n: 0, 2 * n + 1: 1} if more else {},
        compiler_params=SMALL,
        cost_estimate=CHEAP,
        name="finish",
    )(*[v for both in zip(owns, gots) for v in both], *held)


def split_kernel(*refs):
    blocks = [r[...].astype(F32) for r in refs[:EXPERTS]]
    refs[-2][...] = jnp.concatenate([b[:CAP] for b in blocks], axis=0).astype(BF16)
    refs[-1][...] = jnp.concatenate([b[CAP:] for b in blocks], axis=0).astype(BF16)


def split(blocks, earlier):
    width = blocks[0].shape[1]
    return pl.pallas_call(
        split_kernel,
        out_shape=[jax.ShapeDtypeStruct((EXPERTS * CAP, width), BF16)] * 2,
        in_specs=[HERE] * EXPERTS + [ANYWHERE] * len(earlier),
        compiler_params=SMALL,
        cost_estimate=CHEAP,
        name="split",
    )(*blocks, *earlier)


def unpack_kernel(placer_ref, mine_ref, got_ref, *refs):
    chosen = placer_ref[...].astype(F32).T.astype(BF16)
    total = jnp.dot(chosen, mine_ref[...], preferred_element_type=F32)
    total += jnp.dot(chosen, got_ref[...], preferred_element_type=F32)
    refs[-1][...] = total.astype(BF16)


def unpack(placer, mine, got, earlier):
    return pl.pallas_call(
        unpack_kernel,
        out_shape=jax.ShapeDtypeStruct((placer.shape[1], mine.shape[1]), BF16),
        in_specs=[HERE] * 3 + [AFAR] * len(earlier),
        compiler_params=SMALL,
        cost_estimate=DEAR,
        name="unpack",
    )(placer, mine, got, *[kept(v) for v in earlier])


def swap(value, axis):
    return lax.ppermute(value, axis, [(0, 1), (1, 0)])


def across_planes(blocks):
    return [blocks[0]] + [
        lax.ppermute(blocks[k], "arch", [(i, i ^ k) for i in range(EXPERTS)]) for k in range(1, EXPERTS)
    ]


def after(values, earlier):
    n = len(values)
    return list(lax.optimization_barrier((*values, *earlier))[:n])


def gathering(designs, archetype, w_gate, w_up, w_down, cotangent):
    far, core = lax.axis_index("far"), lax.axis_index("core")
    scalars = [lax.axis_index("arch"), 2 * far + core, 2 * far + 1 - core]
    scalars = [v.astype(jnp.int32)[None] for v in scalars]
    tokens, width = designs.shape
    share = width // 4
    placer, *blocks = pack(scalars, archetype.reshape(1, tokens), designs, cotangent)
    wd, wdt = flip(after([w_down], [placer])[0])

    moved = across_planes(blocks[:EXPERTS])
    x_own = join(moved, [wdt])
    x_near, x_far = swap(x_own, "half"), swap(x_own, "far")
    moved = across_planes(blocks[EXPERTS:])
    g_own = join(moved, [x_own])
    g_near, g_far = swap(g_own, "half"), swap(g_own, "far")

    wg, wu = w_gate, w_up
    act0, coef0, share_own = forward([x_own], wg, wu, wd)
    act1, coef1, *shares = forward([x_near, x_far], wg, wu, wd, other=share_own)
    x_pass, g_pass = relay([x_near, g_far], [mark(act1), g_near])
    x_corner, g_corner = swap(x_pass, "far"), swap(g_pass, "half")
    returned = across_planes(shares)
    act2, coef2 = forward([x_corner], wg, wu)
    xt = turn(*scalars[1:], [x_own, x_near, x_far, x_corner], share)

    gs = [g_own, g_near, g_far, g_corner]
    acts, coefs = [act0, act1, act2], [coef0, coef1, coef2]
    cols = w_down.shape[0]
    half = cols // 2
    own0, sib0 = backward(xt, gs, acts, coefs, wdt, 0, half)
    mine, theirs = split(returned, [own0])
    got = swap(theirs, "half")
    own1, sib1 = backward(xt, gs, acts, coefs, wdt, half, half, [mine])
    got0, got1 = swap(sib0, "core"), swap(sib1, "core")
    held = finish([own0], [got0], (0,), cols)
    outputs = unpack(placer, mine, got, held[:1])
    grad_gate, grad_up = finish([own1], [got1], (half,), cols, held)
    return outputs, grad_gate, grad_up


def reducing(designs, archetype, w_gate, w_up, w_down, cotangent):
    width = designs.shape[1]
    owners = lax.axis_size("expert")
    sharers = owners // EXPERTS
    hidden_cols = w_gate.shape[1]
    labels = archetype[:, 0]
    onehot = (labels[:, None] == jnp.arange(EXPERTS, dtype=jnp.int32)[None, :]).astype(jnp.int32)
    ranks = jnp.cumsum(onehot, axis=0) - onehot
    target = labels * CAP + jnp.sum(ranks * onehot, axis=1)
    placer = (jnp.arange(EXPERTS * CAP, dtype=jnp.int32)[:, None] == target[None, :]).astype(BF16)
    received = []
    for rows in (designs, cotangent):
        packed = jnp.dot(placer, rows, preferred_element_type=F32).astype(BF16)
        send = jnp.repeat(packed.reshape(EXPERTS, CAP, width), sharers, axis=0)
        received.append(
            lax.all_to_all(send, "expert", split_axis=0, concat_axis=0, tiled=True).reshape(
                owners * CAP, width
            )
        )
    flat_x, flat_g = received
    gate = jnp.dot(flat_x, w_gate, preferred_element_type=F32)
    up = jnp.dot(flat_x, w_up, preferred_element_type=F32)
    act, slope = silu_parts(gate)
    hidden = (act * up).astype(BF16)
    partial_value = (
        jnp.dot(hidden, w_down, preferred_element_type=F32).astype(BF16).reshape(owners, CAP, width)
    )
    returned = lax.all_to_all(partial_value, "expert", split_axis=0, concat_axis=0, tiled=True)
    summed = jnp.sum(returned.astype(F32).reshape(EXPERTS, sharers, CAP, width), axis=1).reshape(
        EXPERTS * CAP, width
    )
    outputs = jnp.take(summed, target, axis=0).astype(BF16)
    d_hidden = contract_cols(flat_g, w_down)
    d_gate = (d_hidden * up * slope).astype(BF16)
    d_up = (d_hidden * act).astype(BF16)
    grads = jnp.concatenate([contract_rows(flat_x, d_gate), contract_rows(flat_x, d_up)], axis=1)
    mine = lax.psum_scatter(grads.astype(BF16), "dp", scatter_dimension=0, tiled=True)
    return outputs, mine[:, :hidden_cols], mine[:, hidden_cols:]


def solution(mesh):
    dp, owners = mesh.devices.shape
    if (dp, owners) == (4, 2 * EXPERTS):
        rows, cols = ("far", "core"), ("arch", "half")
        mesh = Mesh(mesh.devices.reshape(2, 2, EXPERTS, 2), rows + cols)
        body = gathering
    else:
        rows, cols = ("dp",), ("expert",)
        body = reducing
    tokens = P(rows + cols, None)
    return jax.shard_map(
        body,
        mesh=mesh,
        in_specs=(tokens, tokens, P(None, cols), P(None, cols), P(cols, None), tokens),
        out_specs=(tokens, P(rows, cols), P(rows, cols)),
        check_vma=False,
    )
```

```python
import functools

import jax
import jax.numpy as jnp
from jax import lax
from jax.experimental import pallas as pl
from jax.experimental.pallas import tpu as pltpu
from jax.sharding import Mesh
from jax.sharding import PartitionSpec as P

EXPERTS = 4
CAP = 36
STRIP = 256
PAIR = 2 * STRIP
MIB = 1024 * 1024
LARGE = pltpu.CompilerParams(vmem_limit_bytes=16 * MIB)
SMALL = pltpu.CompilerParams(vmem_limit_bytes=12 * MIB)
CHEAP = pl.CostEstimate(flops=0, bytes_accessed=0, transcendentals=0)
DEAR = pl.CostEstimate(flops=20_000_000_000, bytes_accessed=0, transcendentals=0)
F32 = jnp.float32
BF16 = jnp.bfloat16
HERE = pl.BlockSpec(memory_space=pltpu.VMEM)
AFAR = pl.BlockSpec(memory_space=pltpu.HBM)
ANYWHERE = pl.BlockSpec(memory_space=pl.ANY)


def silu_parts(gate):
    sigma = 0.5 * jnp.tanh(0.5 * gate) + 0.5
    return (gate * sigma, sigma * (1.0 + gate * (1.0 - sigma)))


def contract_rows(left, right):
    return lax.dot_general(left, right, (((0,), (0,)), ((), ())), preferred_element_type=F32)


def contract_cols(left, right):
    return lax.dot_general(left, right, (((1,), (1,)), ((), ())), preferred_element_type=F32)


def stacked(refs):
    return jnp.concatenate([r[...].astype(F32) for r in refs], axis=0)


def kept(value):
    return pltpu.with_memory_space_constraint(value, pltpu.HBM)


def pack_kernel(plane_ref, _, __, kind_ref, x_ref, g_ref, placer_ref, *refs):
    outs, (kind, x, g, sems) = refs[: 2 * EXPERTS], refs[2 * EXPERTS :]
    copies = [
        pltpu.make_async_copy(source, target, sems.at[i])
        for i, (source, target) in enumerate(((kind_ref, kind), (x_ref, x), (g_ref, g)))
    ]
    for copy in copies:
        copy.start()
    tokens = kind.shape[1]
    copies[0].wait()
    key = kind[...] ^ plane_ref[0]
    onehot = (key == lax.broadcasted_iota(jnp.int32, (8, tokens), 0)).astype(F32)
    before = lax.broadcasted_iota(jnp.int32, (tokens, tokens), 0) < lax.broadcasted_iota(
        jnp.int32, (tokens, tokens), 1
    )
    ranks = jnp.dot(onehot.astype(BF16), before.astype(BF16), preferred_element_type=F32)
    rank = jnp.sum(ranks * onehot, axis=0, keepdims=True).astype(jnp.int32)
    place = key * CAP + rank
    slots = EXPERTS * CAP
    placer = (place == lax.broadcasted_iota(jnp.int32, (slots, tokens), 0)).astype(F32).astype(BF16)
    placer_ref[...] = placer
    for copy, source, first in ((copies[1], x, 0), (copies[2], g, EXPERTS)):
        copy.wait()
        packed = jnp.dot(placer, source[...], preferred_element_type=F32)
        for k in range(EXPERTS):
            outs[first + k][...] = packed[k * CAP : (k + 1) * CAP].astype(BF16)


def pack(scalars, kind, x, g):
    tokens, width = x.shape
    return pl.pallas_call(
        pack_kernel,
        out_shape=[jax.ShapeDtypeStruct((EXPERTS * CAP, tokens), BF16)]
        + [jax.ShapeDtypeStruct((CAP, width), BF16)] * (2 * EXPERTS),
        in_specs=[pl.BlockSpec(memory_space=pltpu.SMEM)] * 3 + [AFAR] * 3,
        scratch_shapes=[
            pltpu.VMEM((1, tokens), jnp.int32),
            pltpu.VMEM((tokens, width), BF16),
            pltpu.VMEM((tokens, width), BF16),
            pltpu.SemaphoreType.DMA((3,)),
        ],
        compiler_params=SMALL,
        cost_estimate=CHEAP,
        name="pack",
    )(*scalars, kept(kind), kept(x), kept(g))


def join_kernel(*refs):
    refs[-1][...] = stacked(refs[EXPERTS - 1 :: -1]).astype(BF16)


def join(blocks, earlier=()):
    width = blocks[0].shape[1]
    return pl.pallas_call(
        join_kernel,
        out_shape=jax.ShapeDtypeStruct((EXPERTS * CAP, width), BF16),
        in_specs=[HERE] * EXPERTS + [ANYWHERE] * len(earlier),
        compiler_params=SMALL,
        cost_estimate=CHEAP,
        name="join",
    )(*blocks[::-1], *earlier)


def relay_kernel(n, *refs):
    for i in range(n):
        refs[len(refs) - n + i][...] = refs[i][...]


def relay(values, earlier):
    n = len(values)
    return pl.pallas_call(
        functools.partial(relay_kernel, n),
        out_shape=[jax.ShapeDtypeStruct(v.shape, v.dtype) for v in values],
        in_specs=[HERE] * n + [ANYWHERE] * len(earlier),
        compiler_params=SMALL,
        cost_estimate=CHEAP,
        name="relay",
    )(*values, *earlier)


def mark_kernel(value_ref, mark_ref):
    mark_ref[...] = value_ref[: mark_ref.shape[0], : mark_ref.shape[1]]


def mark(value):
    return pl.pallas_call(
        mark_kernel,
        out_shape=jax.ShapeDtypeStruct((16, 128), value.dtype),
        in_specs=[HERE],
        compiler_params=SMALL,
        cost_estimate=CHEAP,
        name="mark",
    )(value)


def flip_kernel(source_ref, here_ref, flipped_ref, sems):
    steps = source_ref.shape[0] // STRIP
    copies = []
    for j in range(steps):
        rows = pl.ds(j * STRIP, STRIP)
        copies.append(pltpu.make_async_copy(source_ref.at[rows], here_ref.at[rows], sems.at[j]))
        copies[j].start()
    for j in range(steps):
        copies[j].wait()
        rows = slice(j * STRIP, (j + 1) * STRIP)
        flipped_ref[:, rows] = here_ref[rows, :].T


def flip(value):
    return pl.pallas_call(
        flip_kernel,
        out_shape=[pltpu.VMEM(value.shape, value.dtype), pltpu.VMEM(value.shape[::-1], value.dtype)],
        in_specs=[AFAR],
        out_specs=[HERE, HERE],
        scratch_shapes=[pltpu.SemaphoreType.DMA((value.shape[0] // STRIP,))],
        compiler_params=SMALL,
        cost_estimate=CHEAP,
        name="flip",
    )(kept(value))


def forward_kernel(n, fetch, down, pair, unused, *refs):
    refs = list(refs)
    xs = [refs.pop(0) for _ in range(n)]
    wg_ref, wu_ref = refs.pop(0), refs.pop(0)
    wd_ref = refs.pop(0) if down else None
    other_ref = refs.pop(0) if pair else None
    plane_ref = refs.pop(0) if pair else None
    refs = refs[unused:]
    act_ref, coef_ref = refs.pop(0), refs.pop(0)
    share_ref = refs.pop(0) if down else None
    if fetch:
        sources, sems = (wg_ref, wu_ref), refs.pop()
        wg_ref, wu_ref = refs.pop(0), refs.pop(0)
    acc_ref = refs.pop(0) if down else None
    part = xs[0].shape[0]
    x_ref = xs[0]
    if n > 1:
        x_ref = refs.pop(0)
        for i in range(n):
            x_ref[i * part : (i + 1) * part, :] = xs[i][...]
    steps = wg_ref.shape[1] // PAIR

    def copies(j):
        cols = pl.ds(pl.multiple_of(j * PAIR, PAIR), PAIR)
        return [
            pltpu.make_async_copy(source.at[:, cols], target.at[:, cols], sems.at[j, i])
            for i, (source, target) in enumerate(zip(sources, (wg_ref, wu_ref)))
        ]

    if fetch:
        for j in range(steps):
            for copy in copies(j):
                copy.start()
    if down:
        acc_ref[...] = jnp.zeros_like(acc_ref)

    @pl.loop(0, steps)
    def _(j):
        if fetch:
            for copy in copies(j):
                copy.wait()
        for i in range(PAIR // STRIP):
            cols = pl.ds(pl.multiple_of(j * PAIR + i * STRIP, STRIP), STRIP)
            gate = jnp.dot(x_ref[...], wg_ref[:, cols], preferred_element_type=F32)
            up = jnp.dot(x_ref[...], wu_ref[:, cols], preferred_element_type=F32)
            act, slope = silu_parts(gate)
            act_ref[:, cols] = act.astype(BF16)
            coef_ref[:, cols] = (up * slope).astype(BF16)
            if down:
                hidden = (act[:part] * up[:part]).astype(BF16)
                acc_ref[...] += jnp.dot(hidden, wd_ref[cols, :], preferred_element_type=F32)

    if pair:
        other = other_ref[...].astype(F32)
        for k in range(EXPERTS):
            rows = slice(k * CAP, (k + 1) * CAP)
            block = jnp.concatenate([other[rows], acc_ref[rows, :]], axis=0).astype(BF16)
            share_ref[plane_ref[0] ^ k] = block
    elif down:
        share_ref[...] = acc_ref[...].astype(BF16)


def forward(xs, wg, wu, wd=None, other=None, plane=None, fetch=False, earlier=()):
    n, (part, width), cols = len(xs), xs[0].shape, wg.shape[1]
    rows = n * part
    down, pair = wd is not None, other is not None
    shares = jax.ShapeDtypeStruct((EXPERTS, 2 * CAP, width) if pair else (part, width), BF16)
    weights = [kept(wg), kept(wu)] if fetch else [wg, wu]
    return pl.pallas_call(
        functools.partial(forward_kernel, n, fetch, down, pair, len(earlier)),
        out_shape=[jax.ShapeDtypeStruct((rows, cols), BF16)] * 2
        + [shares] * down
        + [pltpu.VMEM(wg.shape, wg.dtype)] * (2 * fetch),
        in_specs=[HERE] * n
        + [AFAR if fetch else HERE] * 2
        + [HERE] * (down + pair)
        + [pl.BlockSpec(memory_space=pltpu.SMEM)] * pair
        + [ANYWHERE] * len(earlier),
        scratch_shapes=[pltpu.VMEM((part, width), F32)] * down
        + [pltpu.VMEM((rows, width), BF16)] * (n > 1)
        + [pltpu.SemaphoreType.DMA((cols // PAIR, 2))] * fetch,
        compiler_params=LARGE,
        cost_estimate=CHEAP,
        name="forward" + "_fetch" * fetch + "_down" * down,
    )(*xs, *weights, *([wd] * down), *([other, plane] if pair else []), *earlier)


def turn_kernel(_, __, *refs):
    refs[8][: refs[0].shape[1], :] = stacked(refs[0:4]).T.astype(BF16)
    refs[8][refs[0].shape[1] :, :] = stacked(refs[4:8]).T.astype(BF16)


def turn(own, sib, xs, share):
    part = xs[0].shape[0]
    rows = len(xs) * part
    return pl.pallas_call(
        turn_kernel,
        grid_spec=pltpu.PrefetchScalarGridSpec(
            num_scalar_prefetch=2,
            grid=(1,),
            in_specs=[pl.BlockSpec((part, share), lambda j, a, b: (0, a[0]))] * 4
            + [pl.BlockSpec((part, share), lambda j, a, b: (0, b[0]))] * 4,
            out_specs=pl.BlockSpec((2 * share, rows), lambda j, a, b: (0, 0)),
        ),
        out_shape=jax.ShapeDtypeStruct((2 * share, rows), BF16),
        compiler_params=SMALL,
        cost_estimate=CHEAP,
        name="turn",
    )(own, sib, *xs, *xs)


def backward_kernel(first, counts, xt_ref, *refs):
    n = len(counts)
    gs, acts, coefs = refs[:4], refs[4 : 4 + n], refs[4 + n : 4 + 2 * n]
    wdt_ref, *_, own_ref, sib_ref, g_ref = refs[4 + 2 * n :]
    part = gs[0].shape[0]
    share = own_ref.shape[0] // 2
    for i in range(4):
        g_ref[i * part : (i + 1) * part, :] = gs[i][...]

    def strip(start):
        here = pl.ds(pl.multiple_of(start, STRIP), STRIP)
        cols = pl.ds(pl.multiple_of(start + first, STRIP), STRIP)
        d_hidden = jnp.dot(g_ref[...], wdt_ref[:, cols], preferred_element_type=F32)
        for row, parts in ((0, coefs), (share, acts)):
            factor = jnp.concatenate([p[:, cols] for p in parts], axis=0).astype(F32)
            d_cols = (d_hidden * factor).astype(BF16)
            total = jnp.dot(xt_ref[...], d_cols, preferred_element_type=F32).astype(BF16)
            own_ref[row : row + share, here] = total[:share]
            sib_ref[row : row + share, here] = total[share:]

    pairs = own_ref.shape[1] // PAIR

    @pl.loop(0, pairs)
    def _(j):
        for i in range(PAIR // STRIP):
            strip(j * PAIR + i * STRIP)

    for start in range(pairs * PAIR, own_ref.shape[1], STRIP):
        strip(start)


def backward(xt, gs, acts, coefs, wdt, first, cols, earlier=()):
    part, width = gs[0].shape
    height, rows = xt.shape
    counts = tuple(a.shape[0] for a in acts)
    return pl.pallas_call(
        functools.partial(backward_kernel, first, counts),
        out_shape=[jax.ShapeDtypeStruct((height, cols), BF16)] * 2,
        in_specs=[HERE] * (6 + 2 * len(acts)) + [ANYWHERE] * len(earlier),
        scratch_shapes=[pltpu.VMEM((rows, width), BF16)],
        compiler_params=LARGE,
        cost_estimate=DEAR,
        name="backward",
    )(xt, *gs, *acts, *coefs, wdt, *earlier)


def finish_kernel(spans, more, *refs):
    n = len(spans)
    pairs = [refs[2 * i : 2 * i + 2] for i in range(n)]
    gate_ref, up_ref, gate, up, sems = refs[2 * n + 2 * more :]
    share = gate_ref.shape[0]
    low = spans[0][0]
    copies = []
    for i, ((first, cols), (own, got)) in enumerate(zip(spans, pairs)):
        for j, (target, held) in enumerate(((gate_ref, gate), (up_ref, up))):
            rows = slice(j * share, (j + 1) * share)
            here = pl.ds(first - low, cols)
            held[:, here] = (own[rows, :].astype(F32) + got[rows, :].astype(F32)).astype(BF16)
            copies.append(
                pltpu.make_async_copy(held.at[:, here], target.at[:, pl.ds(first, cols)], sems.at[i, j])
            )
            copies[-1].start()
    for copy in copies:
        copy.wait()


def finish(owns, gots, firsts, width, held=()):
    share = owns[0].shape[0] // 2
    spans = tuple((first, own.shape[1]) for first, own in zip(firsts, owns))
    total = sum(cols for _, cols in spans)
    n, more = len(owns), len(held) > 0
    return pl.pallas_call(
        functools.partial(finish_kernel, spans, more),
        out_shape=[jax.ShapeDtypeStruct((share, width), BF16)] * 2,
        in_specs=[HERE] * (2 * n) + [ANYWHERE] * (2 * more),
        out_specs=[ANYWHERE] * 2,
        scratch_shapes=[pltpu.VMEM((share, total), BF16)] * 2 + [pltpu.SemaphoreType.DMA((n, 2))],
        input_output_aliases={2 * n: 0, 2 * n + 1: 1} if more else {},
        compiler_params=SMALL,
        cost_estimate=CHEAP,
        name="finish",
    )(*[v for both in zip(owns, gots) for v in both], *held)


def split_kernel(plane_ref, blocks_ref, _, upper_ref, lower_ref):
    blocks = [blocks_ref[plane_ref[0] ^ k].astype(F32) for k in range(EXPERTS)]
    upper_ref[...] = jnp.concatenate([b[:CAP] for b in blocks], axis=0).astype(BF16)
    lower_ref[...] = jnp.concatenate([b[CAP:] for b in blocks], axis=0).astype(BF16)


def split(plane, blocks, earlier):
    width = blocks.shape[2]
    return pl.pallas_call(
        split_kernel,
        out_shape=[jax.ShapeDtypeStruct((EXPERTS * CAP, width), BF16)] * 2,
        in_specs=[pl.BlockSpec(memory_space=pltpu.SMEM), HERE, ANYWHERE],
        compiler_params=SMALL,
        cost_estimate=CHEAP,
        name="split",
    )(plane, blocks, earlier)


def unpack_kernel(placer_ref, mine_ref, got_ref, *refs):
    chosen = placer_ref[...].astype(F32).T.astype(BF16)
    total = jnp.dot(chosen, mine_ref[...], preferred_element_type=F32)
    total += jnp.dot(chosen, got_ref[...], preferred_element_type=F32)
    refs[-1][...] = total.astype(BF16)


def unpack(placer, mine, got, earlier):
    return pl.pallas_call(
        unpack_kernel,
        out_shape=jax.ShapeDtypeStruct((placer.shape[1], mine.shape[1]), BF16),
        in_specs=[HERE] * 3 + [AFAR] * len(earlier),
        compiler_params=SMALL,
        cost_estimate=DEAR,
        name="unpack",
    )(placer, mine, got, *[kept(v) for v in earlier])


def swap(value, axis):
    return lax.ppermute(value, axis, [(0, 1), (1, 0)])


def across_planes(blocks):
    return [blocks[0]] + [
        lax.ppermute(blocks[k], "arch", [(i, i ^ k) for i in range(EXPERTS)]) for k in range(1, EXPERTS)
    ]


def after(values, earlier):
    n = len(values)
    return list(lax.optimization_barrier((*values, *earlier))[:n])


def gathering(designs, archetype, w_gate, w_up, w_down, cotangent):
    far, core = lax.axis_index("far"), lax.axis_index("core")
    scalars = [lax.axis_index("arch"), 2 * far + core, 2 * far + 1 - core]
    scalars = [v.astype(jnp.int32)[None] for v in scalars]
    tokens, width = designs.shape
    share = width // 4
    placer, *blocks = pack(scalars, archetype.reshape(1, tokens), designs, cotangent)
    wd, wdt = flip(after([w_down], [placer])[0])

    moved = across_planes(blocks[:EXPERTS])
    x_own = join(moved, [wdt])
    x_near, x_far = swap(x_own, "half"), swap(x_own, "far")
    moved = across_planes(blocks[EXPERTS:])
    g_own = join(moved, [x_own])
    g_near, g_far = swap(g_own, "half"), swap(g_own, "far")

    wg, wu = w_gate, w_up
    act0, coef0, share_own = forward([x_own], wg, wu, wd)
    act1, coef1, shares = forward([x_near, x_far], wg, wu, wd, other=share_own, plane=scalars[0])
    x_pass, g_pass = relay([x_near, g_far], [mark(act1), g_near])
    x_corner, g_corner = swap(x_pass, "far"), swap(g_pass, "half")
    returned = lax.all_to_all(shares, "arch", split_axis=0, concat_axis=0, tiled=True)
    act2, coef2 = forward([x_corner], wg, wu)
    xt = turn(*scalars[1:], [x_own, x_near, x_far, x_corner], share)

    gs = [g_own, g_near, g_far, g_corner]
    acts, coefs = [act0, act1, act2], [coef0, coef1, coef2]
    cols = w_down.shape[0]
    half = cols // 2
    own0, sib0 = backward(xt, gs, acts, coefs, wdt, 0, half)
    mine, theirs = split(scalars[0], returned, own0)
    got = swap(theirs, "half")
    own1, sib1 = backward(xt, gs, acts, coefs, wdt, half, half, [mine])
    got0, got1 = swap(sib0, "core"), swap(sib1, "core")
    held = finish([own0], [got0], (0,), cols)
    outputs = unpack(placer, mine, got, held[:1])
    grad_gate, grad_up = finish([own1], [got1], (half,), cols, held)
    return outputs, grad_gate, grad_up


def reducing(designs, archetype, w_gate, w_up, w_down, cotangent):
    width = designs.shape[1]
    owners = lax.axis_size("expert")
    sharers = owners // EXPERTS
    hidden_cols = w_gate.shape[1]
    labels = archetype[:, 0]
    onehot = (labels[:, None] == jnp.arange(EXPERTS, dtype=jnp.int32)[None, :]).astype(jnp.int32)
    ranks = jnp.cumsum(onehot, axis=0) - onehot
    target = labels * CAP + jnp.sum(ranks * onehot, axis=1)
    placer = (jnp.arange(EXPERTS * CAP, dtype=jnp.int32)[:, None] == target[None, :]).astype(BF16)
    received = []
    for rows in (designs, cotangent):
        packed = jnp.dot(placer, rows, preferred_element_type=F32).astype(BF16)
        send = jnp.repeat(packed.reshape(EXPERTS, CAP, width), sharers, axis=0)
        received.append(
            lax.all_to_all(send, "expert", split_axis=0, concat_axis=0, tiled=True).reshape(
                owners * CAP, width
            )
        )
    flat_x, flat_g = received
    gate = jnp.dot(flat_x, w_gate, preferred_element_type=F32)
    up = jnp.dot(flat_x, w_up, preferred_element_type=F32)
    act, slope = silu_parts(gate)
    hidden = (act * up).astype(BF16)
    partial_value = (
        jnp.dot(hidden, w_down, preferred_element_type=F32).astype(BF16).reshape(owners, CAP, width)
    )
    returned = lax.all_to_all(partial_value, "expert", split_axis=0, concat_axis=0, tiled=True)
    summed = jnp.sum(returned.astype(F32).reshape(EXPERTS, sharers, CAP, width), axis=1).reshape(
        EXPERTS * CAP, width
    )
    outputs = jnp.take(summed, target, axis=0).astype(BF16)
    d_hidden = contract_cols(flat_g, w_down)
    d_gate = (d_hidden * up * slope).astype(BF16)
    d_up = (d_hidden * act).astype(BF16)
    grads = jnp.concatenate([contract_rows(flat_x, d_gate), contract_rows(flat_x, d_up)], axis=1)
    mine = lax.psum_scatter(grads.astype(BF16), "dp", scatter_dimension=0, tiled=True)
    return outputs, mine[:, :hidden_cols], mine[:, hidden_cols:]


def solution(mesh):
    dp, owners = mesh.devices.shape
    if (dp, owners) == (4, 2 * EXPERTS):
        rows, cols = ("far", "core"), ("arch", "half")
        mesh = Mesh(mesh.devices.reshape(2, 2, EXPERTS, 2), rows + cols)
        body = gathering
    else:
        rows, cols = ("dp",), ("expert",)
        body = reducing
    tokens = P(rows + cols, None)
    return jax.shard_map(
        body,
        mesh=mesh,
        in_specs=(tokens, tokens, P(None, cols), P(None, cols), P(cols, None), tokens),
        out_specs=(tokens, P(rows, cols), P(rows, cols)),
        check_vma=False,
    )
```

```python
import functools

import jax
import jax.numpy as jnp
from jax import lax
from jax.experimental import pallas as pl
from jax.experimental.pallas import tpu as pltpu
from jax.sharding import Mesh
from jax.sharding import PartitionSpec as P

EXPERTS = 4
CAP = 36
STRIP = 512
PAIR = 2 * STRIP
MIB = 1024 * 1024
LARGE = pltpu.CompilerParams(vmem_limit_bytes=16 * MIB)
SMALL = pltpu.CompilerParams(vmem_limit_bytes=12 * MIB)
CHEAP = pl.CostEstimate(flops=0, bytes_accessed=0, transcendentals=0)
DEAR = pl.CostEstimate(flops=20_000_000_000, bytes_accessed=0, transcendentals=0)
F32 = jnp.float32
BF16 = jnp.bfloat16
HERE = pl.BlockSpec(memory_space=pltpu.VMEM)
AFAR = pl.BlockSpec(memory_space=pltpu.HBM)
ANYWHERE = pl.BlockSpec(memory_space=pl.ANY)


def silu_parts(gate):
    sigma = 0.5 * jnp.tanh(0.5 * gate) + 0.5
    return (gate * sigma, sigma * (1.0 + gate * (1.0 - sigma)))


def contract_rows(left, right):
    return lax.dot_general(left, right, (((0,), (0,)), ((), ())), preferred_element_type=F32)


def contract_cols(left, right):
    return lax.dot_general(left, right, (((1,), (1,)), ((), ())), preferred_element_type=F32)


def stacked(refs):
    return jnp.concatenate([r[...].astype(F32) for r in refs], axis=0)


def kept(value):
    return pltpu.with_memory_space_constraint(value, pltpu.HBM)


def pack_kernel(plane_ref, _, __, kind_ref, x_ref, g_ref, placer_ref, *refs):
    outs, (kind, x, g, sems) = refs[: 2 * EXPERTS], refs[2 * EXPERTS :]
    copies = [
        pltpu.make_async_copy(source, target, sems.at[i])
        for i, (source, target) in enumerate(((kind_ref, kind), (x_ref, x), (g_ref, g)))
    ]
    for copy in copies:
        copy.start()
    tokens = kind.shape[1]
    copies[0].wait()
    key = kind[...] ^ plane_ref[0]
    onehot = (key == lax.broadcasted_iota(jnp.int32, (8, tokens), 0)).astype(F32)
    before = lax.broadcasted_iota(jnp.int32, (tokens, tokens), 0) < lax.broadcasted_iota(
        jnp.int32, (tokens, tokens), 1
    )
    ranks = jnp.dot(onehot.astype(BF16), before.astype(BF16), preferred_element_type=F32)
    rank = jnp.sum(ranks * onehot, axis=0, keepdims=True).astype(jnp.int32)
    place = key * CAP + rank
    slots = EXPERTS * CAP
    placer = (place == lax.broadcasted_iota(jnp.int32, (slots, tokens), 0)).astype(F32).astype(BF16)
    placer_ref[...] = placer
    for copy, source, first in ((copies[1], x, 0), (copies[2], g, EXPERTS)):
        copy.wait()
        packed = jnp.dot(placer, source[...], preferred_element_type=F32)
        for k in range(EXPERTS):
            outs[first + k][...] = packed[k * CAP : (k + 1) * CAP].astype(BF16)


def pack(scalars, kind, x, g):
    tokens, width = x.shape
    return pl.pallas_call(
        pack_kernel,
        out_shape=[jax.ShapeDtypeStruct((EXPERTS * CAP, tokens), BF16)]
        + [jax.ShapeDtypeStruct((CAP, width), BF16)] * (2 * EXPERTS),
        in_specs=[pl.BlockSpec(memory_space=pltpu.SMEM)] * 3 + [AFAR] * 3,
        scratch_shapes=[
            pltpu.VMEM((1, tokens), jnp.int32),
            pltpu.VMEM((tokens, width), BF16),
            pltpu.VMEM((tokens, width), BF16),
            pltpu.SemaphoreType.DMA((3,)),
        ],
        compiler_params=SMALL,
        cost_estimate=CHEAP,
        name="pack",
    )(*scalars, kept(kind), kept(x), kept(g))


def join_kernel(*refs):
    refs[-1][...] = stacked(refs[EXPERTS - 1 :: -1]).astype(BF16)


def join(blocks, earlier=()):
    width = blocks[0].shape[1]
    return pl.pallas_call(
        join_kernel,
        out_shape=jax.ShapeDtypeStruct((EXPERTS * CAP, width), BF16),
        in_specs=[HERE] * EXPERTS + [ANYWHERE] * len(earlier),
        compiler_params=SMALL,
        cost_estimate=CHEAP,
        name="join",
    )(*blocks[::-1], *earlier)


def relay_kernel(n, *refs):
    for i in range(n):
        refs[len(refs) - n + i][...] = refs[i][...]


def relay(values, earlier):
    n = len(values)
    return pl.pallas_call(
        functools.partial(relay_kernel, n),
        out_shape=[jax.ShapeDtypeStruct(v.shape, v.dtype) for v in values],
        in_specs=[HERE] * n + [ANYWHERE] * len(earlier),
        compiler_params=SMALL,
        cost_estimate=CHEAP,
        name="relay",
    )(*values, *earlier)


def mark_kernel(value_ref, mark_ref):
    mark_ref[...] = value_ref[: mark_ref.shape[0], : mark_ref.shape[1]]


def mark(value):
    return pl.pallas_call(
        mark_kernel,
        out_shape=jax.ShapeDtypeStruct((16, 128), value.dtype),
        in_specs=[HERE],
        compiler_params=SMALL,
        cost_estimate=CHEAP,
        name="mark",
    )(value)


def flip_kernel(source_ref, here_ref, flipped_ref, sems):
    steps = source_ref.shape[0] // STRIP
    copies = []
    for j in range(steps):
        rows = pl.ds(j * STRIP, STRIP)
        copies.append(pltpu.make_async_copy(source_ref.at[rows], here_ref.at[rows], sems.at[j]))
        copies[j].start()
    for j in range(steps):
        copies[j].wait()
        rows = slice(j * STRIP, (j + 1) * STRIP)
        flipped_ref[:, rows] = here_ref[rows, :].T


def flip(value):
    return pl.pallas_call(
        flip_kernel,
        out_shape=[pltpu.VMEM(value.shape, value.dtype), pltpu.VMEM(value.shape[::-1], value.dtype)],
        in_specs=[AFAR],
        out_specs=[HERE, HERE],
        scratch_shapes=[pltpu.SemaphoreType.DMA((value.shape[0] // STRIP,))],
        compiler_params=SMALL,
        cost_estimate=CHEAP,
        name="flip",
    )(kept(value))


def forward_kernel(n, fetch, down, pair, unused, *refs):
    refs = list(refs)
    xs = [refs.pop(0) for _ in range(n)]
    wg_ref, wu_ref = refs.pop(0), refs.pop(0)
    wd_ref = refs.pop(0) if down else None
    other_ref = refs.pop(0) if pair else None
    refs = refs[unused:]
    act_ref, coef_ref = refs.pop(0), refs.pop(0)
    shares = [refs.pop(0) for _ in range(EXPERTS if pair else down)]
    if fetch:
        sources, sems = (wg_ref, wu_ref), refs.pop()
        wg_ref, wu_ref = refs.pop(0), refs.pop(0)
    acc_ref = refs.pop(0) if down else None
    part = xs[0].shape[0]
    x_ref = xs[0]
    if n > 1:
        x_ref = refs.pop(0)
        for i in range(n):
            x_ref[i * part : (i + 1) * part, :] = xs[i][...]
    steps = wg_ref.shape[1] // PAIR

    def copies(j):
        cols = pl.ds(pl.multiple_of(j * PAIR, PAIR), PAIR)
        return [
            pltpu.make_async_copy(source.at[:, cols], target.at[:, cols], sems.at[j, i])
            for i, (source, target) in enumerate(zip(sources, (wg_ref, wu_ref)))
        ]

    if fetch:
        for j in range(steps):
            for copy in copies(j):
                copy.start()
    if down:
        acc_ref[...] = jnp.zeros_like(acc_ref)

    @pl.loop(0, steps)
    def _(j):
        if fetch:
            for copy in copies(j):
                copy.wait()
        for i in range(PAIR // STRIP):
            cols = pl.ds(pl.multiple_of(j * PAIR + i * STRIP, STRIP), STRIP)
            gate = jnp.dot(x_ref[...], wg_ref[:, cols], preferred_element_type=F32)
            up = jnp.dot(x_ref[...], wu_ref[:, cols], preferred_element_type=F32)
            act, slope = silu_parts(gate)
            act_ref[:, cols] = act.astype(BF16)
            coef_ref[:, cols] = (up * slope).astype(BF16)
            if down:
                hidden = (act[:part] * up[:part]).astype(BF16)
                acc_ref[...] += jnp.dot(hidden, wd_ref[cols, :], preferred_element_type=F32)

    if pair:
        other = other_ref[...].astype(F32)
        for k in range(EXPERTS):
            rows = slice(k * CAP, (k + 1) * CAP)
            block = jnp.concatenate([other[rows], acc_ref[rows, :]], axis=0).astype(BF16)
            shares[k][...] = block
    elif down:
        shares[0][...] = acc_ref[...].astype(BF16)


def forward(xs, wg, wu, wd=None, other=None, fetch=False, earlier=()):
    n, (part, width), cols = len(xs), xs[0].shape, wg.shape[1]
    rows = n * part
    down, pair = wd is not None, other is not None
    shares = [jax.ShapeDtypeStruct((part, width), BF16)] * down
    if pair:
        shares = [jax.ShapeDtypeStruct((2 * CAP, width), BF16)] * EXPERTS
    weights = [kept(wg), kept(wu)] if fetch else [wg, wu]
    return pl.pallas_call(
        functools.partial(forward_kernel, n, fetch, down, pair, len(earlier)),
        out_shape=[jax.ShapeDtypeStruct((rows, cols), BF16)] * 2
        + shares
        + [pltpu.VMEM(wg.shape, wg.dtype)] * (2 * fetch),
        in_specs=[HERE] * n
        + [AFAR if fetch else HERE] * 2
        + [HERE] * (down + pair)
        + [ANYWHERE] * len(earlier),
        scratch_shapes=[pltpu.VMEM((part, width), F32)] * down
        + [pltpu.VMEM((rows, width), BF16)] * (n > 1)
        + [pltpu.SemaphoreType.DMA((cols // PAIR, 2))] * fetch,
        compiler_params=LARGE,
        cost_estimate=CHEAP,
        name="forward" + "_fetch" * fetch + "_down" * down,
    )(*xs, *weights, *([wd] * down), *([other] * pair), *earlier)


def turn_kernel(_, __, *refs):
    refs[8][: refs[0].shape[1], :] = stacked(refs[0:4]).T.astype(BF16)
    refs[8][refs[0].shape[1] :, :] = stacked(refs[4:8]).T.astype(BF16)


def turn(own, sib, xs, share):
    part = xs[0].shape[0]
    rows = len(xs) * part
    return pl.pallas_call(
        turn_kernel,
        grid_spec=pltpu.PrefetchScalarGridSpec(
            num_scalar_prefetch=2,
            grid=(1,),
            in_specs=[pl.BlockSpec((part, share), lambda j, a, b: (0, a[0]))] * 4
            + [pl.BlockSpec((part, share), lambda j, a, b: (0, b[0]))] * 4,
            out_specs=pl.BlockSpec((2 * share, rows), lambda j, a, b: (0, 0)),
        ),
        out_shape=jax.ShapeDtypeStruct((2 * share, rows), BF16),
        compiler_params=SMALL,
        cost_estimate=CHEAP,
        name="turn",
    )(own, sib, *xs, *xs)


def backward_kernel(first, counts, xt_ref, *refs):
    n = len(counts)
    gs, acts, coefs = refs[:4], refs[4 : 4 + n], refs[4 + n : 4 + 2 * n]
    wdt_ref, *_, own_ref, sib_ref, g_ref = refs[4 + 2 * n :]
    part = gs[0].shape[0]
    share = own_ref.shape[0] // 2
    for i in range(4):
        g_ref[i * part : (i + 1) * part, :] = gs[i][...]

    def strip(start):
        here = pl.ds(pl.multiple_of(start, STRIP), STRIP)
        cols = pl.ds(pl.multiple_of(start + first, STRIP), STRIP)
        d_hidden = jnp.dot(g_ref[...], wdt_ref[:, cols], preferred_element_type=F32)
        for row, parts in ((0, coefs), (share, acts)):
            factor = jnp.concatenate([p[:, cols] for p in parts], axis=0).astype(F32)
            d_cols = (d_hidden * factor).astype(BF16)
            total = jnp.dot(xt_ref[...], d_cols, preferred_element_type=F32).astype(BF16)
            own_ref[row : row + share, here] = total[:share]
            sib_ref[row : row + share, here] = total[share:]

    pairs = own_ref.shape[1] // PAIR

    @pl.loop(0, pairs)
    def _(j):
        for i in range(PAIR // STRIP):
            strip(j * PAIR + i * STRIP)

    for start in range(pairs * PAIR, own_ref.shape[1], STRIP):
        strip(start)


def backward(xt, gs, acts, coefs, wdt, first, cols, earlier=()):
    part, width = gs[0].shape
    height, rows = xt.shape
    counts = tuple(a.shape[0] for a in acts)
    return pl.pallas_call(
        functools.partial(backward_kernel, first, counts),
        out_shape=[jax.ShapeDtypeStruct((height, cols), BF16)] * 2,
        in_specs=[HERE] * (6 + 2 * len(acts)) + [ANYWHERE] * len(earlier),
        scratch_shapes=[pltpu.VMEM((rows, width), BF16)],
        compiler_params=LARGE,
        cost_estimate=DEAR,
        name="backward",
    )(xt, *gs, *acts, *coefs, wdt, *earlier)


def finish_kernel(spans, more, *refs):
    n = len(spans)
    pairs = [refs[2 * i : 2 * i + 2] for i in range(n)]
    gate_ref, up_ref, gate, up, sems = refs[2 * n + 2 * more :]
    share = gate_ref.shape[0]
    low = spans[0][0]
    copies = []
    for i, ((first, cols), (own, got)) in enumerate(zip(spans, pairs)):
        for j, (target, held) in enumerate(((gate_ref, gate), (up_ref, up))):
            rows = slice(j * share, (j + 1) * share)
            here = pl.ds(first - low, cols)
            held[:, here] = (own[rows, :].astype(F32) + got[rows, :].astype(F32)).astype(BF16)
            copies.append(
                pltpu.make_async_copy(held.at[:, here], target.at[:, pl.ds(first, cols)], sems.at[i, j])
            )
            copies[-1].start()
    for copy in copies:
        copy.wait()


def finish(owns, gots, firsts, width, held=()):
    share = owns[0].shape[0] // 2
    spans = tuple((first, own.shape[1]) for first, own in zip(firsts, owns))
    total = sum(cols for _, cols in spans)
    n, more = len(owns), len(held) > 0
    return pl.pallas_call(
        functools.partial(finish_kernel, spans, more),
        out_shape=[jax.ShapeDtypeStruct((share, width), BF16)] * 2,
        in_specs=[HERE] * (2 * n) + [ANYWHERE] * (2 * more),
        out_specs=[ANYWHERE] * 2,
        scratch_shapes=[pltpu.VMEM((share, total), BF16)] * 2 + [pltpu.SemaphoreType.DMA((n, 2))],
        input_output_aliases={2 * n: 0, 2 * n + 1: 1} if more else {},
        compiler_params=SMALL,
        cost_estimate=CHEAP,
        name="finish",
    )(*[v for both in zip(owns, gots) for v in both], *held)


def split_kernel(*refs):
    blocks = [r[...].astype(F32) for r in refs[:EXPERTS]]
    refs[-2][...] = jnp.concatenate([b[:CAP] for b in blocks], axis=0).astype(BF16)
    refs[-1][...] = jnp.concatenate([b[CAP:] for b in blocks], axis=0).astype(BF16)


def split(blocks, earlier):
    width = blocks[0].shape[1]
    return pl.pallas_call(
        split_kernel,
        out_shape=[jax.ShapeDtypeStruct((EXPERTS * CAP, width), BF16)] * 2,
        in_specs=[HERE] * EXPERTS + [ANYWHERE] * len(earlier),
        compiler_params=SMALL,
        cost_estimate=CHEAP,
        name="split",
    )(*blocks, *earlier)


def unpack_kernel(placer_ref, mine_ref, got_ref, *refs):
    chosen = placer_ref[...].astype(F32).T.astype(BF16)
    total = jnp.dot(chosen, mine_ref[...], preferred_element_type=F32)
    total += jnp.dot(chosen, got_ref[...], preferred_element_type=F32)
    refs[-1][...] = total.astype(BF16)


def unpack(placer, mine, got, earlier):
    return pl.pallas_call(
        unpack_kernel,
        out_shape=jax.ShapeDtypeStruct((placer.shape[1], mine.shape[1]), BF16),
        in_specs=[HERE] * 3 + [AFAR] * len(earlier),
        compiler_params=SMALL,
        cost_estimate=DEAR,
        name="unpack",
    )(placer, mine, got, *[kept(v) for v in earlier])


def swap(value, axis):
    return lax.ppermute(value, axis, [(0, 1), (1, 0)])


def across_planes(blocks):
    return [blocks[0]] + [
        lax.ppermute(blocks[k], "arch", [(i, i ^ k) for i in range(EXPERTS)]) for k in range(1, EXPERTS)
    ]


def after(values, earlier):
    n = len(values)
    return list(lax.optimization_barrier((*values, *earlier))[:n])


def gathering(designs, archetype, w_gate, w_up, w_down, cotangent):
    far, core = lax.axis_index("far"), lax.axis_index("core")
    scalars = [lax.axis_index("arch"), 2 * far + core, 2 * far + 1 - core]
    scalars = [v.astype(jnp.int32)[None] for v in scalars]
    tokens, width = designs.shape
    share = width // 4
    placer, *blocks = pack(scalars, archetype.reshape(1, tokens), designs, cotangent)
    wd, wdt = flip(after([w_down], [placer])[0])

    moved = across_planes(blocks[:EXPERTS])
    x_own = join(moved, [wdt])
    x_near, x_far = swap(x_own, "half"), swap(x_own, "far")
    moved = across_planes(blocks[EXPERTS:])

    wg, wu = w_gate, w_up
    act0, coef0, share_own = forward([x_own], wg, wu, wd)
    g_own = join(moved, [act0])
    g_near, g_far = swap(g_own, "half"), swap(g_own, "far")
    act1, coef1, *shares = forward([x_near, x_far], wg, wu, wd, other=share_own)
    x_pass, g_pass = relay([x_near, g_far], [mark(act1), g_near])
    x_corner, g_corner = swap(x_pass, "far"), swap(g_pass, "half")
    returned = across_planes(shares)
    act2, coef2 = forward([x_corner], wg, wu)
    xt = turn(*scalars[1:], [x_own, x_near, x_far, x_corner], share)

    gs = [g_own, g_near, g_far, g_corner]
    acts, coefs = [act0, act1, act2], [coef0, coef1, coef2]
    cols = w_down.shape[0]
    half = cols // 2
    own0, sib0 = backward(xt, gs, acts, coefs, wdt, 0, half)
    mine, theirs = split(returned, [own0])
    got = swap(theirs, "half")
    own1, sib1 = backward(xt, gs, acts, coefs, wdt, half, half, [mine])
    got0, got1 = swap(sib0, "core"), swap(sib1, "core")
    held = finish([own0], [got0], (0,), cols)
    outputs = unpack(placer, mine, got, held[:1])
    grad_gate, grad_up = finish([own1], [got1], (half,), cols, held)
    return outputs, grad_gate, grad_up


def reducing(designs, archetype, w_gate, w_up, w_down, cotangent):
    width = designs.shape[1]
    owners = lax.axis_size("expert")
    sharers = owners // EXPERTS
    hidden_cols = w_gate.shape[1]
    labels = archetype[:, 0]
    onehot = (labels[:, None] == jnp.arange(EXPERTS, dtype=jnp.int32)[None, :]).astype(jnp.int32)
    ranks = jnp.cumsum(onehot, axis=0) - onehot
    target = labels * CAP + jnp.sum(ranks * onehot, axis=1)
    placer = (jnp.arange(EXPERTS * CAP, dtype=jnp.int32)[:, None] == target[None, :]).astype(BF16)
    received = []
    for rows in (designs, cotangent):
        packed = jnp.dot(placer, rows, preferred_element_type=F32).astype(BF16)
        send = jnp.repeat(packed.reshape(EXPERTS, CAP, width), sharers, axis=0)
        received.append(
            lax.all_to_all(send, "expert", split_axis=0, concat_axis=0, tiled=True).reshape(
                owners * CAP, width
            )
        )
    flat_x, flat_g = received
    gate = jnp.dot(flat_x, w_gate, preferred_element_type=F32)
    up = jnp.dot(flat_x, w_up, preferred_element_type=F32)
    act, slope = silu_parts(gate)
    hidden = (act * up).astype(BF16)
    partial_value = (
        jnp.dot(hidden, w_down, preferred_element_type=F32).astype(BF16).reshape(owners, CAP, width)
    )
    returned = lax.all_to_all(partial_value, "expert", split_axis=0, concat_axis=0, tiled=True)
    summed = jnp.sum(returned.astype(F32).reshape(EXPERTS, sharers, CAP, width), axis=1).reshape(
        EXPERTS * CAP, width
    )
    outputs = jnp.take(summed, target, axis=0).astype(BF16)
    d_hidden = contract_cols(flat_g, w_down)
    d_gate = (d_hidden * up * slope).astype(BF16)
    d_up = (d_hidden * act).astype(BF16)
    grads = jnp.concatenate([contract_rows(flat_x, d_gate), contract_rows(flat_x, d_up)], axis=1)
    mine = lax.psum_scatter(grads.astype(BF16), "dp", scatter_dimension=0, tiled=True)
    return outputs, mine[:, :hidden_cols], mine[:, hidden_cols:]


def solution(mesh):
    dp, owners = mesh.devices.shape
    if (dp, owners) == (4, 2 * EXPERTS):
        rows, cols = ("far", "core"), ("arch", "half")
        mesh = Mesh(mesh.devices.reshape(2, 2, EXPERTS, 2), rows + cols)
        body = gathering
    else:
        rows, cols = ("dp",), ("expert",)
        body = reducing
    tokens = P(rows + cols, None)
    return jax.shard_map(
        body,
        mesh=mesh,
        in_specs=(tokens, tokens, P(None, cols), P(None, cols), P(cols, None), tokens),
        out_specs=(tokens, P(rows, cols), P(rows, cols)),
        check_vma=False,
    )
```

```python
import functools

import jax
import jax.numpy as jnp
from jax import lax
from jax.experimental import pallas as pl
from jax.experimental.pallas import tpu as pltpu
from jax.sharding import Mesh
from jax.sharding import PartitionSpec as P

EXPERTS = 4
CAP = 36
STRIP = 1024
PAIR = 2 * STRIP
SLICE = 256
MIB = 1024 * 1024
LARGE = pltpu.CompilerParams(vmem_limit_bytes=16 * MIB)
SMALL = pltpu.CompilerParams(vmem_limit_bytes=12 * MIB)
CHEAP = pl.CostEstimate(flops=0, bytes_accessed=0, transcendentals=0)
DEAR = pl.CostEstimate(flops=20_000_000_000, bytes_accessed=0, transcendentals=0)
F32 = jnp.float32
BF16 = jnp.bfloat16
HERE = pl.BlockSpec(memory_space=pltpu.VMEM)
AFAR = pl.BlockSpec(memory_space=pltpu.HBM)
ANYWHERE = pl.BlockSpec(memory_space=pl.ANY)


def silu_parts(gate):
    sigma = 0.5 * jnp.tanh(0.5 * gate) + 0.5
    return (gate * sigma, sigma * (1.0 + gate * (1.0 - sigma)))


def contract_rows(left, right):
    return lax.dot_general(left, right, (((0,), (0,)), ((), ())), preferred_element_type=F32)


def contract_cols(left, right):
    return lax.dot_general(left, right, (((1,), (1,)), ((), ())), preferred_element_type=F32)


def stacked(refs):
    return jnp.concatenate([r[...].astype(F32) for r in refs], axis=0)


def kept(value):
    return pltpu.with_memory_space_constraint(value, pltpu.HBM)


def pack_kernel(plane_ref, _, __, kind_ref, x_ref, g_ref, placer_ref, *refs):
    outs, (kind, x, g, sems) = refs[: 2 * EXPERTS], refs[2 * EXPERTS :]
    copies = [
        pltpu.make_async_copy(source, target, sems.at[i])
        for i, (source, target) in enumerate(((kind_ref, kind), (x_ref, x), (g_ref, g)))
    ]
    for copy in copies:
        copy.start()
    tokens = kind.shape[1]
    copies[0].wait()
    key = kind[...] ^ plane_ref[0]
    onehot = (key == lax.broadcasted_iota(jnp.int32, (8, tokens), 0)).astype(F32)
    before = lax.broadcasted_iota(jnp.int32, (tokens, tokens), 0) < lax.broadcasted_iota(
        jnp.int32, (tokens, tokens), 1
    )
    ranks = jnp.dot(onehot.astype(BF16), before.astype(BF16), preferred_element_type=F32)
    rank = jnp.sum(ranks * onehot, axis=0, keepdims=True).astype(jnp.int32)
    place = key * CAP + rank
    slots = EXPERTS * CAP
    placer = (place == lax.broadcasted_iota(jnp.int32, (slots, tokens), 0)).astype(F32).astype(BF16)
    placer_ref[...] = placer
    for copy, source, first in ((copies[1], x, 0), (copies[2], g, EXPERTS)):
        copy.wait()
        packed = jnp.dot(placer, source[...], preferred_element_type=F32)
        for k in range(EXPERTS):
            outs[first + k][...] = packed[k * CAP : (k + 1) * CAP].astype(BF16)


def pack(scalars, kind, x, g):
    tokens, width = x.shape
    return pl.pallas_call(
        pack_kernel,
        out_shape=[jax.ShapeDtypeStruct((EXPERTS * CAP, tokens), BF16)]
        + [jax.ShapeDtypeStruct((CAP, width), BF16)] * (2 * EXPERTS),
        in_specs=[pl.BlockSpec(memory_space=pltpu.SMEM)] * 3 + [AFAR] * 3,
        scratch_shapes=[
            pltpu.VMEM((1, tokens), jnp.int32),
            pltpu.VMEM((tokens, width), BF16),
            pltpu.VMEM((tokens, width), BF16),
            pltpu.SemaphoreType.DMA((3,)),
        ],
        compiler_params=SMALL,
        cost_estimate=CHEAP,
        name="pack",
    )(*scalars, kept(kind), kept(x), kept(g))


def join_kernel(*refs):
    refs[-1][...] = stacked(refs[EXPERTS - 1 :: -1]).astype(BF16)


def join(blocks, earlier=()):
    width = blocks[0].shape[1]
    return pl.pallas_call(
        join_kernel,
        out_shape=jax.ShapeDtypeStruct((EXPERTS * CAP, width), BF16),
        in_specs=[HERE] * EXPERTS + [ANYWHERE] * len(earlier),
        compiler_params=SMALL,
        cost_estimate=CHEAP,
        name="join",
    )(*blocks[::-1], *earlier)


def relay_kernel(n, *refs):
    for i in range(n):
        refs[len(refs) - n + i][...] = refs[i][...]


def relay(values, earlier):
    n = len(values)
    return pl.pallas_call(
        functools.partial(relay_kernel, n),
        out_shape=[jax.ShapeDtypeStruct(v.shape, v.dtype) for v in values],
        in_specs=[HERE] * n + [ANYWHERE] * len(earlier),
        compiler_params=SMALL,
        cost_estimate=CHEAP,
        name="relay",
    )(*values, *earlier)


def mark_kernel(value_ref, mark_ref):
    mark_ref[...] = value_ref[: mark_ref.shape[0], : mark_ref.shape[1]]


def mark(value):
    return pl.pallas_call(
        mark_kernel,
        out_shape=jax.ShapeDtypeStruct((16, 128), value.dtype),
        in_specs=[HERE],
        compiler_params=SMALL,
        cost_estimate=CHEAP,
        name="mark",
    )(value)


def flip_kernel(source_ref, here_ref, flipped_ref, sems):
    steps = source_ref.shape[0] // SLICE
    copies = []
    for j in range(steps):
        rows = pl.ds(j * SLICE, SLICE)
        copies.append(pltpu.make_async_copy(source_ref.at[rows], here_ref.at[rows], sems.at[j]))
        copies[j].start()
    for j in range(steps):
        copies[j].wait()
        rows = slice(j * SLICE, (j + 1) * SLICE)
        flipped_ref[:, rows] = here_ref[rows, :].T


def flip(value):
    return pl.pallas_call(
        flip_kernel,
        out_shape=[pltpu.VMEM(value.shape, value.dtype), pltpu.VMEM(value.shape[::-1], value.dtype)],
        in_specs=[AFAR],
        out_specs=[HERE, HERE],
        scratch_shapes=[pltpu.SemaphoreType.DMA((value.shape[0] // SLICE,))],
        compiler_params=SMALL,
        cost_estimate=CHEAP,
        name="flip",
    )(kept(value))


def forward_kernel(n, fetch, down, pair, unused, *refs):
    refs = list(refs[unused:])
    xs = [refs.pop(0) for _ in range(n)]
    wg_ref, wu_ref = refs.pop(0), refs.pop(0)
    wd_ref = refs.pop(0) if down else None
    other_ref = refs.pop(0) if pair else None
    act_ref, coef_ref = refs.pop(0), refs.pop(0)
    shares = [refs.pop(0) for _ in range(EXPERTS if pair else down)]
    if fetch:
        sources, sems = (wg_ref, wu_ref), refs.pop()
        wg_ref, wu_ref = refs.pop(0), refs.pop(0)
    acc_ref = refs.pop(0) if down else None
    part = xs[0].shape[0]
    x_ref = xs[0]
    if n > 1:
        x_ref = refs.pop(0)
        for i in range(n):
            x_ref[i * part : (i + 1) * part, :] = xs[i][...]
    steps = wg_ref.shape[1] // PAIR

    def copies(j):
        cols = pl.ds(pl.multiple_of(j * PAIR, PAIR), PAIR)
        return [
            pltpu.make_async_copy(source.at[:, cols], target.at[:, cols], sems.at[j, i])
            for i, (source, target) in enumerate(zip(sources, (wg_ref, wu_ref)))
        ]

    if fetch:
        for j in range(steps):
            for copy in copies(j):
                copy.start()
    if down:
        acc_ref[...] = jnp.zeros_like(acc_ref)

    @pl.loop(0, steps)
    def _(j):
        if fetch:
            for copy in copies(j):
                copy.wait()
        for i in range(PAIR // STRIP):
            cols = pl.ds(pl.multiple_of(j * PAIR + i * STRIP, STRIP), STRIP)
            gate = jnp.dot(x_ref[...], wg_ref[:, cols], preferred_element_type=F32)
            up = jnp.dot(x_ref[...], wu_ref[:, cols], preferred_element_type=F32)
            act, slope = silu_parts(gate)
            act_ref[:, cols] = act.astype(BF16)
            coef_ref[:, cols] = (up * slope).astype(BF16)
            if down:
                hidden = (act[:part] * up[:part]).astype(BF16)
                acc_ref[...] += jnp.dot(hidden, wd_ref[cols, :], preferred_element_type=F32)

    if pair:
        other = other_ref[...].astype(F32)
        for k in range(EXPERTS):
            rows = slice(k * CAP, (k + 1) * CAP)
            block = jnp.concatenate([other[rows], acc_ref[rows, :]], axis=0).astype(BF16)
            shares[k][...] = block
    elif down:
        shares[0][...] = acc_ref[...].astype(BF16)


def forward(xs, wg, wu, wd=None, other=None, fetch=False, earlier=()):
    n, (part, width), cols = len(xs), xs[0].shape, wg.shape[1]
    rows = n * part
    down, pair = wd is not None, other is not None
    shares = [jax.ShapeDtypeStruct((part, width), BF16)] * down
    if pair:
        shares = [jax.ShapeDtypeStruct((2 * CAP, width), BF16)] * EXPERTS
    weights = [kept(wg), kept(wu)] if fetch else [wg, wu]
    return pl.pallas_call(
        functools.partial(forward_kernel, n, fetch, down, pair, len(earlier)),
        out_shape=[jax.ShapeDtypeStruct((rows, cols), BF16)] * 2
        + shares
        + [pltpu.VMEM(wg.shape, wg.dtype)] * (2 * fetch),
        in_specs=[ANYWHERE] * len(earlier)
        + [HERE] * n
        + [AFAR if fetch else HERE] * 2
        + [HERE] * (down + pair),
        scratch_shapes=[pltpu.VMEM((part, width), F32)] * down
        + [pltpu.VMEM((rows, width), BF16)] * (n > 1)
        + [pltpu.SemaphoreType.DMA((cols // PAIR, 2))] * fetch,
        compiler_params=LARGE,
        cost_estimate=CHEAP,
        name="forward" + "_fetch" * fetch + "_down" * down,
    )(*earlier, *xs, *weights, *([wd] * down), *([other] * pair))


def turn_kernel(_, __, *refs):
    refs[8][: refs[0].shape[1], :] = stacked(refs[0:4]).T.astype(BF16)
    refs[8][refs[0].shape[1] :, :] = stacked(refs[4:8]).T.astype(BF16)


def turn(own, sib, xs, share):
    part = xs[0].shape[0]
    rows = len(xs) * part
    return pl.pallas_call(
        turn_kernel,
        grid_spec=pltpu.PrefetchScalarGridSpec(
            num_scalar_prefetch=2,
            grid=(1,),
            in_specs=[pl.BlockSpec((part, share), lambda j, a, b: (0, a[0]))] * 4
            + [pl.BlockSpec((part, share), lambda j, a, b: (0, b[0]))] * 4,
            out_specs=pl.BlockSpec((2 * share, rows), lambda j, a, b: (0, 0)),
        ),
        out_shape=jax.ShapeDtypeStruct((2 * share, rows), BF16),
        compiler_params=SMALL,
        cost_estimate=CHEAP,
        name="turn",
    )(own, sib, *xs, *xs)


def backward_kernel(first, counts, xt_ref, *refs):
    n = len(counts)
    gs, acts, coefs = refs[:4], refs[4 : 4 + n], refs[4 + n : 4 + 2 * n]
    wdt_ref, *_, own_ref, sib_ref, g_ref = refs[4 + 2 * n :]
    part = gs[0].shape[0]
    share = own_ref.shape[0] // 2
    for i in range(4):
        g_ref[i * part : (i + 1) * part, :] = gs[i][...]

    def strip(start):
        here = pl.ds(pl.multiple_of(start, STRIP), STRIP)
        cols = pl.ds(pl.multiple_of(start + first, STRIP), STRIP)
        d_hidden = jnp.dot(g_ref[...], wdt_ref[:, cols], preferred_element_type=F32)
        for row, parts in ((0, coefs), (share, acts)):
            factor = jnp.concatenate([p[:, cols] for p in parts], axis=0).astype(F32)
            d_cols = (d_hidden * factor).astype(BF16)
            total = jnp.dot(xt_ref[...], d_cols, preferred_element_type=F32).astype(BF16)
            own_ref[row : row + share, here] = total[:share]
            sib_ref[row : row + share, here] = total[share:]

    pairs = own_ref.shape[1] // PAIR

    @pl.loop(0, pairs)
    def _(j):
        for i in range(PAIR // STRIP):
            strip(j * PAIR + i * STRIP)

    for start in range(pairs * PAIR, own_ref.shape[1], STRIP):
        strip(start)


def backward(xt, gs, acts, coefs, wdt, first, cols, earlier=()):
    part, width = gs[0].shape
    height, rows = xt.shape
    counts = tuple(a.shape[0] for a in acts)
    return pl.pallas_call(
        functools.partial(backward_kernel, first, counts),
        out_shape=[jax.ShapeDtypeStruct((height, cols), BF16)] * 2,
        in_specs=[HERE] * (6 + 2 * len(acts)) + [ANYWHERE] * len(earlier),
        scratch_shapes=[pltpu.VMEM((rows, width), BF16)],
        compiler_params=LARGE,
        cost_estimate=DEAR,
        name="backward",
    )(xt, *gs, *acts, *coefs, wdt, *earlier)


def finish_kernel(spans, more, *refs):
    n = len(spans)
    pairs = [refs[2 * i : 2 * i + 2] for i in range(n)]
    gate_ref, up_ref, gate, up, sems = refs[2 * n + 2 * more :]
    share = gate_ref.shape[0]
    low = spans[0][0]
    copies = []
    for i, ((first, cols), (own, got)) in enumerate(zip(spans, pairs)):
        for j, (target, held) in enumerate(((gate_ref, gate), (up_ref, up))):
            rows = slice(j * share, (j + 1) * share)
            here = pl.ds(first - low, cols)
            held[:, here] = (own[rows, :].astype(F32) + got[rows, :].astype(F32)).astype(BF16)
            copies.append(
                pltpu.make_async_copy(held.at[:, here], target.at[:, pl.ds(first, cols)], sems.at[i, j])
            )
            copies[-1].start()
    for copy in copies:
        copy.wait()


def finish(owns, gots, firsts, width, held=()):
    share = owns[0].shape[0] // 2
    spans = tuple((first, own.shape[1]) for first, own in zip(firsts, owns))
    total = sum(cols for _, cols in spans)
    n, more = len(owns), len(held) > 0
    return pl.pallas_call(
        functools.partial(finish_kernel, spans, more),
        out_shape=[jax.ShapeDtypeStruct((share, width), BF16)] * 2,
        in_specs=[HERE] * (2 * n) + [ANYWHERE] * (2 * more),
        out_specs=[ANYWHERE] * 2,
        scratch_shapes=[pltpu.VMEM((share, total), BF16)] * 2 + [pltpu.SemaphoreType.DMA((n, 2))],
        input_output_aliases={2 * n: 0, 2 * n + 1: 1} if more else {},
        compiler_params=SMALL,
        cost_estimate=CHEAP,
        name="finish",
    )(*[v for both in zip(owns, gots) for v in both], *held)


def split_kernel(*refs):
    blocks = [r[...].astype(F32) for r in refs[EXPERTS - 1 :: -1]]
    refs[-2][...] = jnp.concatenate([b[:CAP] for b in blocks], axis=0).astype(BF16)
    refs[-1][...] = jnp.concatenate([b[CAP:] for b in blocks], axis=0).astype(BF16)


def split(blocks, earlier):
    width = blocks[0].shape[1]
    return pl.pallas_call(
        split_kernel,
        out_shape=[jax.ShapeDtypeStruct((EXPERTS * CAP, width), BF16)] * 2,
        in_specs=[HERE] * EXPERTS + [ANYWHERE] * len(earlier),
        compiler_params=SMALL,
        cost_estimate=CHEAP,
        name="split",
    )(*blocks[::-1], *earlier)


def unpack_kernel(placer_ref, mine_ref, got_ref, *refs):
    chosen = placer_ref[...].astype(F32).T.astype(BF16)
    total = jnp.dot(chosen, mine_ref[...], preferred_element_type=F32)
    total += jnp.dot(chosen, got_ref[...], preferred_element_type=F32)
    refs[-1][...] = total.astype(BF16)


def unpack(placer, mine, got, earlier):
    return pl.pallas_call(
        unpack_kernel,
        out_shape=jax.ShapeDtypeStruct((placer.shape[1], mine.shape[1]), BF16),
        in_specs=[HERE] * 3 + [AFAR] * len(earlier),
        compiler_params=SMALL,
        cost_estimate=DEAR,
        name="unpack",
    )(placer, mine, got, *[kept(v) for v in earlier])


def swap(value, axis):
    return lax.ppermute(value, axis, [(0, 1), (1, 0)])


def across_planes(blocks):
    return [blocks[0]] + [
        lax.ppermute(blocks[k], "arch", [(i, i ^ k) for i in range(EXPERTS)]) for k in range(1, EXPERTS)
    ]


def after(values, earlier):
    n = len(values)
    return list(lax.optimization_barrier((*values, *earlier))[:n])


def gathering(designs, archetype, w_gate, w_up, w_down, cotangent):
    far, core = lax.axis_index("far"), lax.axis_index("core")
    scalars = [lax.axis_index("arch"), 2 * far + core, 2 * far + 1 - core]
    scalars = [v.astype(jnp.int32)[None] for v in scalars]
    tokens, width = designs.shape
    share = width // 4
    placer, *blocks = pack(scalars, archetype.reshape(1, tokens), designs, cotangent)
    wd, wdt = flip(after([w_down], [placer])[0])

    moved = across_planes(blocks[:EXPERTS])
    x_own = join(moved, [wdt])
    x_far, x_near = swap(x_own, "far"), swap(x_own, "half")
    moved = across_planes(blocks[EXPERTS:])

    wg, wu = w_gate, w_up
    act0, coef0, share_own = forward([x_own], wg, wu, wd)
    g_own = join(moved, [act0])
    g_far, g_near = swap(g_own, "far"), swap(g_own, "half")
    act2, coef2 = forward([x_far], wg, wu)
    act1, coef1, *shares = forward([x_near], wg, wu, wd, other=share_own, earlier=[act2])
    (x_pass,) = relay([x_near], [mark(act1), g_far])
    (g_pass,) = relay([g_far], [x_pass, g_near])
    x_corner, g_corner = swap(x_pass, "far"), swap(g_pass, "half")
    returned = across_planes(shares)
    act3, coef3 = forward([x_corner], wg, wu)
    xt = turn(*scalars[1:], [x_own, x_near, x_far, x_corner], share)

    gs = [g_own, g_near, g_far, g_corner]
    acts, coefs = [act0, act1, act2, act3], [coef0, coef1, coef2, coef3]
    cols = w_down.shape[0]
    half = cols // 2
    own0, sib0 = backward(xt, gs, acts, coefs, wdt, 0, half)
    mine, theirs = split(returned, [own0])
    got = swap(theirs, "half")
    own1, sib1 = backward(xt, gs, acts, coefs, wdt, half, half, [mine])
    got0, got1 = swap(sib0, "core"), swap(sib1, "core")
    held = finish([own0], [got0], (0,), cols)
    outputs = unpack(placer, mine, got, held[:1])
    grad_gate, grad_up = finish([own1], [got1], (half,), cols, held)
    return outputs, grad_gate, grad_up


def reducing(designs, archetype, w_gate, w_up, w_down, cotangent):
    width = designs.shape[1]
    owners = lax.axis_size("expert")
    sharers = owners // EXPERTS
    hidden_cols = w_gate.shape[1]
    labels = archetype[:, 0]
    onehot = (labels[:, None] == jnp.arange(EXPERTS, dtype=jnp.int32)[None, :]).astype(jnp.int32)
    ranks = jnp.cumsum(onehot, axis=0) - onehot
    target = labels * CAP + jnp.sum(ranks * onehot, axis=1)
    placer = (jnp.arange(EXPERTS * CAP, dtype=jnp.int32)[:, None] == target[None, :]).astype(BF16)
    received = []
    for rows in (designs, cotangent):
        packed = jnp.dot(placer, rows, preferred_element_type=F32).astype(BF16)
        send = jnp.repeat(packed.reshape(EXPERTS, CAP, width), sharers, axis=0)
        received.append(
            lax.all_to_all(send, "expert", split_axis=0, concat_axis=0, tiled=True).reshape(
                owners * CAP, width
            )
        )
    flat_x, flat_g = received
    gate = jnp.dot(flat_x, w_gate, preferred_element_type=F32)
    up = jnp.dot(flat_x, w_up, preferred_element_type=F32)
    act, slope = silu_parts(gate)
    hidden = (act * up).astype(BF16)
    partial_value = (
        jnp.dot(hidden, w_down, preferred_element_type=F32).astype(BF16).reshape(owners, CAP, width)
    )
    returned = lax.all_to_all(partial_value, "expert", split_axis=0, concat_axis=0, tiled=True)
    summed = jnp.sum(returned.astype(F32).reshape(EXPERTS, sharers, CAP, width), axis=1).reshape(
        EXPERTS * CAP, width
    )
    outputs = jnp.take(summed, target, axis=0).astype(BF16)
    d_hidden = contract_cols(flat_g, w_down)
    d_gate = (d_hidden * up * slope).astype(BF16)
    d_up = (d_hidden * act).astype(BF16)
    grads = jnp.concatenate([contract_rows(flat_x, d_gate), contract_rows(flat_x, d_up)], axis=1)
    mine = lax.psum_scatter(grads.astype(BF16), "dp", scatter_dimension=0, tiled=True)
    return outputs, mine[:, :hidden_cols], mine[:, hidden_cols:]


def solution(mesh):
    dp, owners = mesh.devices.shape
    if (dp, owners) == (4, 2 * EXPERTS):
        rows, cols = ("far", "core"), ("arch", "half")
        mesh = Mesh(mesh.devices.reshape(2, 2, EXPERTS, 2), rows + cols)
        body = gathering
    else:
        rows, cols = ("dp",), ("expert",)
        body = reducing
    tokens = P(rows + cols, None)
    return jax.shard_map(
        body,
        mesh=mesh,
        in_specs=(tokens, tokens, P(None, cols), P(None, cols), P(cols, None), tokens),
        out_specs=(tokens, P(rows, cols), P(rows, cols)),
        check_vma=False,
    )
```

```python
import functools

import jax
import jax.numpy as jnp
from jax import lax
from jax.experimental import pallas as pl
from jax.experimental.pallas import tpu as pltpu
from jax.sharding import Mesh
from jax.sharding import PartitionSpec as P

EXPERTS = 4
CAP = 36
WIDE = 1024
STRIP = 512
SLICE = 256
MIB = 1024 * 1024
LARGE = pltpu.CompilerParams(vmem_limit_bytes=16 * MIB)
SMALL = pltpu.CompilerParams(vmem_limit_bytes=12 * MIB)
CHEAP = pl.CostEstimate(flops=0, bytes_accessed=0, transcendentals=0)
DEAR = pl.CostEstimate(flops=20_000_000_000, bytes_accessed=0, transcendentals=0)
F32 = jnp.float32
BF16 = jnp.bfloat16
HERE = pl.BlockSpec(memory_space=pltpu.VMEM)
AFAR = pl.BlockSpec(memory_space=pltpu.HBM)
ANYWHERE = pl.BlockSpec(memory_space=pl.ANY)


def silu_parts(gate):
    sigma = 0.5 * jnp.tanh(0.5 * gate) + 0.5
    return (gate * sigma, sigma * (1.0 + gate * (1.0 - sigma)))


def contract_rows(left, right):
    return lax.dot_general(left, right, (((0,), (0,)), ((), ())), preferred_element_type=F32)


def contract_cols(left, right):
    return lax.dot_general(left, right, (((1,), (1,)), ((), ())), preferred_element_type=F32)


def stacked(refs):
    return jnp.concatenate([r[...].astype(F32) for r in refs], axis=0)


def kept(value):
    return pltpu.with_memory_space_constraint(value, pltpu.HBM)


def pack_kernel(plane_ref, _, __, kind_ref, x_ref, g_ref, placer_ref, *refs):
    outs, (kind, x, g, sems) = refs[: 2 * EXPERTS], refs[2 * EXPERTS :]
    copies = [
        pltpu.make_async_copy(source, target, sems.at[i])
        for i, (source, target) in enumerate(((kind_ref, kind), (x_ref, x), (g_ref, g)))
    ]
    for copy in copies:
        copy.start()
    tokens = kind.shape[1]
    copies[0].wait()
    key = kind[...] ^ plane_ref[0]
    onehot = (key == lax.broadcasted_iota(jnp.int32, (8, tokens), 0)).astype(F32)
    before = lax.broadcasted_iota(jnp.int32, (tokens, tokens), 0) < lax.broadcasted_iota(
        jnp.int32, (tokens, tokens), 1
    )
    ranks = jnp.dot(onehot.astype(BF16), before.astype(BF16), preferred_element_type=F32)
    rank = jnp.sum(ranks * onehot, axis=0, keepdims=True).astype(jnp.int32)
    place = key * CAP + rank
    slots = EXPERTS * CAP
    placer = (place == lax.broadcasted_iota(jnp.int32, (slots, tokens), 0)).astype(F32).astype(BF16)
    placer_ref[...] = placer
    for copy, source, first in ((copies[1], x, 0), (copies[2], g, EXPERTS)):
        copy.wait()
        packed = jnp.dot(placer, source[...], preferred_element_type=F32)
        for k in range(EXPERTS):
            outs[first + k][...] = packed[k * CAP : (k + 1) * CAP].astype(BF16)


def pack(scalars, kind, x, g):
    tokens, width = x.shape
    return pl.pallas_call(
        pack_kernel,
        out_shape=[jax.ShapeDtypeStruct((EXPERTS * CAP, tokens), BF16)]
        + [jax.ShapeDtypeStruct((CAP, width), BF16)] * (2 * EXPERTS),
        in_specs=[pl.BlockSpec(memory_space=pltpu.SMEM)] * 3 + [AFAR] * 3,
        scratch_shapes=[
            pltpu.VMEM((1, tokens), jnp.int32),
            pltpu.VMEM((tokens, width), BF16),
            pltpu.VMEM((tokens, width), BF16),
            pltpu.SemaphoreType.DMA((3,)),
        ],
        compiler_params=SMALL,
        cost_estimate=CHEAP,
        name="pack",
    )(*scalars, kept(kind), kept(x), kept(g))


def join_kernel(*refs):
    refs[-1][...] = stacked(refs[-2 : -2 - EXPERTS : -1]).astype(BF16)


def join(blocks, earlier=()):
    width = blocks[0].shape[1]
    return pl.pallas_call(
        join_kernel,
        out_shape=jax.ShapeDtypeStruct((EXPERTS * CAP, width), BF16),
        in_specs=[ANYWHERE] * len(earlier) + [HERE] * EXPERTS,
        compiler_params=SMALL,
        cost_estimate=CHEAP,
        name="join",
    )(*earlier, *blocks[::-1])


def relay_kernel(n, *refs):
    for i in range(n):
        refs[len(refs) - n + i][...] = refs[i][...]


def relay(values, earlier):
    n = len(values)
    return pl.pallas_call(
        functools.partial(relay_kernel, n),
        out_shape=[jax.ShapeDtypeStruct(v.shape, v.dtype) for v in values],
        in_specs=[HERE] * n + [ANYWHERE] * len(earlier),
        compiler_params=SMALL,
        cost_estimate=CHEAP,
        name="relay",
    )(*values, *earlier)


def mark_kernel(value_ref, mark_ref):
    mark_ref[...] = value_ref[: mark_ref.shape[0], : mark_ref.shape[1]]


def mark(value):
    return pl.pallas_call(
        mark_kernel,
        out_shape=jax.ShapeDtypeStruct((16, 128), value.dtype),
        in_specs=[HERE],
        compiler_params=SMALL,
        cost_estimate=CHEAP,
        name="mark",
    )(value)


def flip_kernel(source_ref, here_ref, flipped_ref, sems):
    steps = source_ref.shape[0] // SLICE
    copies = []
    for j in range(steps):
        rows = pl.ds(j * SLICE, SLICE)
        copies.append(pltpu.make_async_copy(source_ref.at[rows], here_ref.at[rows], sems.at[j]))
        copies[j].start()
    for j in range(steps):
        copies[j].wait()
        rows = slice(j * SLICE, (j + 1) * SLICE)
        flipped_ref[:, rows] = here_ref[rows, :].T


def flip(value):
    return pl.pallas_call(
        flip_kernel,
        out_shape=[pltpu.VMEM(value.shape, value.dtype), pltpu.VMEM(value.shape[::-1], value.dtype)],
        in_specs=[AFAR],
        out_specs=[HERE, HERE],
        scratch_shapes=[pltpu.SemaphoreType.DMA((value.shape[0] // SLICE,))],
        compiler_params=SMALL,
        cost_estimate=CHEAP,
        name="flip",
    )(kept(value))


def forward_kernel(n, fetch, down, pair, unused, *refs):
    refs = list(refs[unused:])
    xs = [refs.pop(0) for _ in range(n)]
    wg_ref, wu_ref = refs.pop(0), refs.pop(0)
    wd_ref = refs.pop(0) if down else None
    other_ref = refs.pop(0) if pair else None
    act_ref, coef_ref = refs.pop(0), refs.pop(0)
    shares = [refs.pop(0) for _ in range(EXPERTS if pair else down)]
    if fetch:
        sources, sems = (wg_ref, wu_ref), refs.pop()
        wg_ref, wu_ref = refs.pop(0), refs.pop(0)
    acc_ref = refs.pop(0) if down else None
    part = xs[0].shape[0]
    x_ref = xs[0]
    if n > 1:
        x_ref = refs.pop(0)
        for i in range(n):
            x_ref[i * part : (i + 1) * part, :] = xs[i][...]
    steps = wg_ref.shape[1] // (2 * WIDE)

    def copies(j):
        cols = pl.ds(pl.multiple_of(j * (2 * WIDE), (2 * WIDE)), (2 * WIDE))
        return [
            pltpu.make_async_copy(source.at[:, cols], target.at[:, cols], sems.at[j, i])
            for i, (source, target) in enumerate(zip(sources, (wg_ref, wu_ref)))
        ]

    if fetch:
        for j in range(steps):
            for copy in copies(j):
                copy.start()
    if down:
        acc_ref[...] = jnp.zeros_like(acc_ref)

    @pl.loop(0, steps)
    def _(j):
        if fetch:
            for copy in copies(j):
                copy.wait()
        for i in range(2):
            cols = pl.ds(pl.multiple_of(j * (2 * WIDE) + i * WIDE, WIDE), WIDE)
            gate = jnp.dot(x_ref[...], wg_ref[:, cols], preferred_element_type=F32)
            up = jnp.dot(x_ref[...], wu_ref[:, cols], preferred_element_type=F32)
            act, slope = silu_parts(gate)
            act_ref[:, cols] = act.astype(BF16)
            coef_ref[:, cols] = (up * slope).astype(BF16)
            if down:
                hidden = (act[:part] * up[:part]).astype(BF16)
                acc_ref[...] += jnp.dot(hidden, wd_ref[cols, :], preferred_element_type=F32)

    if pair:
        other = other_ref[...].astype(F32)
        for k in range(EXPERTS):
            rows = slice(k * CAP, (k + 1) * CAP)
            block = jnp.concatenate([other[rows], acc_ref[rows, :]], axis=0).astype(BF16)
            shares[k][...] = block
    elif down:
        shares[0][...] = acc_ref[...].astype(BF16)


def forward(xs, wg, wu, wd=None, other=None, fetch=False, earlier=()):
    n, (part, width), cols = len(xs), xs[0].shape, wg.shape[1]
    rows = n * part
    down, pair = wd is not None, other is not None
    shares = [jax.ShapeDtypeStruct((part, width), BF16)] * down
    if pair:
        shares = [jax.ShapeDtypeStruct((2 * CAP, width), BF16)] * EXPERTS
    weights = [kept(wg), kept(wu)] if fetch else [wg, wu]
    return pl.pallas_call(
        functools.partial(forward_kernel, n, fetch, down, pair, len(earlier)),
        out_shape=[jax.ShapeDtypeStruct((rows, cols), BF16)] * 2
        + shares
        + [pltpu.VMEM(wg.shape, wg.dtype)] * (2 * fetch),
        in_specs=[ANYWHERE] * len(earlier)
        + [HERE] * n
        + [AFAR if fetch else HERE] * 2
        + [HERE] * (down + pair),
        scratch_shapes=[pltpu.VMEM((part, width), F32)] * down
        + [pltpu.VMEM((rows, width), BF16)] * (n > 1)
        + [pltpu.SemaphoreType.DMA((cols // (2 * WIDE), 2))] * fetch,
        compiler_params=LARGE,
        cost_estimate=CHEAP,
        name="forward" + "_fetch" * fetch + "_down" * down,
    )(*earlier, *xs, *weights, *([wd] * down), *([other] * pair))


def turn_kernel(_, __, *refs):
    refs[8][: refs[0].shape[1], :] = stacked(refs[0:4]).T.astype(BF16)
    refs[8][refs[0].shape[1] :, :] = stacked(refs[4:8]).T.astype(BF16)


def turn(own, sib, xs, share):
    part = xs[0].shape[0]
    rows = len(xs) * part
    return pl.pallas_call(
        turn_kernel,
        grid_spec=pltpu.PrefetchScalarGridSpec(
            num_scalar_prefetch=2,
            grid=(1,),
            in_specs=[pl.BlockSpec((part, share), lambda j, a, b: (0, a[0]))] * 4
            + [pl.BlockSpec((part, share), lambda j, a, b: (0, b[0]))] * 4,
            out_specs=pl.BlockSpec((2 * share, rows), lambda j, a, b: (0, 0)),
        ),
        out_shape=jax.ShapeDtypeStruct((2 * share, rows), BF16),
        compiler_params=SMALL,
        cost_estimate=DEAR,
        name="turn",
    )(own, sib, *xs, *xs)


def backward_kernel(first, counts, xt_ref, *refs):
    n = len(counts)
    gs, acts, coefs = refs[:4], refs[4 : 4 + n], refs[4 + n : 4 + 2 * n]
    wdt_ref, *_, own_ref, sib_ref, g_ref = refs[4 + 2 * n :]
    part = gs[0].shape[0]
    share = own_ref.shape[0] // 2
    for i in range(4):
        g_ref[i * part : (i + 1) * part, :] = gs[i][...]

    def strip(start):
        here = pl.ds(pl.multiple_of(start, STRIP), STRIP)
        cols = pl.ds(pl.multiple_of(start + first, STRIP), STRIP)
        d_hidden = jnp.dot(g_ref[...], wdt_ref[:, cols], preferred_element_type=F32)
        for row, parts in ((0, coefs), (share, acts)):
            factor = jnp.concatenate([p[:, cols] for p in parts], axis=0).astype(F32)
            d_cols = (d_hidden * factor).astype(BF16)
            total = jnp.dot(xt_ref[...], d_cols, preferred_element_type=F32).astype(BF16)
            own_ref[row : row + share, here] = total[:share]
            sib_ref[row : row + share, here] = total[share:]

    for start in range(0, own_ref.shape[1], STRIP):
        strip(start)


def backward(xt, gs, acts, coefs, wdt, first, cols, earlier=()):
    part, width = gs[0].shape
    height, rows = xt.shape
    counts = tuple(a.shape[0] for a in acts)
    return pl.pallas_call(
        functools.partial(backward_kernel, first, counts),
        out_shape=[jax.ShapeDtypeStruct((height, cols), BF16)] * 2,
        in_specs=[HERE] * (6 + 2 * len(acts)) + [ANYWHERE] * len(earlier),
        scratch_shapes=[pltpu.VMEM((rows, width), BF16)],
        compiler_params=LARGE,
        cost_estimate=DEAR,
        name="backward",
    )(xt, *gs, *acts, *coefs, wdt, *earlier)


def finish_kernel(spans, more, *refs):
    n = len(spans)
    pairs = [refs[2 * i : 2 * i + 2] for i in range(n)]
    gate_ref, up_ref, gate, up, sems = refs[2 * n + 2 * more :]
    share = gate_ref.shape[0]
    low = spans[0][0]
    copies = []
    for i, ((first, cols), (own, got)) in enumerate(zip(spans, pairs)):
        for j, (target, held) in enumerate(((gate_ref, gate), (up_ref, up))):
            rows = slice(j * share, (j + 1) * share)
            here = pl.ds(first - low, cols)
            held[:, here] = (own[rows, :].astype(F32) + got[rows, :].astype(F32)).astype(BF16)
            copies.append(
                pltpu.make_async_copy(held.at[:, here], target.at[:, pl.ds(first, cols)], sems.at[i, j])
            )
            copies[-1].start()
    for copy in copies:
        copy.wait()


def finish(owns, gots, firsts, width, held=()):
    share = owns[0].shape[0] // 2
    spans = tuple((first, own.shape[1]) for first, own in zip(firsts, owns))
    total = sum(cols for _, cols in spans)
    n, more = len(owns), len(held) > 0
    return pl.pallas_call(
        functools.partial(finish_kernel, spans, more),
        out_shape=[jax.ShapeDtypeStruct((share, width), BF16)] * 2,
        in_specs=[HERE] * (2 * n) + [ANYWHERE] * (2 * more),
        out_specs=[ANYWHERE] * 2,
        scratch_shapes=[pltpu.VMEM((share, total), BF16)] * 2 + [pltpu.SemaphoreType.DMA((n, 2))],
        input_output_aliases={2 * n: 0, 2 * n + 1: 1} if more else {},
        compiler_params=SMALL,
        cost_estimate=CHEAP,
        name="finish",
    )(*[v for both in zip(owns, gots) for v in both], *held)


def split_kernel(*refs):
    blocks = [r[...].astype(F32) for r in refs[:EXPERTS]]
    refs[-2][...] = jnp.concatenate([b[:CAP] for b in blocks], axis=0).astype(BF16)
    refs[-1][...] = jnp.concatenate([b[CAP:] for b in blocks], axis=0).astype(BF16)


def split(blocks, earlier):
    width = blocks[0].shape[1]
    return pl.pallas_call(
        split_kernel,
        out_shape=[jax.ShapeDtypeStruct((EXPERTS * CAP, width), BF16)] * 2,
        in_specs=[HERE] * EXPERTS + [ANYWHERE] * len(earlier),
        compiler_params=SMALL,
        cost_estimate=CHEAP,
        name="split",
    )(*blocks, *earlier)


def unpack_kernel(placer_ref, mine_ref, got_ref, *refs):
    chosen = placer_ref[...].astype(F32).T.astype(BF16)
    total = jnp.dot(chosen, mine_ref[...], preferred_element_type=F32)
    total += jnp.dot(chosen, got_ref[...], preferred_element_type=F32)
    refs[-1][...] = total.astype(BF16)


def unpack(placer, mine, got, earlier):
    return pl.pallas_call(
        unpack_kernel,
        out_shape=jax.ShapeDtypeStruct((placer.shape[1], mine.shape[1]), BF16),
        in_specs=[HERE] * 3 + [AFAR] * len(earlier),
        compiler_params=SMALL,
        cost_estimate=DEAR,
        name="unpack",
    )(placer, mine, got, *[kept(v) for v in earlier])


def swap(value, axis):
    return lax.ppermute(value, axis, [(0, 1), (1, 0)])


def across_planes(blocks):
    return [blocks[0]] + [
        lax.ppermute(blocks[k], "arch", [(i, i ^ k) for i in range(EXPERTS)]) for k in range(1, EXPERTS)
    ]


def after(values, earlier):
    n = len(values)
    return list(lax.optimization_barrier((*values, *earlier))[:n])


def gathering(designs, archetype, w_gate, w_up, w_down, cotangent):
    far, core = lax.axis_index("far"), lax.axis_index("core")
    scalars = [lax.axis_index("arch"), 2 * far + core, 2 * far + 1 - core]
    scalars = [v.astype(jnp.int32)[None] for v in scalars]
    tokens, width = designs.shape
    share = width // 4
    placer, *blocks = pack(scalars, archetype.reshape(1, tokens), designs, cotangent)
    wd, wdt = flip(after([w_down], [placer])[0])

    x_own = join(across_planes(blocks[:EXPERTS]), [wdt])
    x_far, x_near = swap(x_own, "far"), swap(x_own, "half")
    moved = across_planes(relay(blocks[EXPERTS:], [x_own]))

    wg, wu = w_gate, w_up
    act0, coef0, share_own = forward([x_own], wg, wu, wd)
    (x_pass,) = relay([x_near], [act0, x_far])
    x_corner = swap(x_pass, "far")
    act1, coef1, *shares = forward([x_near], wg, wu, wd, other=share_own, earlier=[x_pass])
    g_own = join(moved, [act1])
    g_far, g_near = swap(g_own, "far"), swap(g_own, "half")
    returned = across_planes(shares)
    act2, coef2 = forward([x_far], wg, wu, earlier=[g_own])
    act3, coef3 = forward([x_corner], wg, wu, earlier=[act2])
    xt = turn(*scalars[1:], [x_own, x_near, x_far, x_corner], share)
    (g_pass,) = relay([g_far], [act3])
    (g_pass,) = relay([g_pass], [g_near])
    g_corner = swap(g_pass, "half")

    gs = [g_own, g_near, g_far, g_corner]
    acts, coefs = [act0, act1, act2, act3], [coef0, coef1, coef2, coef3]
    cols = w_down.shape[0]
    half = cols // 2
    mine, theirs = split(returned, [g_corner])
    got = swap(theirs, "half")
    own0, sib0 = backward(xt, gs, acts, coefs, wdt, 0, half, [mine])
    own1, sib1 = backward(xt, gs, acts, coefs, wdt, half, half, [own0])
    got0, got1 = swap(sib0, "core"), swap(sib1, "core")
    held = finish([own0], [got0], (0,), cols)
    outputs = unpack(placer, mine, got, held[:1])
    grad_gate, grad_up = finish([own1], [got1], (half,), cols, held)
    return outputs, grad_gate, grad_up


def reducing(designs, archetype, w_gate, w_up, w_down, cotangent):
    width = designs.shape[1]
    owners = lax.axis_size("expert")
    sharers = owners // EXPERTS
    hidden_cols = w_gate.shape[1]
    labels = archetype[:, 0]
    onehot = (labels[:, None] == jnp.arange(EXPERTS, dtype=jnp.int32)[None, :]).astype(jnp.int32)
    ranks = jnp.cumsum(onehot, axis=0) - onehot
    target = labels * CAP + jnp.sum(ranks * onehot, axis=1)
    placer = (jnp.arange(EXPERTS * CAP, dtype=jnp.int32)[:, None] == target[None, :]).astype(BF16)
    received = []
    for rows in (designs, cotangent):
        packed = jnp.dot(placer, rows, preferred_element_type=F32).astype(BF16)
        send = jnp.repeat(packed.reshape(EXPERTS, CAP, width), sharers, axis=0)
        received.append(
            lax.all_to_all(send, "expert", split_axis=0, concat_axis=0, tiled=True).reshape(
                owners * CAP, width
            )
        )
    flat_x, flat_g = received
    gate = jnp.dot(flat_x, w_gate, preferred_element_type=F32)
    up = jnp.dot(flat_x, w_up, preferred_element_type=F32)
    act, slope = silu_parts(gate)
    hidden = (act * up).astype(BF16)
    partial_value = (
        jnp.dot(hidden, w_down, preferred_element_type=F32).astype(BF16).reshape(owners, CAP, width)
    )
    returned = lax.all_to_all(partial_value, "expert", split_axis=0, concat_axis=0, tiled=True)
    summed = jnp.sum(returned.astype(F32).reshape(EXPERTS, sharers, CAP, width), axis=1).reshape(
        EXPERTS * CAP, width
    )
    outputs = jnp.take(summed, target, axis=0).astype(BF16)
    d_hidden = contract_cols(flat_g, w_down)
    d_gate = (d_hidden * up * slope).astype(BF16)
    d_up = (d_hidden * act).astype(BF16)
    grads = jnp.concatenate([contract_rows(flat_x, d_gate), contract_rows(flat_x, d_up)], axis=1)
    mine = lax.psum_scatter(grads.astype(BF16), "dp", scatter_dimension=0, tiled=True)
    return outputs, mine[:, :hidden_cols], mine[:, hidden_cols:]


def solution(mesh):
    dp, owners = mesh.devices.shape
    if (dp, owners) == (4, 2 * EXPERTS):
        rows, cols = ("far", "core"), ("arch", "half")
        mesh = Mesh(mesh.devices.reshape(2, 2, EXPERTS, 2), rows + cols)
        body = gathering
    else:
        rows, cols = ("dp",), ("expert",)
        body = reducing
    tokens = P(rows + cols, None)
    return jax.shard_map(
        body,
        mesh=mesh,
        in_specs=(tokens, tokens, P(None, cols), P(None, cols), P(cols, None), tokens),
        out_specs=(tokens, P(rows, cols), P(rows, cols)),
        check_vma=False,
    )
```

```python
import functools

import jax
import jax.numpy as jnp
from jax import lax
from jax.experimental import pallas as pl
from jax.experimental.pallas import tpu as pltpu
from jax.sharding import Mesh
from jax.sharding import PartitionSpec as P

EXPERTS = 4
CAP = 36
WIDE = 1024
STRIP = 512
SLICE = 256
MIB = 1024 * 1024
LARGE = pltpu.CompilerParams(vmem_limit_bytes=16 * MIB)
SMALL = pltpu.CompilerParams(vmem_limit_bytes=12 * MIB)
CHEAP = pl.CostEstimate(flops=0, bytes_accessed=0, transcendentals=0)
DEAR = pl.CostEstimate(flops=20_000_000_000, bytes_accessed=0, transcendentals=0)
F32 = jnp.float32
BF16 = jnp.bfloat16
HERE = pl.BlockSpec(memory_space=pltpu.VMEM)
AFAR = pl.BlockSpec(memory_space=pltpu.HBM)
ANYWHERE = pl.BlockSpec(memory_space=pl.ANY)


def silu_parts(gate):
    sigma = 0.5 * jnp.tanh(0.5 * gate) + 0.5
    return (gate * sigma, sigma * (1.0 + gate * (1.0 - sigma)))


def contract_rows(left, right):
    return lax.dot_general(left, right, (((0,), (0,)), ((), ())), preferred_element_type=F32)


def contract_cols(left, right):
    return lax.dot_general(left, right, (((1,), (1,)), ((), ())), preferred_element_type=F32)


def stacked(refs):
    return jnp.concatenate([r[...].astype(F32) for r in refs], axis=0)


def kept(value):
    return pltpu.with_memory_space_constraint(value, pltpu.HBM)


def pack_kernel(plane_ref, _, __, kind_ref, x_ref, g_ref, placer_ref, *refs):
    outs, (kind, x, g, sems) = refs[: 2 * EXPERTS], refs[2 * EXPERTS :]
    copies = [
        pltpu.make_async_copy(source, target, sems.at[i])
        for i, (source, target) in enumerate(((kind_ref, kind), (x_ref, x), (g_ref, g)))
    ]
    for copy in copies:
        copy.start()
    tokens = kind.shape[1]
    copies[0].wait()
    key = kind[...] ^ plane_ref[0]
    onehot = (key == lax.broadcasted_iota(jnp.int32, (8, tokens), 0)).astype(F32)
    before = lax.broadcasted_iota(jnp.int32, (tokens, tokens), 0) < lax.broadcasted_iota(
        jnp.int32, (tokens, tokens), 1
    )
    ranks = jnp.dot(onehot.astype(BF16), before.astype(BF16), preferred_element_type=F32)
    rank = jnp.sum(ranks * onehot, axis=0, keepdims=True).astype(jnp.int32)
    place = key * CAP + rank
    slots = EXPERTS * CAP
    placer = (place == lax.broadcasted_iota(jnp.int32, (slots, tokens), 0)).astype(F32).astype(BF16)
    placer_ref[...] = placer
    for copy, source, first in ((copies[1], x, 0), (copies[2], g, EXPERTS)):
        copy.wait()
        packed = jnp.dot(placer, source[...], preferred_element_type=F32)
        for k in range(EXPERTS):
            outs[first + k][...] = packed[k * CAP : (k + 1) * CAP].astype(BF16)


def pack(scalars, kind, x, g):
    tokens, width = x.shape
    return pl.pallas_call(
        pack_kernel,
        out_shape=[jax.ShapeDtypeStruct((EXPERTS * CAP, tokens), BF16)]
        + [jax.ShapeDtypeStruct((CAP, width), BF16)] * (2 * EXPERTS),
        in_specs=[pl.BlockSpec(memory_space=pltpu.SMEM)] * 3 + [AFAR] * 3,
        scratch_shapes=[
            pltpu.VMEM((1, tokens), jnp.int32),
            pltpu.VMEM((tokens, width), BF16),
            pltpu.VMEM((tokens, width), BF16),
            pltpu.SemaphoreType.DMA((3,)),
        ],
        compiler_params=SMALL,
        cost_estimate=CHEAP,
        name="pack",
    )(*scalars, kept(kind), kept(x), kept(g))


def join_kernel(*refs):
    refs[-1][...] = stacked(refs[-2 : -2 - EXPERTS : -1]).astype(BF16)


def join(blocks, earlier=()):
    width = blocks[0].shape[1]
    return pl.pallas_call(
        join_kernel,
        out_shape=jax.ShapeDtypeStruct((EXPERTS * CAP, width), BF16),
        in_specs=[ANYWHERE] * len(earlier) + [HERE] * EXPERTS,
        compiler_params=SMALL,
        cost_estimate=CHEAP,
        name="join",
    )(*earlier, *blocks[::-1])


def relay_kernel(n, *refs):
    for i in range(n):
        refs[len(refs) - n + i][...] = refs[i][...]


def relay(values, earlier):
    n = len(values)
    return pl.pallas_call(
        functools.partial(relay_kernel, n),
        out_shape=[jax.ShapeDtypeStruct(v.shape, v.dtype) for v in values],
        in_specs=[HERE] * n + [ANYWHERE] * len(earlier),
        compiler_params=SMALL,
        cost_estimate=CHEAP,
        name="relay",
    )(*values, *earlier)


def mark_kernel(value_ref, mark_ref):
    mark_ref[...] = value_ref[: mark_ref.shape[0], : mark_ref.shape[1]]


def mark(value):
    return pl.pallas_call(
        mark_kernel,
        out_shape=jax.ShapeDtypeStruct((16, 128), value.dtype),
        in_specs=[HERE],
        compiler_params=SMALL,
        cost_estimate=CHEAP,
        name="mark",
    )(value)


def flip_kernel(source_ref, here_ref, flipped_ref, sems):
    steps = source_ref.shape[0] // SLICE
    copies = []
    for j in range(steps):
        rows = pl.ds(j * SLICE, SLICE)
        copies.append(pltpu.make_async_copy(source_ref.at[rows], here_ref.at[rows], sems.at[j]))
        copies[j].start()
    for j in range(steps):
        copies[j].wait()
        rows = slice(j * SLICE, (j + 1) * SLICE)
        flipped_ref[:, rows] = here_ref[rows, :].T


def flip(value):
    return pl.pallas_call(
        flip_kernel,
        out_shape=[pltpu.VMEM(value.shape, value.dtype), pltpu.VMEM(value.shape[::-1], value.dtype)],
        in_specs=[AFAR],
        out_specs=[HERE, HERE],
        scratch_shapes=[pltpu.SemaphoreType.DMA((value.shape[0] // SLICE,))],
        compiler_params=SMALL,
        cost_estimate=CHEAP,
        name="flip",
    )(kept(value))


def forward_kernel(n, fetch, down, pair, unused, *refs):
    refs = list(refs[unused:])
    xs = [refs.pop(0) for _ in range(n)]
    wg_ref, wu_ref = refs.pop(0), refs.pop(0)
    wd_ref = refs.pop(0) if down else None
    other_ref = refs.pop(0) if pair else None
    act_ref, coef_ref = refs.pop(0), refs.pop(0)
    shares = [refs.pop(0) for _ in range(EXPERTS if pair else down)]
    if fetch:
        sources, sems = (wg_ref, wu_ref), refs.pop()
        wg_ref, wu_ref = refs.pop(0), refs.pop(0)
    acc_ref = refs.pop(0) if down else None
    part = xs[0].shape[0]
    x_ref = xs[0]
    if n > 1:
        x_ref = refs.pop(0)
        for i in range(n):
            x_ref[i * part : (i + 1) * part, :] = xs[i][...]
    steps = wg_ref.shape[1] // (2 * WIDE)

    def copies(j):
        cols = pl.ds(pl.multiple_of(j * (2 * WIDE), (2 * WIDE)), (2 * WIDE))
        return [
            pltpu.make_async_copy(source.at[:, cols], target.at[:, cols], sems.at[j, i])
            for i, (source, target) in enumerate(zip(sources, (wg_ref, wu_ref)))
        ]

    if fetch:
        for j in range(steps):
            for copy in copies(j):
                copy.start()
    if down:
        acc_ref[...] = jnp.zeros_like(acc_ref)

    @pl.loop(0, steps)
    def _(j):
        if fetch:
            for copy in copies(j):
                copy.wait()
        for i in range(2):
            cols = pl.ds(pl.multiple_of(j * (2 * WIDE) + i * WIDE, WIDE), WIDE)
            gate = jnp.dot(x_ref[...], wg_ref[:, cols], preferred_element_type=F32)
            up = jnp.dot(x_ref[...], wu_ref[:, cols], preferred_element_type=F32)
            act, slope = silu_parts(gate)
            act_ref[:, cols] = act.astype(BF16)
            coef_ref[:, cols] = (up * slope).astype(BF16)
            if down:
                hidden = (act[:part] * up[:part]).astype(BF16)
                acc_ref[...] += jnp.dot(hidden, wd_ref[cols, :], preferred_element_type=F32)

    if pair:
        other = other_ref[...].astype(F32)
        for k in range(EXPERTS):
            rows = slice(k * CAP, (k + 1) * CAP)
            block = jnp.concatenate([other[rows], acc_ref[rows, :]], axis=0).astype(BF16)
            shares[k][...] = block
    elif down:
        shares[0][...] = acc_ref[...].astype(BF16)


def forward(xs, wg, wu, wd=None, other=None, fetch=False, earlier=()):
    n, (part, width), cols = len(xs), xs[0].shape, wg.shape[1]
    rows = n * part
    down, pair = wd is not None, other is not None
    shares = [jax.ShapeDtypeStruct((part, width), BF16)] * down
    if pair:
        shares = [jax.ShapeDtypeStruct((2 * CAP, width), BF16)] * EXPERTS
    weights = [kept(wg), kept(wu)] if fetch else [wg, wu]
    return pl.pallas_call(
        functools.partial(forward_kernel, n, fetch, down, pair, len(earlier)),
        out_shape=[jax.ShapeDtypeStruct((rows, cols), BF16)] * 2
        + shares
        + [pltpu.VMEM(wg.shape, wg.dtype)] * (2 * fetch),
        in_specs=[ANYWHERE] * len(earlier)
        + [HERE] * n
        + [AFAR if fetch else HERE] * 2
        + [HERE] * (down + pair),
        scratch_shapes=[pltpu.VMEM((part, width), F32)] * down
        + [pltpu.VMEM((rows, width), BF16)] * (n > 1)
        + [pltpu.SemaphoreType.DMA((cols // (2 * WIDE), 2))] * fetch,
        compiler_params=LARGE,
        cost_estimate=CHEAP,
        name="forward" + "_fetch" * fetch + "_down" * down,
    )(*earlier, *xs, *weights, *([wd] * down), *([other] * pair))


def turn_kernel(_, __, *refs):
    refs[8][: refs[0].shape[1], :] = stacked(refs[0:4]).T.astype(BF16)
    refs[8][refs[0].shape[1] :, :] = stacked(refs[4:8]).T.astype(BF16)


def turn(own, sib, xs, share):
    part = xs[0].shape[0]
    rows = len(xs) * part
    return pl.pallas_call(
        turn_kernel,
        grid_spec=pltpu.PrefetchScalarGridSpec(
            num_scalar_prefetch=2,
            grid=(1,),
            in_specs=[pl.BlockSpec((part, share), lambda j, a, b: (0, a[0]))] * 4
            + [pl.BlockSpec((part, share), lambda j, a, b: (0, b[0]))] * 4,
            out_specs=pl.BlockSpec((2 * share, rows), lambda j, a, b: (0, 0)),
        ),
        out_shape=jax.ShapeDtypeStruct((2 * share, rows), BF16),
        compiler_params=SMALL,
        cost_estimate=CHEAP,
        name="turn",
    )(own, sib, *xs, *xs)


def backward_kernel(first, counts, xt_ref, *refs):
    n = len(counts)
    gs, acts, coefs = refs[:4], refs[4 : 4 + n], refs[4 + n : 4 + 2 * n]
    wdt_ref, *_, own_ref, sib_ref, g_ref = refs[4 + 2 * n :]
    part = gs[0].shape[0]
    share = own_ref.shape[0] // 2
    for i in range(4):
        g_ref[i * part : (i + 1) * part, :] = gs[i][...]

    def strip(start):
        here = pl.ds(pl.multiple_of(start, STRIP), STRIP)
        cols = pl.ds(pl.multiple_of(start + first, STRIP), STRIP)
        d_hidden = jnp.dot(g_ref[...], wdt_ref[:, cols], preferred_element_type=F32)
        for row, parts in ((0, coefs), (share, acts)):
            factor = jnp.concatenate([p[:, cols] for p in parts], axis=0).astype(F32)
            d_cols = (d_hidden * factor).astype(BF16)
            total = jnp.dot(xt_ref[...], d_cols, preferred_element_type=F32).astype(BF16)
            own_ref[row : row + share, here] = total[:share]
            sib_ref[row : row + share, here] = total[share:]

    for start in range(0, own_ref.shape[1], STRIP):
        strip(start)


def backward(xt, gs, acts, coefs, wdt, first, cols, earlier=()):
    part, width = gs[0].shape
    height, rows = xt.shape
    counts = tuple(a.shape[0] for a in acts)
    return pl.pallas_call(
        functools.partial(backward_kernel, first, counts),
        out_shape=[jax.ShapeDtypeStruct((height, cols), BF16)] * 2,
        in_specs=[HERE] * (6 + 2 * len(acts)) + [ANYWHERE] * len(earlier),
        scratch_shapes=[pltpu.VMEM((rows, width), BF16)],
        compiler_params=LARGE,
        cost_estimate=DEAR,
        name="backward",
    )(xt, *gs, *acts, *coefs, wdt, *earlier)


def finish_kernel(spans, more, *refs):
    n = len(spans)
    pairs = [refs[2 * i : 2 * i + 2] for i in range(n)]
    gate_ref, up_ref, gate, up, sems = refs[2 * n + 2 * more :]
    share = gate_ref.shape[0]
    low = spans[0][0]
    copies = []
    for i, ((first, cols), (own, got)) in enumerate(zip(spans, pairs)):
        for j, (target, held) in enumerate(((gate_ref, gate), (up_ref, up))):
            rows = slice(j * share, (j + 1) * share)
            here = pl.ds(first - low, cols)
            held[:, here] = (own[rows, :].astype(F32) + got[rows, :].astype(F32)).astype(BF16)
            copies.append(
                pltpu.make_async_copy(held.at[:, here], target.at[:, pl.ds(first, cols)], sems.at[i, j])
            )
            copies[-1].start()
    for copy in copies:
        copy.wait()


def finish(owns, gots, firsts, width, held=()):
    share = owns[0].shape[0] // 2
    spans = tuple((first, own.shape[1]) for first, own in zip(firsts, owns))
    total = sum(cols for _, cols in spans)
    n, more = len(owns), len(held) > 0
    return pl.pallas_call(
        functools.partial(finish_kernel, spans, more),
        out_shape=[jax.ShapeDtypeStruct((share, width), BF16)] * 2,
        in_specs=[HERE] * (2 * n) + [ANYWHERE] * (2 * more),
        out_specs=[ANYWHERE] * 2,
        scratch_shapes=[pltpu.VMEM((share, total), BF16)] * 2 + [pltpu.SemaphoreType.DMA((n, 2))],
        input_output_aliases={2 * n: 0, 2 * n + 1: 1} if more else {},
        compiler_params=SMALL,
        cost_estimate=CHEAP,
        name="finish",
    )(*[v for both in zip(owns, gots) for v in both], *held)


def split_kernel(*refs):
    blocks = [r[...].astype(F32) for r in refs[:EXPERTS]]
    refs[-2][...] = jnp.concatenate([b[:CAP] for b in blocks], axis=0).astype(BF16)
    refs[-1][...] = jnp.concatenate([b[CAP:] for b in blocks], axis=0).astype(BF16)


def split(blocks, earlier):
    width = blocks[0].shape[1]
    return pl.pallas_call(
        split_kernel,
        out_shape=[jax.ShapeDtypeStruct((EXPERTS * CAP, width), BF16)] * 2,
        in_specs=[HERE] * EXPERTS + [ANYWHERE] * len(earlier),
        compiler_params=SMALL,
        cost_estimate=CHEAP,
        name="split",
    )(*blocks, *earlier)


def unpack_kernel(placer_ref, mine_ref, got_ref, *refs):
    chosen = placer_ref[...].astype(F32).T.astype(BF16)
    total = jnp.dot(chosen, mine_ref[...], preferred_element_type=F32)
    total += jnp.dot(chosen, got_ref[...], preferred_element_type=F32)
    refs[-1][...] = total.astype(BF16)


def unpack(placer, mine, got, earlier):
    return pl.pallas_call(
        unpack_kernel,
        out_shape=jax.ShapeDtypeStruct((placer.shape[1], mine.shape[1]), BF16),
        in_specs=[HERE] * 3 + [AFAR] * len(earlier),
        compiler_params=SMALL,
        cost_estimate=DEAR,
        name="unpack",
    )(placer, mine, got, *[kept(v) for v in earlier])


def swap(value, axis):
    return lax.ppermute(value, axis, [(0, 1), (1, 0)])


def across_planes(blocks):
    return [blocks[0]] + [
        lax.ppermute(blocks[k], "arch", [(i, i ^ k) for i in range(EXPERTS)]) for k in range(1, EXPERTS)
    ]


def after(values, earlier):
    n = len(values)
    return list(lax.optimization_barrier((*values, *earlier))[:n])


def gathering(designs, archetype, w_gate, w_up, w_down, cotangent):
    far, core = lax.axis_index("far"), lax.axis_index("core")
    scalars = [lax.axis_index("arch"), 2 * far + core, 2 * far + 1 - core]
    scalars = [v.astype(jnp.int32)[None] for v in scalars]
    tokens, width = designs.shape
    share = width // 4
    placer, *blocks = pack(scalars, archetype.reshape(1, tokens), designs, cotangent)
    wd, wdt = flip(after([w_down], [placer])[0])

    x_own = join(across_planes(blocks[:EXPERTS]))
    moved = across_planes(relay(blocks[EXPERTS:], [wdt]))
    x_far, x_near = swap(x_own, "far"), swap(x_own, "half")

    wg, wu = w_gate, w_up
    act0, coef0, share_own = forward([x_own], wg, wu, wd)
    g_own = join(moved, [act0])
    g_far, g_near = swap(g_own, "far"), swap(g_own, "half")
    act1, coef1, *shares = forward([x_near], wg, wu, wd, other=share_own)
    act2, coef2 = forward([x_far], wg, wu, earlier=[act1])
    (x_pass,) = relay([x_near], [mark(act2), g_far])
    (g_pass,) = relay([g_far], [x_pass, g_near])
    x_corner, g_corner = swap(x_pass, "far"), swap(g_pass, "half")
    returned = across_planes(shares)
    act3, coef3 = forward([x_corner], wg, wu)
    xt = turn(*scalars[1:], [x_own, x_near, x_far, x_corner], share)

    gs = [g_own, g_near, g_far, g_corner]
    acts, coefs = [act0, act1, act2, act3], [coef0, coef1, coef2, coef3]
    cols = w_down.shape[0]
    cut = 3 * cols // 4
    own0, sib0 = backward(xt, gs, acts, coefs, wdt, 0, cut)
    mine, theirs = split(returned, [own0])
    got = swap(theirs, "half")
    own1, sib1 = backward(xt, gs, acts, coefs, wdt, cut, cols - cut, [mine])
    got0, got1 = swap(sib0, "core"), swap(sib1, "core")
    held = finish([own0], [got0], (0,), cols)
    outputs = unpack(placer, mine, got, held[:1])
    grad_gate, grad_up = finish([own1], [got1], (cut,), cols, held)
    return outputs, grad_gate, grad_up


def reducing(designs, archetype, w_gate, w_up, w_down, cotangent):
    width = designs.shape[1]
    owners = lax.axis_size("expert")
    sharers = owners // EXPERTS
    hidden_cols = w_gate.shape[1]
    labels = archetype[:, 0]
    onehot = (labels[:, None] == jnp.arange(EXPERTS, dtype=jnp.int32)[None, :]).astype(jnp.int32)
    ranks = jnp.cumsum(onehot, axis=0) - onehot
    target = labels * CAP + jnp.sum(ranks * onehot, axis=1)
    placer = (jnp.arange(EXPERTS * CAP, dtype=jnp.int32)[:, None] == target[None, :]).astype(BF16)
    received = []
    for rows in (designs, cotangent):
        packed = jnp.dot(placer, rows, preferred_element_type=F32).astype(BF16)
        send = jnp.repeat(packed.reshape(EXPERTS, CAP, width), sharers, axis=0)
        received.append(
            lax.all_to_all(send, "expert", split_axis=0, concat_axis=0, tiled=True).reshape(
                owners * CAP, width
            )
        )
    flat_x, flat_g = received
    gate = jnp.dot(flat_x, w_gate, preferred_element_type=F32)
    up = jnp.dot(flat_x, w_up, preferred_element_type=F32)
    act, slope = silu_parts(gate)
    hidden = (act * up).astype(BF16)
    partial_value = (
        jnp.dot(hidden, w_down, preferred_element_type=F32).astype(BF16).reshape(owners, CAP, width)
    )
    returned = lax.all_to_all(partial_value, "expert", split_axis=0, concat_axis=0, tiled=True)
    summed = jnp.sum(returned.astype(F32).reshape(EXPERTS, sharers, CAP, width), axis=1).reshape(
        EXPERTS * CAP, width
    )
    outputs = jnp.take(summed, target, axis=0).astype(BF16)
    d_hidden = contract_cols(flat_g, w_down)
    d_gate = (d_hidden * up * slope).astype(BF16)
    d_up = (d_hidden * act).astype(BF16)
    grads = jnp.concatenate([contract_rows(flat_x, d_gate), contract_rows(flat_x, d_up)], axis=1)
    mine = lax.psum_scatter(grads.astype(BF16), "dp", scatter_dimension=0, tiled=True)
    return outputs, mine[:, :hidden_cols], mine[:, hidden_cols:]


def solution(mesh):
    dp, owners = mesh.devices.shape
    if (dp, owners) == (4, 2 * EXPERTS):
        rows, cols = ("far", "core"), ("arch", "half")
        mesh = Mesh(mesh.devices.reshape(2, 2, EXPERTS, 2), rows + cols)
        body = gathering
    else:
        rows, cols = ("dp",), ("expert",)
        body = reducing
    tokens = P(rows + cols, None)
    return jax.shard_map(
        body,
        mesh=mesh,
        in_specs=(tokens, tokens, P(None, cols), P(None, cols), P(cols, None), tokens),
        out_specs=(tokens, P(rows, cols), P(rows, cols)),
        check_vma=False,
    )
```

```python
import functools

import jax
import jax.numpy as jnp
from jax import lax
from jax.experimental import pallas as pl
from jax.experimental.pallas import tpu as pltpu
from jax.sharding import Mesh
from jax.sharding import PartitionSpec as P

EXPERTS = 4
CAP = 36
WIDE = 1024
STRIP = 512
SLICE = 256
MIB = 1024 * 1024
LARGE = pltpu.CompilerParams(vmem_limit_bytes=16 * MIB)
SMALL = pltpu.CompilerParams(vmem_limit_bytes=12 * MIB)
CHEAP = pl.CostEstimate(flops=0, bytes_accessed=0, transcendentals=0)
DEAR = pl.CostEstimate(flops=20_000_000_000, bytes_accessed=0, transcendentals=0)
F32 = jnp.float32
BF16 = jnp.bfloat16
HERE = pl.BlockSpec(memory_space=pltpu.VMEM)
AFAR = pl.BlockSpec(memory_space=pltpu.HBM)
ANYWHERE = pl.BlockSpec(memory_space=pl.ANY)


def silu_parts(gate):
    sigma = 0.5 * jnp.tanh(0.5 * gate) + 0.5
    return (gate * sigma, sigma * (1.0 + gate * (1.0 - sigma)))


def contract_rows(left, right):
    return lax.dot_general(left, right, (((0,), (0,)), ((), ())), preferred_element_type=F32)


def contract_cols(left, right):
    return lax.dot_general(left, right, (((1,), (1,)), ((), ())), preferred_element_type=F32)


def stacked(refs):
    return jnp.concatenate([r[...].astype(F32) for r in refs], axis=0)


def kept(value):
    return pltpu.with_memory_space_constraint(value, pltpu.HBM)


def pack_kernel(plane_ref, _, __, kind_ref, x_ref, g_ref, placer_ref, *refs):
    outs, (kind, x, g, sems) = refs[: 2 * EXPERTS], refs[2 * EXPERTS :]
    copies = [
        pltpu.make_async_copy(source, target, sems.at[i])
        for i, (source, target) in enumerate(((kind_ref, kind), (x_ref, x), (g_ref, g)))
    ]
    for copy in copies:
        copy.start()
    tokens = kind.shape[1]
    copies[0].wait()
    key = kind[...] ^ plane_ref[0]
    onehot = (key == lax.broadcasted_iota(jnp.int32, (8, tokens), 0)).astype(F32)
    before = lax.broadcasted_iota(jnp.int32, (tokens, tokens), 0) < lax.broadcasted_iota(
        jnp.int32, (tokens, tokens), 1
    )
    ranks = jnp.dot(onehot.astype(BF16), before.astype(BF16), preferred_element_type=F32)
    rank = jnp.sum(ranks * onehot, axis=0, keepdims=True).astype(jnp.int32)
    place = key * CAP + rank
    slots = EXPERTS * CAP
    placer = (place == lax.broadcasted_iota(jnp.int32, (slots, tokens), 0)).astype(F32).astype(BF16)
    placer_ref[...] = placer
    for copy, source, first in ((copies[1], x, 0), (copies[2], g, EXPERTS)):
        copy.wait()
        packed = jnp.dot(placer, source[...], preferred_element_type=F32)
        for k in range(EXPERTS):
            outs[first + k][...] = packed[k * CAP : (k + 1) * CAP].astype(BF16)


def pack(scalars, kind, x, g):
    tokens, width = x.shape
    return pl.pallas_call(
        pack_kernel,
        out_shape=[jax.ShapeDtypeStruct((EXPERTS * CAP, tokens), BF16)]
        + [jax.ShapeDtypeStruct((CAP, width), BF16)] * (2 * EXPERTS),
        in_specs=[pl.BlockSpec(memory_space=pltpu.SMEM)] * 3 + [AFAR] * 3,
        scratch_shapes=[
            pltpu.VMEM((1, tokens), jnp.int32),
            pltpu.VMEM((tokens, width), BF16),
            pltpu.VMEM((tokens, width), BF16),
            pltpu.SemaphoreType.DMA((3,)),
        ],
        compiler_params=SMALL,
        cost_estimate=CHEAP,
        name="pack",
    )(*scalars, kept(kind), kept(x), kept(g))


def join_kernel(*refs):
    refs[-1][...] = stacked(refs[-2 : -2 - EXPERTS : -1]).astype(BF16)


def join(blocks, earlier=()):
    width = blocks[0].shape[1]
    return pl.pallas_call(
        join_kernel,
        out_shape=jax.ShapeDtypeStruct((EXPERTS * CAP, width), BF16),
        in_specs=[ANYWHERE] * len(earlier) + [HERE] * EXPERTS,
        compiler_params=SMALL,
        cost_estimate=CHEAP,
        name="join",
    )(*earlier, *blocks[::-1])


def relay_kernel(n, *refs):
    for i in range(n):
        refs[len(refs) - n + i][...] = refs[i][...]


def relay(values, earlier):
    n = len(values)
    return pl.pallas_call(
        functools.partial(relay_kernel, n),
        out_shape=[jax.ShapeDtypeStruct(v.shape, v.dtype) for v in values],
        in_specs=[HERE] * n + [ANYWHERE] * len(earlier),
        compiler_params=SMALL,
        cost_estimate=CHEAP,
        name="relay",
    )(*values, *earlier)


def mark_kernel(value_ref, mark_ref):
    mark_ref[...] = value_ref[: mark_ref.shape[0], : mark_ref.shape[1]]


def mark(value):
    return pl.pallas_call(
        mark_kernel,
        out_shape=jax.ShapeDtypeStruct((16, 128), value.dtype),
        in_specs=[HERE],
        compiler_params=SMALL,
        cost_estimate=CHEAP,
        name="mark",
    )(value)


def flip_kernel(source_ref, here_ref, flipped_ref, sems):
    steps = source_ref.shape[0] // SLICE
    copies = []
    for j in range(steps):
        rows = pl.ds(j * SLICE, SLICE)
        copies.append(pltpu.make_async_copy(source_ref.at[rows], here_ref.at[rows], sems.at[j]))
        copies[j].start()
    for j in range(steps):
        copies[j].wait()
        rows = slice(j * SLICE, (j + 1) * SLICE)
        flipped_ref[:, rows] = here_ref[rows, :].T


def flip(value):
    return pl.pallas_call(
        flip_kernel,
        out_shape=[pltpu.VMEM(value.shape, value.dtype), pltpu.VMEM(value.shape[::-1], value.dtype)],
        in_specs=[AFAR],
        out_specs=[HERE, HERE],
        scratch_shapes=[pltpu.SemaphoreType.DMA((value.shape[0] // SLICE,))],
        compiler_params=SMALL,
        cost_estimate=CHEAP,
        name="flip",
    )(kept(value))


def forward_kernel(n, fetch, down, pair, unused, *refs):
    refs = list(refs[unused:])
    xs = [refs.pop(0) for _ in range(n)]
    wg_ref, wu_ref = refs.pop(0), refs.pop(0)
    wd_ref = refs.pop(0) if down else None
    other_ref = refs.pop(0) if pair else None
    act_ref, coef_ref = refs.pop(0), refs.pop(0)
    shares = [refs.pop(0) for _ in range(EXPERTS if pair else down)]
    if fetch:
        sources, sems = (wg_ref, wu_ref), refs.pop()
        wg_ref, wu_ref = refs.pop(0), refs.pop(0)
    acc_ref = refs.pop(0) if down else None
    part = xs[0].shape[0]
    x_ref = xs[0]
    if n > 1:
        x_ref = refs.pop(0)
        for i in range(n):
            x_ref[i * part : (i + 1) * part, :] = xs[i][...]
    steps = wg_ref.shape[1] // (2 * WIDE)

    def copies(j):
        cols = pl.ds(pl.multiple_of(j * (2 * WIDE), (2 * WIDE)), (2 * WIDE))
        return [
            pltpu.make_async_copy(source.at[:, cols], target.at[:, cols], sems.at[j, i])
            for i, (source, target) in enumerate(zip(sources, (wg_ref, wu_ref)))
        ]

    if fetch:
        for j in range(steps):
            for copy in copies(j):
                copy.start()
    if down:
        acc_ref[...] = jnp.zeros_like(acc_ref)

    @pl.loop(0, steps)
    def _(j):
        if fetch:
            for copy in copies(j):
                copy.wait()
        for i in range(2):
            cols = pl.ds(pl.multiple_of(j * (2 * WIDE) + i * WIDE, WIDE), WIDE)
            gate = jnp.dot(x_ref[...], wg_ref[:, cols], preferred_element_type=F32)
            up = jnp.dot(x_ref[...], wu_ref[:, cols], preferred_element_type=F32)
            act, slope = silu_parts(gate)
            act_ref[:, cols] = act.astype(BF16)
            coef_ref[:, cols] = (up * slope).astype(BF16)
            if down:
                hidden = (act[:part] * up[:part]).astype(BF16)
                acc_ref[...] += jnp.dot(hidden, wd_ref[cols, :], preferred_element_type=F32)

    if pair:
        other = other_ref[...].astype(F32)
        for k in range(EXPERTS):
            rows = slice(k * CAP, (k + 1) * CAP)
            block = jnp.concatenate([other[rows], acc_ref[rows, :]], axis=0).astype(BF16)
            shares[k][...] = block
    elif down:
        shares[0][...] = acc_ref[...].astype(BF16)


def forward(xs, wg, wu, wd=None, other=None, fetch=False, earlier=(), cost=CHEAP):
    n, (part, width), cols = len(xs), xs[0].shape, wg.shape[1]
    rows = n * part
    down, pair = wd is not None, other is not None
    shares = [jax.ShapeDtypeStruct((part, width), BF16)] * down
    if pair:
        shares = [jax.ShapeDtypeStruct((2 * CAP, width), BF16)] * EXPERTS
    weights = [kept(wg), kept(wu)] if fetch else [wg, wu]
    return pl.pallas_call(
        functools.partial(forward_kernel, n, fetch, down, pair, len(earlier)),
        out_shape=[jax.ShapeDtypeStruct((rows, cols), BF16)] * 2
        + shares
        + [pltpu.VMEM(wg.shape, wg.dtype)] * (2 * fetch),
        in_specs=[ANYWHERE] * len(earlier)
        + [HERE] * n
        + [AFAR if fetch else HERE] * 2
        + [HERE] * (down + pair),
        scratch_shapes=[pltpu.VMEM((part, width), F32)] * down
        + [pltpu.VMEM((rows, width), BF16)] * (n > 1)
        + [pltpu.SemaphoreType.DMA((cols // (2 * WIDE), 2))] * fetch,
        compiler_params=LARGE,
        cost_estimate=cost,
        name="forward" + "_fetch" * fetch + "_down" * down,
    )(*earlier, *xs, *weights, *([wd] * down), *([other] * pair))


def turn_kernel(_, __, *refs):
    refs[8][: refs[0].shape[1], :] = stacked(refs[0:4]).T.astype(BF16)
    refs[8][refs[0].shape[1] :, :] = stacked(refs[4:8]).T.astype(BF16)


def turn(own, sib, xs, share):
    part = xs[0].shape[0]
    rows = len(xs) * part
    return pl.pallas_call(
        turn_kernel,
        grid_spec=pltpu.PrefetchScalarGridSpec(
            num_scalar_prefetch=2,
            grid=(1,),
            in_specs=[pl.BlockSpec((part, share), lambda j, a, b: (0, a[0]))] * 4
            + [pl.BlockSpec((part, share), lambda j, a, b: (0, b[0]))] * 4,
            out_specs=pl.BlockSpec((2 * share, rows), lambda j, a, b: (0, 0)),
        ),
        out_shape=jax.ShapeDtypeStruct((2 * share, rows), BF16),
        compiler_params=SMALL,
        cost_estimate=CHEAP,
        name="turn",
    )(own, sib, *xs, *xs)


def backward_kernel(first, counts, xt_ref, *refs):
    n = len(counts)
    gs, acts, coefs = refs[:4], refs[4 : 4 + n], refs[4 + n : 4 + 2 * n]
    wdt_ref, *_, own_ref, sib_ref, g_ref = refs[4 + 2 * n :]
    part = gs[0].shape[0]
    share = own_ref.shape[0] // 2
    for i in range(4):
        g_ref[i * part : (i + 1) * part, :] = gs[i][...]

    def strip(start):
        here = pl.ds(pl.multiple_of(start, STRIP), STRIP)
        cols = pl.ds(pl.multiple_of(start + first, STRIP), STRIP)
        d_hidden = jnp.dot(g_ref[...], wdt_ref[:, cols], preferred_element_type=F32)
        for row, parts in ((0, coefs), (share, acts)):
            factor = jnp.concatenate([p[:, cols] for p in parts], axis=0).astype(F32)
            d_cols = (d_hidden * factor).astype(BF16)
            total = jnp.dot(xt_ref[...], d_cols, preferred_element_type=F32).astype(BF16)
            own_ref[row : row + share, here] = total[:share]
            sib_ref[row : row + share, here] = total[share:]

    for start in range(0, own_ref.shape[1], STRIP):
        strip(start)


def backward(xt, gs, acts, coefs, wdt, first, cols, earlier=()):
    part, width = gs[0].shape
    height, rows = xt.shape
    counts = tuple(a.shape[0] for a in acts)
    return pl.pallas_call(
        functools.partial(backward_kernel, first, counts),
        out_shape=[jax.ShapeDtypeStruct((height, cols), BF16)] * 2,
        in_specs=[HERE] * (6 + 2 * len(acts)) + [ANYWHERE] * len(earlier),
        scratch_shapes=[pltpu.VMEM((rows, width), BF16)],
        compiler_params=LARGE,
        cost_estimate=DEAR,
        name="backward",
    )(xt, *gs, *acts, *coefs, wdt, *earlier)


def finish_kernel(spans, more, unused, *refs):
    refs = refs[unused:]
    n = len(spans)
    pairs = [refs[2 * i : 2 * i + 2] for i in range(n)]
    gate_ref, up_ref, gate, up, sems = refs[2 * n + 2 * more :]
    share = gate_ref.shape[0]
    low = spans[0][0]
    copies = []
    for i, ((first, cols), (own, got)) in enumerate(zip(spans, pairs)):
        for j, (target, held) in enumerate(((gate_ref, gate), (up_ref, up))):
            rows = slice(j * share, (j + 1) * share)
            here = pl.ds(first - low, cols)
            held[:, here] = (own[rows, :].astype(F32) + got[rows, :].astype(F32)).astype(BF16)
            copies.append(
                pltpu.make_async_copy(held.at[:, here], target.at[:, pl.ds(first, cols)], sems.at[i, j])
            )
            copies[-1].start()
    for copy in copies:
        copy.wait()


def finish(owns, gots, firsts, width, held=(), earlier=()):
    share = owns[0].shape[0] // 2
    spans = tuple((first, own.shape[1]) for first, own in zip(firsts, owns))
    total = sum(cols for _, cols in spans)
    n, more = len(owns), len(held) > 0
    return pl.pallas_call(
        functools.partial(finish_kernel, spans, more, len(earlier)),
        out_shape=[jax.ShapeDtypeStruct((share, width), BF16)] * 2,
        in_specs=[AFAR] * len(earlier) + [HERE] * (2 * n) + [ANYWHERE] * (2 * more),
        out_specs=[ANYWHERE] * 2,
        scratch_shapes=[pltpu.VMEM((share, total), BF16)] * 2 + [pltpu.SemaphoreType.DMA((n, 2))],
        input_output_aliases={len(earlier) + 2 * n: 0, len(earlier) + 2 * n + 1: 1} if more else {},
        compiler_params=SMALL,
        cost_estimate=CHEAP,
        name="finish",
    )(*[kept(v) for v in earlier], *[v for both in zip(owns, gots) for v in both], *held)


def split_kernel(*refs):
    blocks = [r[...].astype(F32) for r in refs[:EXPERTS]]
    refs[-2][...] = jnp.concatenate([b[:CAP] for b in blocks], axis=0).astype(BF16)
    refs[-1][...] = jnp.concatenate([b[CAP:] for b in blocks], axis=0).astype(BF16)


def split(blocks, earlier):
    width = blocks[0].shape[1]
    return pl.pallas_call(
        split_kernel,
        out_shape=[jax.ShapeDtypeStruct((EXPERTS * CAP, width), BF16)] * 2,
        in_specs=[HERE] * EXPERTS + [ANYWHERE] * len(earlier),
        compiler_params=SMALL,
        cost_estimate=CHEAP,
        name="split",
    )(*blocks, *earlier)


def unpack_kernel(placer_ref, mine_ref, got_ref, *refs):
    chosen = placer_ref[...].astype(F32).T.astype(BF16)
    total = jnp.dot(chosen, mine_ref[...], preferred_element_type=F32)
    total += jnp.dot(chosen, got_ref[...], preferred_element_type=F32)
    refs[-1][...] = total.astype(BF16)


def unpack(placer, mine, got, earlier):
    return pl.pallas_call(
        unpack_kernel,
        out_shape=jax.ShapeDtypeStruct((placer.shape[1], mine.shape[1]), BF16),
        in_specs=[HERE] * 3 + [ANYWHERE] * len(earlier),
        compiler_params=SMALL,
        cost_estimate=DEAR,
        name="unpack",
    )(placer, mine, got, *earlier)


def swap(value, axis):
    return lax.ppermute(value, axis, [(0, 1), (1, 0)])


def across_planes(blocks):
    return [blocks[0]] + [
        lax.ppermute(blocks[k], "arch", [(i, i ^ k) for i in range(EXPERTS)]) for k in range(1, EXPERTS)
    ]


def after(values, earlier):
    n = len(values)
    return list(lax.optimization_barrier((*values, *earlier))[:n])


def gathering(designs, archetype, w_gate, w_up, w_down, cotangent):
    far, core = lax.axis_index("far"), lax.axis_index("core")
    scalars = [lax.axis_index("arch"), 2 * far + core, 2 * far + 1 - core]
    scalars = [v.astype(jnp.int32)[None] for v in scalars]
    tokens, width = designs.shape
    share = width // 4
    placer, *blocks = pack(scalars, archetype.reshape(1, tokens), designs, cotangent)
    wd, wdt = flip(after([w_down], [placer])[0])

    x_own = join(across_planes(blocks[:EXPERTS]))
    moved = across_planes(relay(blocks[EXPERTS:], [wdt]))
    x_far, x_near = swap(x_own, "far"), swap(x_own, "half")

    wg, wu = w_gate, w_up
    act0, coef0, share_own = forward([x_own], wg, wu, wd)
    g_own = join(moved, [act0])
    g_far, g_near = swap(g_own, "far"), swap(g_own, "half")
    act1, coef1, *shares = forward([x_near], wg, wu, wd, other=share_own, earlier=[x_far])
    (x_pass,) = relay([x_near], [mark(act1), g_far])
    (g_pass,) = relay([g_far], [x_pass, g_near])
    x_corner, g_corner = swap(x_pass, "far"), swap(g_pass, "half")
    returned = across_planes(shares)
    act2, coef2 = forward([x_far], wg, wu, earlier=[g_pass], cost=DEAR)
    mine, theirs = split(returned, [act2])
    got = swap(theirs, "half")
    act3, coef3 = forward([x_corner], wg, wu, earlier=[mine])
    xt = turn(*scalars[1:], [x_own, x_near, x_far, x_corner], share)

    gs = [g_own, g_near, g_far, g_corner]
    acts, coefs = [act0, act1, act2, act3], [coef0, coef1, coef2, coef3]
    cols = w_down.shape[0]
    cut = cols // 2
    own0, sib0 = backward(xt, gs, acts, coefs, wdt, 0, cut)
    own1, sib1 = backward(xt, gs, acts, coefs, wdt, cut, cols - cut, [own0])
    got0, got1 = swap(sib0, "core"), swap(sib1, "core")
    outputs = unpack(placer, mine, got, [own1, got0])
    held = finish([own0], [got0], (0,), cols, earlier=[outputs])
    grad_gate, grad_up = finish([own1], [got1], (cut,), cols, held)
    return outputs, grad_gate, grad_up


def reducing(designs, archetype, w_gate, w_up, w_down, cotangent):
    width = designs.shape[1]
    owners = lax.axis_size("expert")
    sharers = owners // EXPERTS
    hidden_cols = w_gate.shape[1]
    labels = archetype[:, 0]
    onehot = (labels[:, None] == jnp.arange(EXPERTS, dtype=jnp.int32)[None, :]).astype(jnp.int32)
    ranks = jnp.cumsum(onehot, axis=0) - onehot
    target = labels * CAP + jnp.sum(ranks * onehot, axis=1)
    placer = (jnp.arange(EXPERTS * CAP, dtype=jnp.int32)[:, None] == target[None, :]).astype(BF16)
    received = []
    for rows in (designs, cotangent):
        packed = jnp.dot(placer, rows, preferred_element_type=F32).astype(BF16)
        send = jnp.repeat(packed.reshape(EXPERTS, CAP, width), sharers, axis=0)
        received.append(
            lax.all_to_all(send, "expert", split_axis=0, concat_axis=0, tiled=True).reshape(
                owners * CAP, width
            )
        )
    flat_x, flat_g = received
    gate = jnp.dot(flat_x, w_gate, preferred_element_type=F32)
    up = jnp.dot(flat_x, w_up, preferred_element_type=F32)
    act, slope = silu_parts(gate)
    hidden = (act * up).astype(BF16)
    partial_value = (
        jnp.dot(hidden, w_down, preferred_element_type=F32).astype(BF16).reshape(owners, CAP, width)
    )
    returned = lax.all_to_all(partial_value, "expert", split_axis=0, concat_axis=0, tiled=True)
    summed = jnp.sum(returned.astype(F32).reshape(EXPERTS, sharers, CAP, width), axis=1).reshape(
        EXPERTS * CAP, width
    )
    outputs = jnp.take(summed, target, axis=0).astype(BF16)
    d_hidden = contract_cols(flat_g, w_down)
    d_gate = (d_hidden * up * slope).astype(BF16)
    d_up = (d_hidden * act).astype(BF16)
    grads = jnp.concatenate([contract_rows(flat_x, d_gate), contract_rows(flat_x, d_up)], axis=1)
    mine = lax.psum_scatter(grads.astype(BF16), "dp", scatter_dimension=0, tiled=True)
    return outputs, mine[:, :hidden_cols], mine[:, hidden_cols:]


def solution(mesh):
    dp, owners = mesh.devices.shape
    if (dp, owners) == (4, 2 * EXPERTS):
        rows, cols = ("far", "core"), ("arch", "half")
        mesh = Mesh(mesh.devices.reshape(2, 2, EXPERTS, 2), rows + cols)
        body = gathering
    else:
        rows, cols = ("dp",), ("expert",)
        body = reducing
    tokens = P(rows + cols, None)
    return jax.shard_map(
        body,
        mesh=mesh,
        in_specs=(tokens, tokens, P(None, cols), P(None, cols), P(cols, None), tokens),
        out_specs=(tokens, P(rows, cols), P(rows, cols)),
        check_vma=False,
    )
```

```python
import functools

import jax
import jax.numpy as jnp
from jax import lax
from jax.experimental import pallas as pl
from jax.experimental.pallas import tpu as pltpu
from jax.sharding import Mesh
from jax.sharding import PartitionSpec as P

EXPERTS = 4
CAP = 36
WIDE = 1024
STRIP = 512
SLICE = 256
MIB = 1024 * 1024
LARGE = pltpu.CompilerParams(vmem_limit_bytes=16 * MIB)
SMALL = pltpu.CompilerParams(vmem_limit_bytes=12 * MIB)
CHEAP = pl.CostEstimate(flops=0, bytes_accessed=0, transcendentals=0)
DEAR = pl.CostEstimate(flops=20_000_000_000, bytes_accessed=0, transcendentals=0)
F32 = jnp.float32
BF16 = jnp.bfloat16
HERE = pl.BlockSpec(memory_space=pltpu.VMEM)
AFAR = pl.BlockSpec(memory_space=pltpu.HBM)
ANYWHERE = pl.BlockSpec(memory_space=pl.ANY)


def silu_parts(gate):
    sigma = 0.5 * jnp.tanh(0.5 * gate) + 0.5
    return (gate * sigma, sigma * (1.0 + gate * (1.0 - sigma)))


def contract_rows(left, right):
    return lax.dot_general(left, right, (((0,), (0,)), ((), ())), preferred_element_type=F32)


def contract_cols(left, right):
    return lax.dot_general(left, right, (((1,), (1,)), ((), ())), preferred_element_type=F32)


def stacked(refs):
    return jnp.concatenate([r[...].astype(F32) for r in refs], axis=0)


def kept(value):
    return pltpu.with_memory_space_constraint(value, pltpu.HBM)


def pack_kernel(plane_ref, _, __, kind_ref, x_ref, g_ref, placer_ref, *refs):
    outs, (kind, x, g, sems) = refs[: 2 * EXPERTS], refs[2 * EXPERTS :]
    copies = [
        pltpu.make_async_copy(source, target, sems.at[i])
        for i, (source, target) in enumerate(((kind_ref, kind), (x_ref, x), (g_ref, g)))
    ]
    for copy in copies:
        copy.start()
    tokens = kind.shape[1]
    copies[0].wait()
    key = kind[...] ^ plane_ref[0]
    onehot = (key == lax.broadcasted_iota(jnp.int32, (8, tokens), 0)).astype(F32)
    before = lax.broadcasted_iota(jnp.int32, (tokens, tokens), 0) < lax.broadcasted_iota(
        jnp.int32, (tokens, tokens), 1
    )
    ranks = jnp.dot(onehot.astype(BF16), before.astype(BF16), preferred_element_type=F32)
    rank = jnp.sum(ranks * onehot, axis=0, keepdims=True).astype(jnp.int32)
    place = key * CAP + rank
    slots = EXPERTS * CAP
    placer = (place == lax.broadcasted_iota(jnp.int32, (slots, tokens), 0)).astype(F32).astype(BF16)
    placer_ref[...] = placer
    for copy, source, first in ((copies[1], x, 0), (copies[2], g, EXPERTS)):
        copy.wait()
        packed = jnp.dot(placer, source[...], preferred_element_type=F32)
        for k in range(EXPERTS):
            outs[first + k][...] = packed[k * CAP : (k + 1) * CAP].astype(BF16)


def pack(scalars, kind, x, g):
    tokens, width = x.shape
    return pl.pallas_call(
        pack_kernel,
        out_shape=[jax.ShapeDtypeStruct((EXPERTS * CAP, tokens), BF16)]
        + [jax.ShapeDtypeStruct((CAP, width), BF16)] * (2 * EXPERTS),
        in_specs=[pl.BlockSpec(memory_space=pltpu.SMEM)] * 3 + [AFAR] * 3,
        scratch_shapes=[
            pltpu.VMEM((1, tokens), jnp.int32),
            pltpu.VMEM((tokens, width), BF16),
            pltpu.VMEM((tokens, width), BF16),
            pltpu.SemaphoreType.DMA((3,)),
        ],
        compiler_params=SMALL,
        cost_estimate=CHEAP,
        name="pack",
    )(*scalars, kept(kind), kept(x), kept(g))


def join_kernel(*refs):
    refs[-1][...] = stacked(refs[-2 : -2 - EXPERTS : -1]).astype(BF16)


def join(blocks, earlier=()):
    width = blocks[0].shape[1]
    return pl.pallas_call(
        join_kernel,
        out_shape=jax.ShapeDtypeStruct((EXPERTS * CAP, width), BF16),
        in_specs=[ANYWHERE] * len(earlier) + [HERE] * EXPERTS,
        compiler_params=SMALL,
        cost_estimate=CHEAP,
        name="join",
    )(*earlier, *blocks[::-1])


def relay_kernel(n, *refs):
    for i in range(n):
        refs[len(refs) - n + i][...] = refs[i][...]


def relay(values, earlier):
    n = len(values)
    return pl.pallas_call(
        functools.partial(relay_kernel, n),
        out_shape=[jax.ShapeDtypeStruct(v.shape, v.dtype) for v in values],
        in_specs=[HERE] * n + [ANYWHERE] * len(earlier),
        compiler_params=SMALL,
        cost_estimate=CHEAP,
        name="relay",
    )(*values, *earlier)


def mark_kernel(value_ref, _, mark_ref):
    mark_ref[...] = value_ref[: mark_ref.shape[0], : mark_ref.shape[1]]


def mark(value, earlier):
    return pl.pallas_call(
        mark_kernel,
        out_shape=jax.ShapeDtypeStruct((16, 128), value.dtype),
        in_specs=[HERE, ANYWHERE],
        compiler_params=SMALL,
        cost_estimate=CHEAP,
        name="mark",
    )(value, earlier)


def flip_kernel(source_ref, here_ref, flipped_ref, sems):
    steps = source_ref.shape[0] // SLICE
    copies = []
    for j in range(steps):
        rows = pl.ds(j * SLICE, SLICE)
        copies.append(pltpu.make_async_copy(source_ref.at[rows], here_ref.at[rows], sems.at[j]))
        copies[j].start()
    for j in range(steps):
        copies[j].wait()
        rows = slice(j * SLICE, (j + 1) * SLICE)
        flipped_ref[:, rows] = here_ref[rows, :].T


def flip(value):
    return pl.pallas_call(
        flip_kernel,
        out_shape=[pltpu.VMEM(value.shape, value.dtype), pltpu.VMEM(value.shape[::-1], value.dtype)],
        in_specs=[AFAR],
        out_specs=[HERE, HERE],
        scratch_shapes=[pltpu.SemaphoreType.DMA((value.shape[0] // SLICE,))],
        compiler_params=SMALL,
        cost_estimate=CHEAP,
        name="flip",
    )(kept(value))


def forward_kernel(n, fetch, down, pair, unused, *refs):
    refs = list(refs[unused:])
    xs = [refs.pop(0) for _ in range(n)]
    wg_ref, wu_ref = refs.pop(0), refs.pop(0)
    wd_ref = refs.pop(0) if down else None
    other_ref = refs.pop(0) if pair else None
    act_ref, coef_ref = refs.pop(0), refs.pop(0)
    shares = [refs.pop(0) for _ in range(EXPERTS if pair else down)]
    if fetch:
        sources, sems = (wg_ref, wu_ref), refs.pop()
        wg_ref, wu_ref = refs.pop(0), refs.pop(0)
    acc_ref = refs.pop(0) if down else None
    part = xs[0].shape[0]
    x_ref = xs[0]
    if n > 1:
        x_ref = refs.pop(0)
        for i in range(n):
            x_ref[i * part : (i + 1) * part, :] = xs[i][...]
    steps = wg_ref.shape[1] // (2 * WIDE)

    def copies(j):
        cols = pl.ds(pl.multiple_of(j * (2 * WIDE), (2 * WIDE)), (2 * WIDE))
        return [
            pltpu.make_async_copy(source.at[:, cols], target.at[:, cols], sems.at[j, i])
            for i, (source, target) in enumerate(zip(sources, (wg_ref, wu_ref)))
        ]

    if fetch:
        for j in range(steps):
            for copy in copies(j):
                copy.start()
    if down:
        acc_ref[...] = jnp.zeros_like(acc_ref)

    @pl.loop(0, steps)
    def _(j):
        if fetch:
            for copy in copies(j):
                copy.wait()
        for i in range(2):
            cols = pl.ds(pl.multiple_of(j * (2 * WIDE) + i * WIDE, WIDE), WIDE)
            gate = jnp.dot(x_ref[...], wg_ref[:, cols], preferred_element_type=F32)
            up = jnp.dot(x_ref[...], wu_ref[:, cols], preferred_element_type=F32)
            act, slope = silu_parts(gate)
            act_ref[:, cols] = act.astype(BF16)
            coef_ref[:, cols] = (up * slope).astype(BF16)
            if down:
                hidden = (act[:part] * up[:part]).astype(BF16)
                acc_ref[...] += jnp.dot(hidden, wd_ref[cols, :], preferred_element_type=F32)

    if pair:
        other = other_ref[...].astype(F32)
        for k in range(EXPERTS):
            rows = slice(k * CAP, (k + 1) * CAP)
            block = jnp.concatenate([other[rows], acc_ref[rows, :]], axis=0).astype(BF16)
            shares[k][...] = block
    elif down:
        shares[0][...] = acc_ref[...].astype(BF16)


def forward(xs, wg, wu, wd=None, other=None, fetch=False, earlier=(), cost=CHEAP):
    n, (part, width), cols = len(xs), xs[0].shape, wg.shape[1]
    rows = n * part
    down, pair = wd is not None, other is not None
    shares = [jax.ShapeDtypeStruct((part, width), BF16)] * down
    if pair:
        shares = [jax.ShapeDtypeStruct((2 * CAP, width), BF16)] * EXPERTS
    weights = [kept(wg), kept(wu)] if fetch else [wg, wu]
    return pl.pallas_call(
        functools.partial(forward_kernel, n, fetch, down, pair, len(earlier)),
        out_shape=[jax.ShapeDtypeStruct((rows, cols), BF16)] * 2
        + shares
        + [pltpu.VMEM(wg.shape, wg.dtype)] * (2 * fetch),
        in_specs=[ANYWHERE] * len(earlier)
        + [HERE] * n
        + [AFAR if fetch else HERE] * 2
        + [HERE] * (down + pair),
        scratch_shapes=[pltpu.VMEM((part, width), F32)] * down
        + [pltpu.VMEM((rows, width), BF16)] * (n > 1)
        + [pltpu.SemaphoreType.DMA((cols // (2 * WIDE), 2))] * fetch,
        compiler_params=LARGE,
        cost_estimate=cost,
        name="forward" + "_fetch" * fetch + "_down" * down,
    )(*earlier, *xs, *weights, *([wd] * down), *([other] * pair))


def turn_kernel(_, __, *refs):
    refs[8][: refs[0].shape[1], :] = stacked(refs[0:4]).T.astype(BF16)
    refs[8][refs[0].shape[1] :, :] = stacked(refs[4:8]).T.astype(BF16)


def turn(own, sib, xs, share):
    part = xs[0].shape[0]
    rows = len(xs) * part
    return pl.pallas_call(
        turn_kernel,
        grid_spec=pltpu.PrefetchScalarGridSpec(
            num_scalar_prefetch=2,
            grid=(1,),
            in_specs=[pl.BlockSpec((part, share), lambda j, a, b: (0, a[0]))] * 4
            + [pl.BlockSpec((part, share), lambda j, a, b: (0, b[0]))] * 4,
            out_specs=pl.BlockSpec((2 * share, rows), lambda j, a, b: (0, 0)),
        ),
        out_shape=jax.ShapeDtypeStruct((2 * share, rows), BF16),
        compiler_params=SMALL,
        cost_estimate=CHEAP,
        name="turn",
    )(own, sib, *xs, *xs)


def slopes_kernel(n, *refs):
    gs, acts, coefs = refs[:n], refs[n : 2 * n], refs[2 * n : 3 * n]
    wdt_ref, dg_ref, du_ref, g_ref = refs[3 * n :]
    part = gs[0].shape[0]
    for i in range(n):
        g_ref[i * part : (i + 1) * part, :] = gs[i][...]
    for start in range(0, wdt_ref.shape[1], STRIP):
        cols = slice(start, start + STRIP)
        d_hidden = jnp.dot(g_ref[...], wdt_ref[:, cols], preferred_element_type=F32)
        for i in range(n):
            rows = slice(i * part, (i + 1) * part)
            dg_ref[rows, cols] = (d_hidden[rows] * coefs[i][:, cols].astype(F32)).astype(BF16)
            du_ref[rows, cols] = (d_hidden[rows] * acts[i][:, cols].astype(F32)).astype(BF16)


def slopes(gs, acts, coefs, wdt):
    n, (part, width) = len(gs), gs[0].shape
    return pl.pallas_call(
        functools.partial(slopes_kernel, n),
        out_shape=[jax.ShapeDtypeStruct((n * part, wdt.shape[1]), BF16)] * 2,
        in_specs=[HERE] * (3 * n + 1),
        scratch_shapes=[pltpu.VMEM((n * part, width), BF16)],
        compiler_params=LARGE,
        cost_estimate=CHEAP,
        name="slopes",
    )(*gs, *acts, *coefs, wdt)


def backward_kernel(first, xt_ref, g_ref, act_ref, coef_ref, dg_ref, du_ref, wdt_ref, *refs):
    own_ref, sib_ref = refs[-2:]
    share = own_ref.shape[0] // 2
    for start in range(0, own_ref.shape[1], STRIP):
        here = slice(start, start + STRIP)
        cols = slice(first + start, first + start + STRIP)
        d_hidden = jnp.dot(g_ref[...], wdt_ref[:, cols], preferred_element_type=F32)
        for row, factor_ref, known_ref in ((0, coef_ref, dg_ref), (share, act_ref, du_ref)):
            d_cols = (d_hidden * factor_ref[:, cols].astype(F32)).astype(BF16)
            d_cols = jnp.concatenate([known_ref[:, cols], d_cols], axis=0)
            total = jnp.dot(xt_ref[...], d_cols, preferred_element_type=F32).astype(BF16)
            own_ref[row : row + share, here] = total[:share]
            sib_ref[row : row + share, here] = total[share:]


def backward(xt, g, act, coef, dg, du, wdt, first, cols, earlier=()):
    return pl.pallas_call(
        functools.partial(backward_kernel, first),
        out_shape=[jax.ShapeDtypeStruct((xt.shape[0], cols), BF16)] * 2,
        in_specs=[HERE] * 7 + [ANYWHERE] * len(earlier),
        compiler_params=LARGE,
        cost_estimate=DEAR,
        name="backward",
    )(xt, g, act, coef, dg, du, wdt, *earlier)


def finish_kernel(spans, more, unused, *refs):
    refs = refs[unused:]
    n = len(spans)
    pairs = [refs[2 * i : 2 * i + 2] for i in range(n)]
    gate_ref, up_ref, gate, up, sems = refs[2 * n + 2 * more :]
    share = gate_ref.shape[0]
    low = spans[0][0]
    copies = []
    for i, ((first, cols), (own, got)) in enumerate(zip(spans, pairs)):
        for j, (target, held) in enumerate(((gate_ref, gate), (up_ref, up))):
            rows = slice(j * share, (j + 1) * share)
            here = pl.ds(first - low, cols)
            held[:, here] = (own[rows, :].astype(F32) + got[rows, :].astype(F32)).astype(BF16)
            copies.append(
                pltpu.make_async_copy(held.at[:, here], target.at[:, pl.ds(first, cols)], sems.at[i, j])
            )
            copies[-1].start()
    for copy in copies:
        copy.wait()


def finish(owns, gots, firsts, width, held=(), earlier=()):
    share = owns[0].shape[0] // 2
    spans = tuple((first, own.shape[1]) for first, own in zip(firsts, owns))
    total = sum(cols for _, cols in spans)
    n, more = len(owns), len(held) > 0
    return pl.pallas_call(
        functools.partial(finish_kernel, spans, more, len(earlier)),
        out_shape=[jax.ShapeDtypeStruct((share, width), BF16)] * 2,
        in_specs=[AFAR] * len(earlier) + [HERE] * (2 * n) + [ANYWHERE] * (2 * more),
        out_specs=[ANYWHERE] * 2,
        scratch_shapes=[pltpu.VMEM((share, total), BF16)] * 2 + [pltpu.SemaphoreType.DMA((n, 2))],
        input_output_aliases={len(earlier) + 2 * n: 0, len(earlier) + 2 * n + 1: 1} if more else {},
        compiler_params=SMALL,
        cost_estimate=CHEAP,
        name="finish",
    )(*[kept(v) for v in earlier], *[v for both in zip(owns, gots) for v in both], *held)


def split_kernel(*refs):
    blocks = [r[...].astype(F32) for r in refs[:EXPERTS]]
    refs[-2][...] = jnp.concatenate([b[:CAP] for b in blocks], axis=0).astype(BF16)
    refs[-1][...] = jnp.concatenate([b[CAP:] for b in blocks], axis=0).astype(BF16)


def split(blocks, earlier):
    width = blocks[0].shape[1]
    return pl.pallas_call(
        split_kernel,
        out_shape=[jax.ShapeDtypeStruct((EXPERTS * CAP, width), BF16)] * 2,
        in_specs=[HERE] * EXPERTS + [ANYWHERE] * len(earlier),
        compiler_params=SMALL,
        cost_estimate=CHEAP,
        name="split",
    )(*blocks, *earlier)


def unpack_kernel(placer_ref, mine_ref, got_ref, *refs):
    chosen = placer_ref[...].astype(F32).T.astype(BF16)
    total = jnp.dot(chosen, mine_ref[...], preferred_element_type=F32)
    total += jnp.dot(chosen, got_ref[...], preferred_element_type=F32)
    refs[-1][...] = total.astype(BF16)


def unpack(placer, mine, got, earlier):
    return pl.pallas_call(
        unpack_kernel,
        out_shape=jax.ShapeDtypeStruct((placer.shape[1], mine.shape[1]), BF16),
        in_specs=[HERE] * 3 + [ANYWHERE] * len(earlier),
        compiler_params=SMALL,
        cost_estimate=DEAR,
        name="unpack",
    )(placer, mine, got, *earlier)


def swap(value, axis):
    return lax.ppermute(value, axis, [(0, 1), (1, 0)])


def across_planes(blocks):
    return [blocks[0]] + [
        lax.ppermute(blocks[k], "arch", [(i, i ^ k) for i in range(EXPERTS)]) for k in range(1, EXPERTS)
    ]


def after(values, earlier):
    n = len(values)
    return list(lax.optimization_barrier((*values, *earlier))[:n])


def gathering(designs, archetype, w_gate, w_up, w_down, cotangent):
    far, core = lax.axis_index("far"), lax.axis_index("core")
    scalars = [lax.axis_index("arch"), 2 * far + core, 2 * far + 1 - core]
    scalars = [v.astype(jnp.int32)[None] for v in scalars]
    tokens, width = designs.shape
    share = width // 4
    placer, *blocks = pack(scalars, archetype.reshape(1, tokens), designs, cotangent)
    wd, wdt = flip(after([w_down], [placer])[0])

    x_own = join(across_planes(blocks[:EXPERTS]))
    moved = across_planes(relay(blocks[EXPERTS:], [wdt]))
    x_far, x_near = swap(x_own, "far"), swap(x_own, "half")

    wg, wu = w_gate, w_up
    act0, coef0, share_own = forward([x_own], wg, wu, wd)
    g_own = join(moved, [act0])
    g_far, g_near = swap(g_own, "far"), swap(g_own, "half")
    act1, coef1, *shares = forward([x_near], wg, wu, wd, other=share_own)
    (x_pass,) = relay([x_near], [mark(act1, x_far), g_far])
    (g_pass,) = relay([g_far], [x_pass, g_near])
    x_corner, g_corner = swap(x_pass, "far"), swap(g_pass, "half")
    returned = across_planes(shares)
    act2, coef2 = forward([x_far], wg, wu, earlier=[g_pass], cost=DEAR)
    dg, du = slopes([g_own, g_near, g_far], [act0, act1, act2], [coef0, coef1, coef2], wdt)
    mine, theirs = split(returned, [dg])
    got = swap(theirs, "half")
    act3, coef3 = forward([x_corner], wg, wu, earlier=[mine])
    xt = turn(*scalars[1:], [x_own, x_near, x_far, x_corner], share)

    rest = (xt, g_corner, act3, coef3, dg, du, wdt)
    cols = w_down.shape[0]
    cut = cols // 2
    own0, sib0 = backward(*rest, 0, cut)
    own1, sib1 = backward(*rest, cut, cols - cut, [own0])
    got0, got1 = swap(sib0, "core"), swap(sib1, "core")
    outputs = unpack(placer, mine, got, [own1, got0])
    held = finish([own0], [got0], (0,), cols, earlier=[outputs])
    grad_gate, grad_up = finish([own1], [got1], (cut,), cols, held)
    return outputs, grad_gate, grad_up


def reducing(designs, archetype, w_gate, w_up, w_down, cotangent):
    width = designs.shape[1]
    owners = lax.axis_size("expert")
    sharers = owners // EXPERTS
    hidden_cols = w_gate.shape[1]
    labels = archetype[:, 0]
    onehot = (labels[:, None] == jnp.arange(EXPERTS, dtype=jnp.int32)[None, :]).astype(jnp.int32)
    ranks = jnp.cumsum(onehot, axis=0) - onehot
    target = labels * CAP + jnp.sum(ranks * onehot, axis=1)
    placer = (jnp.arange(EXPERTS * CAP, dtype=jnp.int32)[:, None] == target[None, :]).astype(BF16)
    received = []
    for rows in (designs, cotangent):
        packed = jnp.dot(placer, rows, preferred_element_type=F32).astype(BF16)
        send = jnp.repeat(packed.reshape(EXPERTS, CAP, width), sharers, axis=0)
        received.append(
            lax.all_to_all(send, "expert", split_axis=0, concat_axis=0, tiled=True).reshape(
                owners * CAP, width
            )
        )
    flat_x, flat_g = received
    gate = jnp.dot(flat_x, w_gate, preferred_element_type=F32)
    up = jnp.dot(flat_x, w_up, preferred_element_type=F32)
    act, slope = silu_parts(gate)
    hidden = (act * up).astype(BF16)
    partial_value = (
        jnp.dot(hidden, w_down, preferred_element_type=F32).astype(BF16).reshape(owners, CAP, width)
    )
    returned = lax.all_to_all(partial_value, "expert", split_axis=0, concat_axis=0, tiled=True)
    summed = jnp.sum(returned.astype(F32).reshape(EXPERTS, sharers, CAP, width), axis=1).reshape(
        EXPERTS * CAP, width
    )
    outputs = jnp.take(summed, target, axis=0).astype(BF16)
    d_hidden = contract_cols(flat_g, w_down)
    d_gate = (d_hidden * up * slope).astype(BF16)
    d_up = (d_hidden * act).astype(BF16)
    grads = jnp.concatenate([contract_rows(flat_x, d_gate), contract_rows(flat_x, d_up)], axis=1)
    mine = lax.psum_scatter(grads.astype(BF16), "dp", scatter_dimension=0, tiled=True)
    return outputs, mine[:, :hidden_cols], mine[:, hidden_cols:]


def solution(mesh):
    dp, owners = mesh.devices.shape
    if (dp, owners) == (4, 2 * EXPERTS):
        rows, cols = ("far", "core"), ("arch", "half")
        mesh = Mesh(mesh.devices.reshape(2, 2, EXPERTS, 2), rows + cols)
        body = gathering
    else:
        rows, cols = ("dp",), ("expert",)
        body = reducing
    tokens = P(rows + cols, None)
    return jax.shard_map(
        body,
        mesh=mesh,
        in_specs=(tokens, tokens, P(None, cols), P(None, cols), P(cols, None), tokens),
        out_specs=(tokens, P(rows, cols), P(rows, cols)),
        check_vma=False,
    )
```

```python
import functools

import jax
import jax.numpy as jnp
from jax import lax
from jax.experimental import pallas as pl
from jax.experimental.pallas import tpu as pltpu
from jax.sharding import Mesh
from jax.sharding import PartitionSpec as P

EXPERTS = 4
CAP = 36
WIDE = 1024
STRIP = 512
SLICE = 256
MIB = 1024 * 1024
LARGE = pltpu.CompilerParams(vmem_limit_bytes=16 * MIB)
SMALL = pltpu.CompilerParams(vmem_limit_bytes=12 * MIB)
CHEAP = pl.CostEstimate(flops=0, bytes_accessed=0, transcendentals=0)
DEAR = pl.CostEstimate(flops=20_000_000_000, bytes_accessed=0, transcendentals=0)
F32 = jnp.float32
BF16 = jnp.bfloat16
HERE = pl.BlockSpec(memory_space=pltpu.VMEM)
AFAR = pl.BlockSpec(memory_space=pltpu.HBM)
ANYWHERE = pl.BlockSpec(memory_space=pl.ANY)


def silu_parts(gate):
    sigma = 0.5 * jnp.tanh(0.5 * gate) + 0.5
    return (gate * sigma, sigma * (1.0 + gate * (1.0 - sigma)))


def contract_rows(left, right):
    return lax.dot_general(left, right, (((0,), (0,)), ((), ())), preferred_element_type=F32)


def contract_cols(left, right):
    return lax.dot_general(left, right, (((1,), (1,)), ((), ())), preferred_element_type=F32)


def stacked(refs):
    return jnp.concatenate([r[...].astype(F32) for r in refs], axis=0)


def kept(value):
    return pltpu.with_memory_space_constraint(value, pltpu.HBM)


def pack_kernel(plane_ref, _, __, kind_ref, x_ref, g_ref, placer_ref, *refs):
    outs, (kind, x, g, sems) = refs[: 2 * EXPERTS], refs[2 * EXPERTS :]
    copies = [
        pltpu.make_async_copy(source, target, sems.at[i])
        for i, (source, target) in enumerate(((kind_ref, kind), (x_ref, x), (g_ref, g)))
    ]
    for copy in copies:
        copy.start()
    tokens = kind.shape[1]
    copies[0].wait()
    key = kind[...] ^ plane_ref[0]
    onehot = (key == lax.broadcasted_iota(jnp.int32, (8, tokens), 0)).astype(F32)
    before = lax.broadcasted_iota(jnp.int32, (tokens, tokens), 0) < lax.broadcasted_iota(
        jnp.int32, (tokens, tokens), 1
    )
    ranks = jnp.dot(onehot.astype(BF16), before.astype(BF16), preferred_element_type=F32)
    rank = jnp.sum(ranks * onehot, axis=0, keepdims=True).astype(jnp.int32)
    place = key * CAP + rank
    slots = EXPERTS * CAP
    placer = (place == lax.broadcasted_iota(jnp.int32, (slots, tokens), 0)).astype(F32).astype(BF16)
    placer_ref[...] = placer
    for copy, source, first in ((copies[1], x, 0), (copies[2], g, EXPERTS)):
        copy.wait()
        packed = jnp.dot(placer, source[...], preferred_element_type=F32)
        for k in range(EXPERTS):
            outs[first + k][...] = packed[k * CAP : (k + 1) * CAP].astype(BF16)


def pack(scalars, kind, x, g):
    tokens, width = x.shape
    return pl.pallas_call(
        pack_kernel,
        out_shape=[jax.ShapeDtypeStruct((EXPERTS * CAP, tokens), BF16)]
        + [jax.ShapeDtypeStruct((CAP, width), BF16)] * (2 * EXPERTS),
        in_specs=[pl.BlockSpec(memory_space=pltpu.SMEM)] * 3 + [AFAR] * 3,
        scratch_shapes=[
            pltpu.VMEM((1, tokens), jnp.int32),
            pltpu.VMEM((tokens, width), BF16),
            pltpu.VMEM((tokens, width), BF16),
            pltpu.SemaphoreType.DMA((3,)),
        ],
        compiler_params=SMALL,
        cost_estimate=CHEAP,
        name="pack",
    )(*scalars, kept(kind), kept(x), kept(g))


def join_kernel(*refs):
    refs[-1][...] = stacked(refs[-2 : -2 - EXPERTS : -1]).astype(BF16)


def join(blocks, earlier=()):
    width = blocks[0].shape[1]
    return pl.pallas_call(
        join_kernel,
        out_shape=jax.ShapeDtypeStruct((EXPERTS * CAP, width), BF16),
        in_specs=[ANYWHERE] * len(earlier) + [HERE] * EXPERTS,
        compiler_params=SMALL,
        cost_estimate=CHEAP,
        name="join",
    )(*earlier, *blocks[::-1])


def relay_kernel(n, *refs):
    for i in range(n):
        refs[len(refs) - n + i][...] = refs[i][...]


def relay(values, earlier):
    n = len(values)
    return pl.pallas_call(
        functools.partial(relay_kernel, n),
        out_shape=[jax.ShapeDtypeStruct(v.shape, v.dtype) for v in values],
        in_specs=[HERE] * n + [ANYWHERE] * len(earlier),
        compiler_params=SMALL,
        cost_estimate=CHEAP,
        name="relay",
    )(*values, *earlier)


def mark_kernel(value_ref, _, mark_ref):
    mark_ref[...] = value_ref[: mark_ref.shape[0], : mark_ref.shape[1]]


def mark(value, earlier):
    return pl.pallas_call(
        mark_kernel,
        out_shape=jax.ShapeDtypeStruct((16, 128), value.dtype),
        in_specs=[HERE, ANYWHERE],
        compiler_params=SMALL,
        cost_estimate=CHEAP,
        name="mark",
    )(value, earlier)


def flip_kernel(source_ref, here_ref, flipped_ref, sems):
    steps = source_ref.shape[0] // SLICE
    copies = []
    for j in range(steps):
        rows = pl.ds(j * SLICE, SLICE)
        copies.append(pltpu.make_async_copy(source_ref.at[rows], here_ref.at[rows], sems.at[j]))
        copies[j].start()
    for j in range(steps):
        copies[j].wait()
        rows = slice(j * SLICE, (j + 1) * SLICE)
        flipped_ref[:, rows] = here_ref[rows, :].T


def flip(value):
    return pl.pallas_call(
        flip_kernel,
        out_shape=[pltpu.VMEM(value.shape, value.dtype), pltpu.VMEM(value.shape[::-1], value.dtype)],
        in_specs=[AFAR],
        out_specs=[HERE, HERE],
        scratch_shapes=[pltpu.SemaphoreType.DMA((value.shape[0] // SLICE,))],
        compiler_params=SMALL,
        cost_estimate=CHEAP,
        name="flip",
    )(kept(value))


def forward_kernel(n, fetch, down, pair, unused, *refs):
    refs = list(refs[unused:])
    xs = [refs.pop(0) for _ in range(n)]
    wg_ref, wu_ref = refs.pop(0), refs.pop(0)
    wd_ref = refs.pop(0) if down else None
    other_ref = refs.pop(0) if pair else None
    act_ref, coef_ref = refs.pop(0), refs.pop(0)
    shares = [refs.pop(0) for _ in range(EXPERTS if pair else down)]
    if fetch:
        sources, sems = (wg_ref, wu_ref), refs.pop()
        wg_ref, wu_ref = refs.pop(0), refs.pop(0)
    acc_ref = refs.pop(0) if down else None
    part = xs[0].shape[0]
    x_ref = xs[0]
    if n > 1:
        x_ref = refs.pop(0)
        for i in range(n):
            x_ref[i * part : (i + 1) * part, :] = xs[i][...]
    steps = wg_ref.shape[1] // (2 * WIDE)

    def copies(j):
        cols = pl.ds(pl.multiple_of(j * (2 * WIDE), (2 * WIDE)), (2 * WIDE))
        return [
            pltpu.make_async_copy(source.at[:, cols], target.at[:, cols], sems.at[j, i])
            for i, (source, target) in enumerate(zip(sources, (wg_ref, wu_ref)))
        ]

    if fetch:
        for j in range(steps):
            for copy in copies(j):
                copy.start()
    if down:
        acc_ref[...] = jnp.zeros_like(acc_ref)

    @pl.loop(0, steps)
    def _(j):
        if fetch:
            for copy in copies(j):
                copy.wait()
        for i in range(2):
            cols = pl.ds(pl.multiple_of(j * (2 * WIDE) + i * WIDE, WIDE), WIDE)
            gate = jnp.dot(x_ref[...], wg_ref[:, cols], preferred_element_type=F32)
            up = jnp.dot(x_ref[...], wu_ref[:, cols], preferred_element_type=F32)
            act, slope = silu_parts(gate)
            act_ref[:, cols] = act.astype(BF16)
            coef_ref[:, cols] = (up * slope).astype(BF16)
            if down:
                hidden = (act[:part] * up[:part]).astype(BF16)
                acc_ref[...] += jnp.dot(hidden, wd_ref[cols, :], preferred_element_type=F32)

    if pair:
        other = other_ref[...].astype(F32)
        for k in range(EXPERTS):
            rows = slice(k * CAP, (k + 1) * CAP)
            block = jnp.concatenate([other[rows], acc_ref[rows, :]], axis=0).astype(BF16)
            shares[k][...] = block
    elif down:
        shares[0][...] = acc_ref[...].astype(BF16)


def forward(xs, wg, wu, wd=None, other=None, fetch=False, earlier=(), cost=CHEAP):
    n, (part, width), cols = len(xs), xs[0].shape, wg.shape[1]
    rows = n * part
    down, pair = wd is not None, other is not None
    shares = [jax.ShapeDtypeStruct((part, width), BF16)] * down
    if pair:
        shares = [jax.ShapeDtypeStruct((2 * CAP, width), BF16)] * EXPERTS
    weights = [kept(wg), kept(wu)] if fetch else [wg, wu]
    return pl.pallas_call(
        functools.partial(forward_kernel, n, fetch, down, pair, len(earlier)),
        out_shape=[jax.ShapeDtypeStruct((rows, cols), BF16)] * 2
        + shares
        + [pltpu.VMEM(wg.shape, wg.dtype)] * (2 * fetch),
        in_specs=[ANYWHERE] * len(earlier)
        + [HERE] * n
        + [AFAR if fetch else HERE] * 2
        + [HERE] * (down + pair),
        scratch_shapes=[pltpu.VMEM((part, width), F32)] * down
        + [pltpu.VMEM((rows, width), BF16)] * (n > 1)
        + [pltpu.SemaphoreType.DMA((cols // (2 * WIDE), 2))] * fetch,
        compiler_params=LARGE,
        cost_estimate=cost,
        name="forward" + "_fetch" * fetch + "_down" * down,
    )(*earlier, *xs, *weights, *([wd] * down), *([other] * pair))


def turn_kernel(_, __, *refs):
    refs[8][: refs[0].shape[1], :] = stacked(refs[0:4]).T.astype(BF16)
    refs[8][refs[0].shape[1] :, :] = stacked(refs[4:8]).T.astype(BF16)


def turn(own, sib, xs, share):
    part = xs[0].shape[0]
    rows = len(xs) * part
    return pl.pallas_call(
        turn_kernel,
        grid_spec=pltpu.PrefetchScalarGridSpec(
            num_scalar_prefetch=2,
            grid=(1,),
            in_specs=[pl.BlockSpec((part, share), lambda j, a, b: (0, a[0]))] * 4
            + [pl.BlockSpec((part, share), lambda j, a, b: (0, b[0]))] * 4,
            out_specs=pl.BlockSpec((2 * share, rows), lambda j, a, b: (0, 0)),
        ),
        out_shape=jax.ShapeDtypeStruct((2 * share, rows), BF16),
        compiler_params=SMALL,
        cost_estimate=CHEAP,
        name="turn",
    )(own, sib, *xs, *xs)


def slopes_kernel(n, *refs):
    gs, acts, coefs = refs[:n], refs[n : 2 * n], refs[2 * n : 3 * n]
    wdt_ref, dg_ref, du_ref, g_ref = refs[3 * n :]
    part = gs[0].shape[0]
    for i in range(n):
        g_ref[i * part : (i + 1) * part, :] = gs[i][...]
    for start in range(0, wdt_ref.shape[1], STRIP):
        cols = slice(start, start + STRIP)
        d_hidden = jnp.dot(g_ref[...], wdt_ref[:, cols], preferred_element_type=F32)
        for i in range(n):
            rows = slice(i * part, (i + 1) * part)
            dg_ref[rows, cols] = (d_hidden[rows] * coefs[i][:, cols].astype(F32)).astype(BF16)
            du_ref[rows, cols] = (d_hidden[rows] * acts[i][:, cols].astype(F32)).astype(BF16)


def slopes(gs, acts, coefs, wdt):
    n, (part, width) = len(gs), gs[0].shape
    return pl.pallas_call(
        functools.partial(slopes_kernel, n),
        out_shape=[jax.ShapeDtypeStruct((n * part, wdt.shape[1]), BF16)] * 2,
        in_specs=[HERE] * (3 * n + 1),
        scratch_shapes=[pltpu.VMEM((n * part, width), BF16)],
        compiler_params=LARGE,
        cost_estimate=CHEAP,
        name="slopes",
    )(*gs, *acts, *coefs, wdt)


def backward_kernel(first, xt_ref, g_ref, act_ref, coef_ref, dg_ref, du_ref, wdt_ref, *refs):
    own_ref, sib_ref = refs[-2:]
    share = own_ref.shape[0] // 2
    for start in range(0, own_ref.shape[1], STRIP):
        here = slice(start, start + STRIP)
        cols = slice(first + start, first + start + STRIP)
        d_hidden = jnp.dot(g_ref[...], wdt_ref[:, cols], preferred_element_type=F32)
        for row, factor_ref, known_ref in ((0, coef_ref, dg_ref), (share, act_ref, du_ref)):
            d_cols = (d_hidden * factor_ref[:, cols].astype(F32)).astype(BF16)
            d_cols = jnp.concatenate([known_ref[:, cols], d_cols], axis=0)
            total = jnp.dot(xt_ref[...], d_cols, preferred_element_type=F32).astype(BF16)
            own_ref[row : row + share, here] = total[:share]
            sib_ref[row : row + share, here] = total[share:]


def backward(xt, g, act, coef, dg, du, wdt, first, cols, earlier=()):
    return pl.pallas_call(
        functools.partial(backward_kernel, first),
        out_shape=[jax.ShapeDtypeStruct((xt.shape[0], cols), BF16)] * 2,
        in_specs=[HERE] * 7 + [ANYWHERE] * len(earlier),
        compiler_params=LARGE,
        cost_estimate=DEAR,
        name="backward",
    )(xt, g, act, coef, dg, du, wdt, *earlier)


def finish_kernel(spans, more, unused, *refs):
    refs = refs[unused:]
    n = len(spans)
    pairs = [refs[2 * i : 2 * i + 2] for i in range(n)]
    gate_ref, up_ref, gate, up, sems = refs[2 * n + 2 * more :]
    share = gate_ref.shape[0]
    low = spans[0][0]
    copies = []
    for i, ((first, cols), (own, got)) in enumerate(zip(spans, pairs)):
        for j, (target, held) in enumerate(((gate_ref, gate), (up_ref, up))):
            rows = slice(j * share, (j + 1) * share)
            here = pl.ds(first - low, cols)
            held[:, here] = (own[rows, :].astype(F32) + got[rows, :].astype(F32)).astype(BF16)
            copies.append(
                pltpu.make_async_copy(held.at[:, here], target.at[:, pl.ds(first, cols)], sems.at[i, j])
            )
            copies[-1].start()
    for copy in copies:
        copy.wait()


def finish(owns, gots, firsts, width, held=(), earlier=()):
    share = owns[0].shape[0] // 2
    spans = tuple((first, own.shape[1]) for first, own in zip(firsts, owns))
    total = sum(cols for _, cols in spans)
    n, more = len(owns), len(held) > 0
    return pl.pallas_call(
        functools.partial(finish_kernel, spans, more, len(earlier)),
        out_shape=[jax.ShapeDtypeStruct((share, width), BF16)] * 2,
        in_specs=[AFAR] * len(earlier) + [HERE] * (2 * n) + [ANYWHERE] * (2 * more),
        out_specs=[ANYWHERE] * 2,
        scratch_shapes=[pltpu.VMEM((share, total), BF16)] * 2 + [pltpu.SemaphoreType.DMA((n, 2))],
        input_output_aliases={len(earlier) + 2 * n: 0, len(earlier) + 2 * n + 1: 1} if more else {},
        compiler_params=SMALL,
        cost_estimate=CHEAP,
        name="finish",
    )(*[kept(v) for v in earlier], *[v for both in zip(owns, gots) for v in both], *held)


def split_kernel(*refs):
    blocks = [r[...].astype(F32) for r in refs[:EXPERTS]]
    refs[-2][...] = jnp.concatenate([b[:CAP] for b in blocks], axis=0).astype(BF16)
    refs[-1][...] = jnp.concatenate([b[CAP:] for b in blocks], axis=0).astype(BF16)


def split(blocks, earlier):
    width = blocks[0].shape[1]
    return pl.pallas_call(
        split_kernel,
        out_shape=[jax.ShapeDtypeStruct((EXPERTS * CAP, width), BF16)] * 2,
        in_specs=[HERE] * EXPERTS + [ANYWHERE] * len(earlier),
        compiler_params=SMALL,
        cost_estimate=CHEAP,
        name="split",
    )(*blocks, *earlier)


def unpack_kernel(placer_ref, mine_ref, got_ref, *refs):
    chosen = placer_ref[...].astype(F32).T.astype(BF16)
    total = jnp.dot(chosen, mine_ref[...], preferred_element_type=F32)
    total += jnp.dot(chosen, got_ref[...], preferred_element_type=F32)
    refs[-1][...] = total.astype(BF16)


def unpack(placer, mine, got, earlier):
    return pl.pallas_call(
        unpack_kernel,
        out_shape=jax.ShapeDtypeStruct((placer.shape[1], mine.shape[1]), BF16),
        in_specs=[HERE] * 3 + [AFAR] * len(earlier),
        compiler_params=SMALL,
        cost_estimate=DEAR,
        name="unpack",
    )(placer, mine, got, *[kept(v) for v in earlier])


def swap(value, axis):
    return lax.ppermute(value, axis, [(0, 1), (1, 0)])


def across_planes(blocks):
    return [blocks[0]] + [
        lax.ppermute(blocks[k], "arch", [(i, i ^ k) for i in range(EXPERTS)]) for k in range(1, EXPERTS)
    ]


def after(values, earlier):
    n = len(values)
    return list(lax.optimization_barrier((*values, *earlier))[:n])


def gathering(designs, archetype, w_gate, w_up, w_down, cotangent):
    far, core = lax.axis_index("far"), lax.axis_index("core")
    scalars = [lax.axis_index("arch"), 2 * far + core, 2 * far + 1 - core]
    scalars = [v.astype(jnp.int32)[None] for v in scalars]
    tokens, width = designs.shape
    share = width // 4
    placer, *blocks = pack(scalars, archetype.reshape(1, tokens), designs, cotangent)
    wd, wdt = flip(after([w_down], [placer])[0])

    x_own = join(across_planes(blocks[:EXPERTS]))
    moved = across_planes(relay(blocks[EXPERTS:], [wdt]))
    x_far, x_near = swap(x_own, "far"), swap(x_own, "half")

    wg, wu = w_gate, w_up
    act0, coef0, share_own = forward([x_own], wg, wu, wd)
    g_own = join(moved, [act0])
    g_far, g_near = swap(g_own, "far"), swap(g_own, "half")
    act1, coef1, *shares = forward([x_near], wg, wu, wd, other=share_own)
    (x_pass,) = relay([x_near], [mark(act1, x_far), g_far])
    (g_pass,) = relay([g_far], [x_pass, g_near])
    x_corner, g_corner = swap(x_pass, "far"), swap(g_pass, "half")
    returned = across_planes(shares)
    act2, coef2 = forward([x_far], wg, wu, earlier=[g_pass], cost=DEAR)
    dg, du = slopes([g_own, g_near, g_far], [act0, act1, act2], [coef0, coef1, coef2], wdt)
    act3, coef3 = forward([x_corner], wg, wu, earlier=[dg])
    mine, theirs = split(returned, [act3])
    got = swap(theirs, "half")
    xt = turn(*scalars[1:], [x_own, x_near, x_far, x_corner], share)

    rest = (xt, g_corner, act3, coef3, dg, du, wdt)
    cols = w_down.shape[0]
    cut = cols // 2
    own0, sib0 = backward(*rest, 0, cut)
    own1, sib1 = backward(*rest, cut, cols - cut, [own0])
    got0, got1 = swap(sib0, "core"), swap(sib1, "core")
    held = finish([own0], [got0], (0,), cols)
    outputs = unpack(placer, mine, got, held[:1])
    grad_gate, grad_up = finish([own1], [got1], (cut,), cols, held)
    return outputs, grad_gate, grad_up


def reducing(designs, archetype, w_gate, w_up, w_down, cotangent):
    width = designs.shape[1]
    owners = lax.axis_size("expert")
    sharers = owners // EXPERTS
    hidden_cols = w_gate.shape[1]
    labels = archetype[:, 0]
    onehot = (labels[:, None] == jnp.arange(EXPERTS, dtype=jnp.int32)[None, :]).astype(jnp.int32)
    ranks = jnp.cumsum(onehot, axis=0) - onehot
    target = labels * CAP + jnp.sum(ranks * onehot, axis=1)
    placer = (jnp.arange(EXPERTS * CAP, dtype=jnp.int32)[:, None] == target[None, :]).astype(BF16)
    received = []
    for rows in (designs, cotangent):
        packed = jnp.dot(placer, rows, preferred_element_type=F32).astype(BF16)
        send = jnp.repeat(packed.reshape(EXPERTS, CAP, width), sharers, axis=0)
        received.append(
            lax.all_to_all(send, "expert", split_axis=0, concat_axis=0, tiled=True).reshape(
                owners * CAP, width
            )
        )
    flat_x, flat_g = received
    gate = jnp.dot(flat_x, w_gate, preferred_element_type=F32)
    up = jnp.dot(flat_x, w_up, preferred_element_type=F32)
    act, slope = silu_parts(gate)
    hidden = (act * up).astype(BF16)
    partial_value = (
        jnp.dot(hidden, w_down, preferred_element_type=F32).astype(BF16).reshape(owners, CAP, width)
    )
    returned = lax.all_to_all(partial_value, "expert", split_axis=0, concat_axis=0, tiled=True)
    summed = jnp.sum(returned.astype(F32).reshape(EXPERTS, sharers, CAP, width), axis=1).reshape(
        EXPERTS * CAP, width
    )
    outputs = jnp.take(summed, target, axis=0).astype(BF16)
    d_hidden = contract_cols(flat_g, w_down)
    d_gate = (d_hidden * up * slope).astype(BF16)
    d_up = (d_hidden * act).astype(BF16)
    grads = jnp.concatenate([contract_rows(flat_x, d_gate), contract_rows(flat_x, d_up)], axis=1)
    mine = lax.psum_scatter(grads.astype(BF16), "dp", scatter_dimension=0, tiled=True)
    return outputs, mine[:, :hidden_cols], mine[:, hidden_cols:]


def solution(mesh):
    dp, owners = mesh.devices.shape
    if (dp, owners) == (4, 2 * EXPERTS):
        rows, cols = ("far", "core"), ("arch", "half")
        mesh = Mesh(mesh.devices.reshape(2, 2, EXPERTS, 2), rows + cols)
        body = gathering
    else:
        rows, cols = ("dp",), ("expert",)
        body = reducing
    tokens = P(rows + cols, None)
    return jax.shard_map(
        body,
        mesh=mesh,
        in_specs=(tokens, tokens, P(None, cols), P(None, cols), P(cols, None), tokens),
        out_specs=(tokens, P(rows, cols), P(rows, cols)),
        check_vma=False,
    )
```

```python
import functools

import jax
import jax.numpy as jnp
from jax import lax
from jax.experimental import pallas as pl
from jax.experimental.pallas import tpu as pltpu
from jax.sharding import Mesh
from jax.sharding import PartitionSpec as P

EXPERTS = 4
CAP = 36
WIDE = 2048
STRIP = 512
SLOPES = 1024
SLICE = 256
MIB = 1024 * 1024
LARGE = pltpu.CompilerParams(vmem_limit_bytes=16 * MIB)
SMALL = pltpu.CompilerParams(vmem_limit_bytes=12 * MIB)
CHEAP = pl.CostEstimate(flops=0, bytes_accessed=0, transcendentals=0)
DEAR = pl.CostEstimate(flops=20_000_000_000, bytes_accessed=0, transcendentals=0)
F32 = jnp.float32
BF16 = jnp.bfloat16
HERE = pl.BlockSpec(memory_space=pltpu.VMEM)
AFAR = pl.BlockSpec(memory_space=pltpu.HBM)
ANYWHERE = pl.BlockSpec(memory_space=pl.ANY)


def silu_parts(gate):
    sigma = 0.5 * jnp.tanh(0.5 * gate) + 0.5
    return (gate * sigma, sigma * (1.0 + gate * (1.0 - sigma)))


def contract_rows(left, right):
    return lax.dot_general(left, right, (((0,), (0,)), ((), ())), preferred_element_type=F32)


def contract_cols(left, right):
    return lax.dot_general(left, right, (((1,), (1,)), ((), ())), preferred_element_type=F32)


def stacked(refs):
    return jnp.concatenate([r[...].astype(F32) for r in refs], axis=0)


def kept(value):
    return pltpu.with_memory_space_constraint(value, pltpu.HBM)


def pack_kernel(plane_ref, _, __, kind_ref, x_ref, g_ref, placer_ref, *refs):
    outs, (kind, x, g, sems) = refs[: 2 * EXPERTS], refs[2 * EXPERTS :]
    copies = [
        pltpu.make_async_copy(source, target, sems.at[i])
        for i, (source, target) in enumerate(((kind_ref, kind), (x_ref, x), (g_ref, g)))
    ]
    for copy in copies:
        copy.start()
    tokens = kind.shape[1]
    copies[0].wait()
    key = kind[...] ^ plane_ref[0]
    onehot = (key == lax.broadcasted_iota(jnp.int32, (8, tokens), 0)).astype(F32)
    before = lax.broadcasted_iota(jnp.int32, (tokens, tokens), 0) < lax.broadcasted_iota(
        jnp.int32, (tokens, tokens), 1
    )
    ranks = jnp.dot(onehot.astype(BF16), before.astype(BF16), preferred_element_type=F32)
    rank = jnp.sum(ranks * onehot, axis=0, keepdims=True).astype(jnp.int32)
    place = key * CAP + rank
    slots = EXPERTS * CAP
    placer = (place == lax.broadcasted_iota(jnp.int32, (slots, tokens), 0)).astype(F32).astype(BF16)
    placer_ref[...] = placer
    for copy, source, first in ((copies[1], x, 0), (copies[2], g, EXPERTS)):
        copy.wait()
        packed = jnp.dot(placer, source[...], preferred_element_type=F32)
        for k in range(EXPERTS):
            outs[first + k][...] = packed[k * CAP : (k + 1) * CAP].astype(BF16)


def pack(scalars, kind, x, g):
    tokens, width = x.shape
    return pl.pallas_call(
        pack_kernel,
        out_shape=[jax.ShapeDtypeStruct((EXPERTS * CAP, tokens), BF16)]
        + [jax.ShapeDtypeStruct((CAP, width), BF16)] * (2 * EXPERTS),
        in_specs=[pl.BlockSpec(memory_space=pltpu.SMEM)] * 3 + [AFAR] * 3,
        scratch_shapes=[
            pltpu.VMEM((1, tokens), jnp.int32),
            pltpu.VMEM((tokens, width), BF16),
            pltpu.VMEM((tokens, width), BF16),
            pltpu.SemaphoreType.DMA((3,)),
        ],
        compiler_params=SMALL,
        cost_estimate=CHEAP,
        name="pack",
    )(*scalars, kept(kind), kept(x), kept(g))


def join_kernel(*refs):
    refs[-1][...] = stacked(refs[-2 : -2 - EXPERTS : -1]).astype(BF16)


def join(blocks, earlier=()):
    width = blocks[0].shape[1]
    return pl.pallas_call(
        join_kernel,
        out_shape=jax.ShapeDtypeStruct((EXPERTS * CAP, width), BF16),
        in_specs=[ANYWHERE] * len(earlier) + [HERE] * EXPERTS,
        compiler_params=SMALL,
        cost_estimate=CHEAP,
        name="join",
    )(*earlier, *blocks[::-1])


def relay_kernel(n, *refs):
    for i in range(n):
        refs[len(refs) - n + i][...] = refs[i][...]


def relay(values, earlier):
    n = len(values)
    return pl.pallas_call(
        functools.partial(relay_kernel, n),
        out_shape=[jax.ShapeDtypeStruct(v.shape, v.dtype) for v in values],
        in_specs=[HERE] * n + [ANYWHERE] * len(earlier),
        compiler_params=SMALL,
        cost_estimate=CHEAP,
        name="relay",
    )(*values, *earlier)


def mark_kernel(value_ref, _, mark_ref):
    mark_ref[...] = value_ref[: mark_ref.shape[0], : mark_ref.shape[1]]


def mark(value, earlier):
    return pl.pallas_call(
        mark_kernel,
        out_shape=jax.ShapeDtypeStruct((16, 128), value.dtype),
        in_specs=[HERE, ANYWHERE],
        compiler_params=SMALL,
        cost_estimate=CHEAP,
        name="mark",
    )(value, earlier)


def flip_kernel(source_ref, here_ref, flipped_ref, sems):
    steps = source_ref.shape[0] // SLICE
    copies = []
    for j in range(steps):
        rows = pl.ds(j * SLICE, SLICE)
        copies.append(pltpu.make_async_copy(source_ref.at[rows], here_ref.at[rows], sems.at[j]))
        copies[j].start()
    for j in range(steps):
        copies[j].wait()
        rows = slice(j * SLICE, (j + 1) * SLICE)
        flipped_ref[:, rows] = here_ref[rows, :].T


def flip(value):
    return pl.pallas_call(
        flip_kernel,
        out_shape=[pltpu.VMEM(value.shape, value.dtype), pltpu.VMEM(value.shape[::-1], value.dtype)],
        in_specs=[AFAR],
        out_specs=[HERE, HERE],
        scratch_shapes=[pltpu.SemaphoreType.DMA((value.shape[0] // SLICE,))],
        compiler_params=SMALL,
        cost_estimate=CHEAP,
        name="flip",
    )(kept(value))


def forward_kernel(n, down, pair, unused, *refs):
    refs = list(refs[unused:])
    xs = [refs.pop(0) for _ in range(n)]
    wg_ref, wu_ref = refs.pop(0), refs.pop(0)
    wd_ref = refs.pop(0) if down else None
    other_ref = refs.pop(0) if pair else None
    act_ref, coef_ref = refs.pop(0), refs.pop(0)
    shares = [refs.pop(0) for _ in range(EXPERTS if pair else down)]
    part = xs[0].shape[0]
    x_ref = xs[0]
    if n > 1:
        x_ref = refs.pop(0)
        for i in range(n):
            x_ref[i * part : (i + 1) * part, :] = xs[i][...]
    total = None
    for start in range(0, wg_ref.shape[1], WIDE):
        cols = slice(start, start + WIDE)
        gate = jnp.dot(x_ref[...], wg_ref[:, cols], preferred_element_type=F32)
        up = jnp.dot(x_ref[...], wu_ref[:, cols], preferred_element_type=F32)
        act, slope = silu_parts(gate)
        act_ref[:, cols] = act.astype(BF16)
        coef_ref[:, cols] = (up * slope).astype(BF16)
        if down:
            hidden = (act[:part] * up[:part]).astype(BF16)
            share = jnp.dot(hidden, wd_ref[cols, :], preferred_element_type=F32)
            total = share if total is None else total + share

    if pair:
        other = other_ref[...].astype(F32)
        for k in range(EXPERTS):
            rows = slice(k * CAP, (k + 1) * CAP)
            block = jnp.concatenate([other[rows], total[rows]], axis=0).astype(BF16)
            shares[k][...] = block
    elif down:
        shares[0][...] = total.astype(BF16)


def forward(xs, wg, wu, wd=None, other=None, earlier=(), cost=CHEAP):
    n, (part, width), cols = len(xs), xs[0].shape, wg.shape[1]
    rows = n * part
    down, pair = wd is not None, other is not None
    shares = [jax.ShapeDtypeStruct((part, width), BF16)] * down
    if pair:
        shares = [jax.ShapeDtypeStruct((2 * CAP, width), BF16)] * EXPERTS
    return pl.pallas_call(
        functools.partial(forward_kernel, n, down, pair, len(earlier)),
        out_shape=[jax.ShapeDtypeStruct((rows, cols), BF16)] * 2
        + shares,
        in_specs=[ANYWHERE] * len(earlier)
        + [HERE] * n
        + [HERE] * (2 + down + pair),
        scratch_shapes=[pltpu.VMEM((rows, width), BF16)] * (n > 1),
        compiler_params=LARGE,
        cost_estimate=cost,
        name="forward" + "_down" * down,
    )(*earlier, *xs, wg, wu, *([wd] * down), *([other] * pair))


def turn_kernel(_, __, *refs):
    refs[8][: refs[0].shape[1], :] = stacked(refs[0:4]).T.astype(BF16)
    refs[8][refs[0].shape[1] :, :] = stacked(refs[4:8]).T.astype(BF16)


def turn(own, sib, xs, share):
    part = xs[0].shape[0]
    rows = len(xs) * part
    return pl.pallas_call(
        turn_kernel,
        grid_spec=pltpu.PrefetchScalarGridSpec(
            num_scalar_prefetch=2,
            grid=(1,),
            in_specs=[pl.BlockSpec((part, share), lambda j, a, b: (0, a[0]))] * 4
            + [pl.BlockSpec((part, share), lambda j, a, b: (0, b[0]))] * 4,
            out_specs=pl.BlockSpec((2 * share, rows), lambda j, a, b: (0, 0)),
        ),
        out_shape=jax.ShapeDtypeStruct((2 * share, rows), BF16),
        compiler_params=SMALL,
        cost_estimate=CHEAP,
        name="turn",
    )(own, sib, *xs, *xs)


def slopes_kernel(n, *refs):
    gs, acts, coefs = refs[:n], refs[n : 2 * n], refs[2 * n : 3 * n]
    wdt_ref, dg_ref, du_ref, g_ref = refs[3 * n :]
    part = gs[0].shape[0]
    for i in range(n):
        g_ref[i * part : (i + 1) * part, :] = gs[i][...]
    for start in range(0, wdt_ref.shape[1], SLOPES):
        cols = slice(start, start + SLOPES)
        d_hidden = jnp.dot(g_ref[...], wdt_ref[:, cols], preferred_element_type=F32)
        for i in range(n):
            rows = slice(i * part, (i + 1) * part)
            dg_ref[rows, cols] = (d_hidden[rows] * coefs[i][:, cols].astype(F32)).astype(BF16)
            du_ref[rows, cols] = (d_hidden[rows] * acts[i][:, cols].astype(F32)).astype(BF16)


def slopes(gs, acts, coefs, wdt):
    n, (part, width) = len(gs), gs[0].shape
    return pl.pallas_call(
        functools.partial(slopes_kernel, n),
        out_shape=[jax.ShapeDtypeStruct((n * part, wdt.shape[1]), BF16)] * 2,
        in_specs=[HERE] * (3 * n + 1),
        scratch_shapes=[pltpu.VMEM((n * part, width), BF16)],
        compiler_params=LARGE,
        cost_estimate=CHEAP,
        name="slopes",
    )(*gs, *acts, *coefs, wdt)


def backward_kernel(first, xt_ref, g_ref, act_ref, coef_ref, dg_ref, du_ref, wdt_ref, *refs):
    own_ref, sib_ref = refs[-2:]
    share = own_ref.shape[0] // 2
    for start in range(0, own_ref.shape[1], STRIP):
        here = slice(start, start + STRIP)
        cols = slice(first + start, first + start + STRIP)
        d_hidden = jnp.dot(g_ref[...], wdt_ref[:, cols], preferred_element_type=F32)
        for row, factor_ref, known_ref in ((0, coef_ref, dg_ref), (share, act_ref, du_ref)):
            d_cols = (d_hidden * factor_ref[:, cols].astype(F32)).astype(BF16)
            d_cols = jnp.concatenate([known_ref[:, cols], d_cols], axis=0)
            total = jnp.dot(xt_ref[...], d_cols, preferred_element_type=F32).astype(BF16)
            own_ref[row : row + share, here] = total[:share]
            sib_ref[row : row + share, here] = total[share:]


def backward(xt, g, act, coef, dg, du, wdt, first, cols, earlier=()):
    return pl.pallas_call(
        functools.partial(backward_kernel, first),
        out_shape=[jax.ShapeDtypeStruct((xt.shape[0], cols), BF16)] * 2,
        in_specs=[HERE] * 7 + [ANYWHERE] * len(earlier),
        compiler_params=LARGE,
        cost_estimate=DEAR,
        name="backward",
    )(xt, g, act, coef, dg, du, wdt, *earlier)


def finish_kernel(spans, more, unused, *refs):
    refs = refs[unused:]
    n = len(spans)
    pairs = [refs[2 * i : 2 * i + 2] for i in range(n)]
    gate_ref, up_ref, gate, up, sems = refs[2 * n + 2 * more :]
    share = gate_ref.shape[0]
    low = spans[0][0]
    copies = []
    for i, ((first, cols), (own, got)) in enumerate(zip(spans, pairs)):
        for j, (target, held) in enumerate(((gate_ref, gate), (up_ref, up))):
            rows = slice(j * share, (j + 1) * share)
            here = pl.ds(first - low, cols)
            held[:, here] = (own[rows, :].astype(F32) + got[rows, :].astype(F32)).astype(BF16)
            copies.append(
                pltpu.make_async_copy(held.at[:, here], target.at[:, pl.ds(first, cols)], sems.at[i, j])
            )
            copies[-1].start()
    for copy in copies:
        copy.wait()


def finish(owns, gots, firsts, width, held=(), earlier=()):
    share = owns[0].shape[0] // 2
    spans = tuple((first, own.shape[1]) for first, own in zip(firsts, owns))
    total = sum(cols for _, cols in spans)
    n, more = len(owns), len(held) > 0
    return pl.pallas_call(
        functools.partial(finish_kernel, spans, more, len(earlier)),
        out_shape=[jax.ShapeDtypeStruct((share, width), BF16)] * 2,
        in_specs=[AFAR] * len(earlier) + [HERE] * (2 * n) + [ANYWHERE] * (2 * more),
        out_specs=[ANYWHERE] * 2,
        scratch_shapes=[pltpu.VMEM((share, total), BF16)] * 2 + [pltpu.SemaphoreType.DMA((n, 2))],
        input_output_aliases={len(earlier) + 2 * n: 0, len(earlier) + 2 * n + 1: 1} if more else {},
        compiler_params=SMALL,
        cost_estimate=CHEAP,
        name="finish",
    )(*[kept(v) for v in earlier], *[v for both in zip(owns, gots) for v in both], *held)


def split_kernel(*refs):
    blocks = [r[...].astype(F32) for r in refs[:EXPERTS]]
    refs[-2][...] = jnp.concatenate([b[:CAP] for b in blocks], axis=0).astype(BF16)
    refs[-1][...] = jnp.concatenate([b[CAP:] for b in blocks], axis=0).astype(BF16)


def split(blocks, earlier):
    width = blocks[0].shape[1]
    return pl.pallas_call(
        split_kernel,
        out_shape=[jax.ShapeDtypeStruct((EXPERTS * CAP, width), BF16)] * 2,
        in_specs=[HERE] * EXPERTS + [ANYWHERE] * len(earlier),
        compiler_params=SMALL,
        cost_estimate=CHEAP,
        name="split",
    )(*blocks, *earlier)


def unpack_kernel(placer_ref, mine_ref, got_ref, *refs):
    chosen = placer_ref[...].astype(F32).T.astype(BF16)
    total = jnp.dot(chosen, mine_ref[...], preferred_element_type=F32)
    total += jnp.dot(chosen, got_ref[...], preferred_element_type=F32)
    refs[-1][...] = total.astype(BF16)


def unpack(placer, mine, got, earlier):
    return pl.pallas_call(
        unpack_kernel,
        out_shape=jax.ShapeDtypeStruct((placer.shape[1], mine.shape[1]), BF16),
        in_specs=[HERE] * 3 + [AFAR] * len(earlier),
        compiler_params=SMALL,
        cost_estimate=DEAR,
        name="unpack",
    )(placer, mine, got, *[kept(v) for v in earlier])


def swap(value, axis):
    return lax.ppermute(value, axis, [(0, 1), (1, 0)])


def across_planes(blocks):
    return [blocks[0]] + [
        lax.ppermute(blocks[k], "arch", [(i, i ^ k) for i in range(EXPERTS)]) for k in range(1, EXPERTS)
    ]


def after(values, earlier):
    n = len(values)
    return list(lax.optimization_barrier((*values, *earlier))[:n])


def gathering(designs, archetype, w_gate, w_up, w_down, cotangent):
    far, core = lax.axis_index("far"), lax.axis_index("core")
    scalars = [lax.axis_index("arch"), 2 * far + core, 2 * far + 1 - core]
    scalars = [v.astype(jnp.int32)[None] for v in scalars]
    tokens, width = designs.shape
    share = width // 4
    placer, *blocks = pack(scalars, archetype.reshape(1, tokens), designs, cotangent)
    wd, wdt = flip(after([w_down], [placer])[0])

    x_own = join(across_planes(blocks[:EXPERTS]))
    moved = across_planes(relay(blocks[EXPERTS:], [wdt]))
    x_far, x_near = swap(x_own, "far"), swap(x_own, "half")

    wg, wu = w_gate, w_up
    act0, coef0, share_own = forward([x_own], wg, wu, wd)
    g_own = join(moved, [act0])
    g_far, g_near = swap(g_own, "far"), swap(g_own, "half")
    act1, coef1, *shares = forward([x_near], wg, wu, wd, other=share_own)
    (x_pass,) = relay([x_near], [mark(act1, x_far), g_far])
    (g_pass,) = relay([g_far], [x_pass, g_near])
    x_corner, g_corner = swap(x_pass, "far"), swap(g_pass, "half")
    returned = across_planes(shares)
    act2, coef2 = forward([x_far], wg, wu, earlier=[g_pass], cost=DEAR)
    dg, du = slopes([g_own, g_near, g_far], [act0, act1, act2], [coef0, coef1, coef2], wdt)
    act3, coef3 = forward([x_corner], wg, wu, earlier=[dg])
    mine, theirs = split(returned, [act3])
    got = swap(theirs, "half")
    xt = turn(*scalars[1:], [x_own, x_near, x_far, x_corner], share)

    rest = (xt, g_corner, act3, coef3, dg, du, wdt)
    cols = w_down.shape[0]
    cut = cols // 2
    own0, sib0 = backward(*rest, 0, cut)
    own1, sib1 = backward(*rest, cut, cols - cut, [own0])
    got0, got1 = swap(sib0, "core"), swap(sib1, "core")
    held = finish([own0], [got0], (0,), cols)
    outputs = unpack(placer, mine, got, held[:1])
    grad_gate, grad_up = finish([own1], [got1], (cut,), cols, held)
    return outputs, grad_gate, grad_up


def reducing(designs, archetype, w_gate, w_up, w_down, cotangent):
    width = designs.shape[1]
    owners = lax.axis_size("expert")
    sharers = owners // EXPERTS
    hidden_cols = w_gate.shape[1]
    labels = archetype[:, 0]
    onehot = (labels[:, None] == jnp.arange(EXPERTS, dtype=jnp.int32)[None, :]).astype(jnp.int32)
    ranks = jnp.cumsum(onehot, axis=0) - onehot
    target = labels * CAP + jnp.sum(ranks * onehot, axis=1)
    placer = (jnp.arange(EXPERTS * CAP, dtype=jnp.int32)[:, None] == target[None, :]).astype(BF16)
    received = []
    for rows in (designs, cotangent):
        packed = jnp.dot(placer, rows, preferred_element_type=F32).astype(BF16)
        send = jnp.repeat(packed.reshape(EXPERTS, CAP, width), sharers, axis=0)
        received.append(
            lax.all_to_all(send, "expert", split_axis=0, concat_axis=0, tiled=True).reshape(
                owners * CAP, width
            )
        )
    flat_x, flat_g = received
    gate = jnp.dot(flat_x, w_gate, preferred_element_type=F32)
    up = jnp.dot(flat_x, w_up, preferred_element_type=F32)
    act, slope = silu_parts(gate)
    hidden = (act * up).astype(BF16)
    partial_value = (
        jnp.dot(hidden, w_down, preferred_element_type=F32).astype(BF16).reshape(owners, CAP, width)
    )
    returned = lax.all_to_all(partial_value, "expert", split_axis=0, concat_axis=0, tiled=True)
    summed = jnp.sum(returned.astype(F32).reshape(EXPERTS, sharers, CAP, width), axis=1).reshape(
        EXPERTS * CAP, width
    )
    outputs = jnp.take(summed, target, axis=0).astype(BF16)
    d_hidden = contract_cols(flat_g, w_down)
    d_gate = (d_hidden * up * slope).astype(BF16)
    d_up = (d_hidden * act).astype(BF16)
    grads = jnp.concatenate([contract_rows(flat_x, d_gate), contract_rows(flat_x, d_up)], axis=1)
    mine = lax.psum_scatter(grads.astype(BF16), "dp", scatter_dimension=0, tiled=True)
    return outputs, mine[:, :hidden_cols], mine[:, hidden_cols:]


def solution(mesh):
    dp, owners = mesh.devices.shape
    if (dp, owners) == (4, 2 * EXPERTS):
        rows, cols = ("far", "core"), ("arch", "half")
        mesh = Mesh(mesh.devices.reshape(2, 2, EXPERTS, 2), rows + cols)
        body = gathering
    else:
        rows, cols = ("dp",), ("expert",)
        body = reducing
    tokens = P(rows + cols, None)
    return jax.shard_map(
        body,
        mesh=mesh,
        in_specs=(tokens, tokens, P(None, cols), P(None, cols), P(cols, None), tokens),
        out_specs=(tokens, P(rows, cols), P(rows, cols)),
        check_vma=False,
    )
```

```python
import functools

import jax
import jax.numpy as jnp
from jax import lax
from jax.experimental import pallas as pl
from jax.experimental.pallas import tpu as pltpu
from jax.sharding import Mesh
from jax.sharding import PartitionSpec as P

EXPERTS = 4
CAP = 36
WIDE = 1024
STRIP = 512
SLICE = 256
MIB = 1024 * 1024
LARGE = pltpu.CompilerParams(vmem_limit_bytes=16 * MIB)
SMALL = pltpu.CompilerParams(vmem_limit_bytes=12 * MIB)
CHEAP = pl.CostEstimate(flops=0, bytes_accessed=0, transcendentals=0)
DEAR = pl.CostEstimate(flops=20_000_000_000, bytes_accessed=0, transcendentals=0)
F32 = jnp.float32
BF16 = jnp.bfloat16
HERE = pl.BlockSpec(memory_space=pltpu.VMEM)
AFAR = pl.BlockSpec(memory_space=pltpu.HBM)
ANYWHERE = pl.BlockSpec(memory_space=pl.ANY)


def silu_parts(gate):
    sigma = 0.5 * jnp.tanh(0.5 * gate) + 0.5
    return (gate * sigma, sigma * (1.0 + gate * (1.0 - sigma)))


def contract_rows(left, right):
    return lax.dot_general(left, right, (((0,), (0,)), ((), ())), preferred_element_type=F32)


def contract_cols(left, right):
    return lax.dot_general(left, right, (((1,), (1,)), ((), ())), preferred_element_type=F32)


def stacked(refs):
    return jnp.concatenate([r[...].astype(F32) for r in refs], axis=0)


def kept(value):
    return pltpu.with_memory_space_constraint(value, pltpu.HBM)


def pack_kernel(plane_ref, _, __, kind_ref, x_ref, g_ref, placer_ref, *refs):
    outs, (kind, x, g, sems) = refs[: 2 * EXPERTS], refs[2 * EXPERTS :]
    copies = [
        pltpu.make_async_copy(source, target, sems.at[i])
        for i, (source, target) in enumerate(((kind_ref, kind), (x_ref, x), (g_ref, g)))
    ]
    for copy in copies:
        copy.start()
    tokens = kind.shape[1]
    copies[0].wait()
    key = kind[...] ^ plane_ref[0]
    onehot = (key == lax.broadcasted_iota(jnp.int32, (8, tokens), 0)).astype(F32)
    before = lax.broadcasted_iota(jnp.int32, (tokens, tokens), 0) < lax.broadcasted_iota(
        jnp.int32, (tokens, tokens), 1
    )
    ranks = jnp.dot(onehot.astype(BF16), before.astype(BF16), preferred_element_type=F32)
    rank = jnp.sum(ranks * onehot, axis=0, keepdims=True).astype(jnp.int32)
    place = key * CAP + rank
    slots = EXPERTS * CAP
    placer = (place == lax.broadcasted_iota(jnp.int32, (slots, tokens), 0)).astype(F32).astype(BF16)
    placer_ref[...] = placer
    for copy, source, first in ((copies[1], x, 0), (copies[2], g, EXPERTS)):
        copy.wait()
        packed = jnp.dot(placer, source[...], preferred_element_type=F32)
        for k in range(EXPERTS):
            outs[first + k][...] = packed[k * CAP : (k + 1) * CAP].astype(BF16)


def pack(scalars, kind, x, g):
    tokens, width = x.shape
    return pl.pallas_call(
        pack_kernel,
        out_shape=[jax.ShapeDtypeStruct((EXPERTS * CAP, tokens), BF16)]
        + [jax.ShapeDtypeStruct((CAP, width), BF16)] * (2 * EXPERTS),
        in_specs=[pl.BlockSpec(memory_space=pltpu.SMEM)] * 3 + [AFAR] * 3,
        scratch_shapes=[
            pltpu.VMEM((1, tokens), jnp.int32),
            pltpu.VMEM((tokens, width), BF16),
            pltpu.VMEM((tokens, width), BF16),
            pltpu.SemaphoreType.DMA((3,)),
        ],
        compiler_params=SMALL,
        cost_estimate=CHEAP,
        name="pack",
    )(*scalars, kept(kind), kept(x), kept(g))


def join_kernel(*refs):
    refs[-1][...] = stacked(refs[-1 - EXPERTS : -1]).astype(BF16)


def join(blocks, earlier=()):
    width = blocks[0].shape[1]
    return pl.pallas_call(
        join_kernel,
        out_shape=jax.ShapeDtypeStruct((EXPERTS * CAP, width), BF16),
        in_specs=[ANYWHERE] * len(earlier) + [HERE] * EXPERTS,
        compiler_params=SMALL,
        cost_estimate=CHEAP,
        name="join",
    )(*earlier, *blocks)


def relay_kernel(n, *refs):
    for i in range(n):
        refs[len(refs) - n + i][...] = refs[i][...]


def relay(values, earlier):
    n = len(values)
    return pl.pallas_call(
        functools.partial(relay_kernel, n),
        out_shape=[jax.ShapeDtypeStruct(v.shape, v.dtype) for v in values],
        in_specs=[HERE] * n + [ANYWHERE] * len(earlier),
        compiler_params=SMALL,
        cost_estimate=CHEAP,
        name="relay",
    )(*values, *earlier)


def mark_kernel(value_ref, _, mark_ref):
    mark_ref[...] = value_ref[: mark_ref.shape[0], : mark_ref.shape[1]]


def mark(value, earlier):
    return pl.pallas_call(
        mark_kernel,
        out_shape=jax.ShapeDtypeStruct((16, 128), value.dtype),
        in_specs=[HERE, ANYWHERE],
        compiler_params=SMALL,
        cost_estimate=CHEAP,
        name="mark",
    )(value, earlier)


def flip_kernel(source_ref, here_ref, flipped_ref, sems):
    steps = source_ref.shape[0] // SLICE
    copies = []
    for j in range(steps):
        rows = pl.ds(j * SLICE, SLICE)
        copies.append(pltpu.make_async_copy(source_ref.at[rows], here_ref.at[rows], sems.at[j]))
        copies[j].start()
    for j in range(steps):
        copies[j].wait()
        rows = slice(j * SLICE, (j + 1) * SLICE)
        flipped_ref[:, rows] = here_ref[rows, :].T


def flip(value):
    return pl.pallas_call(
        flip_kernel,
        out_shape=[pltpu.VMEM(value.shape, value.dtype), pltpu.VMEM(value.shape[::-1], value.dtype)],
        in_specs=[AFAR],
        out_specs=[HERE, HERE],
        scratch_shapes=[pltpu.SemaphoreType.DMA((value.shape[0] // SLICE,))],
        compiler_params=SMALL,
        cost_estimate=CHEAP,
        name="flip",
    )(kept(value))


def forward_kernel(n, fetch, down, pair, unused, *refs):
    refs = list(refs[unused:])
    xs = [refs.pop(0) for _ in range(n)]
    wg_ref, wu_ref = refs.pop(0), refs.pop(0)
    wd_ref = refs.pop(0) if down else None
    other_ref = refs.pop(0) if pair else None
    act_ref, coef_ref = refs.pop(0), refs.pop(0)
    shares = [refs.pop(0) for _ in range(EXPERTS if pair else down)]
    if fetch:
        sources, sems = (wg_ref, wu_ref), refs.pop()
        wg_ref, wu_ref = refs.pop(0), refs.pop(0)
    acc_ref = refs.pop(0) if down else None
    part = xs[0].shape[0]
    x_ref = xs[0]
    if n > 1:
        x_ref = refs.pop(0)
        for i in range(n):
            x_ref[i * part : (i + 1) * part, :] = xs[i][...]
    steps = wg_ref.shape[1] // (2 * WIDE)

    def copies(j):
        cols = pl.ds(pl.multiple_of(j * (2 * WIDE), (2 * WIDE)), (2 * WIDE))
        return [
            pltpu.make_async_copy(source.at[:, cols], target.at[:, cols], sems.at[j, i])
            for i, (source, target) in enumerate(zip(sources, (wg_ref, wu_ref)))
        ]

    if fetch:
        for j in range(steps):
            for copy in copies(j):
                copy.start()
    if down:
        acc_ref[...] = jnp.zeros_like(acc_ref)

    @pl.loop(0, steps)
    def _(j):
        if fetch:
            for copy in copies(j):
                copy.wait()
        for i in range(2):
            cols = pl.ds(pl.multiple_of(j * (2 * WIDE) + i * WIDE, WIDE), WIDE)
            gate = jnp.dot(x_ref[...], wg_ref[:, cols], preferred_element_type=F32)
            up = jnp.dot(x_ref[...], wu_ref[:, cols], preferred_element_type=F32)
            act, slope = silu_parts(gate)
            act_ref[:, cols] = act.astype(BF16)
            coef_ref[:, cols] = (up * slope).astype(BF16)
            if down:
                hidden = (act[:part] * up[:part]).astype(BF16)
                acc_ref[...] += jnp.dot(hidden, wd_ref[cols, :], preferred_element_type=F32)

    if pair:
        other = other_ref[...].astype(F32)
        for k in range(EXPERTS):
            rows = slice(k * CAP, (k + 1) * CAP)
            block = jnp.concatenate([other[rows], acc_ref[rows, :]], axis=0).astype(BF16)
            shares[k][...] = block
    elif down:
        shares[0][...] = acc_ref[...].astype(BF16)


def forward(xs, wg, wu, wd=None, other=None, fetch=False, earlier=(), cost=CHEAP):
    n, (part, width), cols = len(xs), xs[0].shape, wg.shape[1]
    rows = n * part
    down, pair = wd is not None, other is not None
    shares = [jax.ShapeDtypeStruct((part, width), BF16)] * down
    if pair:
        shares = [jax.ShapeDtypeStruct((2 * CAP, width), BF16)] * EXPERTS
    weights = [kept(wg), kept(wu)] if fetch else [wg, wu]
    return pl.pallas_call(
        functools.partial(forward_kernel, n, fetch, down, pair, len(earlier)),
        out_shape=[jax.ShapeDtypeStruct((rows, cols), BF16)] * 2
        + shares
        + [pltpu.VMEM(wg.shape, wg.dtype)] * (2 * fetch),
        in_specs=[ANYWHERE] * len(earlier)
        + [HERE] * n
        + [AFAR if fetch else HERE] * 2
        + [HERE] * (down + pair),
        scratch_shapes=[pltpu.VMEM((part, width), F32)] * down
        + [pltpu.VMEM((rows, width), BF16)] * (n > 1)
        + [pltpu.SemaphoreType.DMA((cols // (2 * WIDE), 2))] * fetch,
        compiler_params=LARGE,
        cost_estimate=cost,
        name="forward" + "_fetch" * fetch + "_down" * down,
    )(*earlier, *xs, *weights, *([wd] * down), *([other] * pair))


def turn_kernel(_, __, *refs):
    refs[8][: refs[0].shape[1], :] = stacked(refs[0:4]).T.astype(BF16)
    refs[8][refs[0].shape[1] :, :] = stacked(refs[4:8]).T.astype(BF16)


def turn(own, sib, xs, share):
    part = xs[0].shape[0]
    rows = len(xs) * part
    return pl.pallas_call(
        turn_kernel,
        grid_spec=pltpu.PrefetchScalarGridSpec(
            num_scalar_prefetch=2,
            grid=(1,),
            in_specs=[pl.BlockSpec((part, share), lambda j, a, b: (0, a[0]))] * 4
            + [pl.BlockSpec((part, share), lambda j, a, b: (0, b[0]))] * 4,
            out_specs=pl.BlockSpec((2 * share, rows), lambda j, a, b: (0, 0)),
        ),
        out_shape=jax.ShapeDtypeStruct((2 * share, rows), BF16),
        compiler_params=SMALL,
        cost_estimate=CHEAP,
        name="turn",
    )(own, sib, *xs, *xs)


def slopes_kernel(n, *refs):
    gs, acts, coefs = refs[:n], refs[n : 2 * n], refs[2 * n : 3 * n]
    wdt_ref, dg_ref, du_ref, g_ref = refs[3 * n :]
    part = gs[0].shape[0]
    for i in range(n):
        g_ref[i * part : (i + 1) * part, :] = gs[i][...]
    for start in range(0, wdt_ref.shape[1], STRIP):
        cols = slice(start, start + STRIP)
        d_hidden = jnp.dot(g_ref[...], wdt_ref[:, cols], preferred_element_type=F32)
        for i in range(n):
            rows = slice(i * part, (i + 1) * part)
            dg_ref[rows, cols] = (d_hidden[rows] * coefs[i][:, cols].astype(F32)).astype(BF16)
            du_ref[rows, cols] = (d_hidden[rows] * acts[i][:, cols].astype(F32)).astype(BF16)


def slopes(gs, acts, coefs, wdt):
    n, (part, width) = len(gs), gs[0].shape
    return pl.pallas_call(
        functools.partial(slopes_kernel, n),
        out_shape=[jax.ShapeDtypeStruct((n * part, wdt.shape[1]), BF16)] * 2,
        in_specs=[HERE] * (3 * n + 1),
        scratch_shapes=[pltpu.VMEM((n * part, width), BF16)],
        compiler_params=LARGE,
        cost_estimate=CHEAP,
        name="slopes",
    )(*gs, *acts, *coefs, wdt)


def backward_kernel(first, xt_ref, g_ref, act_ref, coef_ref, dg_ref, du_ref, wdt_ref, *refs):
    own_ref, sib_ref = refs[-2:]
    share = own_ref.shape[0] // 2
    for start in range(0, own_ref.shape[1], STRIP):
        here = slice(start, start + STRIP)
        cols = slice(first + start, first + start + STRIP)
        d_hidden = jnp.dot(g_ref[...], wdt_ref[:, cols], preferred_element_type=F32)
        for row, factor_ref, known_ref in ((0, coef_ref, dg_ref), (share, act_ref, du_ref)):
            d_cols = (d_hidden * factor_ref[:, cols].astype(F32)).astype(BF16)
            d_cols = jnp.concatenate([known_ref[:, cols], d_cols], axis=0)
            total = jnp.dot(xt_ref[...], d_cols, preferred_element_type=F32).astype(BF16)
            own_ref[row : row + share, here] = total[:share]
            sib_ref[row : row + share, here] = total[share:]


def backward(xt, g, act, coef, dg, du, wdt, first, cols, earlier=()):
    return pl.pallas_call(
        functools.partial(backward_kernel, first),
        out_shape=[jax.ShapeDtypeStruct((xt.shape[0], cols), BF16)] * 2,
        in_specs=[HERE] * 7 + [ANYWHERE] * len(earlier),
        compiler_params=LARGE,
        cost_estimate=DEAR,
        name="backward",
    )(xt, g, act, coef, dg, du, wdt, *earlier)


def finish_kernel(spans, more, unused, *refs):
    refs = refs[unused:]
    n = len(spans)
    pairs = [refs[2 * i : 2 * i + 2] for i in range(n)]
    gate_ref, up_ref, gate, up, sems = refs[2 * n + 2 * more :]
    share = gate_ref.shape[0]
    low = spans[0][0]
    copies = []
    for i, ((first, cols), (own, got)) in enumerate(zip(spans, pairs)):
        for j, (target, held) in enumerate(((gate_ref, gate), (up_ref, up))):
            rows = slice(j * share, (j + 1) * share)
            here = pl.ds(first - low, cols)
            held[:, here] = (own[rows, :].astype(F32) + got[rows, :].astype(F32)).astype(BF16)
            copies.append(
                pltpu.make_async_copy(held.at[:, here], target.at[:, pl.ds(first, cols)], sems.at[i, j])
            )
            copies[-1].start()
    for copy in copies:
        copy.wait()


def finish(owns, gots, firsts, width, held=(), earlier=()):
    share = owns[0].shape[0] // 2
    spans = tuple((first, own.shape[1]) for first, own in zip(firsts, owns))
    total = sum(cols for _, cols in spans)
    n, more = len(owns), len(held) > 0
    return pl.pallas_call(
        functools.partial(finish_kernel, spans, more, len(earlier)),
        out_shape=[jax.ShapeDtypeStruct((share, width), BF16)] * 2,
        in_specs=[AFAR] * len(earlier) + [HERE] * (2 * n) + [ANYWHERE] * (2 * more),
        out_specs=[ANYWHERE] * 2,
        scratch_shapes=[pltpu.VMEM((share, total), BF16)] * 2 + [pltpu.SemaphoreType.DMA((n, 2))],
        input_output_aliases={len(earlier) + 2 * n: 0, len(earlier) + 2 * n + 1: 1} if more else {},
        compiler_params=SMALL,
        cost_estimate=CHEAP,
        name="finish",
    )(*[kept(v) for v in earlier], *[v for both in zip(owns, gots) for v in both], *held)


def split_kernel(*refs):
    blocks = [r[...].astype(F32) for r in refs[:EXPERTS]]
    refs[-2][...] = jnp.concatenate([b[:CAP] for b in blocks], axis=0).astype(BF16)
    refs[-1][...] = jnp.concatenate([b[CAP:] for b in blocks], axis=0).astype(BF16)


def split(blocks, earlier):
    width = blocks[0].shape[1]
    return pl.pallas_call(
        split_kernel,
        out_shape=[jax.ShapeDtypeStruct((EXPERTS * CAP, width), BF16)] * 2,
        in_specs=[HERE] * EXPERTS + [ANYWHERE] * len(earlier),
        compiler_params=SMALL,
        cost_estimate=CHEAP,
        name="split",
    )(*blocks, *earlier)


def unpack_kernel(placer_ref, mine_ref, got_ref, *refs):
    chosen = placer_ref[...].astype(F32).T.astype(BF16)
    total = jnp.dot(chosen, mine_ref[...], preferred_element_type=F32)
    total += jnp.dot(chosen, got_ref[...], preferred_element_type=F32)
    refs[-1][...] = total.astype(BF16)


def unpack(placer, mine, got, earlier):
    return pl.pallas_call(
        unpack_kernel,
        out_shape=jax.ShapeDtypeStruct((placer.shape[1], mine.shape[1]), BF16),
        in_specs=[HERE] * 3 + [AFAR] * len(earlier),
        compiler_params=SMALL,
        cost_estimate=DEAR,
        name="unpack",
    )(placer, mine, got, *[kept(v) for v in earlier])


def swap(value, axis):
    return lax.ppermute(value, axis, [(0, 1), (1, 0)])


def across_planes(blocks):
    return [blocks[0]] + [
        lax.ppermute(blocks[k], "arch", [(i, i ^ k) for i in range(EXPERTS)]) for k in range(1, EXPERTS)
    ]


def after(values, earlier):
    n = len(values)
    return list(lax.optimization_barrier((*values, *earlier))[:n])


def gathering(designs, archetype, w_gate, w_up, w_down, cotangent):
    far, core = lax.axis_index("far"), lax.axis_index("core")
    scalars = [lax.axis_index("arch"), 2 * far + core, 2 * far + 1 - core]
    scalars = [v.astype(jnp.int32)[None] for v in scalars]
    tokens, width = designs.shape
    share = width // 4
    placer, *blocks = pack(scalars, archetype.reshape(1, tokens), designs, cotangent)
    wd, wdt = flip(after([w_down], [placer])[0])

    x_own = join(across_planes(blocks[:EXPERTS]))
    moved = across_planes(relay(blocks[EXPERTS:], [wdt]))
    x_far, x_near = swap(x_own, "far"), swap(x_own, "half")

    wg, wu = w_gate, w_up
    act0, coef0, share_own = forward([x_own], wg, wu, wd)
    g_own = join(moved, [act0])
    g_far, g_near = swap(g_own, "far"), swap(g_own, "half")
    act1, coef1, *shares = forward([x_near], wg, wu, wd, other=share_own)
    (x_pass,) = relay([x_near], [mark(act1, x_far), g_far])
    (g_pass,) = relay([g_far], [x_pass, g_near])
    x_corner, g_corner = swap(x_pass, "far"), swap(g_pass, "half")
    returned = across_planes(shares)
    act2, coef2 = forward([x_far], wg, wu, earlier=[g_pass], cost=DEAR)
    dg, du = slopes([g_own, g_near, g_far], [act0, act1, act2], [coef0, coef1, coef2], wdt)
    act3, coef3 = forward([x_corner], wg, wu, earlier=[dg])
    mine, theirs = split(returned, [act3])
    got = swap(theirs, "half")
    xt = turn(*scalars[1:], [x_own, x_near, x_far, x_corner], share)

    rest = (xt, g_corner, act3, coef3, dg, du, wdt)
    cols = w_down.shape[0]
    cut = cols // 2
    own0, sib0 = backward(*rest, 0, cut)
    own1, sib1 = backward(*rest, cut, cols - cut, [own0])
    got0, got1 = swap(sib0, "core"), swap(sib1, "core")
    held = finish([own0], [got0], (0,), cols)
    outputs = unpack(placer, mine, got, held[:1])
    grad_gate, grad_up = finish([own1], [got1], (cut,), cols, held)
    return outputs, grad_gate, grad_up


def reducing(designs, archetype, w_gate, w_up, w_down, cotangent):
    width = designs.shape[1]
    owners = lax.axis_size("expert")
    sharers = owners // EXPERTS
    hidden_cols = w_gate.shape[1]
    labels = archetype[:, 0]
    onehot = (labels[:, None] == jnp.arange(EXPERTS, dtype=jnp.int32)[None, :]).astype(jnp.int32)
    ranks = jnp.cumsum(onehot, axis=0) - onehot
    target = labels * CAP + jnp.sum(ranks * onehot, axis=1)
    placer = (jnp.arange(EXPERTS * CAP, dtype=jnp.int32)[:, None] == target[None, :]).astype(BF16)
    received = []
    for rows in (designs, cotangent):
        packed = jnp.dot(placer, rows, preferred_element_type=F32).astype(BF16)
        send = jnp.repeat(packed.reshape(EXPERTS, CAP, width), sharers, axis=0)
        received.append(
            lax.all_to_all(send, "expert", split_axis=0, concat_axis=0, tiled=True).reshape(
                owners * CAP, width
            )
        )
    flat_x, flat_g = received
    gate = jnp.dot(flat_x, w_gate, preferred_element_type=F32)
    up = jnp.dot(flat_x, w_up, preferred_element_type=F32)
    act, slope = silu_parts(gate)
    hidden = (act * up).astype(BF16)
    partial_value = (
        jnp.dot(hidden, w_down, preferred_element_type=F32).astype(BF16).reshape(owners, CAP, width)
    )
    returned = lax.all_to_all(partial_value, "expert", split_axis=0, concat_axis=0, tiled=True)
    summed = jnp.sum(returned.astype(F32).reshape(EXPERTS, sharers, CAP, width), axis=1).reshape(
        EXPERTS * CAP, width
    )
    outputs = jnp.take(summed, target, axis=0).astype(BF16)
    d_hidden = contract_cols(flat_g, w_down)
    d_gate = (d_hidden * up * slope).astype(BF16)
    d_up = (d_hidden * act).astype(BF16)
    grads = jnp.concatenate([contract_rows(flat_x, d_gate), contract_rows(flat_x, d_up)], axis=1)
    mine = lax.psum_scatter(grads.astype(BF16), "dp", scatter_dimension=0, tiled=True)
    return outputs, mine[:, :hidden_cols], mine[:, hidden_cols:]


def solution(mesh):
    dp, owners = mesh.devices.shape
    if (dp, owners) == (4, 2 * EXPERTS):
        rows, cols = ("far", "core"), ("arch", "half")
        mesh = Mesh(mesh.devices.reshape(2, 2, EXPERTS, 2), rows + cols)
        body = gathering
    else:
        rows, cols = ("dp",), ("expert",)
        body = reducing
    tokens = P(rows + cols, None)
    return jax.shard_map(
        body,
        mesh=mesh,
        in_specs=(tokens, tokens, P(None, cols), P(None, cols), P(cols, None), tokens),
        out_specs=(tokens, P(rows, cols), P(rows, cols)),
        check_vma=False,
    )
```

```python
import functools

import jax
import jax.numpy as jnp
from jax import lax
from jax.experimental import pallas as pl
from jax.experimental.pallas import tpu as pltpu
from jax.sharding import Mesh
from jax.sharding import PartitionSpec as P

EXPERTS = 4
CAP = 36
WIDE = 1024
STRIP = 512
SLICE = 256
MIB = 1024 * 1024
LARGE = pltpu.CompilerParams(vmem_limit_bytes=16 * MIB)
SMALL = pltpu.CompilerParams(vmem_limit_bytes=12 * MIB)
CHEAP = pl.CostEstimate(flops=0, bytes_accessed=0, transcendentals=0)
DEAR = pl.CostEstimate(flops=20_000_000_000, bytes_accessed=0, transcendentals=0)
F32 = jnp.float32
BF16 = jnp.bfloat16
HERE = pl.BlockSpec(memory_space=pltpu.VMEM)
AFAR = pl.BlockSpec(memory_space=pltpu.HBM)
ANYWHERE = pl.BlockSpec(memory_space=pl.ANY)


def silu_parts(gate):
    sigma = 0.5 * jnp.tanh(0.5 * gate) + 0.5
    return (gate * sigma, sigma * (1.0 + gate * (1.0 - sigma)))


def contract_rows(left, right):
    return lax.dot_general(left, right, (((0,), (0,)), ((), ())), preferred_element_type=F32)


def contract_cols(left, right):
    return lax.dot_general(left, right, (((1,), (1,)), ((), ())), preferred_element_type=F32)


def stacked(refs):
    return jnp.concatenate([r[...].astype(F32) for r in refs], axis=0)


def kept(value):
    return pltpu.with_memory_space_constraint(value, pltpu.HBM)


def pack_kernel(plane_ref, _, __, kind_ref, x_ref, g_ref, placer_ref, *refs):
    outs, (kind, x, g, sems) = refs[: 2 * EXPERTS], refs[2 * EXPERTS :]
    copies = [
        pltpu.make_async_copy(source, target, sems.at[i])
        for i, (source, target) in enumerate(((kind_ref, kind), (x_ref, x), (g_ref, g)))
    ]
    for copy in copies:
        copy.start()
    tokens = kind.shape[1]
    copies[0].wait()
    key = kind[...] ^ plane_ref[0]
    onehot = (key == lax.broadcasted_iota(jnp.int32, (8, tokens), 0)).astype(F32)
    before = lax.broadcasted_iota(jnp.int32, (tokens, tokens), 0) < lax.broadcasted_iota(
        jnp.int32, (tokens, tokens), 1
    )
    ranks = jnp.dot(onehot.astype(BF16), before.astype(BF16), preferred_element_type=F32)
    rank = jnp.sum(ranks * onehot, axis=0, keepdims=True).astype(jnp.int32)
    place = key * CAP + rank
    slots = EXPERTS * CAP
    placer = (place == lax.broadcasted_iota(jnp.int32, (slots, tokens), 0)).astype(F32).astype(BF16)
    placer_ref[...] = placer
    for copy, source, first in ((copies[1], x, 0), (copies[2], g, EXPERTS)):
        copy.wait()
        packed = jnp.dot(placer, source[...], preferred_element_type=F32)
        for k in range(EXPERTS):
            outs[first + k][...] = packed[k * CAP : (k + 1) * CAP].astype(BF16)


def pack(scalars, kind, x, g):
    tokens, width = x.shape
    return pl.pallas_call(
        pack_kernel,
        out_shape=[jax.ShapeDtypeStruct((EXPERTS * CAP, tokens), BF16)]
        + [jax.ShapeDtypeStruct((CAP, width), BF16)] * (2 * EXPERTS),
        in_specs=[pl.BlockSpec(memory_space=pltpu.SMEM)] * 3 + [AFAR] * 3,
        scratch_shapes=[
            pltpu.VMEM((1, tokens), jnp.int32),
            pltpu.VMEM((tokens, width), BF16),
            pltpu.VMEM((tokens, width), BF16),
            pltpu.SemaphoreType.DMA((3,)),
        ],
        compiler_params=SMALL,
        cost_estimate=DEAR,
        name="pack",
    )(*scalars, kept(kind), kept(x), kept(g))


def join_kernel(*refs):
    refs[-1][...] = stacked(refs[-2 : -2 - EXPERTS : -1]).astype(BF16)


def join(blocks, earlier=()):
    width = blocks[0].shape[1]
    return pl.pallas_call(
        join_kernel,
        out_shape=jax.ShapeDtypeStruct((EXPERTS * CAP, width), BF16),
        in_specs=[ANYWHERE] * len(earlier) + [HERE] * EXPERTS,
        compiler_params=SMALL,
        cost_estimate=CHEAP,
        name="join",
    )(*earlier, *blocks[::-1])


def relay_kernel(n, *refs):
    for i in range(n):
        refs[len(refs) - n + i][...] = refs[i][...]


def relay(values, earlier):
    n = len(values)
    return pl.pallas_call(
        functools.partial(relay_kernel, n),
        out_shape=[jax.ShapeDtypeStruct(v.shape, v.dtype) for v in values],
        in_specs=[HERE] * n + [ANYWHERE] * len(earlier),
        compiler_params=SMALL,
        cost_estimate=CHEAP,
        name="relay",
    )(*values, *earlier)


def mark_kernel(value_ref, _, mark_ref):
    mark_ref[...] = value_ref[: mark_ref.shape[0], : mark_ref.shape[1]]


def mark(value, earlier):
    return pl.pallas_call(
        mark_kernel,
        out_shape=jax.ShapeDtypeStruct((16, 128), value.dtype),
        in_specs=[HERE, ANYWHERE],
        compiler_params=SMALL,
        cost_estimate=CHEAP,
        name="mark",
    )(value, earlier)


def flip_kernel(source_ref, *refs):
    flipped_ref = refs[-1]
    for j in range(source_ref.shape[0] // SLICE):
        rows = slice(j * SLICE, (j + 1) * SLICE)
        flipped_ref[:, rows] = source_ref[rows, :].T


def flip(value, earlier):
    return pl.pallas_call(
        flip_kernel,
        out_shape=pltpu.VMEM(value.shape[::-1], value.dtype),
        in_specs=[HERE] + [ANYWHERE] * len(earlier),
        out_specs=HERE,
        compiler_params=SMALL,
        cost_estimate=CHEAP,
        name="flip",
    )(value, *earlier)


def forward_kernel(n, fetch, down, pair, unused, *refs):
    refs = list(refs[unused:])
    xs = [refs.pop(0) for _ in range(n)]
    wg_ref, wu_ref = refs.pop(0), refs.pop(0)
    wd_ref = refs.pop(0) if down else None
    other_ref = refs.pop(0) if pair else None
    act_ref, coef_ref = refs.pop(0), refs.pop(0)
    shares = [refs.pop(0) for _ in range(EXPERTS if pair else down)]
    if fetch:
        sources, sems = (wg_ref, wu_ref), refs.pop()
        wg_ref, wu_ref = refs.pop(0), refs.pop(0)
    acc_ref = refs.pop(0) if down else None
    part = xs[0].shape[0]
    x_ref = xs[0]
    if n > 1:
        x_ref = refs.pop(0)
        for i in range(n):
            x_ref[i * part : (i + 1) * part, :] = xs[i][...]
    steps = wg_ref.shape[1] // (2 * WIDE)

    def copies(j):
        cols = pl.ds(pl.multiple_of(j * (2 * WIDE), (2 * WIDE)), (2 * WIDE))
        return [
            pltpu.make_async_copy(source.at[:, cols], target.at[:, cols], sems.at[j, i])
            for i, (source, target) in enumerate(zip(sources, (wg_ref, wu_ref)))
        ]

    if fetch:
        for j in range(steps):
            for copy in copies(j):
                copy.start()
    if down:
        acc_ref[...] = jnp.zeros_like(acc_ref)

    @pl.loop(0, steps)
    def _(j):
        if fetch:
            for copy in copies(j):
                copy.wait()
        for i in range(2):
            cols = pl.ds(pl.multiple_of(j * (2 * WIDE) + i * WIDE, WIDE), WIDE)
            gate = jnp.dot(x_ref[...], wg_ref[:, cols], preferred_element_type=F32)
            up = jnp.dot(x_ref[...], wu_ref[:, cols], preferred_element_type=F32)
            act, slope = silu_parts(gate)
            act_ref[:, cols] = act.astype(BF16)
            coef_ref[:, cols] = (up * slope).astype(BF16)
            if down:
                hidden = (act[:part] * up[:part]).astype(BF16)
                acc_ref[...] += jnp.dot(hidden, wd_ref[cols, :], preferred_element_type=F32)

    if pair:
        other = other_ref[...].astype(F32)
        for k in range(EXPERTS):
            rows = slice(k * CAP, (k + 1) * CAP)
            block = jnp.concatenate([other[rows], acc_ref[rows, :]], axis=0).astype(BF16)
            shares[k][...] = block
    elif down:
        shares[0][...] = acc_ref[...].astype(BF16)


def forward(xs, wg, wu, wd=None, other=None, fetch=False, earlier=(), cost=CHEAP):
    n, (part, width), cols = len(xs), xs[0].shape, wg.shape[1]
    rows = n * part
    down, pair = wd is not None, other is not None
    shares = [jax.ShapeDtypeStruct((part, width), BF16)] * down
    if pair:
        shares = [jax.ShapeDtypeStruct((2 * CAP, width), BF16)] * EXPERTS
    weights = [kept(wg), kept(wu)] if fetch else [wg, wu]
    return pl.pallas_call(
        functools.partial(forward_kernel, n, fetch, down, pair, len(earlier)),
        out_shape=[jax.ShapeDtypeStruct((rows, cols), BF16)] * 2
        + shares
        + [pltpu.VMEM(wg.shape, wg.dtype)] * (2 * fetch),
        in_specs=[ANYWHERE] * len(earlier)
        + [HERE] * n
        + [AFAR if fetch else HERE] * 2
        + [HERE] * (down + pair),
        scratch_shapes=[pltpu.VMEM((part, width), F32)] * down
        + [pltpu.VMEM((rows, width), BF16)] * (n > 1)
        + [pltpu.SemaphoreType.DMA((cols // (2 * WIDE), 2))] * fetch,
        compiler_params=LARGE,
        cost_estimate=cost,
        name="forward" + "_fetch" * fetch + "_down" * down,
    )(*earlier, *xs, *weights, *([wd] * down), *([other] * pair))


def turn_kernel(_, __, *refs):
    refs[8][: refs[0].shape[1], :] = stacked(refs[0:4]).T.astype(BF16)
    refs[8][refs[0].shape[1] :, :] = stacked(refs[4:8]).T.astype(BF16)


def turn(own, sib, xs, share):
    part = xs[0].shape[0]
    rows = len(xs) * part
    return pl.pallas_call(
        turn_kernel,
        grid_spec=pltpu.PrefetchScalarGridSpec(
            num_scalar_prefetch=2,
            grid=(1,),
            in_specs=[pl.BlockSpec((part, share), lambda j, a, b: (0, a[0]))] * 4
            + [pl.BlockSpec((part, share), lambda j, a, b: (0, b[0]))] * 4,
            out_specs=pl.BlockSpec((2 * share, rows), lambda j, a, b: (0, 0)),
        ),
        out_shape=jax.ShapeDtypeStruct((2 * share, rows), BF16),
        compiler_params=SMALL,
        cost_estimate=CHEAP,
        name="turn",
    )(own, sib, *xs, *xs)


def slopes_kernel(n, *refs):
    gs, acts, coefs = refs[:n], refs[n : 2 * n], refs[2 * n : 3 * n]
    wdt_ref, dg_ref, du_ref, g_ref = refs[3 * n :]
    part = gs[0].shape[0]
    for i in range(n):
        g_ref[i * part : (i + 1) * part, :] = gs[i][...]
    for start in range(0, wdt_ref.shape[1], STRIP):
        cols = slice(start, start + STRIP)
        d_hidden = jnp.dot(g_ref[...], wdt_ref[:, cols], preferred_element_type=F32)
        for i in range(n):
            rows = slice(i * part, (i + 1) * part)
            dg_ref[rows, cols] = (d_hidden[rows] * coefs[i][:, cols].astype(F32)).astype(BF16)
            du_ref[rows, cols] = (d_hidden[rows] * acts[i][:, cols].astype(F32)).astype(BF16)


def slopes(gs, acts, coefs, wdt):
    n, (part, width) = len(gs), gs[0].shape
    return pl.pallas_call(
        functools.partial(slopes_kernel, n),
        out_shape=[jax.ShapeDtypeStruct((n * part, wdt.shape[1]), BF16)] * 2,
        in_specs=[HERE] * (3 * n + 1),
        scratch_shapes=[pltpu.VMEM((n * part, width), BF16)],
        compiler_params=LARGE,
        cost_estimate=CHEAP,
        name="slopes",
    )(*gs, *acts, *coefs, wdt)


def backward_kernel(first, xt_ref, g_ref, act_ref, coef_ref, dg_ref, du_ref, wdt_ref, *refs):
    own_ref, sib_ref = refs[-2:]
    share = own_ref.shape[0] // 2
    for start in range(0, own_ref.shape[1], STRIP):
        here = slice(start, start + STRIP)
        cols = slice(first + start, first + start + STRIP)
        d_hidden = jnp.dot(g_ref[...], wdt_ref[:, cols], preferred_element_type=F32)
        for row, factor_ref, known_ref in ((0, coef_ref, dg_ref), (share, act_ref, du_ref)):
            d_cols = (d_hidden * factor_ref[:, cols].astype(F32)).astype(BF16)
            d_cols = jnp.concatenate([known_ref[:, cols], d_cols], axis=0)
            total = jnp.dot(xt_ref[...], d_cols, preferred_element_type=F32).astype(BF16)
            own_ref[row : row + share, here] = total[:share]
            sib_ref[row : row + share, here] = total[share:]


def backward(xt, g, act, coef, dg, du, wdt, first, cols, earlier=()):
    return pl.pallas_call(
        functools.partial(backward_kernel, first),
        out_shape=[jax.ShapeDtypeStruct((xt.shape[0], cols), BF16)] * 2,
        in_specs=[HERE] * 7 + [ANYWHERE] * len(earlier),
        compiler_params=LARGE,
        cost_estimate=DEAR,
        name="backward",
    )(xt, g, act, coef, dg, du, wdt, *earlier)


def finish_kernel(spans, more, unused, *refs):
    refs = refs[unused:]
    n = len(spans)
    pairs = [refs[2 * i : 2 * i + 2] for i in range(n)]
    gate_ref, up_ref, gate, up, sems = refs[2 * n + 2 * more :]
    share = gate_ref.shape[0]
    low = spans[0][0]
    copies = []
    for i, ((first, cols), (own, got)) in enumerate(zip(spans, pairs)):
        for j, (target, held) in enumerate(((gate_ref, gate), (up_ref, up))):
            rows = slice(j * share, (j + 1) * share)
            here = pl.ds(first - low, cols)
            held[:, here] = (own[rows, :].astype(F32) + got[rows, :].astype(F32)).astype(BF16)
            copies.append(
                pltpu.make_async_copy(held.at[:, here], target.at[:, pl.ds(first, cols)], sems.at[i, j])
            )
            copies[-1].start()
    for copy in copies:
        copy.wait()


def finish(owns, gots, firsts, width, held=(), earlier=()):
    share = owns[0].shape[0] // 2
    spans = tuple((first, own.shape[1]) for first, own in zip(firsts, owns))
    total = sum(cols for _, cols in spans)
    n, more = len(owns), len(held) > 0
    return pl.pallas_call(
        functools.partial(finish_kernel, spans, more, len(earlier)),
        out_shape=[jax.ShapeDtypeStruct((share, width), BF16)] * 2,
        in_specs=[AFAR] * len(earlier) + [HERE] * (2 * n) + [ANYWHERE] * (2 * more),
        out_specs=[ANYWHERE] * 2,
        scratch_shapes=[pltpu.VMEM((share, total), BF16)] * 2 + [pltpu.SemaphoreType.DMA((n, 2))],
        input_output_aliases={len(earlier) + 2 * n: 0, len(earlier) + 2 * n + 1: 1} if more else {},
        compiler_params=SMALL,
        cost_estimate=CHEAP,
        name="finish",
    )(*[kept(v) for v in earlier], *[v for both in zip(owns, gots) for v in both], *held)


def split_kernel(*refs):
    blocks = [r[...].astype(F32) for r in refs[:EXPERTS]]
    refs[-2][...] = jnp.concatenate([b[:CAP] for b in blocks], axis=0).astype(BF16)
    refs[-1][...] = jnp.concatenate([b[CAP:] for b in blocks], axis=0).astype(BF16)


def split(blocks, earlier):
    width = blocks[0].shape[1]
    return pl.pallas_call(
        split_kernel,
        out_shape=[jax.ShapeDtypeStruct((EXPERTS * CAP, width), BF16)] * 2,
        in_specs=[HERE] * EXPERTS + [ANYWHERE] * len(earlier),
        compiler_params=SMALL,
        cost_estimate=CHEAP,
        name="split",
    )(*blocks, *earlier)


def unpack_kernel(placer_ref, mine_ref, got_ref, *refs):
    chosen = placer_ref[...].astype(F32).T.astype(BF16)
    total = jnp.dot(chosen, mine_ref[...], preferred_element_type=F32)
    total += jnp.dot(chosen, got_ref[...], preferred_element_type=F32)
    refs[-1][...] = total.astype(BF16)


def unpack(placer, mine, got, earlier):
    return pl.pallas_call(
        unpack_kernel,
        out_shape=jax.ShapeDtypeStruct((placer.shape[1], mine.shape[1]), BF16),
        in_specs=[HERE] * 3 + [AFAR] * len(earlier),
        compiler_params=SMALL,
        cost_estimate=DEAR,
        name="unpack",
    )(placer, mine, got, *[kept(v) for v in earlier])


def swap(value, axis):
    return lax.ppermute(value, axis, [(0, 1), (1, 0)])


def across_planes(blocks):
    return [blocks[0]] + [
        lax.ppermute(blocks[k], "arch", [(i, i ^ k) for i in range(EXPERTS)]) for k in range(1, EXPERTS)
    ]


def after(values, earlier):
    n = len(values)
    return list(lax.optimization_barrier((*values, *earlier))[:n])


def gathering(designs, archetype, w_gate, w_up, w_down, cotangent):
    far, core = lax.axis_index("far"), lax.axis_index("core")
    scalars = [lax.axis_index("arch"), 2 * far + core, 2 * far + 1 - core]
    scalars = [v.astype(jnp.int32)[None] for v in scalars]
    tokens, width = designs.shape
    share = width // 4
    placer, *blocks = pack(scalars, archetype.reshape(1, tokens), designs, cotangent)
    wd, wdt = w_down, flip(w_down, [placer])

    x_own = join(across_planes(blocks[:EXPERTS]))
    moved = across_planes(relay(blocks[EXPERTS:], [wdt]))
    x_far, x_near = swap(x_own, "far"), swap(x_own, "half")

    wg, wu = w_gate, w_up
    act0, coef0, share_own = forward([x_own], wg, wu, wd)
    g_own = join(moved, [act0])
    g_far, g_near = swap(g_own, "far"), swap(g_own, "half")
    act1, coef1, *shares = forward([x_near], wg, wu, wd, other=share_own)
    (x_pass,) = relay([x_near], [mark(act1, x_far), g_far])
    (g_pass,) = relay([g_far], [x_pass, g_near])
    x_corner, g_corner = swap(x_pass, "far"), swap(g_pass, "half")
    returned = across_planes(shares)
    act2, coef2 = forward([x_far], wg, wu, earlier=[g_pass], cost=DEAR)
    dg, du = slopes([g_own, g_near, g_far], [act0, act1, act2], [coef0, coef1, coef2], wdt)
    act3, coef3 = forward([x_corner], wg, wu, earlier=[dg])
    mine, theirs = split(returned, [act3])
    got = swap(theirs, "half")
    xt = turn(*scalars[1:], [x_own, x_near, x_far, x_corner], share)

    rest = (xt, g_corner, act3, coef3, dg, du, wdt)
    cols = w_down.shape[0]
    cut = cols // 2
    own0, sib0 = backward(*rest, 0, cut)
    own1, sib1 = backward(*rest, cut, cols - cut, [own0])
    got0, got1 = swap(sib0, "core"), swap(sib1, "core")
    held = finish([own0], [got0], (0,), cols)
    outputs = unpack(placer, mine, got, held[:1])
    grad_gate, grad_up = finish([own1], [got1], (cut,), cols, held)
    return outputs, grad_gate, grad_up


def reducing(designs, archetype, w_gate, w_up, w_down, cotangent):
    width = designs.shape[1]
    owners = lax.axis_size("expert")
    sharers = owners // EXPERTS
    hidden_cols = w_gate.shape[1]
    labels = archetype[:, 0]
    onehot = (labels[:, None] == jnp.arange(EXPERTS, dtype=jnp.int32)[None, :]).astype(jnp.int32)
    ranks = jnp.cumsum(onehot, axis=0) - onehot
    target = labels * CAP + jnp.sum(ranks * onehot, axis=1)
    placer = (jnp.arange(EXPERTS * CAP, dtype=jnp.int32)[:, None] == target[None, :]).astype(BF16)
    received = []
    for rows in (designs, cotangent):
        packed = jnp.dot(placer, rows, preferred_element_type=F32).astype(BF16)
        send = jnp.repeat(packed.reshape(EXPERTS, CAP, width), sharers, axis=0)
        received.append(
            lax.all_to_all(send, "expert", split_axis=0, concat_axis=0, tiled=True).reshape(
                owners * CAP, width
            )
        )
    flat_x, flat_g = received
    gate = jnp.dot(flat_x, w_gate, preferred_element_type=F32)
    up = jnp.dot(flat_x, w_up, preferred_element_type=F32)
    act, slope = silu_parts(gate)
    hidden = (act * up).astype(BF16)
    partial_value = (
        jnp.dot(hidden, w_down, preferred_element_type=F32).astype(BF16).reshape(owners, CAP, width)
    )
    returned = lax.all_to_all(partial_value, "expert", split_axis=0, concat_axis=0, tiled=True)
    summed = jnp.sum(returned.astype(F32).reshape(EXPERTS, sharers, CAP, width), axis=1).reshape(
        EXPERTS * CAP, width
    )
    outputs = jnp.take(summed, target, axis=0).astype(BF16)
    d_hidden = contract_cols(flat_g, w_down)
    d_gate = (d_hidden * up * slope).astype(BF16)
    d_up = (d_hidden * act).astype(BF16)
    grads = jnp.concatenate([contract_rows(flat_x, d_gate), contract_rows(flat_x, d_up)], axis=1)
    mine = lax.psum_scatter(grads.astype(BF16), "dp", scatter_dimension=0, tiled=True)
    return outputs, mine[:, :hidden_cols], mine[:, hidden_cols:]


def solution(mesh):
    dp, owners = mesh.devices.shape
    if (dp, owners) == (4, 2 * EXPERTS):
        rows, cols = ("far", "core"), ("arch", "half")
        mesh = Mesh(mesh.devices.reshape(2, 2, EXPERTS, 2), rows + cols)
        body = gathering
    else:
        rows, cols = ("dp",), ("expert",)
        body = reducing
    tokens = P(rows + cols, None)
    return jax.shard_map(
        body,
        mesh=mesh,
        in_specs=(tokens, tokens, P(None, cols), P(None, cols), P(cols, None), tokens),
        out_specs=(tokens, P(rows, cols), P(rows, cols)),
        check_vma=False,
    )
```

```python
import functools

import jax
import jax.numpy as jnp
from jax import lax
from jax.experimental import pallas as pl
from jax.experimental.pallas import tpu as pltpu
from jax.sharding import Mesh
from jax.sharding import PartitionSpec as P

EXPERTS = 4
CAP = 36
WIDE = 1024
STRIP = 512
SLICE = 256
MIB = 1024 * 1024
LARGE = pltpu.CompilerParams(vmem_limit_bytes=16 * MIB)
SMALL = pltpu.CompilerParams(vmem_limit_bytes=12 * MIB)
CHEAP = pl.CostEstimate(flops=0, bytes_accessed=0, transcendentals=0)
DEAR = pl.CostEstimate(flops=20_000_000_000, bytes_accessed=0, transcendentals=0)
F32 = jnp.float32
BF16 = jnp.bfloat16
HERE = pl.BlockSpec(memory_space=pltpu.VMEM)
AFAR = pl.BlockSpec(memory_space=pltpu.HBM)
ANYWHERE = pl.BlockSpec(memory_space=pl.ANY)


def silu_parts(gate):
    sigma = 0.5 * jnp.tanh(0.5 * gate) + 0.5
    return (gate * sigma, sigma * (1.0 + gate * (1.0 - sigma)))


def contract_rows(left, right):
    return lax.dot_general(left, right, (((0,), (0,)), ((), ())), preferred_element_type=F32)


def contract_cols(left, right):
    return lax.dot_general(left, right, (((1,), (1,)), ((), ())), preferred_element_type=F32)


def stacked(refs):
    return jnp.concatenate([r[...].astype(F32) for r in refs], axis=0)


def kept(value):
    return pltpu.with_memory_space_constraint(value, pltpu.HBM)


def pack_kernel(plane_ref, _, __, kind_ref, x_ref, g_ref, placer_ref, *refs):
    outs, (kind, x, g, sems) = refs[: 2 * EXPERTS], refs[2 * EXPERTS :]
    copies = [
        pltpu.make_async_copy(source, target, sems.at[i])
        for i, (source, target) in enumerate(((kind_ref, kind), (x_ref, x), (g_ref, g)))
    ]
    for copy in copies:
        copy.start()
    tokens = kind.shape[1]
    copies[0].wait()
    key = kind[...] ^ plane_ref[0]
    onehot = (key == lax.broadcasted_iota(jnp.int32, (8, tokens), 0)).astype(F32)
    before = lax.broadcasted_iota(jnp.int32, (tokens, tokens), 0) < lax.broadcasted_iota(
        jnp.int32, (tokens, tokens), 1
    )
    ranks = jnp.dot(onehot.astype(BF16), before.astype(BF16), preferred_element_type=F32)
    rank = jnp.sum(ranks * onehot, axis=0, keepdims=True).astype(jnp.int32)
    place = key * CAP + rank
    slots = EXPERTS * CAP
    placer = (place == lax.broadcasted_iota(jnp.int32, (slots, tokens), 0)).astype(F32).astype(BF16)
    placer_ref[...] = placer
    for copy, source, first in ((copies[1], x, 0), (copies[2], g, EXPERTS)):
        copy.wait()
        packed = jnp.dot(placer, source[...], preferred_element_type=F32)
        for k in range(EXPERTS):
            outs[first + k][...] = packed[k * CAP : (k + 1) * CAP].astype(BF16)


def pack(scalars, kind, x, g):
    tokens, width = x.shape
    return pl.pallas_call(
        pack_kernel,
        out_shape=[jax.ShapeDtypeStruct((EXPERTS * CAP, tokens), BF16)]
        + [jax.ShapeDtypeStruct((CAP, width), BF16)] * (2 * EXPERTS),
        in_specs=[pl.BlockSpec(memory_space=pltpu.SMEM)] * 3 + [AFAR] * 3,
        scratch_shapes=[
            pltpu.VMEM((1, tokens), jnp.int32),
            pltpu.VMEM((tokens, width), BF16),
            pltpu.VMEM((tokens, width), BF16),
            pltpu.SemaphoreType.DMA((3,)),
        ],
        compiler_params=SMALL,
        cost_estimate=DEAR,
        name="pack",
    )(*scalars, kept(kind), kept(x), kept(g))


def join_kernel(order, *refs):
    blocks = refs[-1 - EXPERTS : -1]
    refs[-1][...] = stacked([blocks[order.index(k)] for k in range(EXPERTS)]).astype(BF16)


def join(blocks, order, earlier=()):
    width = blocks[0].shape[1]
    return pl.pallas_call(
        functools.partial(join_kernel, order),
        out_shape=jax.ShapeDtypeStruct((EXPERTS * CAP, width), BF16),
        in_specs=[ANYWHERE] * len(earlier) + [HERE] * EXPERTS,
        compiler_params=SMALL,
        cost_estimate=CHEAP,
        name="join",
    )(*earlier, *[blocks[k] for k in order])


def relay_kernel(n, *refs):
    for i in range(n):
        refs[len(refs) - n + i][...] = refs[i][...]


def relay(values, earlier):
    n = len(values)
    return pl.pallas_call(
        functools.partial(relay_kernel, n),
        out_shape=[jax.ShapeDtypeStruct(v.shape, v.dtype) for v in values],
        in_specs=[HERE] * n + [ANYWHERE] * len(earlier),
        compiler_params=SMALL,
        cost_estimate=CHEAP,
        name="relay",
    )(*values, *earlier)


def mark_kernel(value_ref, _, mark_ref):
    mark_ref[...] = value_ref[: mark_ref.shape[0], : mark_ref.shape[1]]


def mark(value, earlier):
    return pl.pallas_call(
        mark_kernel,
        out_shape=jax.ShapeDtypeStruct((16, 128), value.dtype),
        in_specs=[HERE, ANYWHERE],
        compiler_params=SMALL,
        cost_estimate=CHEAP,
        name="mark",
    )(value, earlier)


def flip_kernel(source_ref, *refs):
    flipped_ref = refs[-1]
    for j in range(source_ref.shape[0] // SLICE):
        rows = slice(j * SLICE, (j + 1) * SLICE)
        flipped_ref[:, rows] = source_ref[rows, :].T


def flip(value, earlier):
    return pl.pallas_call(
        flip_kernel,
        out_shape=pltpu.VMEM(value.shape[::-1], value.dtype),
        in_specs=[HERE] + [ANYWHERE] * len(earlier),
        out_specs=HERE,
        compiler_params=SMALL,
        cost_estimate=CHEAP,
        name="flip",
    )(value, *earlier)


def forward_kernel(n, fetch, down, pair, unused, *refs):
    refs = list(refs[unused:])
    xs = [refs.pop(0) for _ in range(n)]
    wg_ref, wu_ref = refs.pop(0), refs.pop(0)
    wd_ref = refs.pop(0) if down else None
    other_ref = refs.pop(0) if pair else None
    act_ref, coef_ref = refs.pop(0), refs.pop(0)
    shares = [refs.pop(0) for _ in range(EXPERTS if pair else down)]
    if fetch:
        sources, sems = (wg_ref, wu_ref), refs.pop()
        wg_ref, wu_ref = refs.pop(0), refs.pop(0)
    acc_ref = refs.pop(0) if down else None
    part = xs[0].shape[0]
    x_ref = xs[0]
    if n > 1:
        x_ref = refs.pop(0)
        for i in range(n):
            x_ref[i * part : (i + 1) * part, :] = xs[i][...]
    steps = wg_ref.shape[1] // (2 * WIDE)

    def copies(j):
        cols = pl.ds(pl.multiple_of(j * (2 * WIDE), (2 * WIDE)), (2 * WIDE))
        return [
            pltpu.make_async_copy(source.at[:, cols], target.at[:, cols], sems.at[j, i])
            for i, (source, target) in enumerate(zip(sources, (wg_ref, wu_ref)))
        ]

    if fetch:
        for j in range(steps):
            for copy in copies(j):
                copy.start()
    if down:
        acc_ref[...] = jnp.zeros_like(acc_ref)

    @pl.loop(0, steps)
    def _(j):
        if fetch:
            for copy in copies(j):
                copy.wait()
        for i in range(2):
            cols = pl.ds(pl.multiple_of(j * (2 * WIDE) + i * WIDE, WIDE), WIDE)
            gate = jnp.dot(x_ref[...], wg_ref[:, cols], preferred_element_type=F32)
            up = jnp.dot(x_ref[...], wu_ref[:, cols], preferred_element_type=F32)
            act, slope = silu_parts(gate)
            act_ref[:, cols] = act.astype(BF16)
            coef_ref[:, cols] = (up * slope).astype(BF16)
            if down:
                hidden = (act[:part] * up[:part]).astype(BF16)
                acc_ref[...] += jnp.dot(hidden, wd_ref[cols, :], preferred_element_type=F32)

    if pair:
        other = other_ref[...].astype(F32)
        for k in range(EXPERTS):
            rows = slice(k * CAP, (k + 1) * CAP)
            block = jnp.concatenate([other[rows], acc_ref[rows, :]], axis=0).astype(BF16)
            shares[k][...] = block
    elif down:
        shares[0][...] = acc_ref[...].astype(BF16)


def forward(xs, wg, wu, wd=None, other=None, fetch=False, earlier=(), cost=CHEAP):
    n, (part, width), cols = len(xs), xs[0].shape, wg.shape[1]
    rows = n * part
    down, pair = wd is not None, other is not None
    shares = [jax.ShapeDtypeStruct((part, width), BF16)] * down
    if pair:
        shares = [jax.ShapeDtypeStruct((2 * CAP, width), BF16)] * EXPERTS
    weights = [kept(wg), kept(wu)] if fetch else [wg, wu]
    return pl.pallas_call(
        functools.partial(forward_kernel, n, fetch, down, pair, len(earlier)),
        out_shape=[jax.ShapeDtypeStruct((rows, cols), BF16)] * 2
        + shares
        + [pltpu.VMEM(wg.shape, wg.dtype)] * (2 * fetch),
        in_specs=[ANYWHERE] * len(earlier)
        + [HERE] * n
        + [AFAR if fetch else HERE] * 2
        + [HERE] * (down + pair),
        scratch_shapes=[pltpu.VMEM((part, width), F32)] * down
        + [pltpu.VMEM((rows, width), BF16)] * (n > 1)
        + [pltpu.SemaphoreType.DMA((cols // (2 * WIDE), 2))] * fetch,
        compiler_params=LARGE,
        cost_estimate=cost,
        name="forward" + "_fetch" * fetch + "_down" * down,
    )(*earlier, *xs, *weights, *([wd] * down), *([other] * pair))


def turn_kernel(_, __, *refs):
    refs[8][: refs[0].shape[1], :] = stacked(refs[0:4]).T.astype(BF16)
    refs[8][refs[0].shape[1] :, :] = stacked(refs[4:8]).T.astype(BF16)


def turn(own, sib, xs, share):
    part = xs[0].shape[0]
    rows = len(xs) * part
    return pl.pallas_call(
        turn_kernel,
        grid_spec=pltpu.PrefetchScalarGridSpec(
            num_scalar_prefetch=2,
            grid=(1,),
            in_specs=[pl.BlockSpec((part, share), lambda j, a, b: (0, a[0]))] * 4
            + [pl.BlockSpec((part, share), lambda j, a, b: (0, b[0]))] * 4,
            out_specs=pl.BlockSpec((2 * share, rows), lambda j, a, b: (0, 0)),
        ),
        out_shape=jax.ShapeDtypeStruct((2 * share, rows), BF16),
        compiler_params=SMALL,
        cost_estimate=CHEAP,
        name="turn",
    )(own, sib, *xs, *xs)


def slopes_kernel(n, *refs):
    gs, acts, coefs = refs[:n], refs[n : 2 * n], refs[2 * n : 3 * n]
    wdt_ref, dg_ref, du_ref, g_ref = refs[3 * n :]
    part = gs[0].shape[0]
    for i in range(n):
        g_ref[i * part : (i + 1) * part, :] = gs[i][...]
    for start in range(0, wdt_ref.shape[1], STRIP):
        cols = slice(start, start + STRIP)
        d_hidden = jnp.dot(g_ref[...], wdt_ref[:, cols], preferred_element_type=F32)
        for i in range(n):
            rows = slice(i * part, (i + 1) * part)
            dg_ref[rows, cols] = (d_hidden[rows] * coefs[i][:, cols].astype(F32)).astype(BF16)
            du_ref[rows, cols] = (d_hidden[rows] * acts[i][:, cols].astype(F32)).astype(BF16)


def slopes(gs, acts, coefs, wdt):
    n, (part, width) = len(gs), gs[0].shape
    return pl.pallas_call(
        functools.partial(slopes_kernel, n),
        out_shape=[jax.ShapeDtypeStruct((n * part, wdt.shape[1]), BF16)] * 2,
        in_specs=[HERE] * (3 * n + 1),
        scratch_shapes=[pltpu.VMEM((n * part, width), BF16)],
        compiler_params=LARGE,
        cost_estimate=CHEAP,
        name="slopes",
    )(*gs, *acts, *coefs, wdt)


def backward_kernel(first, xt_ref, g_ref, act_ref, coef_ref, dg_ref, du_ref, wdt_ref, *refs):
    own_ref, sib_ref = refs[-2:]
    share = own_ref.shape[0] // 2
    for start in range(0, own_ref.shape[1], STRIP):
        here = slice(start, start + STRIP)
        cols = slice(first + start, first + start + STRIP)
        d_hidden = jnp.dot(g_ref[...], wdt_ref[:, cols], preferred_element_type=F32)
        for row, factor_ref, known_ref in ((0, coef_ref, dg_ref), (share, act_ref, du_ref)):
            d_cols = (d_hidden * factor_ref[:, cols].astype(F32)).astype(BF16)
            d_cols = jnp.concatenate([known_ref[:, cols], d_cols], axis=0)
            total = jnp.dot(xt_ref[...], d_cols, preferred_element_type=F32).astype(BF16)
            own_ref[row : row + share, here] = total[:share]
            sib_ref[row : row + share, here] = total[share:]


def backward(xt, g, act, coef, dg, du, wdt, first, cols, earlier=()):
    return pl.pallas_call(
        functools.partial(backward_kernel, first),
        out_shape=[jax.ShapeDtypeStruct((xt.shape[0], cols), BF16)] * 2,
        in_specs=[HERE] * 7 + [ANYWHERE] * len(earlier),
        compiler_params=LARGE,
        cost_estimate=DEAR,
        name="backward",
    )(xt, g, act, coef, dg, du, wdt, *earlier)


def finish_kernel(spans, more, unused, *refs):
    refs = refs[unused:]
    n = len(spans)
    pairs = [refs[2 * i : 2 * i + 2] for i in range(n)]
    gate_ref, up_ref, gate, up, sems = refs[2 * n + 2 * more :]
    share = gate_ref.shape[0]
    low = spans[0][0]
    copies = []
    for i, ((first, cols), (own, got)) in enumerate(zip(spans, pairs)):
        for j, (target, held) in enumerate(((gate_ref, gate), (up_ref, up))):
            rows = slice(j * share, (j + 1) * share)
            here = pl.ds(first - low, cols)
            held[:, here] = (own[rows, :].astype(F32) + got[rows, :].astype(F32)).astype(BF16)
            copies.append(
                pltpu.make_async_copy(held.at[:, here], target.at[:, pl.ds(first, cols)], sems.at[i, j])
            )
            copies[-1].start()
    for copy in copies:
        copy.wait()


def finish(owns, gots, firsts, width, held=(), earlier=()):
    share = owns[0].shape[0] // 2
    spans = tuple((first, own.shape[1]) for first, own in zip(firsts, owns))
    total = sum(cols for _, cols in spans)
    n, more = len(owns), len(held) > 0
    return pl.pallas_call(
        functools.partial(finish_kernel, spans, more, len(earlier)),
        out_shape=[jax.ShapeDtypeStruct((share, width), BF16)] * 2,
        in_specs=[AFAR] * len(earlier) + [HERE] * (2 * n) + [ANYWHERE] * (2 * more),
        out_specs=[ANYWHERE] * 2,
        scratch_shapes=[pltpu.VMEM((share, total), BF16)] * 2 + [pltpu.SemaphoreType.DMA((n, 2))],
        input_output_aliases={len(earlier) + 2 * n: 0, len(earlier) + 2 * n + 1: 1} if more else {},
        compiler_params=SMALL,
        cost_estimate=CHEAP,
        name="finish",
    )(*[kept(v) for v in earlier], *[v for both in zip(owns, gots) for v in both], *held)


def split_kernel(*refs):
    blocks = [r[...].astype(F32) for r in refs[:EXPERTS]]
    refs[-2][...] = jnp.concatenate([b[:CAP] for b in blocks], axis=0).astype(BF16)
    refs[-1][...] = jnp.concatenate([b[CAP:] for b in blocks], axis=0).astype(BF16)


def split(blocks, earlier):
    width = blocks[0].shape[1]
    return pl.pallas_call(
        split_kernel,
        out_shape=[jax.ShapeDtypeStruct((EXPERTS * CAP, width), BF16)] * 2,
        in_specs=[HERE] * EXPERTS + [ANYWHERE] * len(earlier),
        compiler_params=SMALL,
        cost_estimate=CHEAP,
        name="split",
    )(*blocks, *earlier)


def unpack_kernel(placer_ref, mine_ref, got_ref, *refs):
    chosen = placer_ref[...].astype(F32).T.astype(BF16)
    total = jnp.dot(chosen, mine_ref[...], preferred_element_type=F32)
    total += jnp.dot(chosen, got_ref[...], preferred_element_type=F32)
    refs[-1][...] = total.astype(BF16)


def unpack(placer, mine, got, earlier):
    return pl.pallas_call(
        unpack_kernel,
        out_shape=jax.ShapeDtypeStruct((placer.shape[1], mine.shape[1]), BF16),
        in_specs=[HERE] * 3 + [AFAR] * len(earlier),
        compiler_params=SMALL,
        cost_estimate=DEAR,
        name="unpack",
    )(placer, mine, got, *[kept(v) for v in earlier])


def swap(value, axis):
    return lax.ppermute(value, axis, [(0, 1), (1, 0)])


def across_planes(blocks):
    return [blocks[0]] + [
        lax.ppermute(blocks[k], "arch", [(i, i ^ k) for i in range(EXPERTS)]) for k in range(1, EXPERTS)
    ]


def after(values, earlier):
    n = len(values)
    return list(lax.optimization_barrier((*values, *earlier))[:n])


def gathering(designs, archetype, w_gate, w_up, w_down, cotangent):
    far, core = lax.axis_index("far"), lax.axis_index("core")
    scalars = [lax.axis_index("arch"), 2 * far + core, 2 * far + 1 - core]
    scalars = [v.astype(jnp.int32)[None] for v in scalars]
    tokens, width = designs.shape
    share = width // 4
    placer, *blocks = pack(scalars, archetype.reshape(1, tokens), designs, cotangent)
    wd, wdt = w_down, flip(w_down, [placer])

    x_own = join(across_planes(blocks[:EXPERTS]), (3, 2, 1, 0))
    moved = across_planes(relay(blocks[EXPERTS:], [wdt]))
    x_far, x_near = swap(x_own, "far"), swap(x_own, "half")

    wg, wu = w_gate, w_up
    act0, coef0, share_own = forward([x_own], wg, wu, wd)
    g_own = join(moved, (1, 3, 2, 0), [act0])
    g_far, g_near = swap(g_own, "far"), swap(g_own, "half")
    act1, coef1, *shares = forward([x_near], wg, wu, wd, other=share_own)
    (x_pass,) = relay([x_near], [mark(act1, x_far), g_far])
    (g_pass,) = relay([g_far], [x_pass, g_near])
    x_corner, g_corner = swap(x_pass, "far"), swap(g_pass, "half")
    returned = across_planes(shares)
    act2, coef2 = forward([x_far], wg, wu, earlier=[g_pass], cost=DEAR)
    dg, du = slopes([g_own, g_near, g_far], [act0, act1, act2], [coef0, coef1, coef2], wdt)
    act3, coef3 = forward([x_corner], wg, wu, earlier=[dg])
    mine, theirs = split(returned, [act3])
    got = swap(theirs, "half")
    xt = turn(*scalars[1:], [x_own, x_near, x_far, x_corner], share)

    rest = (xt, g_corner, act3, coef3, dg, du, wdt)
    cols = w_down.shape[0]
    cut = cols // 2
    own0, sib0 = backward(*rest, 0, cut)
    own1, sib1 = backward(*rest, cut, cols - cut, [own0])
    got0, got1 = swap(sib0, "core"), swap(sib1, "core")
    held = finish([own0], [got0], (0,), cols)
    outputs = unpack(placer, mine, got, held[:1])
    grad_gate, grad_up = finish([own1], [got1], (cut,), cols, held)
    return outputs, grad_gate, grad_up


def reducing(designs, archetype, w_gate, w_up, w_down, cotangent):
    width = designs.shape[1]
    owners = lax.axis_size("expert")
    sharers = owners // EXPERTS
    hidden_cols = w_gate.shape[1]
    labels = archetype[:, 0]
    onehot = (labels[:, None] == jnp.arange(EXPERTS, dtype=jnp.int32)[None, :]).astype(jnp.int32)
    ranks = jnp.cumsum(onehot, axis=0) - onehot
    target = labels * CAP + jnp.sum(ranks * onehot, axis=1)
    placer = (jnp.arange(EXPERTS * CAP, dtype=jnp.int32)[:, None] == target[None, :]).astype(BF16)
    received = []
    for rows in (designs, cotangent):
        packed = jnp.dot(placer, rows, preferred_element_type=F32).astype(BF16)
        send = jnp.repeat(packed.reshape(EXPERTS, CAP, width), sharers, axis=0)
        received.append(
            lax.all_to_all(send, "expert", split_axis=0, concat_axis=0, tiled=True).reshape(
                owners * CAP, width
            )
        )
    flat_x, flat_g = received
    gate = jnp.dot(flat_x, w_gate, preferred_element_type=F32)
    up = jnp.dot(flat_x, w_up, preferred_element_type=F32)
    act, slope = silu_parts(gate)
    hidden = (act * up).astype(BF16)
    partial_value = (
        jnp.dot(hidden, w_down, preferred_element_type=F32).astype(BF16).reshape(owners, CAP, width)
    )
    returned = lax.all_to_all(partial_value, "expert", split_axis=0, concat_axis=0, tiled=True)
    summed = jnp.sum(returned.astype(F32).reshape(EXPERTS, sharers, CAP, width), axis=1).reshape(
        EXPERTS * CAP, width
    )
    outputs = jnp.take(summed, target, axis=0).astype(BF16)
    d_hidden = contract_cols(flat_g, w_down)
    d_gate = (d_hidden * up * slope).astype(BF16)
    d_up = (d_hidden * act).astype(BF16)
    grads = jnp.concatenate([contract_rows(flat_x, d_gate), contract_rows(flat_x, d_up)], axis=1)
    mine = lax.psum_scatter(grads.astype(BF16), "dp", scatter_dimension=0, tiled=True)
    return outputs, mine[:, :hidden_cols], mine[:, hidden_cols:]


def solution(mesh):
    dp, owners = mesh.devices.shape
    if (dp, owners) == (4, 2 * EXPERTS):
        rows, cols = ("far", "core"), ("arch", "half")
        mesh = Mesh(mesh.devices.reshape(2, 2, EXPERTS, 2), rows + cols)
        body = gathering
    else:
        rows, cols = ("dp",), ("expert",)
        body = reducing
    tokens = P(rows + cols, None)
    return jax.shard_map(
        body,
        mesh=mesh,
        in_specs=(tokens, tokens, P(None, cols), P(None, cols), P(cols, None), tokens),
        out_specs=(tokens, P(rows, cols), P(rows, cols)),
        check_vma=False,
    )
```

```python
import functools

import jax
import jax.numpy as jnp
from jax import lax
from jax.experimental import pallas as pl
from jax.experimental.pallas import tpu as pltpu
from jax.sharding import Mesh
from jax.sharding import PartitionSpec as P

EXPERTS = 4
CAP = 36
WIDE = 1024
STRIP = 512
SLICE = 256
MIB = 1024 * 1024
LARGE = pltpu.CompilerParams(vmem_limit_bytes=16 * MIB)
SMALL = pltpu.CompilerParams(vmem_limit_bytes=12 * MIB)
CHEAP = pl.CostEstimate(flops=0, bytes_accessed=0, transcendentals=0)
DEAR = pl.CostEstimate(flops=20_000_000_000, bytes_accessed=0, transcendentals=0)
F32 = jnp.float32
BF16 = jnp.bfloat16
HERE = pl.BlockSpec(memory_space=pltpu.VMEM)
AFAR = pl.BlockSpec(memory_space=pltpu.HBM)
ANYWHERE = pl.BlockSpec(memory_space=pl.ANY)


def silu_parts(gate):
    sigma = 0.5 * jnp.tanh(0.5 * gate) + 0.5
    return (gate * sigma, sigma * (1.0 + gate * (1.0 - sigma)))


def contract_rows(left, right):
    return lax.dot_general(left, right, (((0,), (0,)), ((), ())), preferred_element_type=F32)


def contract_cols(left, right):
    return lax.dot_general(left, right, (((1,), (1,)), ((), ())), preferred_element_type=F32)


def stacked(refs):
    return jnp.concatenate([r[...].astype(F32) for r in refs], axis=0)


def kept(value):
    return pltpu.with_memory_space_constraint(value, pltpu.HBM)


def pack_kernel(plane_ref, _, __, kind_ref, x_ref, g_ref, placer_ref, *refs):
    outs, (kind, x, g, sems) = refs[: 2 * EXPERTS], refs[2 * EXPERTS :]
    copies = [
        pltpu.make_async_copy(source, target, sems.at[i])
        for i, (source, target) in enumerate(((kind_ref, kind), (x_ref, x), (g_ref, g)))
    ]
    for copy in copies:
        copy.start()
    tokens = kind.shape[1]
    copies[0].wait()
    key = kind[...] ^ plane_ref[0]
    onehot = (key == lax.broadcasted_iota(jnp.int32, (8, tokens), 0)).astype(F32)
    before = lax.broadcasted_iota(jnp.int32, (tokens, tokens), 0) < lax.broadcasted_iota(
        jnp.int32, (tokens, tokens), 1
    )
    ranks = jnp.dot(onehot.astype(BF16), before.astype(BF16), preferred_element_type=F32)
    rank = jnp.sum(ranks * onehot, axis=0, keepdims=True).astype(jnp.int32)
    place = key * CAP + rank
    slots = EXPERTS * CAP
    placer = (place == lax.broadcasted_iota(jnp.int32, (slots, tokens), 0)).astype(F32).astype(BF16)
    placer_ref[...] = placer
    for copy, source, first in ((copies[1], x, 0), (copies[2], g, EXPERTS)):
        copy.wait()
        packed = jnp.dot(placer, source[...], preferred_element_type=F32)
        for k in range(EXPERTS):
            outs[first + k][...] = packed[k * CAP : (k + 1) * CAP].astype(BF16)


def pack(scalars, kind, x, g):
    tokens, width = x.shape
    return pl.pallas_call(
        pack_kernel,
        out_shape=[jax.ShapeDtypeStruct((EXPERTS * CAP, tokens), BF16)]
        + [jax.ShapeDtypeStruct((CAP, width), BF16)] * (2 * EXPERTS),
        in_specs=[pl.BlockSpec(memory_space=pltpu.SMEM)] * 3 + [AFAR] * 3,
        scratch_shapes=[
            pltpu.VMEM((1, tokens), jnp.int32),
            pltpu.VMEM((tokens, width), BF16),
            pltpu.VMEM((tokens, width), BF16),
            pltpu.SemaphoreType.DMA((3,)),
        ],
        compiler_params=SMALL,
        cost_estimate=CHEAP,
        name="pack",
    )(*scalars, kept(kind), kept(x), kept(g))


def join_kernel(*refs):
    refs[-1][...] = stacked(refs[-2 : -2 - EXPERTS : -1]).astype(BF16)


def join(blocks, earlier=()):
    width = blocks[0].shape[1]
    return pl.pallas_call(
        join_kernel,
        out_shape=jax.ShapeDtypeStruct((EXPERTS * CAP, width), BF16),
        in_specs=[ANYWHERE] * len(earlier) + [HERE] * EXPERTS,
        compiler_params=SMALL,
        cost_estimate=CHEAP,
        name="join",
    )(*earlier, *blocks[::-1])


def relay_kernel(n, *refs):
    for i in range(n):
        refs[len(refs) - n + i][...] = refs[i][...]


def relay(values, earlier):
    n = len(values)
    return pl.pallas_call(
        functools.partial(relay_kernel, n),
        out_shape=[jax.ShapeDtypeStruct(v.shape, v.dtype) for v in values],
        in_specs=[HERE] * n + [ANYWHERE] * len(earlier),
        compiler_params=SMALL,
        cost_estimate=CHEAP,
        name="relay",
    )(*values, *earlier)


def mark_kernel(value_ref, _, mark_ref):
    mark_ref[...] = value_ref[: mark_ref.shape[0], : mark_ref.shape[1]]


def mark(value, earlier):
    return pl.pallas_call(
        mark_kernel,
        out_shape=jax.ShapeDtypeStruct((16, 128), value.dtype),
        in_specs=[HERE, ANYWHERE],
        compiler_params=SMALL,
        cost_estimate=CHEAP,
        name="mark",
    )(value, earlier)


def flip_kernel(source_ref, here_ref, flipped_ref, sems):
    steps = source_ref.shape[0] // SLICE
    copies = []
    for j in range(steps):
        rows = pl.ds(j * SLICE, SLICE)
        copies.append(pltpu.make_async_copy(source_ref.at[rows], here_ref.at[rows], sems.at[j]))
        copies[j].start()
    for j in range(steps):
        copies[j].wait()
        rows = slice(j * SLICE, (j + 1) * SLICE)
        flipped_ref[:, rows] = here_ref[rows, :].T


def flip(value):
    return pl.pallas_call(
        flip_kernel,
        out_shape=[pltpu.VMEM(value.shape, value.dtype), pltpu.VMEM(value.shape[::-1], value.dtype)],
        in_specs=[AFAR],
        out_specs=[HERE, HERE],
        scratch_shapes=[pltpu.SemaphoreType.DMA((value.shape[0] // SLICE,))],
        compiler_params=SMALL,
        cost_estimate=CHEAP,
        name="flip",
    )(kept(value))


def forward_kernel(n, fetch, down, pair, unused, *refs):
    refs = list(refs[unused:])
    xs = [refs.pop(0) for _ in range(n)]
    wg_ref, wu_ref = refs.pop(0), refs.pop(0)
    wd_ref = refs.pop(0) if down else None
    other_ref = refs.pop(0) if pair else None
    act_ref, coef_ref = refs.pop(0), refs.pop(0)
    shares = [refs.pop(0) for _ in range(EXPERTS if pair else down)]
    if fetch:
        sources, sems = (wg_ref, wu_ref), refs.pop()
        wg_ref, wu_ref = refs.pop(0), refs.pop(0)
    acc_ref = refs.pop(0) if down else None
    part = xs[0].shape[0]
    x_ref = xs[0]
    if n > 1:
        x_ref = refs.pop(0)
        for i in range(n):
            x_ref[i * part : (i + 1) * part, :] = xs[i][...]
    steps = wg_ref.shape[1] // (2 * WIDE)

    def copies(j):
        cols = pl.ds(pl.multiple_of(j * (2 * WIDE), (2 * WIDE)), (2 * WIDE))
        return [
            pltpu.make_async_copy(source.at[:, cols], target.at[:, cols], sems.at[j, i])
            for i, (source, target) in enumerate(zip(sources, (wg_ref, wu_ref)))
        ]

    if fetch:
        for j in range(steps):
            for copy in copies(j):
                copy.start()
    if down:
        acc_ref[...] = jnp.zeros_like(acc_ref)

    @pl.loop(0, steps)
    def _(j):
        if fetch:
            for copy in copies(j):
                copy.wait()
        for i in range(2):
            cols = pl.ds(pl.multiple_of(j * (2 * WIDE) + i * WIDE, WIDE), WIDE)
            gate = jnp.dot(x_ref[...], wg_ref[:, cols], preferred_element_type=F32)
            up = jnp.dot(x_ref[...], wu_ref[:, cols], preferred_element_type=F32)
            act, slope = silu_parts(gate)
            act_ref[:, cols] = act.astype(BF16)
            coef_ref[:, cols] = (up * slope).astype(BF16)
            if down:
                hidden = (act[:part] * up[:part]).astype(BF16)
                acc_ref[...] += jnp.dot(hidden, wd_ref[cols, :], preferred_element_type=F32)

    if pair:
        other = other_ref[...].astype(F32)
        for k in range(EXPERTS):
            rows = slice(k * CAP, (k + 1) * CAP)
            block = jnp.concatenate([other[rows], acc_ref[rows, :]], axis=0).astype(BF16)
            shares[k][...] = block
    elif down:
        shares[0][...] = acc_ref[...].astype(BF16)


def forward(xs, wg, wu, wd=None, other=None, fetch=False, earlier=(), cost=CHEAP):
    n, (part, width), cols = len(xs), xs[0].shape, wg.shape[1]
    rows = n * part
    down, pair = wd is not None, other is not None
    shares = [jax.ShapeDtypeStruct((part, width), BF16)] * down
    if pair:
        shares = [jax.ShapeDtypeStruct((2 * CAP, width), BF16)] * EXPERTS
    weights = [kept(wg), kept(wu)] if fetch else [wg, wu]
    return pl.pallas_call(
        functools.partial(forward_kernel, n, fetch, down, pair, len(earlier)),
        out_shape=[jax.ShapeDtypeStruct((rows, cols), BF16)] * 2
        + shares
        + [pltpu.VMEM(wg.shape, wg.dtype)] * (2 * fetch),
        in_specs=[ANYWHERE] * len(earlier)
        + [HERE] * n
        + [AFAR if fetch else HERE] * 2
        + [HERE] * (down + pair),
        scratch_shapes=[pltpu.VMEM((part, width), F32)] * down
        + [pltpu.VMEM((rows, width), BF16)] * (n > 1)
        + [pltpu.SemaphoreType.DMA((cols // (2 * WIDE), 2))] * fetch,
        compiler_params=LARGE,
        cost_estimate=cost,
        name="forward" + "_fetch" * fetch + "_down" * down,
    )(*earlier, *xs, *weights, *([wd] * down), *([other] * pair))


def turn_kernel(_, __, *refs):
    refs[8][: refs[0].shape[1], :] = stacked(refs[0:4]).T.astype(BF16)
    refs[8][refs[0].shape[1] :, :] = stacked(refs[4:8]).T.astype(BF16)


def turn(own, sib, xs, share):
    part = xs[0].shape[0]
    rows = len(xs) * part
    return pl.pallas_call(
        turn_kernel,
        grid_spec=pltpu.PrefetchScalarGridSpec(
            num_scalar_prefetch=2,
            grid=(1,),
            in_specs=[pl.BlockSpec((part, share), lambda j, a, b: (0, a[0]))] * 4
            + [pl.BlockSpec((part, share), lambda j, a, b: (0, b[0]))] * 4,
            out_specs=pl.BlockSpec((2 * share, rows), lambda j, a, b: (0, 0)),
        ),
        out_shape=jax.ShapeDtypeStruct((2 * share, rows), BF16),
        compiler_params=SMALL,
        cost_estimate=CHEAP,
        name="turn",
    )(own, sib, *xs, *xs)


def slopes_kernel(n, *refs):
    gs, acts, coefs = refs[:n], refs[n : 2 * n], refs[2 * n : 3 * n]
    wdt_ref, dg_ref, du_ref, g_ref = refs[3 * n :]
    part = gs[0].shape[0]
    for i in range(n):
        g_ref[i * part : (i + 1) * part, :] = gs[i][...]
    for start in range(0, wdt_ref.shape[1], STRIP):
        cols = slice(start, start + STRIP)
        d_hidden = jnp.dot(g_ref[...], wdt_ref[:, cols], preferred_element_type=F32)
        for i in range(n):
            rows = slice(i * part, (i + 1) * part)
            dg_ref[rows, cols] = (d_hidden[rows] * coefs[i][:, cols].astype(F32)).astype(BF16)
            du_ref[rows, cols] = (d_hidden[rows] * acts[i][:, cols].astype(F32)).astype(BF16)


def slopes(gs, acts, coefs, wdt):
    n, (part, width) = len(gs), gs[0].shape
    return pl.pallas_call(
        functools.partial(slopes_kernel, n),
        out_shape=[jax.ShapeDtypeStruct((n * part, wdt.shape[1]), BF16)] * 2,
        in_specs=[HERE] * (3 * n + 1),
        scratch_shapes=[pltpu.VMEM((n * part, width), BF16)],
        compiler_params=LARGE,
        cost_estimate=CHEAP,
        name="slopes",
    )(*gs, *acts, *coefs, wdt)


def backward_kernel(first, xt_ref, g_ref, act_ref, coef_ref, dg_ref, du_ref, wdt_ref, *refs):
    own_ref, sib_ref = refs[-2:]
    share = own_ref.shape[0] // 2
    for start in range(0, own_ref.shape[1], STRIP):
        here = slice(start, start + STRIP)
        cols = slice(first + start, first + start + STRIP)
        d_hidden = jnp.dot(g_ref[...], wdt_ref[:, cols], preferred_element_type=F32)
        for row, factor_ref, known_ref in ((0, coef_ref, dg_ref), (share, act_ref, du_ref)):
            d_cols = (d_hidden * factor_ref[:, cols].astype(F32)).astype(BF16)
            d_cols = jnp.concatenate([known_ref[:, cols], d_cols], axis=0)
            total = jnp.dot(xt_ref[...], d_cols, preferred_element_type=F32).astype(BF16)
            own_ref[row : row + share, here] = total[:share]
            sib_ref[row : row + share, here] = total[share:]


def backward(xt, g, act, coef, dg, du, wdt, first, cols, earlier=()):
    return pl.pallas_call(
        functools.partial(backward_kernel, first),
        out_shape=[jax.ShapeDtypeStruct((xt.shape[0], cols), BF16)] * 2,
        in_specs=[HERE] * 7 + [ANYWHERE] * len(earlier),
        compiler_params=LARGE,
        cost_estimate=DEAR,
        name="backward",
    )(xt, g, act, coef, dg, du, wdt, *earlier)


def finish_kernel(spans, more, unused, *refs):
    refs = refs[unused:]
    n = len(spans)
    pairs = [refs[2 * i : 2 * i + 2] for i in range(n)]
    gate_ref, up_ref, gate, up, sems = refs[2 * n + 2 * more :]
    share = gate_ref.shape[0]
    low = spans[0][0]
    copies = []
    for i, ((first, cols), (own, got)) in enumerate(zip(spans, pairs)):
        for j, (target, held) in enumerate(((gate_ref, gate), (up_ref, up))):
            rows = slice(j * share, (j + 1) * share)
            here = pl.ds(first - low, cols)
            held[:, here] = (own[rows, :].astype(F32) + got[rows, :].astype(F32)).astype(BF16)
            copies.append(
                pltpu.make_async_copy(held.at[:, here], target.at[:, pl.ds(first, cols)], sems.at[i, j])
            )
            copies[-1].start()
    for copy in copies:
        copy.wait()


def finish(owns, gots, firsts, width, held=(), earlier=()):
    share = owns[0].shape[0] // 2
    spans = tuple((first, own.shape[1]) for first, own in zip(firsts, owns))
    total = sum(cols for _, cols in spans)
    n, more = len(owns), len(held) > 0
    return pl.pallas_call(
        functools.partial(finish_kernel, spans, more, len(earlier)),
        out_shape=[jax.ShapeDtypeStruct((share, width), BF16)] * 2,
        in_specs=[AFAR] * len(earlier) + [HERE] * (2 * n) + [ANYWHERE] * (2 * more),
        out_specs=[ANYWHERE] * 2,
        scratch_shapes=[pltpu.VMEM((share, total), BF16)] * 2 + [pltpu.SemaphoreType.DMA((n, 2))],
        input_output_aliases={len(earlier) + 2 * n: 0, len(earlier) + 2 * n + 1: 1} if more else {},
        compiler_params=SMALL,
        cost_estimate=CHEAP,
        name="finish",
    )(*[kept(v) for v in earlier], *[v for both in zip(owns, gots) for v in both], *held)


def split_kernel(*refs):
    blocks = [r[...].astype(F32) for r in refs[:EXPERTS]]
    refs[-2][...] = jnp.concatenate([b[:CAP] for b in blocks], axis=0).astype(BF16)
    refs[-1][...] = jnp.concatenate([b[CAP:] for b in blocks], axis=0).astype(BF16)


def split(blocks, earlier):
    width = blocks[0].shape[1]
    return pl.pallas_call(
        split_kernel,
        out_shape=[jax.ShapeDtypeStruct((EXPERTS * CAP, width), BF16)] * 2,
        in_specs=[HERE] * EXPERTS + [ANYWHERE] * len(earlier),
        compiler_params=SMALL,
        cost_estimate=CHEAP,
        name="split",
    )(*blocks, *earlier)


def unpack_kernel(placer_ref, mine_ref, got_ref, *refs):
    chosen = placer_ref[...].astype(F32).T.astype(BF16)
    total = jnp.dot(chosen, mine_ref[...], preferred_element_type=F32)
    total += jnp.dot(chosen, got_ref[...], preferred_element_type=F32)
    refs[-1][...] = total.astype(BF16)


def unpack(placer, mine, got, earlier):
    return pl.pallas_call(
        unpack_kernel,
        out_shape=jax.ShapeDtypeStruct((placer.shape[1], mine.shape[1]), BF16),
        in_specs=[HERE] * 3 + [AFAR] * len(earlier),
        compiler_params=SMALL,
        cost_estimate=DEAR,
        name="unpack",
    )(placer, mine, got, *[kept(v) for v in earlier])


def swap(value, axis):
    return lax.ppermute(value, axis, [(0, 1), (1, 0)])


def across_planes(blocks):
    return [blocks[0]] + [
        lax.ppermute(blocks[k], "arch", [(i, i ^ k) for i in range(EXPERTS)]) for k in range(1, EXPERTS)
    ]


def after(values, earlier):
    n = len(values)
    return list(lax.optimization_barrier((*values, *earlier))[:n])


def gathering(designs, archetype, w_gate, w_up, w_down, cotangent):
    far, core = lax.axis_index("far"), lax.axis_index("core")
    scalars = [lax.axis_index("arch"), 2 * far + core, 2 * far + 1 - core]
    scalars = [v.astype(jnp.int32)[None] for v in scalars]
    tokens, width = designs.shape
    share = width // 4
    placer, *blocks = pack(scalars, archetype.reshape(1, tokens), designs, cotangent)
    wd, wdt = flip(after([w_down], [placer])[0])

    x_own = join(across_planes(blocks[:EXPERTS]))
    moved = across_planes(relay(blocks[EXPERTS:], [wdt]))
    x_far, x_near = swap(x_own, "far"), swap(x_own, "half")

    wg, wu = w_gate, w_up
    act0, coef0, share_own = forward([x_own], wg, wu, wd)
    g_own = join(moved, [act0])
    g_far, g_near = swap(g_own, "far"), swap(g_own, "half")
    act1, coef1, *shares = forward([x_near], wg, wu, wd, other=share_own)
    (x_pass,) = relay([x_near], [mark(act1, x_far), g_far])
    (g_pass,) = relay([g_far], [x_pass, g_near])
    x_corner, g_corner = swap(x_pass, "far"), swap(g_pass, "half")
    returned = across_planes([*shares[:3], *relay(shares[3:], [g_pass])])
    act2, coef2 = forward([x_far], wg, wu, earlier=[g_pass], cost=DEAR)
    dg, du = slopes([g_own, g_near, g_far], [act0, act1, act2], [coef0, coef1, coef2], wdt)
    act3, coef3 = forward([x_corner], wg, wu, earlier=[dg])
    mine, theirs = split(returned, [act3])
    got = swap(theirs, "half")
    xt = turn(*scalars[1:], [x_own, x_near, x_far, x_corner], share)

    rest = (xt, g_corner, act3, coef3, dg, du, wdt)
    cols = w_down.shape[0]
    cut = cols // 2
    own0, sib0 = backward(*rest, 0, cut)
    own1, sib1 = backward(*rest, cut, cols - cut, [own0])
    got0, got1 = swap(sib0, "core"), swap(sib1, "core")
    held = finish([own0], [got0], (0,), cols)
    outputs = unpack(placer, mine, got, held[:1])
    grad_gate, grad_up = finish([own1], [got1], (cut,), cols, held)
    return outputs, grad_gate, grad_up


def reducing(designs, archetype, w_gate, w_up, w_down, cotangent):
    width = designs.shape[1]
    owners = lax.axis_size("expert")
    sharers = owners // EXPERTS
    hidden_cols = w_gate.shape[1]
    labels = archetype[:, 0]
    onehot = (labels[:, None] == jnp.arange(EXPERTS, dtype=jnp.int32)[None, :]).astype(jnp.int32)
    ranks = jnp.cumsum(onehot, axis=0) - onehot
    target = labels * CAP + jnp.sum(ranks * onehot, axis=1)
    placer = (jnp.arange(EXPERTS * CAP, dtype=jnp.int32)[:, None] == target[None, :]).astype(BF16)
    received = []
    for rows in (designs, cotangent):
        packed = jnp.dot(placer, rows, preferred_element_type=F32).astype(BF16)
        send = jnp.repeat(packed.reshape(EXPERTS, CAP, width), sharers, axis=0)
        received.append(
            lax.all_to_all(send, "expert", split_axis=0, concat_axis=0, tiled=True).reshape(
                owners * CAP, width
            )
        )
    flat_x, flat_g = received
    gate = jnp.dot(flat_x, w_gate, preferred_element_type=F32)
    up = jnp.dot(flat_x, w_up, preferred_element_type=F32)
    act, slope = silu_parts(gate)
    hidden = (act * up).astype(BF16)
    partial_value = (
        jnp.dot(hidden, w_down, preferred_element_type=F32).astype(BF16).reshape(owners, CAP, width)
    )
    returned = lax.all_to_all(partial_value, "expert", split_axis=0, concat_axis=0, tiled=True)
    summed = jnp.sum(returned.astype(F32).reshape(EXPERTS, sharers, CAP, width), axis=1).reshape(
        EXPERTS * CAP, width
    )
    outputs = jnp.take(summed, target, axis=0).astype(BF16)
    d_hidden = contract_cols(flat_g, w_down)
    d_gate = (d_hidden * up * slope).astype(BF16)
    d_up = (d_hidden * act).astype(BF16)
    grads = jnp.concatenate([contract_rows(flat_x, d_gate), contract_rows(flat_x, d_up)], axis=1)
    mine = lax.psum_scatter(grads.astype(BF16), "dp", scatter_dimension=0, tiled=True)
    return outputs, mine[:, :hidden_cols], mine[:, hidden_cols:]


def solution(mesh):
    dp, owners = mesh.devices.shape
    if (dp, owners) == (4, 2 * EXPERTS):
        rows, cols = ("far", "core"), ("arch", "half")
        mesh = Mesh(mesh.devices.reshape(2, 2, EXPERTS, 2), rows + cols)
        body = gathering
    else:
        rows, cols = ("dp",), ("expert",)
        body = reducing
    tokens = P(rows + cols, None)
    return jax.shard_map(
        body,
        mesh=mesh,
        in_specs=(tokens, tokens, P(None, cols), P(None, cols), P(cols, None), tokens),
        out_specs=(tokens, P(rows, cols), P(rows, cols)),
        check_vma=False,
    )
```

```python
import functools

import jax
import jax.numpy as jnp
from jax import lax
from jax.experimental import pallas as pl
from jax.experimental.pallas import tpu as pltpu
from jax.sharding import Mesh
from jax.sharding import PartitionSpec as P

EXPERTS = 4
CAP = 36
WIDE = 1024
STRIP = 512
SLICE = 256
SENT = (0, 2, 1, 3)
MIB = 1024 * 1024
LARGE = pltpu.CompilerParams(vmem_limit_bytes=16 * MIB)
SMALL = pltpu.CompilerParams(vmem_limit_bytes=12 * MIB)
CHEAP = pl.CostEstimate(flops=0, bytes_accessed=0, transcendentals=0)
DEAR = pl.CostEstimate(flops=20_000_000_000, bytes_accessed=0, transcendentals=0)
F32 = jnp.float32
BF16 = jnp.bfloat16
HERE = pl.BlockSpec(memory_space=pltpu.VMEM)
AFAR = pl.BlockSpec(memory_space=pltpu.HBM)
ANYWHERE = pl.BlockSpec(memory_space=pl.ANY)


def silu_parts(gate):
    sigma = 0.5 * jnp.tanh(0.5 * gate) + 0.5
    return (gate * sigma, sigma * (1.0 + gate * (1.0 - sigma)))


def contract_rows(left, right):
    return lax.dot_general(left, right, (((0,), (0,)), ((), ())), preferred_element_type=F32)


def contract_cols(left, right):
    return lax.dot_general(left, right, (((1,), (1,)), ((), ())), preferred_element_type=F32)


def stacked(refs):
    return jnp.concatenate([r[...].astype(F32) for r in refs], axis=0)


def kept(value):
    return pltpu.with_memory_space_constraint(value, pltpu.HBM)


def pack_kernel(plane_ref, _, __, kind_ref, x_ref, g_ref, placer_ref, *refs):
    outs, (kind, x, g, sems) = refs[: 2 * EXPERTS], refs[2 * EXPERTS :]
    copies = [
        pltpu.make_async_copy(source, target, sems.at[i])
        for i, (source, target) in enumerate(((kind_ref, kind), (x_ref, x), (g_ref, g)))
    ]
    for copy in copies:
        copy.start()
    tokens = kind.shape[1]
    copies[0].wait()
    key = kind[...] ^ plane_ref[0]
    onehot = (key == lax.broadcasted_iota(jnp.int32, (8, tokens), 0)).astype(F32)
    before = lax.broadcasted_iota(jnp.int32, (tokens, tokens), 0) < lax.broadcasted_iota(
        jnp.int32, (tokens, tokens), 1
    )
    ranks = jnp.dot(onehot.astype(BF16), before.astype(BF16), preferred_element_type=F32)
    rank = jnp.sum(ranks * onehot, axis=0, keepdims=True).astype(jnp.int32)
    place = key * CAP + rank
    slots = EXPERTS * CAP
    placer = (place == lax.broadcasted_iota(jnp.int32, (slots, tokens), 0)).astype(F32).astype(BF16)
    placer_ref[...] = placer
    for copy, source, first in ((copies[1], x, 0), (copies[2], g, EXPERTS)):
        copy.wait()
        packed = jnp.dot(placer, source[...], preferred_element_type=F32)
        for k in range(EXPERTS):
            outs[first + k][...] = packed[k * CAP : (k + 1) * CAP].astype(BF16)


def pack(scalars, kind, x, g):
    tokens, width = x.shape
    return pl.pallas_call(
        pack_kernel,
        out_shape=[jax.ShapeDtypeStruct((EXPERTS * CAP, tokens), BF16)]
        + [jax.ShapeDtypeStruct((CAP, width), BF16)] * (2 * EXPERTS),
        in_specs=[pl.BlockSpec(memory_space=pltpu.SMEM)] * 3 + [AFAR] * 3,
        scratch_shapes=[
            pltpu.VMEM((1, tokens), jnp.int32),
            pltpu.VMEM((tokens, width), BF16),
            pltpu.VMEM((tokens, width), BF16),
            pltpu.SemaphoreType.DMA((3,)),
        ],
        compiler_params=SMALL,
        cost_estimate=CHEAP,
        name="pack",
    )(*scalars, kept(kind), kept(x), kept(g))


def join_kernel(*refs):
    refs[-1][...] = stacked(refs[-2 : -2 - EXPERTS : -1]).astype(BF16)


def join(blocks, earlier=()):
    width = blocks[0].shape[1]
    return pl.pallas_call(
        join_kernel,
        out_shape=jax.ShapeDtypeStruct((EXPERTS * CAP, width), BF16),
        in_specs=[ANYWHERE] * len(earlier) + [HERE] * EXPERTS,
        compiler_params=SMALL,
        cost_estimate=CHEAP,
        name="join",
    )(*earlier, *blocks[::-1])


def relay_kernel(n, *refs):
    for i in range(n):
        refs[len(refs) - n + i][...] = refs[i][...]


def relay(values, earlier):
    n = len(values)
    return pl.pallas_call(
        functools.partial(relay_kernel, n),
        out_shape=[jax.ShapeDtypeStruct(v.shape, v.dtype) for v in values],
        in_specs=[HERE] * n + [ANYWHERE] * len(earlier),
        compiler_params=SMALL,
        cost_estimate=CHEAP,
        name="relay",
    )(*values, *earlier)


def mark_kernel(value_ref, _, mark_ref):
    mark_ref[...] = value_ref[: mark_ref.shape[0], : mark_ref.shape[1]]


def mark(value, earlier):
    return pl.pallas_call(
        mark_kernel,
        out_shape=jax.ShapeDtypeStruct((16, 128), value.dtype),
        in_specs=[HERE, ANYWHERE],
        compiler_params=SMALL,
        cost_estimate=CHEAP,
        name="mark",
    )(value, earlier)


def flip_kernel(source_ref, here_ref, flipped_ref, sems):
    steps = source_ref.shape[0] // SLICE
    copies = []
    for j in range(steps):
        rows = pl.ds(j * SLICE, SLICE)
        copies.append(pltpu.make_async_copy(source_ref.at[rows], here_ref.at[rows], sems.at[j]))
        copies[j].start()
    for j in range(steps):
        copies[j].wait()
        rows = slice(j * SLICE, (j + 1) * SLICE)
        flipped_ref[:, rows] = here_ref[rows, :].T


def flip(value):
    return pl.pallas_call(
        flip_kernel,
        out_shape=[pltpu.VMEM(value.shape, value.dtype), pltpu.VMEM(value.shape[::-1], value.dtype)],
        in_specs=[AFAR],
        out_specs=[HERE, HERE],
        scratch_shapes=[pltpu.SemaphoreType.DMA((value.shape[0] // SLICE,))],
        compiler_params=SMALL,
        cost_estimate=CHEAP,
        name="flip",
    )(kept(value))


def forward_kernel(n, fetch, down, pair, unused, *refs):
    refs = list(refs[unused:])
    xs = [refs.pop(0) for _ in range(n)]
    wg_ref, wu_ref = refs.pop(0), refs.pop(0)
    wd_ref = refs.pop(0) if down else None
    other_ref = refs.pop(0) if pair else None
    act_ref, coef_ref = refs.pop(0), refs.pop(0)
    shares = [refs.pop(0) for _ in range(EXPERTS if pair else down)]
    if fetch:
        sources, sems = (wg_ref, wu_ref), refs.pop()
        wg_ref, wu_ref = refs.pop(0), refs.pop(0)
    acc_ref = refs.pop(0) if down else None
    part = xs[0].shape[0]
    x_ref = xs[0]
    if n > 1:
        x_ref = refs.pop(0)
        for i in range(n):
            x_ref[i * part : (i + 1) * part, :] = xs[i][...]
    steps = wg_ref.shape[1] // (2 * WIDE)

    def copies(j):
        cols = pl.ds(pl.multiple_of(j * (2 * WIDE), (2 * WIDE)), (2 * WIDE))
        return [
            pltpu.make_async_copy(source.at[:, cols], target.at[:, cols], sems.at[j, i])
            for i, (source, target) in enumerate(zip(sources, (wg_ref, wu_ref)))
        ]

    if fetch:
        for j in range(steps):
            for copy in copies(j):
                copy.start()
    if down:
        acc_ref[...] = jnp.zeros_like(acc_ref)

    @pl.loop(0, steps)
    def _(j):
        if fetch:
            for copy in copies(j):
                copy.wait()
        for i in range(2):
            cols = pl.ds(pl.multiple_of(j * (2 * WIDE) + i * WIDE, WIDE), WIDE)
            gate = jnp.dot(x_ref[...], wg_ref[:, cols], preferred_element_type=F32)
            up = jnp.dot(x_ref[...], wu_ref[:, cols], preferred_element_type=F32)
            act, slope = silu_parts(gate)
            act_ref[:, cols] = act.astype(BF16)
            coef_ref[:, cols] = (up * slope).astype(BF16)
            if down:
                hidden = (act[:part] * up[:part]).astype(BF16)
                acc_ref[...] += jnp.dot(hidden, wd_ref[cols, :], preferred_element_type=F32)

    if pair:
        other = other_ref[...].astype(F32)
        for k in range(EXPERTS):
            rows = slice(k * CAP, (k + 1) * CAP)
            block = jnp.concatenate([other[rows], acc_ref[rows, :]], axis=0).astype(BF16)
            shares[k][...] = block
    elif down:
        shares[0][...] = acc_ref[...].astype(BF16)


def forward(xs, wg, wu, wd=None, other=None, fetch=False, earlier=(), cost=CHEAP):
    n, (part, width), cols = len(xs), xs[0].shape, wg.shape[1]
    rows = n * part
    down, pair = wd is not None, other is not None
    shares = [jax.ShapeDtypeStruct((part, width), BF16)] * down
    if pair:
        shares = [jax.ShapeDtypeStruct((2 * CAP, width), BF16)] * EXPERTS
    weights = [kept(wg), kept(wu)] if fetch else [wg, wu]
    return pl.pallas_call(
        functools.partial(forward_kernel, n, fetch, down, pair, len(earlier)),
        out_shape=[jax.ShapeDtypeStruct((rows, cols), BF16)] * 2
        + shares
        + [pltpu.VMEM(wg.shape, wg.dtype)] * (2 * fetch),
        in_specs=[ANYWHERE] * len(earlier)
        + [HERE] * n
        + [AFAR if fetch else HERE] * 2
        + [HERE] * (down + pair),
        scratch_shapes=[pltpu.VMEM((part, width), F32)] * down
        + [pltpu.VMEM((rows, width), BF16)] * (n > 1)
        + [pltpu.SemaphoreType.DMA((cols // (2 * WIDE), 2))] * fetch,
        compiler_params=LARGE,
        cost_estimate=cost,
        name="forward" + "_fetch" * fetch + "_down" * down,
    )(*earlier, *xs, *weights, *([wd] * down), *([other] * pair))


def turn_kernel(_, __, *refs):
    refs[8][: refs[0].shape[1], :] = stacked(refs[0:4]).T.astype(BF16)
    refs[8][refs[0].shape[1] :, :] = stacked(refs[4:8]).T.astype(BF16)


def turn(own, sib, xs, share):
    part = xs[0].shape[0]
    rows = len(xs) * part
    return pl.pallas_call(
        turn_kernel,
        grid_spec=pltpu.PrefetchScalarGridSpec(
            num_scalar_prefetch=2,
            grid=(1,),
            in_specs=[pl.BlockSpec((part, share), lambda j, a, b: (0, a[0]))] * 4
            + [pl.BlockSpec((part, share), lambda j, a, b: (0, b[0]))] * 4,
            out_specs=pl.BlockSpec((2 * share, rows), lambda j, a, b: (0, 0)),
        ),
        out_shape=jax.ShapeDtypeStruct((2 * share, rows), BF16),
        compiler_params=SMALL,
        cost_estimate=CHEAP,
        name="turn",
    )(own, sib, *xs, *xs)


def slopes_kernel(n, *refs):
    gs, acts, coefs = refs[:n], refs[n : 2 * n], refs[2 * n : 3 * n]
    wdt_ref, dg_ref, du_ref, g_ref = refs[3 * n :]
    part = gs[0].shape[0]
    for i in range(n):
        g_ref[i * part : (i + 1) * part, :] = gs[i][...]
    for start in range(0, wdt_ref.shape[1], STRIP):
        cols = slice(start, start + STRIP)
        d_hidden = jnp.dot(g_ref[...], wdt_ref[:, cols], preferred_element_type=F32)
        for i in range(n):
            rows = slice(i * part, (i + 1) * part)
            dg_ref[rows, cols] = (d_hidden[rows] * coefs[i][:, cols].astype(F32)).astype(BF16)
            du_ref[rows, cols] = (d_hidden[rows] * acts[i][:, cols].astype(F32)).astype(BF16)


def slopes(gs, acts, coefs, wdt):
    n, (part, width) = len(gs), gs[0].shape
    return pl.pallas_call(
        functools.partial(slopes_kernel, n),
        out_shape=[jax.ShapeDtypeStruct((n * part, wdt.shape[1]), BF16)] * 2,
        in_specs=[HERE] * (3 * n + 1),
        scratch_shapes=[pltpu.VMEM((n * part, width), BF16)],
        compiler_params=LARGE,
        cost_estimate=CHEAP,
        name="slopes",
    )(*gs, *acts, *coefs, wdt)


def backward_kernel(first, xt_ref, g_ref, act_ref, coef_ref, dg_ref, du_ref, wdt_ref, *refs):
    own_ref, sib_ref = refs[-2:]
    share = own_ref.shape[0] // 2
    for start in range(0, own_ref.shape[1], STRIP):
        here = slice(start, start + STRIP)
        cols = slice(first + start, first + start + STRIP)
        d_hidden = jnp.dot(g_ref[...], wdt_ref[:, cols], preferred_element_type=F32)
        for row, factor_ref, known_ref in ((0, coef_ref, dg_ref), (share, act_ref, du_ref)):
            d_cols = (d_hidden * factor_ref[:, cols].astype(F32)).astype(BF16)
            d_cols = jnp.concatenate([known_ref[:, cols], d_cols], axis=0)
            total = jnp.dot(xt_ref[...], d_cols, preferred_element_type=F32).astype(BF16)
            own_ref[row : row + share, here] = total[:share]
            sib_ref[row : row + share, here] = total[share:]


def backward(xt, g, act, coef, dg, du, wdt, first, cols, earlier=()):
    return pl.pallas_call(
        functools.partial(backward_kernel, first),
        out_shape=[jax.ShapeDtypeStruct((xt.shape[0], cols), BF16)] * 2,
        in_specs=[HERE] * 7 + [ANYWHERE] * len(earlier),
        compiler_params=LARGE,
        cost_estimate=DEAR,
        name="backward",
    )(xt, g, act, coef, dg, du, wdt, *earlier)


def finish_kernel(spans, more, unused, *refs):
    refs = refs[unused:]
    n = len(spans)
    pairs = [refs[2 * i : 2 * i + 2] for i in range(n)]
    gate_ref, up_ref, gate, up, sems = refs[2 * n + 2 * more :]
    share = gate_ref.shape[0]
    low = spans[0][0]
    copies = []
    for i, ((first, cols), (own, got)) in enumerate(zip(spans, pairs)):
        for j, (target, held) in enumerate(((gate_ref, gate), (up_ref, up))):
            rows = slice(j * share, (j + 1) * share)
            here = pl.ds(first - low, cols)
            held[:, here] = (own[rows, :].astype(F32) + got[rows, :].astype(F32)).astype(BF16)
            copies.append(
                pltpu.make_async_copy(held.at[:, here], target.at[:, pl.ds(first, cols)], sems.at[i, j])
            )
            copies[-1].start()
    for copy in copies:
        copy.wait()


def finish(owns, gots, firsts, width, held=(), earlier=()):
    share = owns[0].shape[0] // 2
    spans = tuple((first, own.shape[1]) for first, own in zip(firsts, owns))
    total = sum(cols for _, cols in spans)
    n, more = len(owns), len(held) > 0
    return pl.pallas_call(
        functools.partial(finish_kernel, spans, more, len(earlier)),
        out_shape=[jax.ShapeDtypeStruct((share, width), BF16)] * 2,
        in_specs=[AFAR] * len(earlier) + [HERE] * (2 * n) + [ANYWHERE] * (2 * more),
        out_specs=[ANYWHERE] * 2,
        scratch_shapes=[pltpu.VMEM((share, total), BF16)] * 2 + [pltpu.SemaphoreType.DMA((n, 2))],
        input_output_aliases={len(earlier) + 2 * n: 0, len(earlier) + 2 * n + 1: 1} if more else {},
        compiler_params=SMALL,
        cost_estimate=CHEAP,
        name="finish",
    )(*[kept(v) for v in earlier], *[v for both in zip(owns, gots) for v in both], *held)


def split_kernel(*refs):
    blocks = [refs[SENT.index(k)][...].astype(F32) for k in range(EXPERTS)]
    refs[-2][...] = jnp.concatenate([b[:CAP] for b in blocks], axis=0).astype(BF16)
    refs[-1][...] = jnp.concatenate([b[CAP:] for b in blocks], axis=0).astype(BF16)


def split(blocks, earlier):
    width = blocks[0].shape[1]
    return pl.pallas_call(
        split_kernel,
        out_shape=[jax.ShapeDtypeStruct((EXPERTS * CAP, width), BF16)] * 2,
        in_specs=[HERE] * EXPERTS + [ANYWHERE] * len(earlier),
        compiler_params=SMALL,
        cost_estimate=CHEAP,
        name="split",
    )(*[blocks[k] for k in SENT], *earlier)


def unpack_kernel(placer_ref, mine_ref, got_ref, *refs):
    chosen = placer_ref[...].astype(F32).T.astype(BF16)
    total = jnp.dot(chosen, mine_ref[...], preferred_element_type=F32)
    total += jnp.dot(chosen, got_ref[...], preferred_element_type=F32)
    refs[-1][...] = total.astype(BF16)


def unpack(placer, mine, got, earlier):
    return pl.pallas_call(
        unpack_kernel,
        out_shape=jax.ShapeDtypeStruct((placer.shape[1], mine.shape[1]), BF16),
        in_specs=[HERE] * 3 + [AFAR] * len(earlier),
        compiler_params=SMALL,
        cost_estimate=DEAR,
        name="unpack",
    )(placer, mine, got, *[kept(v) for v in earlier])


def swap(value, axis):
    return lax.ppermute(value, axis, [(0, 1), (1, 0)])


def across_planes(blocks):
    return [blocks[0]] + [
        lax.ppermute(blocks[k], "arch", [(i, i ^ k) for i in range(EXPERTS)]) for k in range(1, EXPERTS)
    ]


def after(values, earlier):
    n = len(values)
    return list(lax.optimization_barrier((*values, *earlier))[:n])


def gathering(designs, archetype, w_gate, w_up, w_down, cotangent):
    far, core = lax.axis_index("far"), lax.axis_index("core")
    scalars = [lax.axis_index("arch"), 2 * far + core, 2 * far + 1 - core]
    scalars = [v.astype(jnp.int32)[None] for v in scalars]
    tokens, width = designs.shape
    share = width // 4
    placer, *blocks = pack(scalars, archetype.reshape(1, tokens), designs, cotangent)
    wd, wdt = flip(after([w_down], [placer])[0])

    x_own = join(across_planes(blocks[:EXPERTS]))
    moved = across_planes(relay(blocks[EXPERTS:], [wdt]))
    x_far, x_near = swap(x_own, "far"), swap(x_own, "half")

    wg, wu = w_gate, w_up
    act0, coef0, share_own = forward([x_own], wg, wu, wd)
    g_own = join(moved, [act0])
    g_far, g_near = swap(g_own, "far"), swap(g_own, "half")
    act1, coef1, *shares = forward([x_near], wg, wu, wd, other=share_own)
    (x_pass,) = relay([x_near], [mark(act1, x_far), g_far])
    (g_pass,) = relay([g_far], [x_pass, g_near])
    x_corner, g_corner = swap(x_pass, "far"), swap(g_pass, "half")
    returned = across_planes(shares)
    act2, coef2 = forward([x_far], wg, wu, earlier=[g_pass], cost=DEAR)
    dg, du = slopes([g_own, g_near, g_far], [act0, act1, act2], [coef0, coef1, coef2], wdt)
    act3, coef3 = forward([x_corner], wg, wu, earlier=[dg])
    mine, theirs = split(returned, [act3])
    got = swap(theirs, "half")
    xt = turn(*scalars[1:], [x_own, x_near, x_far, x_corner], share)

    rest = (xt, g_corner, act3, coef3, dg, du, wdt)
    cols = w_down.shape[0]
    cut = cols // 2
    own0, sib0 = backward(*rest, 0, cut)
    own1, sib1 = backward(*rest, cut, cols - cut, [own0])
    got0, got1 = swap(sib0, "core"), swap(sib1, "core")
    held = finish([own0], [got0], (0,), cols)
    outputs = unpack(placer, mine, got, held[:1])
    grad_gate, grad_up = finish([own1], [got1], (cut,), cols, held)
    return outputs, grad_gate, grad_up


def reducing(designs, archetype, w_gate, w_up, w_down, cotangent):
    width = designs.shape[1]
    owners = lax.axis_size("expert")
    sharers = owners // EXPERTS
    hidden_cols = w_gate.shape[1]
    labels = archetype[:, 0]
    onehot = (labels[:, None] == jnp.arange(EXPERTS, dtype=jnp.int32)[None, :]).astype(jnp.int32)
    ranks = jnp.cumsum(onehot, axis=0) - onehot
    target = labels * CAP + jnp.sum(ranks * onehot, axis=1)
    placer = (jnp.arange(EXPERTS * CAP, dtype=jnp.int32)[:, None] == target[None, :]).astype(BF16)
    received = []
    for rows in (designs, cotangent):
        packed = jnp.dot(placer, rows, preferred_element_type=F32).astype(BF16)
        send = jnp.repeat(packed.reshape(EXPERTS, CAP, width), sharers, axis=0)
        received.append(
            lax.all_to_all(send, "expert", split_axis=0, concat_axis=0, tiled=True).reshape(
                owners * CAP, width
            )
        )
    flat_x, flat_g = received
    gate = jnp.dot(flat_x, w_gate, preferred_element_type=F32)
    up = jnp.dot(flat_x, w_up, preferred_element_type=F32)
    act, slope = silu_parts(gate)
    hidden = (act * up).astype(BF16)
    partial_value = (
        jnp.dot(hidden, w_down, preferred_element_type=F32).astype(BF16).reshape(owners, CAP, width)
    )
    returned = lax.all_to_all(partial_value, "expert", split_axis=0, concat_axis=0, tiled=True)
    summed = jnp.sum(returned.astype(F32).reshape(EXPERTS, sharers, CAP, width), axis=1).reshape(
        EXPERTS * CAP, width
    )
    outputs = jnp.take(summed, target, axis=0).astype(BF16)
    d_hidden = contract_cols(flat_g, w_down)
    d_gate = (d_hidden * up * slope).astype(BF16)
    d_up = (d_hidden * act).astype(BF16)
    grads = jnp.concatenate([contract_rows(flat_x, d_gate), contract_rows(flat_x, d_up)], axis=1)
    mine = lax.psum_scatter(grads.astype(BF16), "dp", scatter_dimension=0, tiled=True)
    return outputs, mine[:, :hidden_cols], mine[:, hidden_cols:]


def solution(mesh):
    dp, owners = mesh.devices.shape
    if (dp, owners) == (4, 2 * EXPERTS):
        rows, cols = ("far", "core"), ("arch", "half")
        mesh = Mesh(mesh.devices.reshape(2, 2, EXPERTS, 2), rows + cols)
        body = gathering
    else:
        rows, cols = ("dp",), ("expert",)
        body = reducing
    tokens = P(rows + cols, None)
    return jax.shard_map(
        body,
        mesh=mesh,
        in_specs=(tokens, tokens, P(None, cols), P(None, cols), P(cols, None), tokens),
        out_specs=(tokens, P(rows, cols), P(rows, cols)),
        check_vma=False,
    )
```

```python
import functools

import jax
import jax.numpy as jnp
from jax import lax
from jax.experimental import pallas as pl
from jax.experimental.pallas import tpu as pltpu
from jax.sharding import Mesh
from jax.sharding import PartitionSpec as P

EXPERTS = 4
CAP = 36
WIDE = 1024
STRIP = 512
SLICE = 256
SENT = (0, 2, 3, 1)
MIB = 1024 * 1024
LARGE = pltpu.CompilerParams(vmem_limit_bytes=16 * MIB)
SMALL = pltpu.CompilerParams(vmem_limit_bytes=12 * MIB)
CHEAP = pl.CostEstimate(flops=0, bytes_accessed=0, transcendentals=0)
DEAR = pl.CostEstimate(flops=20_000_000_000, bytes_accessed=0, transcendentals=0)
F32 = jnp.float32
BF16 = jnp.bfloat16
HERE = pl.BlockSpec(memory_space=pltpu.VMEM)
AFAR = pl.BlockSpec(memory_space=pltpu.HBM)
ANYWHERE = pl.BlockSpec(memory_space=pl.ANY)


def silu_parts(gate):
    sigma = 0.5 * jnp.tanh(0.5 * gate) + 0.5
    return (gate * sigma, sigma * (1.0 + gate * (1.0 - sigma)))


def contract_rows(left, right):
    return lax.dot_general(left, right, (((0,), (0,)), ((), ())), preferred_element_type=F32)


def contract_cols(left, right):
    return lax.dot_general(left, right, (((1,), (1,)), ((), ())), preferred_element_type=F32)


def stacked(refs):
    return jnp.concatenate([r[...].astype(F32) for r in refs], axis=0)


def kept(value):
    return pltpu.with_memory_space_constraint(value, pltpu.HBM)


def pack_kernel(plane_ref, _, __, kind_ref, x_ref, g_ref, placer_ref, *refs):
    outs, (kind, x, g, sems) = refs[: 2 * EXPERTS], refs[2 * EXPERTS :]
    copies = [
        pltpu.make_async_copy(source, target, sems.at[i])
        for i, (source, target) in enumerate(((kind_ref, kind), (x_ref, x), (g_ref, g)))
    ]
    for copy in copies:
        copy.start()
    tokens = kind.shape[1]
    copies[0].wait()
    key = kind[...] ^ plane_ref[0]
    onehot = (key == lax.broadcasted_iota(jnp.int32, (8, tokens), 0)).astype(F32)
    before = lax.broadcasted_iota(jnp.int32, (tokens, tokens), 0) < lax.broadcasted_iota(
        jnp.int32, (tokens, tokens), 1
    )
    ranks = jnp.dot(onehot.astype(BF16), before.astype(BF16), preferred_element_type=F32)
    rank = jnp.sum(ranks * onehot, axis=0, keepdims=True).astype(jnp.int32)
    place = key * CAP + rank
    slots = EXPERTS * CAP
    placer = (place == lax.broadcasted_iota(jnp.int32, (slots, tokens), 0)).astype(F32).astype(BF16)
    placer_ref[...] = placer
    for copy, source, first in ((copies[1], x, 0), (copies[2], g, EXPERTS)):
        copy.wait()
        packed = jnp.dot(placer, source[...], preferred_element_type=F32)
        for k in range(EXPERTS):
            outs[first + k][...] = packed[k * CAP : (k + 1) * CAP].astype(BF16)


def pack(scalars, kind, x, g):
    tokens, width = x.shape
    return pl.pallas_call(
        pack_kernel,
        out_shape=[jax.ShapeDtypeStruct((EXPERTS * CAP, tokens), BF16)]
        + [jax.ShapeDtypeStruct((CAP, width), BF16)] * (2 * EXPERTS),
        in_specs=[pl.BlockSpec(memory_space=pltpu.SMEM)] * 3 + [AFAR] * 3,
        scratch_shapes=[
            pltpu.VMEM((1, tokens), jnp.int32),
            pltpu.VMEM((tokens, width), BF16),
            pltpu.VMEM((tokens, width), BF16),
            pltpu.SemaphoreType.DMA((3,)),
        ],
        compiler_params=SMALL,
        cost_estimate=CHEAP,
        name="pack",
    )(*scalars, kept(kind), kept(x), kept(g))


def join_kernel(*refs):
    refs[-1][...] = stacked(refs[-2 : -2 - EXPERTS : -1]).astype(BF16)


def join(blocks, earlier=()):
    width = blocks[0].shape[1]
    return pl.pallas_call(
        join_kernel,
        out_shape=jax.ShapeDtypeStruct((EXPERTS * CAP, width), BF16),
        in_specs=[ANYWHERE] * len(earlier) + [HERE] * EXPERTS,
        compiler_params=SMALL,
        cost_estimate=CHEAP,
        name="join",
    )(*earlier, *blocks[::-1])


def relay_kernel(n, *refs):
    for i in range(n):
        refs[len(refs) - n + i][...] = refs[i][...]


def relay(values, earlier):
    n = len(values)
    return pl.pallas_call(
        functools.partial(relay_kernel, n),
        out_shape=[jax.ShapeDtypeStruct(v.shape, v.dtype) for v in values],
        in_specs=[HERE] * n + [ANYWHERE] * len(earlier),
        compiler_params=SMALL,
        cost_estimate=CHEAP,
        name="relay",
    )(*values, *earlier)


def mark_kernel(value_ref, _, mark_ref):
    mark_ref[...] = value_ref[: mark_ref.shape[0], : mark_ref.shape[1]]


def mark(value, earlier):
    return pl.pallas_call(
        mark_kernel,
        out_shape=jax.ShapeDtypeStruct((16, 128), value.dtype),
        in_specs=[HERE, ANYWHERE],
        compiler_params=SMALL,
        cost_estimate=CHEAP,
        name="mark",
    )(value, earlier)


def flip_kernel(source_ref, here_ref, flipped_ref, sems):
    steps = source_ref.shape[0] // SLICE
    copies = []
    for j in range(steps):
        rows = pl.ds(j * SLICE, SLICE)
        copies.append(pltpu.make_async_copy(source_ref.at[rows], here_ref.at[rows], sems.at[j]))
        copies[j].start()
    for j in range(steps):
        copies[j].wait()
        rows = slice(j * SLICE, (j + 1) * SLICE)
        flipped_ref[:, rows] = here_ref[rows, :].T


def flip(value):
    return pl.pallas_call(
        flip_kernel,
        out_shape=[pltpu.VMEM(value.shape, value.dtype), pltpu.VMEM(value.shape[::-1], value.dtype)],
        in_specs=[AFAR],
        out_specs=[HERE, HERE],
        scratch_shapes=[pltpu.SemaphoreType.DMA((value.shape[0] // SLICE,))],
        compiler_params=SMALL,
        cost_estimate=CHEAP,
        name="flip",
    )(kept(value))


def forward_kernel(n, fetch, down, pair, unused, *refs):
    refs = list(refs[unused:])
    xs = [refs.pop(0) for _ in range(n)]
    wg_ref, wu_ref = refs.pop(0), refs.pop(0)
    wd_ref = refs.pop(0) if down else None
    other_ref = refs.pop(0) if pair else None
    act_ref, coef_ref = refs.pop(0), refs.pop(0)
    shares = [refs.pop(0) for _ in range(EXPERTS if pair else down)]
    if fetch:
        sources, sems = (wg_ref, wu_ref), refs.pop()
        wg_ref, wu_ref = refs.pop(0), refs.pop(0)
    acc_ref = refs.pop(0) if down else None
    part = xs[0].shape[0]
    x_ref = xs[0]
    if n > 1:
        x_ref = refs.pop(0)
        for i in range(n):
            x_ref[i * part : (i + 1) * part, :] = xs[i][...]
    steps = wg_ref.shape[1] // (2 * WIDE)

    def copies(j):
        cols = pl.ds(pl.multiple_of(j * (2 * WIDE), (2 * WIDE)), (2 * WIDE))
        return [
            pltpu.make_async_copy(source.at[:, cols], target.at[:, cols], sems.at[j, i])
            for i, (source, target) in enumerate(zip(sources, (wg_ref, wu_ref)))
        ]

    if fetch:
        for j in range(steps):
            for copy in copies(j):
                copy.start()
    if down:
        acc_ref[...] = jnp.zeros_like(acc_ref)

    @pl.loop(0, steps)
    def _(j):
        if fetch:
            for copy in copies(j):
                copy.wait()
        for i in range(2):
            cols = pl.ds(pl.multiple_of(j * (2 * WIDE) + i * WIDE, WIDE), WIDE)
            gate = jnp.dot(x_ref[...], wg_ref[:, cols], preferred_element_type=F32)
            up = jnp.dot(x_ref[...], wu_ref[:, cols], preferred_element_type=F32)
            act, slope = silu_parts(gate)
            act_ref[:, cols] = act.astype(BF16)
            coef_ref[:, cols] = (up * slope).astype(BF16)
            if down:
                hidden = (act[:part] * up[:part]).astype(BF16)
                acc_ref[...] += jnp.dot(hidden, wd_ref[cols, :], preferred_element_type=F32)

    if pair:
        other = other_ref[...].astype(F32)
        for k in range(EXPERTS):
            rows = slice(k * CAP, (k + 1) * CAP)
            block = jnp.concatenate([other[rows], acc_ref[rows, :]], axis=0).astype(BF16)
            shares[k][...] = block
    elif down:
        shares[0][...] = acc_ref[...].astype(BF16)


def forward(xs, wg, wu, wd=None, other=None, fetch=False, earlier=(), cost=CHEAP):
    n, (part, width), cols = len(xs), xs[0].shape, wg.shape[1]
    rows = n * part
    down, pair = wd is not None, other is not None
    shares = [jax.ShapeDtypeStruct((part, width), BF16)] * down
    if pair:
        shares = [jax.ShapeDtypeStruct((2 * CAP, width), BF16)] * EXPERTS
    weights = [kept(wg), kept(wu)] if fetch else [wg, wu]
    return pl.pallas_call(
        functools.partial(forward_kernel, n, fetch, down, pair, len(earlier)),
        out_shape=[jax.ShapeDtypeStruct((rows, cols), BF16)] * 2
        + shares
        + [pltpu.VMEM(wg.shape, wg.dtype)] * (2 * fetch),
        in_specs=[ANYWHERE] * len(earlier)
        + [HERE] * n
        + [AFAR if fetch else HERE] * 2
        + [HERE] * (down + pair),
        scratch_shapes=[pltpu.VMEM((part, width), F32)] * down
        + [pltpu.VMEM((rows, width), BF16)] * (n > 1)
        + [pltpu.SemaphoreType.DMA((cols // (2 * WIDE), 2))] * fetch,
        compiler_params=LARGE,
        cost_estimate=cost,
        name="forward" + "_fetch" * fetch + "_down" * down,
    )(*earlier, *xs, *weights, *([wd] * down), *([other] * pair))


def turn_kernel(_, __, *refs):
    refs[8][: refs[0].shape[1], :] = stacked(refs[0:4]).T.astype(BF16)
    refs[8][refs[0].shape[1] :, :] = stacked(refs[4:8]).T.astype(BF16)


def turn(own, sib, xs, share):
    part = xs[0].shape[0]
    rows = len(xs) * part
    return pl.pallas_call(
        turn_kernel,
        grid_spec=pltpu.PrefetchScalarGridSpec(
            num_scalar_prefetch=2,
            grid=(1,),
            in_specs=[pl.BlockSpec((part, share), lambda j, a, b: (0, a[0]))] * 4
            + [pl.BlockSpec((part, share), lambda j, a, b: (0, b[0]))] * 4,
            out_specs=pl.BlockSpec((2 * share, rows), lambda j, a, b: (0, 0)),
        ),
        out_shape=jax.ShapeDtypeStruct((2 * share, rows), BF16),
        compiler_params=SMALL,
        cost_estimate=CHEAP,
        name="turn",
    )(own, sib, *xs, *xs)


def slopes_kernel(n, *refs):
    gs, acts, coefs = refs[:n], refs[n : 2 * n], refs[2 * n : 3 * n]
    wdt_ref, dg_ref, du_ref, g_ref = refs[3 * n :]
    part = gs[0].shape[0]
    for i in range(n):
        g_ref[i * part : (i + 1) * part, :] = gs[i][...]
    for start in range(0, wdt_ref.shape[1], STRIP):
        cols = slice(start, start + STRIP)
        d_hidden = jnp.dot(g_ref[...], wdt_ref[:, cols], preferred_element_type=F32)
        for i in range(n):
            rows = slice(i * part, (i + 1) * part)
            dg_ref[rows, cols] = (d_hidden[rows] * coefs[i][:, cols].astype(F32)).astype(BF16)
            du_ref[rows, cols] = (d_hidden[rows] * acts[i][:, cols].astype(F32)).astype(BF16)


def slopes(gs, acts, coefs, wdt):
    n, (part, width) = len(gs), gs[0].shape
    return pl.pallas_call(
        functools.partial(slopes_kernel, n),
        out_shape=[jax.ShapeDtypeStruct((n * part, wdt.shape[1]), BF16)] * 2,
        in_specs=[HERE] * (3 * n + 1),
        scratch_shapes=[pltpu.VMEM((n * part, width), BF16)],
        compiler_params=LARGE,
        cost_estimate=CHEAP,
        name="slopes",
    )(*gs, *acts, *coefs, wdt)


def backward_kernel(first, xt_ref, g_ref, act_ref, coef_ref, dg_ref, du_ref, wdt_ref, *refs):
    own_ref, sib_ref = refs[-2:]
    share = own_ref.shape[0] // 2
    for start in range(0, own_ref.shape[1], STRIP):
        here = slice(start, start + STRIP)
        cols = slice(first + start, first + start + STRIP)
        d_hidden = jnp.dot(g_ref[...], wdt_ref[:, cols], preferred_element_type=F32)
        for row, factor_ref, known_ref in ((0, coef_ref, dg_ref), (share, act_ref, du_ref)):
            d_cols = (d_hidden * factor_ref[:, cols].astype(F32)).astype(BF16)
            d_cols = jnp.concatenate([known_ref[:, cols], d_cols], axis=0)
            total = jnp.dot(xt_ref[...], d_cols, preferred_element_type=F32).astype(BF16)
            own_ref[row : row + share, here] = total[:share]
            sib_ref[row : row + share, here] = total[share:]


def backward(xt, g, act, coef, dg, du, wdt, first, cols, earlier=()):
    return pl.pallas_call(
        functools.partial(backward_kernel, first),
        out_shape=[jax.ShapeDtypeStruct((xt.shape[0], cols), BF16)] * 2,
        in_specs=[HERE] * 7 + [ANYWHERE] * len(earlier),
        compiler_params=LARGE,
        cost_estimate=DEAR,
        name="backward",
    )(xt, g, act, coef, dg, du, wdt, *earlier)


def finish_kernel(spans, more, unused, *refs):
    refs = refs[unused:]
    n = len(spans)
    pairs = [refs[2 * i : 2 * i + 2] for i in range(n)]
    gate_ref, up_ref, gate, up, sems = refs[2 * n + 2 * more :]
    share = gate_ref.shape[0]
    low = spans[0][0]
    copies = []
    for i, ((first, cols), (own, got)) in enumerate(zip(spans, pairs)):
        for j, (target, held) in enumerate(((gate_ref, gate), (up_ref, up))):
            rows = slice(j * share, (j + 1) * share)
            here = pl.ds(first - low, cols)
            held[:, here] = (own[rows, :].astype(F32) + got[rows, :].astype(F32)).astype(BF16)
            copies.append(
                pltpu.make_async_copy(held.at[:, here], target.at[:, pl.ds(first, cols)], sems.at[i, j])
            )
            copies[-1].start()
    for copy in copies:
        copy.wait()


def finish(owns, gots, firsts, width, held=(), earlier=()):
    share = owns[0].shape[0] // 2
    spans = tuple((first, own.shape[1]) for first, own in zip(firsts, owns))
    total = sum(cols for _, cols in spans)
    n, more = len(owns), len(held) > 0
    return pl.pallas_call(
        functools.partial(finish_kernel, spans, more, len(earlier)),
        out_shape=[jax.ShapeDtypeStruct((share, width), BF16)] * 2,
        in_specs=[AFAR] * len(earlier) + [HERE] * (2 * n) + [ANYWHERE] * (2 * more),
        out_specs=[ANYWHERE] * 2,
        scratch_shapes=[pltpu.VMEM((share, total), BF16)] * 2 + [pltpu.SemaphoreType.DMA((n, 2))],
        input_output_aliases={len(earlier) + 2 * n: 0, len(earlier) + 2 * n + 1: 1} if more else {},
        compiler_params=SMALL,
        cost_estimate=CHEAP,
        name="finish",
    )(*[kept(v) for v in earlier], *[v for both in zip(owns, gots) for v in both], *held)


def split_kernel(*refs):
    blocks = [refs[SENT.index(k)][...].astype(F32) for k in range(EXPERTS)]
    refs[-2][...] = jnp.concatenate([b[:CAP] for b in blocks], axis=0).astype(BF16)
    refs[-1][...] = jnp.concatenate([b[CAP:] for b in blocks], axis=0).astype(BF16)


def split(blocks, earlier):
    width = blocks[0].shape[1]
    return pl.pallas_call(
        split_kernel,
        out_shape=[jax.ShapeDtypeStruct((EXPERTS * CAP, width), BF16)] * 2,
        in_specs=[HERE] * EXPERTS + [ANYWHERE] * len(earlier),
        compiler_params=SMALL,
        cost_estimate=CHEAP,
        name="split",
    )(*[blocks[k] for k in SENT], *earlier)


def unpack_kernel(placer_ref, mine_ref, got_ref, *refs):
    chosen = placer_ref[...].astype(F32).T.astype(BF16)
    total = jnp.dot(chosen, mine_ref[...], preferred_element_type=F32)
    total += jnp.dot(chosen, got_ref[...], preferred_element_type=F32)
    refs[-1][...] = total.astype(BF16)


def unpack(placer, mine, got, earlier):
    return pl.pallas_call(
        unpack_kernel,
        out_shape=jax.ShapeDtypeStruct((placer.shape[1], mine.shape[1]), BF16),
        in_specs=[HERE] * 3 + [AFAR] * len(earlier),
        compiler_params=SMALL,
        cost_estimate=DEAR,
        name="unpack",
    )(placer, mine, got, *[kept(v) for v in earlier])


def swap(value, axis):
    return lax.ppermute(value, axis, [(0, 1), (1, 0)])


def across_planes(blocks):
    return [blocks[0]] + [
        lax.ppermute(blocks[k], "arch", [(i, i ^ k) for i in range(EXPERTS)]) for k in range(1, EXPERTS)
    ]


def after(values, earlier):
    n = len(values)
    return list(lax.optimization_barrier((*values, *earlier))[:n])


def gathering(designs, archetype, w_gate, w_up, w_down, cotangent):
    far, core = lax.axis_index("far"), lax.axis_index("core")
    scalars = [lax.axis_index("arch"), 2 * far + core, 2 * far + 1 - core]
    scalars = [v.astype(jnp.int32)[None] for v in scalars]
    tokens, width = designs.shape
    share = width // 4
    placer, *blocks = pack(scalars, archetype.reshape(1, tokens), designs, cotangent)
    wd, wdt = flip(after([w_down], [placer])[0])

    x_own = join(across_planes(blocks[:EXPERTS]))
    moved = across_planes(relay(blocks[EXPERTS:], [wdt]))
    x_far, x_near = swap(x_own, "far"), swap(x_own, "half")

    wg, wu = w_gate, w_up
    act0, coef0, share_own = forward([x_own], wg, wu, wd)
    g_own = join(moved, [act0])
    g_far, g_near = swap(g_own, "far"), swap(g_own, "half")
    act1, coef1, *shares = forward([x_near], wg, wu, wd, other=share_own)
    (x_pass,) = relay([x_near], [mark(act1, x_far), g_far])
    (g_pass,) = relay([g_far], [x_pass, g_near])
    x_corner, g_corner = swap(x_pass, "far"), swap(g_pass, "half")
    returned = across_planes(shares)
    act2, coef2 = forward([x_far], wg, wu, earlier=[g_pass], cost=DEAR)
    dg, du = slopes([g_own, g_near, g_far], [act0, act1, act2], [coef0, coef1, coef2], wdt)
    act3, coef3 = forward([x_corner], wg, wu, earlier=[dg])
    mine, theirs = split(returned, [act3])
    got = swap(theirs, "half")
    xt = turn(*scalars[1:], [x_own, x_near, x_far, x_corner], share)

    rest = (xt, g_corner, act3, coef3, dg, du, wdt)
    cols = w_down.shape[0]
    cut = cols // 2
    own0, sib0 = backward(*rest, 0, cut)
    own1, sib1 = backward(*rest, cut, cols - cut, [own0])
    got0, got1 = swap(sib0, "core"), swap(sib1, "core")
    held = finish([own0], [got0], (0,), cols)
    outputs = unpack(placer, mine, got, held[:1])
    grad_gate, grad_up = finish([own1], [got1], (cut,), cols, held)
    return outputs, grad_gate, grad_up


def reducing(designs, archetype, w_gate, w_up, w_down, cotangent):
    width = designs.shape[1]
    owners = lax.axis_size("expert")
    sharers = owners // EXPERTS
    hidden_cols = w_gate.shape[1]
    labels = archetype[:, 0]
    onehot = (labels[:, None] == jnp.arange(EXPERTS, dtype=jnp.int32)[None, :]).astype(jnp.int32)
    ranks = jnp.cumsum(onehot, axis=0) - onehot
    target = labels * CAP + jnp.sum(ranks * onehot, axis=1)
    placer = (jnp.arange(EXPERTS * CAP, dtype=jnp.int32)[:, None] == target[None, :]).astype(BF16)
    received = []
    for rows in (designs, cotangent):
        packed = jnp.dot(placer, rows, preferred_element_type=F32).astype(BF16)
        send = jnp.repeat(packed.reshape(EXPERTS, CAP, width), sharers, axis=0)
        received.append(
            lax.all_to_all(send, "expert", split_axis=0, concat_axis=0, tiled=True).reshape(
                owners * CAP, width
            )
        )
    flat_x, flat_g = received
    gate = jnp.dot(flat_x, w_gate, preferred_element_type=F32)
    up = jnp.dot(flat_x, w_up, preferred_element_type=F32)
    act, slope = silu_parts(gate)
    hidden = (act * up).astype(BF16)
    partial_value = (
        jnp.dot(hidden, w_down, preferred_element_type=F32).astype(BF16).reshape(owners, CAP, width)
    )
    returned = lax.all_to_all(partial_value, "expert", split_axis=0, concat_axis=0, tiled=True)
    summed = jnp.sum(returned.astype(F32).reshape(EXPERTS, sharers, CAP, width), axis=1).reshape(
        EXPERTS * CAP, width
    )
    outputs = jnp.take(summed, target, axis=0).astype(BF16)
    d_hidden = contract_cols(flat_g, w_down)
    d_gate = (d_hidden * up * slope).astype(BF16)
    d_up = (d_hidden * act).astype(BF16)
    grads = jnp.concatenate([contract_rows(flat_x, d_gate), contract_rows(flat_x, d_up)], axis=1)
    mine = lax.psum_scatter(grads.astype(BF16), "dp", scatter_dimension=0, tiled=True)
    return outputs, mine[:, :hidden_cols], mine[:, hidden_cols:]


def solution(mesh):
    dp, owners = mesh.devices.shape
    if (dp, owners) == (4, 2 * EXPERTS):
        rows, cols = ("far", "core"), ("arch", "half")
        mesh = Mesh(mesh.devices.reshape(2, 2, EXPERTS, 2), rows + cols)
        body = gathering
    else:
        rows, cols = ("dp",), ("expert",)
        body = reducing
    tokens = P(rows + cols, None)
    return jax.shard_map(
        body,
        mesh=mesh,
        in_specs=(tokens, tokens, P(None, cols), P(None, cols), P(cols, None), tokens),
        out_specs=(tokens, P(rows, cols), P(rows, cols)),
        check_vma=False,
    )
```

```python
import functools

import jax
import jax.numpy as jnp
from jax import lax
from jax.experimental import pallas as pl
from jax.experimental.pallas import tpu as pltpu
from jax.sharding import Mesh
from jax.sharding import PartitionSpec as P

EXPERTS = 4
CAP = 36
WIDE = 1024
STRIP = 512
SLICE = 256
SENT = (0, 2, 1, 3)
MIB = 1024 * 1024
LARGE = pltpu.CompilerParams(vmem_limit_bytes=16 * MIB)
SMALL = pltpu.CompilerParams(vmem_limit_bytes=12 * MIB)
CHEAP = pl.CostEstimate(flops=0, bytes_accessed=0, transcendentals=0)
DEAR = pl.CostEstimate(flops=20_000_000_000, bytes_accessed=0, transcendentals=0)
F32 = jnp.float32
BF16 = jnp.bfloat16
HERE = pl.BlockSpec(memory_space=pltpu.VMEM)
AFAR = pl.BlockSpec(memory_space=pltpu.HBM)
ANYWHERE = pl.BlockSpec(memory_space=pl.ANY)


def silu_parts(gate):
    sigma = 0.5 * jnp.tanh(0.5 * gate) + 0.5
    return (gate * sigma, sigma * (1.0 + gate * (1.0 - sigma)))


def contract_rows(left, right):
    return lax.dot_general(left, right, (((0,), (0,)), ((), ())), preferred_element_type=F32)


def contract_cols(left, right):
    return lax.dot_general(left, right, (((1,), (1,)), ((), ())), preferred_element_type=F32)


def stacked(refs):
    return jnp.concatenate([r[...].astype(F32) for r in refs], axis=0)


def kept(value):
    return pltpu.with_memory_space_constraint(value, pltpu.HBM)


def pack_kernel(plane_ref, _, __, kind_ref, x_ref, g_ref, placer_ref, *refs):
    outs, (kind, x, g, sems) = refs[: 2 * EXPERTS], refs[2 * EXPERTS :]
    copies = [
        pltpu.make_async_copy(source, target, sems.at[i])
        for i, (source, target) in enumerate(((kind_ref, kind), (x_ref, x), (g_ref, g)))
    ]
    for copy in copies:
        copy.start()
    tokens = kind.shape[1]
    copies[0].wait()
    key = kind[...] ^ plane_ref[0]
    onehot = (key == lax.broadcasted_iota(jnp.int32, (8, tokens), 0)).astype(F32)
    before = lax.broadcasted_iota(jnp.int32, (tokens, tokens), 0) < lax.broadcasted_iota(
        jnp.int32, (tokens, tokens), 1
    )
    ranks = jnp.dot(onehot.astype(BF16), before.astype(BF16), preferred_element_type=F32)
    rank = jnp.sum(ranks * onehot, axis=0, keepdims=True).astype(jnp.int32)
    place = key * CAP + rank
    slots = EXPERTS * CAP
    placer = (place == lax.broadcasted_iota(jnp.int32, (slots, tokens), 0)).astype(F32).astype(BF16)
    placer_ref[...] = placer
    for copy, source, first in ((copies[1], x, 0), (copies[2], g, EXPERTS)):
        copy.wait()
        packed = jnp.dot(placer, source[...], preferred_element_type=F32)
        for k in range(EXPERTS):
            outs[first + k][...] = packed[k * CAP : (k + 1) * CAP].astype(BF16)


def pack(scalars, kind, x, g):
    tokens, width = x.shape
    return pl.pallas_call(
        pack_kernel,
        out_shape=[jax.ShapeDtypeStruct((EXPERTS * CAP, tokens), BF16)]
        + [jax.ShapeDtypeStruct((CAP, width), BF16)] * (2 * EXPERTS),
        in_specs=[pl.BlockSpec(memory_space=pltpu.SMEM)] * 3 + [AFAR] * 3,
        scratch_shapes=[
            pltpu.VMEM((1, tokens), jnp.int32),
            pltpu.VMEM((tokens, width), BF16),
            pltpu.VMEM((tokens, width), BF16),
            pltpu.SemaphoreType.DMA((3,)),
        ],
        compiler_params=SMALL,
        cost_estimate=DEAR,
        name="pack",
    )(*scalars, kept(kind), kept(x), kept(g))


def join_kernel(order, *refs):
    blocks = refs[-1 - EXPERTS : -1]
    refs[-1][...] = stacked([blocks[order.index(k)] for k in range(EXPERTS)]).astype(BF16)


def join(blocks, order, earlier=()):
    width = blocks[0].shape[1]
    return pl.pallas_call(
        functools.partial(join_kernel, order),
        out_shape=jax.ShapeDtypeStruct((EXPERTS * CAP, width), BF16),
        in_specs=[ANYWHERE] * len(earlier) + [HERE] * EXPERTS,
        compiler_params=SMALL,
        cost_estimate=CHEAP,
        name="join",
    )(*earlier, *[blocks[k] for k in order])


def relay_kernel(n, *refs):
    for i in range(n):
        refs[len(refs) - n + i][...] = refs[i][...]


def relay(values, earlier):
    n = len(values)
    return pl.pallas_call(
        functools.partial(relay_kernel, n),
        out_shape=[jax.ShapeDtypeStruct(v.shape, v.dtype) for v in values],
        in_specs=[HERE] * n + [ANYWHERE] * len(earlier),
        compiler_params=SMALL,
        cost_estimate=CHEAP,
        name="relay",
    )(*values, *earlier)


def mark_kernel(value_ref, _, mark_ref):
    mark_ref[...] = value_ref[: mark_ref.shape[0], : mark_ref.shape[1]]


def mark(value, earlier):
    return pl.pallas_call(
        mark_kernel,
        out_shape=jax.ShapeDtypeStruct((16, 128), value.dtype),
        in_specs=[HERE, ANYWHERE],
        compiler_params=SMALL,
        cost_estimate=CHEAP,
        name="mark",
    )(value, earlier)


def flip_kernel(source_ref, *refs):
    flipped_ref = refs[-1]
    for j in range(source_ref.shape[0] // SLICE):
        rows = slice(j * SLICE, (j + 1) * SLICE)
        flipped_ref[:, rows] = source_ref[rows, :].T


def flip(value, earlier):
    return pl.pallas_call(
        flip_kernel,
        out_shape=pltpu.VMEM(value.shape[::-1], value.dtype),
        in_specs=[HERE] + [ANYWHERE] * len(earlier),
        out_specs=HERE,
        compiler_params=SMALL,
        cost_estimate=CHEAP,
        name="flip",
    )(value, *earlier)


def forward_kernel(n, fetch, down, pair, unused, *refs):
    refs = list(refs[unused:])
    xs = [refs.pop(0) for _ in range(n)]
    wg_ref, wu_ref = refs.pop(0), refs.pop(0)
    wd_ref = refs.pop(0) if down else None
    other_ref = refs.pop(0) if pair else None
    act_ref, coef_ref = refs.pop(0), refs.pop(0)
    shares = [refs.pop(0) for _ in range(EXPERTS if pair else down)]
    if fetch:
        sources, sems = (wg_ref, wu_ref), refs.pop()
        wg_ref, wu_ref = refs.pop(0), refs.pop(0)
    acc_ref = refs.pop(0) if down else None
    part = xs[0].shape[0]
    x_ref = xs[0]
    if n > 1:
        x_ref = refs.pop(0)
        for i in range(n):
            x_ref[i * part : (i + 1) * part, :] = xs[i][...]
    steps = wg_ref.shape[1] // (2 * WIDE)

    def copies(j):
        cols = pl.ds(pl.multiple_of(j * (2 * WIDE), (2 * WIDE)), (2 * WIDE))
        return [
            pltpu.make_async_copy(source.at[:, cols], target.at[:, cols], sems.at[j, i])
            for i, (source, target) in enumerate(zip(sources, (wg_ref, wu_ref)))
        ]

    if fetch:
        for j in range(steps):
            for copy in copies(j):
                copy.start()
    if down:
        acc_ref[...] = jnp.zeros_like(acc_ref)

    @pl.loop(0, steps)
    def _(j):
        if fetch:
            for copy in copies(j):
                copy.wait()
        for i in range(2):
            cols = pl.ds(pl.multiple_of(j * (2 * WIDE) + i * WIDE, WIDE), WIDE)
            gate = jnp.dot(x_ref[...], wg_ref[:, cols], preferred_element_type=F32)
            up = jnp.dot(x_ref[...], wu_ref[:, cols], preferred_element_type=F32)
            act, slope = silu_parts(gate)
            act_ref[:, cols] = act.astype(BF16)
            coef_ref[:, cols] = (up * slope).astype(BF16)
            if down:
                hidden = (act[:part] * up[:part]).astype(BF16)
                acc_ref[...] += jnp.dot(hidden, wd_ref[cols, :], preferred_element_type=F32)

    if pair:
        other = other_ref[...].astype(F32)
        for k in range(EXPERTS):
            rows = slice(k * CAP, (k + 1) * CAP)
            block = jnp.concatenate([other[rows], acc_ref[rows, :]], axis=0).astype(BF16)
            shares[k][...] = block
    elif down:
        shares[0][...] = acc_ref[...].astype(BF16)


def forward(xs, wg, wu, wd=None, other=None, fetch=False, earlier=(), cost=CHEAP):
    n, (part, width), cols = len(xs), xs[0].shape, wg.shape[1]
    rows = n * part
    down, pair = wd is not None, other is not None
    shares = [jax.ShapeDtypeStruct((part, width), BF16)] * down
    if pair:
        shares = [jax.ShapeDtypeStruct((2 * CAP, width), BF16)] * EXPERTS
    weights = [kept(wg), kept(wu)] if fetch else [wg, wu]
    return pl.pallas_call(
        functools.partial(forward_kernel, n, fetch, down, pair, len(earlier)),
        out_shape=[jax.ShapeDtypeStruct((rows, cols), BF16)] * 2
        + shares
        + [pltpu.VMEM(wg.shape, wg.dtype)] * (2 * fetch),
        in_specs=[ANYWHERE] * len(earlier)
        + [HERE] * n
        + [AFAR if fetch else HERE] * 2
        + [HERE] * (down + pair),
        scratch_shapes=[pltpu.VMEM((part, width), F32)] * down
        + [pltpu.VMEM((rows, width), BF16)] * (n > 1)
        + [pltpu.SemaphoreType.DMA((cols // (2 * WIDE), 2))] * fetch,
        compiler_params=LARGE,
        cost_estimate=cost,
        name="forward" + "_fetch" * fetch + "_down" * down,
    )(*earlier, *xs, *weights, *([wd] * down), *([other] * pair))


def turn_kernel(_, __, *refs):
    refs[8][: refs[0].shape[1], :] = stacked(refs[0:4]).T.astype(BF16)
    refs[8][refs[0].shape[1] :, :] = stacked(refs[4:8]).T.astype(BF16)


def turn(own, sib, xs, share):
    part = xs[0].shape[0]
    rows = len(xs) * part
    return pl.pallas_call(
        turn_kernel,
        grid_spec=pltpu.PrefetchScalarGridSpec(
            num_scalar_prefetch=2,
            grid=(1,),
            in_specs=[pl.BlockSpec((part, share), lambda j, a, b: (0, a[0]))] * 4
            + [pl.BlockSpec((part, share), lambda j, a, b: (0, b[0]))] * 4,
            out_specs=pl.BlockSpec((2 * share, rows), lambda j, a, b: (0, 0)),
        ),
        out_shape=jax.ShapeDtypeStruct((2 * share, rows), BF16),
        compiler_params=SMALL,
        cost_estimate=CHEAP,
        name="turn",
    )(own, sib, *xs, *xs)


def slopes_kernel(n, *refs):
    gs, acts, coefs = refs[:n], refs[n : 2 * n], refs[2 * n : 3 * n]
    wdt_ref, dg_ref, du_ref, g_ref = refs[3 * n :]
    part = gs[0].shape[0]
    for i in range(n):
        g_ref[i * part : (i + 1) * part, :] = gs[i][...]
    for start in range(0, wdt_ref.shape[1], STRIP):
        cols = slice(start, start + STRIP)
        d_hidden = jnp.dot(g_ref[...], wdt_ref[:, cols], preferred_element_type=F32)
        for i in range(n):
            rows = slice(i * part, (i + 1) * part)
            dg_ref[rows, cols] = (d_hidden[rows] * coefs[i][:, cols].astype(F32)).astype(BF16)
            du_ref[rows, cols] = (d_hidden[rows] * acts[i][:, cols].astype(F32)).astype(BF16)


def slopes(gs, acts, coefs, wdt):
    n, (part, width) = len(gs), gs[0].shape
    return pl.pallas_call(
        functools.partial(slopes_kernel, n),
        out_shape=[jax.ShapeDtypeStruct((n * part, wdt.shape[1]), BF16)] * 2,
        in_specs=[HERE] * (3 * n + 1),
        scratch_shapes=[pltpu.VMEM((n * part, width), BF16)],
        compiler_params=LARGE,
        cost_estimate=CHEAP,
        name="slopes",
    )(*gs, *acts, *coefs, wdt)


def backward_kernel(first, xt_ref, g_ref, act_ref, coef_ref, dg_ref, du_ref, wdt_ref, *refs):
    own_ref, sib_ref = refs[-2:]
    share = own_ref.shape[0] // 2
    for start in range(0, own_ref.shape[1], STRIP):
        here = slice(start, start + STRIP)
        cols = slice(first + start, first + start + STRIP)
        d_hidden = jnp.dot(g_ref[...], wdt_ref[:, cols], preferred_element_type=F32)
        for row, factor_ref, known_ref in ((0, coef_ref, dg_ref), (share, act_ref, du_ref)):
            d_cols = (d_hidden * factor_ref[:, cols].astype(F32)).astype(BF16)
            d_cols = jnp.concatenate([known_ref[:, cols], d_cols], axis=0)
            total = jnp.dot(xt_ref[...], d_cols, preferred_element_type=F32).astype(BF16)
            own_ref[row : row + share, here] = total[:share]
            sib_ref[row : row + share, here] = total[share:]


def backward(xt, g, act, coef, dg, du, wdt, first, cols, earlier=()):
    return pl.pallas_call(
        functools.partial(backward_kernel, first),
        out_shape=[jax.ShapeDtypeStruct((xt.shape[0], cols), BF16)] * 2,
        in_specs=[HERE] * 7 + [ANYWHERE] * len(earlier),
        compiler_params=LARGE,
        cost_estimate=DEAR,
        name="backward",
    )(xt, g, act, coef, dg, du, wdt, *earlier)


def finish_kernel(spans, more, unused, *refs):
    refs = refs[unused:]
    n = len(spans)
    pairs = [refs[2 * i : 2 * i + 2] for i in range(n)]
    gate_ref, up_ref, gate, up, sems = refs[2 * n + 2 * more :]
    share = gate_ref.shape[0]
    low = spans[0][0]
    copies = []
    for i, ((first, cols), (own, got)) in enumerate(zip(spans, pairs)):
        for j, (target, held) in enumerate(((gate_ref, gate), (up_ref, up))):
            rows = slice(j * share, (j + 1) * share)
            here = pl.ds(first - low, cols)
            held[:, here] = (own[rows, :].astype(F32) + got[rows, :].astype(F32)).astype(BF16)
            copies.append(
                pltpu.make_async_copy(held.at[:, here], target.at[:, pl.ds(first, cols)], sems.at[i, j])
            )
            copies[-1].start()
    for copy in copies:
        copy.wait()


def finish(owns, gots, firsts, width, held=(), earlier=()):
    share = owns[0].shape[0] // 2
    spans = tuple((first, own.shape[1]) for first, own in zip(firsts, owns))
    total = sum(cols for _, cols in spans)
    n, more = len(owns), len(held) > 0
    return pl.pallas_call(
        functools.partial(finish_kernel, spans, more, len(earlier)),
        out_shape=[jax.ShapeDtypeStruct((share, width), BF16)] * 2,
        in_specs=[AFAR] * len(earlier) + [HERE] * (2 * n) + [ANYWHERE] * (2 * more),
        out_specs=[ANYWHERE] * 2,
        scratch_shapes=[pltpu.VMEM((share, total), BF16)] * 2 + [pltpu.SemaphoreType.DMA((n, 2))],
        input_output_aliases={len(earlier) + 2 * n: 0, len(earlier) + 2 * n + 1: 1} if more else {},
        compiler_params=SMALL,
        cost_estimate=CHEAP,
        name="finish",
    )(*[kept(v) for v in earlier], *[v for both in zip(owns, gots) for v in both], *held)


def split_kernel(*refs):
    blocks = [refs[SENT.index(k)][...].astype(F32) for k in range(EXPERTS)]
    refs[-2][...] = jnp.concatenate([b[:CAP] for b in blocks], axis=0).astype(BF16)
    refs[-1][...] = jnp.concatenate([b[CAP:] for b in blocks], axis=0).astype(BF16)


def split(blocks, earlier):
    width = blocks[0].shape[1]
    return pl.pallas_call(
        split_kernel,
        out_shape=[jax.ShapeDtypeStruct((EXPERTS * CAP, width), BF16)] * 2,
        in_specs=[HERE] * EXPERTS + [ANYWHERE] * len(earlier),
        compiler_params=SMALL,
        cost_estimate=CHEAP,
        name="split",
    )(*[blocks[k] for k in SENT], *earlier)


def unpack_kernel(placer_ref, mine_ref, got_ref, *refs):
    chosen = placer_ref[...].astype(F32).T.astype(BF16)
    total = jnp.dot(chosen, mine_ref[...], preferred_element_type=F32)
    total += jnp.dot(chosen, got_ref[...], preferred_element_type=F32)
    refs[-1][...] = total.astype(BF16)


def unpack(placer, mine, got, earlier):
    return pl.pallas_call(
        unpack_kernel,
        out_shape=jax.ShapeDtypeStruct((placer.shape[1], mine.shape[1]), BF16),
        in_specs=[HERE] * 3 + [AFAR] * len(earlier),
        compiler_params=SMALL,
        cost_estimate=DEAR,
        name="unpack",
    )(placer, mine, got, *[kept(v) for v in earlier])


def swap(value, axis):
    return lax.ppermute(value, axis, [(0, 1), (1, 0)])


def across_planes(blocks):
    return [blocks[0]] + [
        lax.ppermute(blocks[k], "arch", [(i, i ^ k) for i in range(EXPERTS)]) for k in range(1, EXPERTS)
    ]


def after(values, earlier):
    n = len(values)
    return list(lax.optimization_barrier((*values, *earlier))[:n])


def gathering(designs, archetype, w_gate, w_up, w_down, cotangent):
    far, core = lax.axis_index("far"), lax.axis_index("core")
    scalars = [lax.axis_index("arch"), 2 * far + core, 2 * far + 1 - core]
    scalars = [v.astype(jnp.int32)[None] for v in scalars]
    tokens, width = designs.shape
    share = width // 4
    placer, *blocks = pack(scalars, archetype.reshape(1, tokens), designs, cotangent)
    wd, wdt = w_down, flip(w_down, [placer])

    x_own = join(across_planes(blocks[:EXPERTS]), (3, 2, 1, 0))
    moved = across_planes(relay(blocks[EXPERTS:], [wdt]))
    x_far, x_near = swap(x_own, "far"), swap(x_own, "half")

    wg, wu = w_gate, w_up
    act0, coef0, share_own = forward([x_own], wg, wu, wd)
    g_own = join(moved, (1, 3, 2, 0), [act0])
    g_far, g_near = swap(g_own, "far"), swap(g_own, "half")
    act1, coef1, *shares = forward([x_near], wg, wu, wd, other=share_own)
    (x_pass,) = relay([x_near], [mark(act1, x_far), g_far])
    (g_pass,) = relay([g_far], [x_pass, g_near])
    x_corner, g_corner = swap(x_pass, "far"), swap(g_pass, "half")
    returned = across_planes(shares)
    act2, coef2 = forward([x_far], wg, wu, earlier=[g_pass], cost=DEAR)
    dg, du = slopes([g_own, g_near, g_far], [act0, act1, act2], [coef0, coef1, coef2], wdt)
    act3, coef3 = forward([x_corner], wg, wu, earlier=[dg])
    mine, theirs = split(returned, [act3])
    got = swap(theirs, "half")
    xt = turn(*scalars[1:], [x_own, x_near, x_far, x_corner], share)

    rest = (xt, g_corner, act3, coef3, dg, du, wdt)
    cols = w_down.shape[0]
    cut = cols // 2
    own0, sib0 = backward(*rest, 0, cut)
    own1, sib1 = backward(*rest, cut, cols - cut, [own0])
    got0, got1 = swap(sib0, "core"), swap(sib1, "core")
    held = finish([own0], [got0], (0,), cols)
    outputs = unpack(placer, mine, got, held[:1])
    grad_gate, grad_up = finish([own1], [got1], (cut,), cols, held)
    return outputs, grad_gate, grad_up


def reducing(designs, archetype, w_gate, w_up, w_down, cotangent):
    width = designs.shape[1]
    owners = lax.axis_size("expert")
    sharers = owners // EXPERTS
    hidden_cols = w_gate.shape[1]
    labels = archetype[:, 0]
    onehot = (labels[:, None] == jnp.arange(EXPERTS, dtype=jnp.int32)[None, :]).astype(jnp.int32)
    ranks = jnp.cumsum(onehot, axis=0) - onehot
    target = labels * CAP + jnp.sum(ranks * onehot, axis=1)
    placer = (jnp.arange(EXPERTS * CAP, dtype=jnp.int32)[:, None] == target[None, :]).astype(BF16)
    received = []
    for rows in (designs, cotangent):
        packed = jnp.dot(placer, rows, preferred_element_type=F32).astype(BF16)
        send = jnp.repeat(packed.reshape(EXPERTS, CAP, width), sharers, axis=0)
        received.append(
            lax.all_to_all(send, "expert", split_axis=0, concat_axis=0, tiled=True).reshape(
                owners * CAP, width
            )
        )
    flat_x, flat_g = received
    gate = jnp.dot(flat_x, w_gate, preferred_element_type=F32)
    up = jnp.dot(flat_x, w_up, preferred_element_type=F32)
    act, slope = silu_parts(gate)
    hidden = (act * up).astype(BF16)
    partial_value = (
        jnp.dot(hidden, w_down, preferred_element_type=F32).astype(BF16).reshape(owners, CAP, width)
    )
    returned = lax.all_to_all(partial_value, "expert", split_axis=0, concat_axis=0, tiled=True)
    summed = jnp.sum(returned.astype(F32).reshape(EXPERTS, sharers, CAP, width), axis=1).reshape(
        EXPERTS * CAP, width
    )
    outputs = jnp.take(summed, target, axis=0).astype(BF16)
    d_hidden = contract_cols(flat_g, w_down)
    d_gate = (d_hidden * up * slope).astype(BF16)
    d_up = (d_hidden * act).astype(BF16)
    grads = jnp.concatenate([contract_rows(flat_x, d_gate), contract_rows(flat_x, d_up)], axis=1)
    mine = lax.psum_scatter(grads.astype(BF16), "dp", scatter_dimension=0, tiled=True)
    return outputs, mine[:, :hidden_cols], mine[:, hidden_cols:]


def solution(mesh):
    dp, owners = mesh.devices.shape
    if (dp, owners) == (4, 2 * EXPERTS):
        rows, cols = ("far", "core"), ("arch", "half")
        mesh = Mesh(mesh.devices.reshape(2, 2, EXPERTS, 2), rows + cols)
        body = gathering
    else:
        rows, cols = ("dp",), ("expert",)
        body = reducing
    tokens = P(rows + cols, None)
    return jax.shard_map(
        body,
        mesh=mesh,
        in_specs=(tokens, tokens, P(None, cols), P(None, cols), P(cols, None), tokens),
        out_specs=(tokens, P(rows, cols), P(rows, cols)),
        check_vma=False,
    )
```

```python
import functools

import jax
import jax.numpy as jnp
from jax import lax
from jax.experimental import pallas as pl
from jax.experimental.pallas import tpu as pltpu
from jax.sharding import Mesh
from jax.sharding import PartitionSpec as P

EXPERTS = 4
CAP = 36
WIDE = 1024
STRIP = 1024
SLICE = 256
SENT = (0, 2, 1, 3)
MIB = 1024 * 1024
LARGE = pltpu.CompilerParams(vmem_limit_bytes=16 * MIB)
SMALL = pltpu.CompilerParams(vmem_limit_bytes=12 * MIB)
CHEAP = pl.CostEstimate(flops=0, bytes_accessed=0, transcendentals=0)
DEAR = pl.CostEstimate(flops=20_000_000_000, bytes_accessed=0, transcendentals=0)
F32 = jnp.float32
BF16 = jnp.bfloat16
HERE = pl.BlockSpec(memory_space=pltpu.VMEM)
AFAR = pl.BlockSpec(memory_space=pltpu.HBM)
ANYWHERE = pl.BlockSpec(memory_space=pl.ANY)


def silu_parts(gate):
    sigma = 0.5 * jnp.tanh(0.5 * gate) + 0.5
    return (gate * sigma, sigma * (1.0 + gate * (1.0 - sigma)))


def contract_rows(left, right):
    return lax.dot_general(left, right, (((0,), (0,)), ((), ())), preferred_element_type=F32)


def contract_cols(left, right):
    return lax.dot_general(left, right, (((1,), (1,)), ((), ())), preferred_element_type=F32)


def stacked(refs):
    return jnp.concatenate([r[...].astype(F32) for r in refs], axis=0)


def kept(value):
    return pltpu.with_memory_space_constraint(value, pltpu.HBM)


def pack_kernel(plane_ref, _, __, kind_ref, x_ref, g_ref, placer_ref, *refs):
    outs, (kind, x, g, sems) = refs[: 2 * EXPERTS], refs[2 * EXPERTS :]
    copies = [
        pltpu.make_async_copy(source, target, sems.at[i])
        for i, (source, target) in enumerate(((kind_ref, kind), (x_ref, x), (g_ref, g)))
    ]
    for copy in copies:
        copy.start()
    tokens = kind.shape[1]
    copies[0].wait()
    key = kind[...] ^ plane_ref[0]
    onehot = (key == lax.broadcasted_iota(jnp.int32, (8, tokens), 0)).astype(F32)
    before = lax.broadcasted_iota(jnp.int32, (tokens, tokens), 0) < lax.broadcasted_iota(
        jnp.int32, (tokens, tokens), 1
    )
    ranks = jnp.dot(onehot.astype(BF16), before.astype(BF16), preferred_element_type=F32)
    rank = jnp.sum(ranks * onehot, axis=0, keepdims=True).astype(jnp.int32)
    place = key * CAP + rank
    slots = EXPERTS * CAP
    placer = (place == lax.broadcasted_iota(jnp.int32, (slots, tokens), 0)).astype(F32).astype(BF16)
    placer_ref[...] = placer
    for copy, source, first in ((copies[1], x, 0), (copies[2], g, EXPERTS)):
        copy.wait()
        packed = jnp.dot(placer, source[...], preferred_element_type=F32)
        for k in range(EXPERTS):
            outs[first + k][...] = packed[k * CAP : (k + 1) * CAP].astype(BF16)


def pack(scalars, kind, x, g):
    tokens, width = x.shape
    return pl.pallas_call(
        pack_kernel,
        out_shape=[jax.ShapeDtypeStruct((EXPERTS * CAP, tokens), BF16)]
        + [jax.ShapeDtypeStruct((CAP, width), BF16)] * (2 * EXPERTS),
        in_specs=[pl.BlockSpec(memory_space=pltpu.SMEM)] * 3 + [AFAR] * 3,
        scratch_shapes=[
            pltpu.VMEM((1, tokens), jnp.int32),
            pltpu.VMEM((tokens, width), BF16),
            pltpu.VMEM((tokens, width), BF16),
            pltpu.SemaphoreType.DMA((3,)),
        ],
        compiler_params=SMALL,
        cost_estimate=CHEAP,
        name="pack",
    )(*scalars, kept(kind), kept(x), kept(g))


def join_kernel(*refs):
    refs[-1][...] = stacked(refs[-2 : -2 - EXPERTS : -1]).astype(BF16)


def join(blocks, earlier=()):
    width = blocks[0].shape[1]
    return pl.pallas_call(
        join_kernel,
        out_shape=jax.ShapeDtypeStruct((EXPERTS * CAP, width), BF16),
        in_specs=[ANYWHERE] * len(earlier) + [HERE] * EXPERTS,
        compiler_params=SMALL,
        cost_estimate=CHEAP,
        name="join",
    )(*earlier, *blocks[::-1])


def relay_kernel(n, *refs):
    for i in range(n):
        refs[len(refs) - n + i][...] = refs[i][...]


def relay(values, earlier):
    n = len(values)
    return pl.pallas_call(
        functools.partial(relay_kernel, n),
        out_shape=[jax.ShapeDtypeStruct(v.shape, v.dtype) for v in values],
        in_specs=[HERE] * n + [ANYWHERE] * len(earlier),
        compiler_params=SMALL,
        cost_estimate=CHEAP,
        name="relay",
    )(*values, *earlier)


def mark_kernel(value_ref, _, mark_ref):
    mark_ref[...] = value_ref[: mark_ref.shape[0], : mark_ref.shape[1]]


def mark(value, earlier):
    return pl.pallas_call(
        mark_kernel,
        out_shape=jax.ShapeDtypeStruct((16, 128), value.dtype),
        in_specs=[HERE, ANYWHERE],
        compiler_params=SMALL,
        cost_estimate=CHEAP,
        name="mark",
    )(value, earlier)


def flip_kernel(source_ref, here_ref, flipped_ref, sems):
    steps = source_ref.shape[0] // SLICE
    copies = []
    for j in range(steps):
        rows = pl.ds(j * SLICE, SLICE)
        copies.append(pltpu.make_async_copy(source_ref.at[rows], here_ref.at[rows], sems.at[j]))
        copies[j].start()
    for j in range(steps):
        copies[j].wait()
        rows = slice(j * SLICE, (j + 1) * SLICE)
        flipped_ref[:, rows] = here_ref[rows, :].T


def flip(value):
    return pl.pallas_call(
        flip_kernel,
        out_shape=[pltpu.VMEM(value.shape, value.dtype), pltpu.VMEM(value.shape[::-1], value.dtype)],
        in_specs=[AFAR],
        out_specs=[HERE, HERE],
        scratch_shapes=[pltpu.SemaphoreType.DMA((value.shape[0] // SLICE,))],
        compiler_params=SMALL,
        cost_estimate=CHEAP,
        name="flip",
    )(kept(value))


def forward_kernel(n, fetch, down, pair, unused, *refs):
    refs = list(refs[unused:])
    xs = [refs.pop(0) for _ in range(n)]
    wg_ref, wu_ref = refs.pop(0), refs.pop(0)
    wd_ref = refs.pop(0) if down else None
    other_ref = refs.pop(0) if pair else None
    act_ref, coef_ref = refs.pop(0), refs.pop(0)
    shares = [refs.pop(0) for _ in range(EXPERTS if pair else down)]
    if fetch:
        sources, sems = (wg_ref, wu_ref), refs.pop()
        wg_ref, wu_ref = refs.pop(0), refs.pop(0)
    acc_ref = refs.pop(0) if down else None
    part = xs[0].shape[0]
    x_ref = xs[0]
    if n > 1:
        x_ref = refs.pop(0)
        for i in range(n):
            x_ref[i * part : (i + 1) * part, :] = xs[i][...]
    steps = wg_ref.shape[1] // (2 * WIDE)

    def copies(j):
        cols = pl.ds(pl.multiple_of(j * (2 * WIDE), (2 * WIDE)), (2 * WIDE))
        return [
            pltpu.make_async_copy(source.at[:, cols], target.at[:, cols], sems.at[j, i])
            for i, (source, target) in enumerate(zip(sources, (wg_ref, wu_ref)))
        ]

    if fetch:
        for j in range(steps):
            for copy in copies(j):
                copy.start()
    if down:
        acc_ref[...] = jnp.zeros_like(acc_ref)

    @pl.loop(0, steps)
    def _(j):
        if fetch:
            for copy in copies(j):
                copy.wait()
        for i in range(2):
            cols = pl.ds(pl.multiple_of(j * (2 * WIDE) + i * WIDE, WIDE), WIDE)
            gate = jnp.dot(x_ref[...], wg_ref[:, cols], preferred_element_type=F32)
            up = jnp.dot(x_ref[...], wu_ref[:, cols], preferred_element_type=F32)
            act, slope = silu_parts(gate)
            act_ref[:, cols] = act.astype(BF16)
            coef_ref[:, cols] = (up * slope).astype(BF16)
            if down:
                hidden = (act[:part] * up[:part]).astype(BF16)
                acc_ref[...] += jnp.dot(hidden, wd_ref[cols, :], preferred_element_type=F32)

    if pair:
        other = other_ref[...].astype(F32)
        for k in range(EXPERTS):
            rows = slice(k * CAP, (k + 1) * CAP)
            block = jnp.concatenate([other[rows], acc_ref[rows, :]], axis=0).astype(BF16)
            shares[k][...] = block
    elif down:
        shares[0][...] = acc_ref[...].astype(BF16)


def forward(xs, wg, wu, wd=None, other=None, fetch=False, earlier=(), cost=CHEAP):
    n, (part, width), cols = len(xs), xs[0].shape, wg.shape[1]
    rows = n * part
    down, pair = wd is not None, other is not None
    shares = [jax.ShapeDtypeStruct((part, width), BF16)] * down
    if pair:
        shares = [jax.ShapeDtypeStruct((2 * CAP, width), BF16)] * EXPERTS
    weights = [kept(wg), kept(wu)] if fetch else [wg, wu]
    return pl.pallas_call(
        functools.partial(forward_kernel, n, fetch, down, pair, len(earlier)),
        out_shape=[jax.ShapeDtypeStruct((rows, cols), BF16)] * 2
        + shares
        + [pltpu.VMEM(wg.shape, wg.dtype)] * (2 * fetch),
        in_specs=[ANYWHERE] * len(earlier)
        + [HERE] * n
        + [AFAR if fetch else HERE] * 2
        + [HERE] * (down + pair),
        scratch_shapes=[pltpu.VMEM((part, width), F32)] * down
        + [pltpu.VMEM((rows, width), BF16)] * (n > 1)
        + [pltpu.SemaphoreType.DMA((cols // (2 * WIDE), 2))] * fetch,
        compiler_params=LARGE,
        cost_estimate=cost,
        name="forward" + "_fetch" * fetch + "_down" * down,
    )(*earlier, *xs, *weights, *([wd] * down), *([other] * pair))


def turn_kernel(_, __, *refs):
    refs[8][: refs[0].shape[1], :] = stacked(refs[0:4]).T.astype(BF16)
    refs[8][refs[0].shape[1] :, :] = stacked(refs[4:8]).T.astype(BF16)


def turn(own, sib, xs, share):
    part = xs[0].shape[0]
    rows = len(xs) * part
    return pl.pallas_call(
        turn_kernel,
        grid_spec=pltpu.PrefetchScalarGridSpec(
            num_scalar_prefetch=2,
            grid=(1,),
            in_specs=[pl.BlockSpec((part, share), lambda j, a, b: (0, a[0]))] * 4
            + [pl.BlockSpec((part, share), lambda j, a, b: (0, b[0]))] * 4,
            out_specs=pl.BlockSpec((2 * share, rows), lambda j, a, b: (0, 0)),
        ),
        out_shape=jax.ShapeDtypeStruct((2 * share, rows), BF16),
        compiler_params=SMALL,
        cost_estimate=CHEAP,
        name="turn",
    )(own, sib, *xs, *xs)


def slopes_kernel(n, *refs):
    gs, acts, coefs = refs[:n], refs[n : 2 * n], refs[2 * n : 3 * n]
    wdt_ref, dg_ref, du_ref, g_ref = refs[3 * n :]
    part = gs[0].shape[0]
    for i in range(n):
        g_ref[i * part : (i + 1) * part, :] = gs[i][...]
    for start in range(0, wdt_ref.shape[1], STRIP):
        cols = slice(start, start + STRIP)
        d_hidden = jnp.dot(g_ref[...], wdt_ref[:, cols], preferred_element_type=F32)
        for i in range(n):
            rows = slice(i * part, (i + 1) * part)
            dg_ref[rows, cols] = (d_hidden[rows] * coefs[i][:, cols].astype(F32)).astype(BF16)
            du_ref[rows, cols] = (d_hidden[rows] * acts[i][:, cols].astype(F32)).astype(BF16)


def slopes(gs, acts, coefs, wdt):
    n, (part, width) = len(gs), gs[0].shape
    return pl.pallas_call(
        functools.partial(slopes_kernel, n),
        out_shape=[jax.ShapeDtypeStruct((n * part, wdt.shape[1]), BF16)] * 2,
        in_specs=[HERE] * (3 * n + 1),
        scratch_shapes=[pltpu.VMEM((n * part, width), BF16)],
        compiler_params=LARGE,
        cost_estimate=CHEAP,
        name="slopes",
    )(*gs, *acts, *coefs, wdt)


def backward_kernel(first, xt_ref, g_ref, act_ref, coef_ref, dg_ref, du_ref, wdt_ref, *refs):
    own_ref, sib_ref = refs[-2:]
    share = own_ref.shape[0] // 2
    for start in range(0, own_ref.shape[1], STRIP):
        here = slice(start, start + STRIP)
        cols = slice(first + start, first + start + STRIP)
        d_hidden = jnp.dot(g_ref[...], wdt_ref[:, cols], preferred_element_type=F32)
        for row, factor_ref, known_ref in ((0, coef_ref, dg_ref), (share, act_ref, du_ref)):
            d_cols = (d_hidden * factor_ref[:, cols].astype(F32)).astype(BF16)
            d_cols = jnp.concatenate([known_ref[:, cols], d_cols], axis=0)
            total = jnp.dot(xt_ref[...], d_cols, preferred_element_type=F32).astype(BF16)
            own_ref[row : row + share, here] = total[:share]
            sib_ref[row : row + share, here] = total[share:]


def backward(xt, g, act, coef, dg, du, wdt, first, cols, earlier=()):
    return pl.pallas_call(
        functools.partial(backward_kernel, first),
        out_shape=[jax.ShapeDtypeStruct((xt.shape[0], cols), BF16)] * 2,
        in_specs=[HERE] * 7 + [ANYWHERE] * len(earlier),
        compiler_params=LARGE,
        cost_estimate=DEAR,
        name="backward",
    )(xt, g, act, coef, dg, du, wdt, *earlier)


def finish_kernel(spans, more, unused, *refs):
    refs = refs[unused:]
    n = len(spans)
    pairs = [refs[2 * i : 2 * i + 2] for i in range(n)]
    gate_ref, up_ref, gate, up, sems = refs[2 * n + 2 * more :]
    share = gate_ref.shape[0]
    low = spans[0][0]
    copies = []
    for i, ((first, cols), (own, got)) in enumerate(zip(spans, pairs)):
        for j, (target, held) in enumerate(((gate_ref, gate), (up_ref, up))):
            rows = slice(j * share, (j + 1) * share)
            here = pl.ds(first - low, cols)
            held[:, here] = (own[rows, :].astype(F32) + got[rows, :].astype(F32)).astype(BF16)
            copies.append(
                pltpu.make_async_copy(held.at[:, here], target.at[:, pl.ds(first, cols)], sems.at[i, j])
            )
            copies[-1].start()
    for copy in copies:
        copy.wait()


def finish(owns, gots, firsts, width, held=(), earlier=()):
    share = owns[0].shape[0] // 2
    spans = tuple((first, own.shape[1]) for first, own in zip(firsts, owns))
    total = sum(cols for _, cols in spans)
    n, more = len(owns), len(held) > 0
    return pl.pallas_call(
        functools.partial(finish_kernel, spans, more, len(earlier)),
        out_shape=[jax.ShapeDtypeStruct((share, width), BF16)] * 2,
        in_specs=[AFAR] * len(earlier) + [HERE] * (2 * n) + [ANYWHERE] * (2 * more),
        out_specs=[ANYWHERE] * 2,
        scratch_shapes=[pltpu.VMEM((share, total), BF16)] * 2 + [pltpu.SemaphoreType.DMA((n, 2))],
        input_output_aliases={len(earlier) + 2 * n: 0, len(earlier) + 2 * n + 1: 1} if more else {},
        compiler_params=SMALL,
        cost_estimate=CHEAP,
        name="finish",
    )(*[kept(v) for v in earlier], *[v for both in zip(owns, gots) for v in both], *held)


def split_kernel(*refs):
    blocks = [refs[SENT.index(k)][...].astype(F32) for k in range(EXPERTS)]
    refs[-2][...] = jnp.concatenate([b[:CAP] for b in blocks], axis=0).astype(BF16)
    refs[-1][...] = jnp.concatenate([b[CAP:] for b in blocks], axis=0).astype(BF16)


def split(blocks, earlier):
    width = blocks[0].shape[1]
    return pl.pallas_call(
        split_kernel,
        out_shape=[jax.ShapeDtypeStruct((EXPERTS * CAP, width), BF16)] * 2,
        in_specs=[HERE] * EXPERTS + [ANYWHERE] * len(earlier),
        compiler_params=SMALL,
        cost_estimate=CHEAP,
        name="split",
    )(*[blocks[k] for k in SENT], *earlier)


def unpack_kernel(placer_ref, mine_ref, got_ref, *refs):
    chosen = placer_ref[...].astype(F32).T.astype(BF16)
    total = jnp.dot(chosen, mine_ref[...], preferred_element_type=F32)
    total += jnp.dot(chosen, got_ref[...], preferred_element_type=F32)
    refs[-1][...] = total.astype(BF16)


def unpack(placer, mine, got, earlier):
    return pl.pallas_call(
        unpack_kernel,
        out_shape=jax.ShapeDtypeStruct((placer.shape[1], mine.shape[1]), BF16),
        in_specs=[HERE] * 3 + [AFAR] * len(earlier),
        compiler_params=SMALL,
        cost_estimate=DEAR,
        name="unpack",
    )(placer, mine, got, *[kept(v) for v in earlier])


def swap(value, axis):
    return lax.ppermute(value, axis, [(0, 1), (1, 0)])


def across_planes(blocks):
    return [blocks[0]] + [
        lax.ppermute(blocks[k], "arch", [(i, i ^ k) for i in range(EXPERTS)]) for k in range(1, EXPERTS)
    ]


def after(values, earlier):
    n = len(values)
    return list(lax.optimization_barrier((*values, *earlier))[:n])


def gathering(designs, archetype, w_gate, w_up, w_down, cotangent):
    far, core = lax.axis_index("far"), lax.axis_index("core")
    scalars = [lax.axis_index("arch"), 2 * far + core, 2 * far + 1 - core]
    scalars = [v.astype(jnp.int32)[None] for v in scalars]
    tokens, width = designs.shape
    share = width // 4
    placer, *blocks = pack(scalars, archetype.reshape(1, tokens), designs, cotangent)
    wd, wdt = flip(after([w_down], [placer])[0])

    x_own = join(across_planes(blocks[:EXPERTS]))
    moved = across_planes(relay(blocks[EXPERTS:], [wdt]))
    x_far, x_near = swap(x_own, "far"), swap(x_own, "half")

    wg, wu = w_gate, w_up
    act0, coef0, share_own = forward([x_own], wg, wu, wd)
    g_own = join(moved, [act0])
    g_far, g_near = swap(g_own, "far"), swap(g_own, "half")
    act1, coef1, *shares = forward([x_near], wg, wu, wd, other=share_own)
    (x_pass,) = relay([x_near], [mark(act1, x_far), g_far])
    (g_pass,) = relay([g_far], [x_pass, g_near])
    x_corner, g_corner = swap(x_pass, "far"), swap(g_pass, "half")
    returned = across_planes(shares)
    act2, coef2 = forward([x_far], wg, wu, earlier=[g_pass], cost=DEAR)
    dg, du = slopes([g_own, g_near, g_far], [act0, act1, act2], [coef0, coef1, coef2], wdt)
    act3, coef3 = forward([x_corner], wg, wu, earlier=[dg])
    mine, theirs = split(returned, [act3])
    got = swap(theirs, "half")
    xt = turn(*scalars[1:], [x_own, x_near, x_far, x_corner], share)

    rest = (xt, g_corner, act3, coef3, dg, du, wdt)
    cols = w_down.shape[0]
    cut = cols // 2
    own0, sib0 = backward(*rest, 0, cut)
    own1, sib1 = backward(*rest, cut, cols - cut, [own0])
    got0, got1 = swap(sib0, "core"), swap(sib1, "core")
    held = finish([own0], [got0], (0,), cols)
    outputs = unpack(placer, mine, got, held[:1])
    grad_gate, grad_up = finish([own1], [got1], (cut,), cols, held)
    return outputs, grad_gate, grad_up


def reducing(designs, archetype, w_gate, w_up, w_down, cotangent):
    width = designs.shape[1]
    owners = lax.axis_size("expert")
    sharers = owners // EXPERTS
    hidden_cols = w_gate.shape[1]
    labels = archetype[:, 0]
    onehot = (labels[:, None] == jnp.arange(EXPERTS, dtype=jnp.int32)[None, :]).astype(jnp.int32)
    ranks = jnp.cumsum(onehot, axis=0) - onehot
    target = labels * CAP + jnp.sum(ranks * onehot, axis=1)
    placer = (jnp.arange(EXPERTS * CAP, dtype=jnp.int32)[:, None] == target[None, :]).astype(BF16)
    received = []
    for rows in (designs, cotangent):
        packed = jnp.dot(placer, rows, preferred_element_type=F32).astype(BF16)
        send = jnp.repeat(packed.reshape(EXPERTS, CAP, width), sharers, axis=0)
        received.append(
            lax.all_to_all(send, "expert", split_axis=0, concat_axis=0, tiled=True).reshape(
                owners * CAP, width
            )
        )
    flat_x, flat_g = received
    gate = jnp.dot(flat_x, w_gate, preferred_element_type=F32)
    up = jnp.dot(flat_x, w_up, preferred_element_type=F32)
    act, slope = silu_parts(gate)
    hidden = (act * up).astype(BF16)
    partial_value = (
        jnp.dot(hidden, w_down, preferred_element_type=F32).astype(BF16).reshape(owners, CAP, width)
    )
    returned = lax.all_to_all(partial_value, "expert", split_axis=0, concat_axis=0, tiled=True)
    summed = jnp.sum(returned.astype(F32).reshape(EXPERTS, sharers, CAP, width), axis=1).reshape(
        EXPERTS * CAP, width
    )
    outputs = jnp.take(summed, target, axis=0).astype(BF16)
    d_hidden = contract_cols(flat_g, w_down)
    d_gate = (d_hidden * up * slope).astype(BF16)
    d_up = (d_hidden * act).astype(BF16)
    grads = jnp.concatenate([contract_rows(flat_x, d_gate), contract_rows(flat_x, d_up)], axis=1)
    mine = lax.psum_scatter(grads.astype(BF16), "dp", scatter_dimension=0, tiled=True)
    return outputs, mine[:, :hidden_cols], mine[:, hidden_cols:]


def solution(mesh):
    dp, owners = mesh.devices.shape
    if (dp, owners) == (4, 2 * EXPERTS):
        rows, cols = ("far", "core"), ("arch", "half")
        mesh = Mesh(mesh.devices.reshape(2, 2, EXPERTS, 2), rows + cols)
        body = gathering
    else:
        rows, cols = ("dp",), ("expert",)
        body = reducing
    tokens = P(rows + cols, None)
    return jax.shard_map(
        body,
        mesh=mesh,
        in_specs=(tokens, tokens, P(None, cols), P(None, cols), P(cols, None), tokens),
        out_specs=(tokens, P(rows, cols), P(rows, cols)),
        check_vma=False,
    )
```
